128 devices in a mesh: dp: 8 (over y, core), fs: 16 (over z, x).
Axes of the slice: x: 4, y: 4, z: 4, core: 2. Of those that a mesh axis runs over, the one named last changes fastest.
Arguments:
- hidden_in: bfloat16 [2, 32768, 768], P(None, ('dp', 'fs')), may hold values from -24 to 24
- out_grad: bfloat16 [2, 32768, 768], P(None, ('dp', 'fs')), may hold values from -24 to 24
- segments: int32 [2, 32768], P(None, ('dp', 'fs')), may hold values from -1 to 4, as said below
- mask_pos: int32 [2, 128, 16, 2], P(None, ('dp', 'fs')), may hold values from -1 to 255, as said below
- mask_labels: int32 [2, 128, 16, 2], replicated, may hold values from -1 to 51199, as said below
- loss_scale: float32 [], replicated, may hold values from 8192 to 32768
- w_qkv: bfloat16 [768, 2304], P(('dp', 'fs')), may hold values from -0.21875 to 0.21875
- b_query: bfloat16 [768], P(('dp', 'fs')), may hold values from -1.75 to 1.75
- b_value: bfloat16 [768], P(('dp', 'fs')), may hold values from -1.75 to 1.75
- w_attn: bfloat16 [768, 768], P(('dp', 'fs')), may hold values from -1.75 to 1.75
- b_attn: bfloat16 [768], P(('dp', 'fs')), may hold values from -1.75 to 1.75
- attn_gain: bfloat16 [768], P(('dp', 'fs')), may hold values from 0.25 to 1.75
- attn_shift: bfloat16 [768], P(('dp', 'fs')), may hold values from -1.75 to 1.75
- w_expand: bfloat16 [768, 3072], P(('dp', 'fs')), may hold values from -0.21875 to 0.21875
- b_expand: bfloat16 [3072], P(('dp', 'fs')), may hold values from -1.75 to 1.75
- w_shrink: bfloat16 [3072, 768], P(('dp', 'fs')), may hold values from -0.109375 to 0.109375
- b_shrink: bfloat16 [768], P(('dp', 'fs')), may hold values from -1.75 to 1.75
- ffn_gain: bfloat16 [768], P(('dp', 'fs')), may hold values from 0.25 to 1.75
- ffn_shift: bfloat16 [768], P(('dp', 'fs')), may hold values from -1.75 to 1.75
- w_dense: bfloat16 [768, 768], P(('dp', 'fs')), may hold values from -0.21875 to 0.21875
- b_dense: bfloat16 [768], P(('dp', 'fs')), may hold values from -1.75 to 1.75
- dense_gain: bfloat16 [768], P(('dp', 'fs')), may hold values from 0.25 to 1.75
- dense_shift: bfloat16 [768], P(('dp', 'fs')), may hold values from -1.75 to 1.75
- w_vocab: bfloat16 [768, 51200], P(None, ('dp', 'fs')), may hold values from -0.21875 to 0.21875
- b_vocab: bfloat16 [51200], P(('dp', 'fs'))
Outputs:
- activations: bfloat16 [2, 32768, 768], P(None, ('dp', 'fs'))
- loss: float32 [], replicated
- hidden_grad: float32 [2, 32768, 768], P(None, ('dp', 'fs'))
- g_qkv: float32 [768, 2304], P(('dp', 'fs'))
- g_query: float32 [768], P(('dp', 'fs'))
- g_value: float32 [768], P(('dp', 'fs'))
- g_attn: float32 [768, 768], P(('dp', 'fs'))
- g_attn_bias: float32 [768], P(('dp', 'fs'))
- g_attn_gain: float32 [768], P(('dp', 'fs'))
- g_attn_shift: float32 [768], P(('dp', 'fs'))
- g_expand: float32 [768, 3072], P(('dp', 'fs'))
- g_expand_bias: float32 [3072], P(('dp', 'fs'))
- g_shrink: float32 [3072, 768], P(('dp', 'fs'))
- g_shrink_bias: float32 [768], P(('dp', 'fs'))
- g_ffn_gain: float32 [768], P(('dp', 'fs'))
- g_ffn_shift: float32 [768], P(('dp', 'fs'))
- g_dense: float32 [768, 768], P(('dp', 'fs'))
- g_dense_bias: float32 [768], P(('dp', 'fs'))
- g_dense_gain: float32 [768], P(('dp', 'fs'))
- g_dense_shift: float32 [768], P(('dp', 'fs'))
- g_vocab: float32 [768, 51200], P(None, ('dp', 'fs'))
- g_vocab_bias: float32 [51200], P(('dp', 'fs'))
The draws below stay inside these ranges and needn't reach their ends.
Inputs may be any that keep to these rules, and one draw needn't show every extreme that they name: `segments`: in each micro-batch each device's block of 256 tokens holds sequences numbered 0, 1, ... in order, then -1 on padding at its end; each sequence has 32 to 256 tokens and the first at least half of 256; in every micro-batch some device's block is one sequence of 256 tokens, and some other device's block holds the most sequences. `mask_pos`: entry [m, d, f, s] is the place within device d's block of a masked token whose row goes to the device with d's dp index and fs index f, or -1 for an empty slot; the places of one device and micro-batch are distinct and never padding; in every micro-batch some device fills all its slots, and some device receives 2 rows from every device with its dp index. `mask_labels`: entry [m, o, j, s] is the label of the row in slot s that device o receives from the device with o's dp index and fs index j, and -1 exactly where that slot of mask_pos is empty.
All inputs are finite; a program needn't handle non-finite values.
Results may differ from the reference program's by a relative error of at most 0.015.
Values may be sent and summed in bfloat16 or wider, within the bound.
No kernel may reach another device: no remote copies, remote signals or barrier semaphores. Data moves between devices by JAX's collectives and lax.ppermute only.
A program may use at most 256 MiB of HBM per device.

```python
import math
import jax
import jax.numpy as jnp
from jax import lax

D = 768
HEADS = 12
FF = 3072
V = 51200
TOK_DEV = 256
MB = 2
SLOT = 2
MIN_SEQ = 32
HEAD_DIM = 64
DP_ROWS = 8
FS_PEERS = 16
TOKENS = 32768
N_DP = 8
N_FS = 16
DEVICES = 128


def token_layout(key):
    seq_keys = jax.random.split(jax.random.fold_in(key, 101), 5)
    blocks = MB * DEVICES
    count = TOK_DEV // MIN_SEQ
    first = jax.random.randint(seq_keys[0], (blocks, 1), TOK_DEV // 2, TOK_DEV + 1)
    chosen = jax.random.randint(seq_keys[1], (MB, 1), 0, DEVICES)
    chosen_many = (chosen + 1 + jax.random.randint(seq_keys[4], (MB, 1), 0, DEVICES - 1)) % DEVICES
    device_ids = jnp.broadcast_to(jnp.arange(DEVICES, dtype=jnp.int32)[None, :], (MB, DEVICES))
    is_long = (device_ids == chosen).reshape(blocks, 1)
    is_many = (device_ids == chosen_many).reshape(blocks, 1)
    first = jnp.where(is_long, TOK_DEV, first)
    first = jnp.where(is_many, TOK_DEV // 2, first)
    power = jax.random.randint(seq_keys[2], (blocks, count), 0, 4)
    extra = jax.random.randint(seq_keys[3], (blocks, count), 0, MIN_SEQ)
    others = jnp.minimum(jnp.left_shift(jnp.int32(MIN_SEQ), power) + extra, TOK_DEV)
    others = jnp.where(is_many, MIN_SEQ, others)
    lengths = jnp.concatenate([first, others], axis=1)
    ends = jnp.cumsum(lengths, axis=1)
    fits = ends <= TOK_DEV
    used = jnp.max(jnp.where(fits, ends, 0), axis=1)
    place = jnp.arange(TOK_DEV, dtype=jnp.int32)
    bounds = jnp.where(fits, ends, TOK_DEV + 1)
    number = jnp.sum((bounds[:, None, :] <= place[None, :, None]).astype(jnp.int32), axis=2)
    segments = jnp.where(place[None, :] < used[:, None], number, -1)
    mask_keys = jax.random.split(jax.random.fold_in(key, 202), 7)
    draw = jax.random.randint(mask_keys[0], (MB, DEVICES, FS_PEERS, SLOT), 0, 3 * (DEVICES - 1))
    device = jnp.arange(DEVICES, dtype=jnp.int32)[None, :, None, None]
    valid = draw < DEVICES - 1 + 2 * device
    row_star = jax.random.randint(mask_keys[1], (MB, 1, 1, 1), 0, DP_ROWS)
    col_star = jax.random.randint(mask_keys[2], (MB, 1, 1, 1), 0, FS_PEERS)
    dest = jnp.arange(FS_PEERS, dtype=jnp.int32)[None, None, :, None]
    valid = valid | (device // FS_PEERS == row_star) & (dest == col_star)
    flat_valid = valid.reshape(blocks, FS_PEERS * SLOT)
    score = jax.random.randint(mask_keys[3], (blocks, TOK_DEV), 0, 65536) * TOK_DEV + place[None, :]
    score = score + jnp.where(segments < 0, 1 << 28, 0)
    order = jnp.argsort(score, axis=1).astype(jnp.int32)
    rank = jnp.cumsum(flat_valid.astype(jnp.int32), axis=1) - 1
    taken = jnp.take_along_axis(order, jnp.maximum(rank, 0), axis=1)
    positions = jnp.where(flat_valid, taken, -1).reshape(MB, DEVICES, FS_PEERS, SLOT)
    common = jax.random.randint(mask_keys[4], (MB, DEVICES, FS_PEERS, SLOT), 0, 256)
    broad = jax.random.randint(mask_keys[5], (MB, DEVICES, FS_PEERS, SLOT), 0, V)
    pick = jax.random.randint(mask_keys[6], (MB, DEVICES, FS_PEERS, SLOT), 0, 4)
    labels = jnp.where(pick == 0, common, broad)
    labels = jnp.where(valid, labels, -1)
    owner = labels.reshape(MB, DP_ROWS, FS_PEERS, FS_PEERS, SLOT).transpose(0, 1, 3, 2, 4).reshape(MB, DEVICES, FS_PEERS, SLOT)
    return (segments.reshape(MB, DEVICES * TOK_DEV).astype(jnp.int32), positions.astype(jnp.int32), owner.astype(jnp.int32))


def draw_segments(key, part):
    return token_layout(key)[0]


def draw_mask_pos(key, part):
    return token_layout(key)[1]


def draw_mask_labels(key, part):
    return token_layout(key)[2]


def draw_b_vocab(key, part):
    place = jnp.arange(V, dtype=jnp.float32) / V
    noise = jax.random.normal(key, (V,), jnp.float32)
    return (noise + 1.1 * place + 4.0).astype(jnp.bfloat16)


def raised(entries, own_key, source, target, blocks, factor):
    owner, partner = [(jnp.arange(entries.shape[dim]) // (entries.shape[dim] // blocks)).reshape([-1 if axis == dim else 1 for axis in range(entries.ndim)]) for dim in (source, target)]
    chosen = jax.random.permutation(own_key, blocks)[partner]
    strong = (owner == chosen) | (owner == (partner + blocks // 2) % blocks)
    return jnp.where(strong, factor * entries, entries)


def steps_of(rng, shape, cuts, low, top_value):
    level, own = 1.0, jax.random.fold_in(rng, 6)
    for axis_at, parts in cuts:
        draws = jnp.exp(jax.random.uniform(jax.random.fold_in(own, axis_at), (parts,), jnp.float32, low / len(cuts), top_value / len(cuts)))
        level = level * jnp.repeat(draws, shape[axis_at] // parts).reshape([-1 if axis == axis_at else 1 for axis in range(len(shape))])
    return level


def bell_draw(key, dims, scale, limit, pieces=(), held_as=jnp.bfloat16):
    drawn = jax.random.normal(key, dims, jnp.float32) * scale
    if len(pieces) > 0:
        drawn = steps_of(key, dims, pieces, -0.22, 0.18) * drawn
    return jnp.clip(drawn, min=-limit, max=limit).astype(held_as)


def bell_draw_with(rng, extent, width, most, cuts, heavy, kind=jnp.bfloat16):
    values = width * jax.random.normal(rng, extent, jnp.float32)
    if cuts:
        values = values * steps_of(rng, extent, cuts, -0.22, 0.18)
    return jnp.clip(raised(values, jax.random.fold_in(rng, 3), *heavy), -most, most).astype(kind)


def setup_inputs(seed: int = 0) -> dict:
    streams_of = jax.random.split(jax.random.key(seed), 26)
    return {
        "hidden_in": bell_draw_with(streams_of[0], (MB, TOKENS, D), 1.0, 24.0, ((1, 128),), (1, 2, 128, 5.5)),
        "out_grad": bell_draw_with(streams_of[1], (MB, TOKENS, D), 1.0, 24.0, ((1, 128),), (1, 2, 128, 5.5)),
        "segments": draw_segments(jax.random.fold_in(streams_of[25], 71), 0),
        "mask_pos": draw_mask_pos(jax.random.fold_in(streams_of[25], 71), 0),
        "mask_labels": draw_mask_labels(jax.random.fold_in(streams_of[25], 71), 0),
        "loss_scale": jnp.clip(jnp.exp(jax.random.uniform(streams_of[5], (), jnp.float32, math.log(8192.0), math.log(32768.0))), 8192.0, 32768.0),
        "w_qkv": bell_draw(streams_of[6], (D, 3 * D), D ** -0.5, 0.21875, ((0, 128),)),
        "b_query": bell_draw(streams_of[7], (D,), 0.3, 1.75, ((0, 128),)),
        "b_value": bell_draw(streams_of[8], (D,), 0.3, 1.75, ((0, 128),)),
        "w_attn": bell_draw(streams_of[9], (D, D), (D // 64) ** -0.5, 1.75, ((0, 128),)),
        "b_attn": bell_draw(streams_of[10], (D,), 0.3, 1.75, ((0, 128),)),
        "attn_gain": jnp.clip(1.0 + 0.15 * jax.random.normal(streams_of[11], (D,), jnp.float32), 0.25, 1.75).astype(jnp.bfloat16),
        "attn_shift": bell_draw(streams_of[12], (D,), 0.3, 1.75, ((0, 128),)),
        "w_expand": bell_draw(streams_of[13], (D, FF), D ** -0.5, 0.21875, ((0, 128),)),
        "b_expand": bell_draw(streams_of[14], (FF,), 0.3, 1.75, ((0, 128),)),
        "w_shrink": bell_draw(streams_of[15], (FF, D), FF ** -0.5, 0.109375, ((0, 128),)),
        "b_shrink": bell_draw(streams_of[16], (D,), 0.3, 1.75, ((0, 128),)),
        "ffn_gain": jnp.clip(1.0 + 0.15 * jax.random.normal(streams_of[17], (D,), jnp.float32), 0.25, 1.75).astype(jnp.bfloat16),
        "ffn_shift": bell_draw(streams_of[18], (D,), 0.3, 1.75, ((0, 128),)),
        "w_dense": bell_draw(streams_of[19], (D, D), D ** -0.5, 0.21875, ((0, 128),)),
        "b_dense": bell_draw(streams_of[20], (D,), 0.3, 1.75, ((0, 128),)),
        "dense_gain": jnp.clip(1.0 + 0.15 * jax.random.normal(streams_of[21], (D,), jnp.float32), 0.25, 1.75).astype(jnp.bfloat16),
        "dense_shift": bell_draw(streams_of[22], (D,), 0.3, 1.75, ((0, 128),)),
        "w_vocab": bell_draw(streams_of[23], (D, V), D ** -0.5, 0.21875, ((1, 128),)),
        "b_vocab": draw_b_vocab(jax.random.fold_in(streams_of[25], 71), 0),
    }


HIGH = lax.Precision.HIGHEST
EPS = 1e-05
MASKED = -1e+30

@jax.custom_vjp
def low(v):
    return lax.optimization_barrier(v.astype(jnp.bfloat16)).astype(jnp.float32)

@jax.custom_vjp
def low_back(v):
    return v

def low_keep(v):
    return (low(v), None)

def low_pass(kept, grad):
    return (grad,)

def back_keep(v):
    return (v, None)

def back_low(kept, grad):
    return (low(grad),)
low.defvjp(low_keep, low_pass)
low_back.defvjp(back_keep, back_low)

def rounded_both(values):
    return low_back(low(values))

def matmul(left, right):
    return jnp.dot(left, right, precision=HIGH, preferred_element_type=jnp.float32)

def layer_norm(values, gain, shift):
    center = values - lax.optimization_barrier(jnp.mean(values, axis=-1, keepdims=True))
    return center * lax.rsqrt(lax.optimization_barrier(jnp.mean(center * center, axis=-1, keepdims=True)) + EPS) * gain + shift

def gelu_exact(values):
    return jax.nn.gelu(values, approximate=False)

def encode_block(layer, block, seg):
    w_qkv, b_query, b_value, w_attn, b_attn, attn_gain, attn_shift, w_expand, b_expand, w_shrink, b_shrink, ffn_gain, ffn_shift = layer
    tokens = block.shape[0]
    united = matmul(block, w_qkv)
    query = rounded_both(united[:, :D] + b_query).reshape(tokens, HEADS, HEAD_DIM)
    keys = rounded_both(united[:, D:2 * D]).reshape(tokens, HEADS, HEAD_DIM)
    values = rounded_both(united[:, 2 * D:] + b_value).reshape(tokens, HEADS, HEAD_DIM)
    raw = jnp.einsum('qhd,khd->hqk', query, keys, precision=HIGH)
    scores = low_back(raw * HEAD_DIM ** (-0.5))
    allowed = (seg[:, None] == seg[None, :])[None]
    probs = jax.nn.softmax(jnp.where(allowed, scores, MASKED), axis=-1)
    attended = rounded_both(jnp.einsum('hqk,khd->qhd', low(probs), values, precision=HIGH).reshape(tokens, D))
    branch = low_back(matmul(attended, w_attn) + b_attn)
    first = layer_norm(block + branch, attn_gain, attn_shift)
    pre = low_back(matmul(low(first), w_expand) + b_expand)
    ffn = low_back(matmul(low(gelu_exact(pre)), w_shrink) + b_shrink)
    return layer_norm(first + ffn, ffn_gain, ffn_shift)

def reference(hidden_in, out_grad, segments, mask_pos, mask_labels, loss_scale, w_qkv, b_query, b_value, w_attn, b_attn, attn_gain, attn_shift, w_expand, b_expand, w_shrink, b_shrink, ffn_gain, ffn_shift, w_dense, b_dense, dense_gain, dense_shift, w_vocab, b_vocab):
    params = (w_qkv, b_query, b_value, w_attn, b_attn, attn_gain, attn_shift, w_expand, b_expand, w_shrink, b_shrink, ffn_gain, ffn_shift, w_dense, b_dense, dense_gain, dense_shift, w_vocab, b_vocab)
    weights = tuple((item.astype(jnp.float32) for item in params))
    group = math.gcd(MB * DEVICES, max(1, 4096 // TOK_DEV))
    seg_blocks = segments.reshape(-1, group, TOK_DEV)
    owner_pos = mask_pos.reshape(MB, N_DP, N_FS, N_FS, SLOT).transpose(0, 1, 3, 2, 4)
    source = jnp.arange(N_DP, dtype=jnp.int32)[:, None] * N_FS + jnp.arange(N_FS, dtype=jnp.int32)[None, :]
    source = jnp.broadcast_to(source[None, :, None, :, None], owner_pos.shape)
    batch_base = jnp.broadcast_to((jnp.arange(MB, dtype=jnp.int32) * TOKENS)[:, None, None, None, None], owner_pos.shape)
    flat_index = (batch_base + source * TOK_DEV + jnp.maximum(owner_pos, 0)).reshape(-1).astype(jnp.int32)
    row_live = (owner_pos >= 0).reshape(-1)
    labels = mask_labels.reshape(MB, -1)
    label_live = (labels >= 0).astype(jnp.float32)
    counts = lax.optimization_barrier(jnp.sum(label_live, axis=1))
    row_weight = (label_live / (counts[:, None] * MB)).reshape(-1)
    flat_labels = jnp.maximum(labels, 0).reshape(-1).astype(jnp.int32)
    total_rows = flat_labels.shape[0]
    row_block = math.gcd(total_rows, 1024)

    def forward(inner, tokens_in):
        layer = inner[:13]
        w_dense_f, b_dense_f, dense_gain_f, dense_shift_f, w_vocab_f, b_vocab_f = inner[13:]
        blocks = tokens_in.reshape(-1, group, TOK_DEV, D)

        def encode_group(pair):
            return jax.vmap(lambda one, seg: encode_block(layer, one, seg))(pair[0], pair[1])
        outputs = lax.map(jax.checkpoint(encode_group), (blocks, seg_blocks))
        settled = low(outputs.reshape(MB, TOKENS, D))
        picked = jnp.take(settled.reshape(MB * TOKENS, D), flat_index, axis=0)
        rows_in = low_back(jnp.where(row_live[:, None], picked, 0.0))
        dense = low_back(matmul(rows_in, w_dense_f) + b_dense_f)
        head_rows = low(layer_norm(gelu_exact(dense), dense_gain_f, dense_shift_f))

        def block_loss(pair):
            rows, labs, wts = pair
            logits = low_back(matmul(rows, w_vocab_f) + b_vocab_f)
            chosen = jnp.take_along_axis(logits, labs[:, None], axis=1)[:, 0]
            return jnp.sum(wts * (jax.nn.logsumexp(logits, axis=1) - chosen))
        losses = lax.map(jax.checkpoint(block_loss), (head_rows.reshape(-1, row_block, D), flat_labels.reshape(-1, row_block), row_weight.reshape(-1, row_block)))
        return (settled, jnp.sum(losses))
    outputs, pullback = jax.vjp(forward, weights, hidden_in.astype(jnp.float32))
    grads, input_grad = pullback((out_grad.astype(jnp.float32), loss_scale))
    return (outputs[0].astype(jnp.bfloat16), outputs[1], input_grad, grads[0], grads[1], grads[2], grads[3], grads[4], grads[5], grads[6], grads[7], grads[8], grads[9], grads[10], grads[11], grads[12], grads[13], grads[14], grads[15], grads[16], grads[17], grads[18])
```

```python
import functools

import jax
import jax.numpy as jnp
from jax import lax
from jax.experimental import pallas as pl
from jax.experimental.pallas import tpu as pltpu
from jax.sharding import Mesh
from jax.sharding import PartitionSpec as P

HEAD_DIM = 64
EPS = 1e-05
HALF_ROOT = 0.7071067811865476
NORMAL_PEAK = 0.3989422804014327
MASKED = -1e30

BF = jnp.bfloat16
F32 = jnp.float32
NY, NC, NZ, NX = 4, 2, 4, 4
SIZES = {"y": NY, "c": NC, "z": NZ, "x": NX}
EVERY = ("y", "c", "z", "x")


def fetch(array, axis, k):
    n = SIZES[axis]
    return lax.ppermute(array, axis, [((i + k) % n, i) for i in range(n)])


def give(array, axis, k):
    n = SIZES[axis]
    return lax.ppermute(array, axis, [(i, (i + k) % n) for i in range(n)])


def yz_pairs(a, b):
    return [
        (((y + a) % NY) * NZ + (z + b) % NZ, y * NZ + z) for y in range(NY) for z in range(NZ)
    ]


def fetch_yz(array, a, b):
    if a == 0 and b == 0:
        return array
    return lax.ppermute(array, ("y", "z"), yz_pairs(a, b))


def give_yz(array, a, b):
    if a == 0 and b == 0:
        return array
    return lax.ppermute(array, ("y", "z"), [(j, i) for i, j in yz_pairs(a, b)])


def in_order(pieces, index):
    n = len(pieces)
    twice = jnp.stack(pieces + pieces)
    return lax.dynamic_slice_in_dim(twice, (n - index) % n, n, 0)


def place_kernel(route, coords, *refs):
    first, second = route
    own, other, out, sems = refs[0:4], refs[4:8], refs[8], refs[9]
    at = {"y": coords[0], "c": coords[1], "z": coords[2]}
    copies = []
    for kb in range(4):
        for ka in range(4):
            place = {
                first: lax.rem(at[first] + ka, 4),
                second: lax.rem(at[second] + kb, 4),
            }
            for kc, source in enumerate((own, other)):
                core = lax.rem(at["c"] + kc, 2)
                copy = pltpu.make_async_copy(
                    source[kb].at[ka],
                    out.at[place["y"], core, place["z"]],
                    sems.at[kc, kb, ka],
                )
                copy.start()
                copies.append(copy)
    for copy in copies:
        copy.wait()


def place(own, other, route, coords):
    _, rows, width = own[0].shape
    anywhere = pl.BlockSpec(memory_space=pl.ANY)
    return pl.pallas_call(
        functools.partial(place_kernel, route),
        out_shape=jax.ShapeDtypeStruct((NY, NC, NZ, rows, width), own[0].dtype),
        in_specs=[pl.BlockSpec(memory_space=pltpu.SMEM)] + [anywhere] * 8,
        out_specs=anywhere,
        scratch_shapes=[pltpu.SemaphoreType.DMA((2, 4, 4))],
        cost_estimate=pl.CostEstimate(
            flops=0, bytes_accessed=2 * 32 * rows * width * 2, transcendentals=0
        ),
    )(coords, *own, *other)


def gather_pieces(block, route):
    first, second = route
    plane = jnp.stack([block] + [fetch(block, first, k) for k in (1, 2, 3)])
    own = [plane] + [fetch(plane, second, k) for k in (1, 2, 3)]
    other = [fetch(piece, "c", 1) for piece in own]
    return own, other


def gather_weight(shard, route, coords):
    pieces = [shard] + [fetch(shard, "x", k) for k in (1, 2, 3)]
    block = in_order(pieces, lax.axis_index("x")).reshape(NX * shard.shape[0], shard.shape[1])
    own, other = gather_pieces(block, route)
    return place(own, other, route, coords).reshape(-1, shard.shape[1])


def total(parts):
    out = parts[0].astype(F32)
    for part in parts[1:]:
        out = out + part.astype(F32)
    return out


def scatter_sum(grad, route):
    n = grad.shape[1]
    rows = grad.shape[0] // 128
    at = {axis: lax.axis_index(axis) for axis in EVERY}
    grad = grad.astype(BF).reshape(NY, NC, NZ, NX * rows, n)
    away = lax.dynamic_index_in_dim(grad, 1 - at["c"], 1, False)
    here = lax.dynamic_index_in_dim(grad, at["c"], 1, False)
    got = give(away, "c", 1)
    for axis in route:
        dim = 0 if (axis == "y" or here.ndim == 3) else 1

        def cut(k):
            index = (at[axis] + k) % 4
            mine = lax.dynamic_index_in_dim(here, index, dim, False)
            if got is None:
                return mine
            theirs = lax.dynamic_index_in_dim(got, index, dim, False)
            return (mine.astype(F32) + theirs.astype(F32)).astype(BF)

        parts = [cut(0)] + [give(cut(k), axis, k) for k in (1, 2, 3)]
        here, got = total(parts).astype(BF), None
    here = here.reshape(NX, rows, n)
    parts = [lax.dynamic_index_in_dim(here, at["x"], 0, False)]
    for k in (1, 2, 3):
        parts.append(
            give(lax.dynamic_index_in_dim(here, (at["x"] + k) % NX, 0, False), "x", k)
        )
    return total(parts)


def sum_everywhere(value):
    for axis in EVERY:
        n = SIZES[axis]
        pieces = [value] + [fetch(value, axis, k) for k in range(1, n)]
        value = jnp.sum(in_order(pieces, lax.axis_index(axis)), axis=0)
    return value


def gelu_value(values):
    return 0.5 * values * (1.0 + lax.erf(values * HALF_ROOT))


def gelu_slope(values):
    return 0.5 * (1.0 + lax.erf(values * HALF_ROOT)) + values * NORMAL_PEAK * jnp.exp(
        -0.5 * values * values
    )


def layer_norm(values, gain, shift):
    center = values - jnp.mean(values, axis=-1, keepdims=True)
    inverse = lax.rsqrt(jnp.mean(center * center, axis=-1, keepdims=True) + EPS)
    normed = center * inverse
    return (normed * gain + shift, normed, inverse)


def norm_back(grad, normed, inverse, gain):
    scaled = grad * gain
    inner = (
        scaled
        - jnp.mean(scaled, axis=-1, keepdims=True)
        - normed * jnp.mean(scaled * normed, axis=-1, keepdims=True)
    )
    return inner * inverse


def column_sum(values):
    return jnp.sum(values, axis=0, dtype=F32)


def matmul(left, right):
    return jnp.dot(left, right, preferred_element_type=F32)


def matmul_tn(left, right):
    return lax.dot_general(left, right, (((0,), (0,)), ((), ())), preferred_element_type=F32)


def matmul_nt(left, right):
    return lax.dot_general(left, right, (((1,), (1,)), ((), ())), preferred_element_type=F32)


def body(
    hidden_in,
    out_grad,
    segments,
    mask_pos,
    mask_labels,
    loss_scale,
    w_qkv,
    b_query,
    b_value,
    w_attn,
    b_attn,
    attn_gain,
    attn_shift,
    w_expand,
    b_expand,
    w_shrink,
    b_shrink,
    ffn_gain,
    ffn_shift,
    w_dense,
    b_dense,
    dense_gain,
    dense_shift,
    w_vocab,
    b_vocab,
):
    micro, block, width = hidden_in.shape
    tokens = micro * block
    heads = width // HEAD_DIM
    factor = HEAD_DIM ** (-0.5)
    at = {axis: lax.axis_index(axis) for axis in EVERY}
    coords = jnp.stack([at["y"], at["c"], at["z"]]).astype(jnp.int32)

    vectors = (
        b_query,
        b_value,
        b_attn,
        attn_gain,
        attn_shift,
        b_shrink,
        ffn_gain,
        ffn_shift,
        b_dense,
        dense_gain,
        dense_shift,
    )
    small = jnp.concatenate(
        [jnp.stack(vectors, axis=1), b_expand.reshape(w_qkv.shape[0], -1)], axis=1
    )
    small = jnp.pad(small, ((0, 0), (0, 128 - small.shape[1])))
    qkv_all = gather_weight(jnp.concatenate([w_qkv, small], axis=1), ("y", "z"), coords)
    attn_full = gather_weight(w_attn, ("z", "y"), coords)
    expand_full = gather_weight(w_expand, ("z", "y"), coords)
    shrink_full = gather_weight(w_shrink, ("y", "z"), coords)
    dense_full = gather_weight(w_dense, ("z", "y"), coords)
    qkv_full = qkv_all[:, : 3 * width]
    rows_of = qkv_all[:, 3 * width :].T.astype(F32)
    (
        b_query,
        b_value,
        b_attn,
        attn_gain,
        attn_shift,
        b_shrink,
        ffn_gain,
        ffn_shift,
        b_dense,
        dense_gain,
        dense_shift,
    ) = (rows_of[i] for i in range(len(vectors)))
    b_expand = qkv_all[:, 3 * width + 11 : 3 * width + 15].astype(F32).reshape(-1)

    own_w = w_vocab.T
    piece_w = [own_w] + [fetch(own_w, "x", k) for k in (1, 2, 3)]
    piece_b = [b_vocab] + [fetch(b_vocab, "x", k) for k in (1, 2, 3)]
    half_w = jnp.stack(piece_w)
    half_b = jnp.stack(piece_b)
    per = own_w.shape[0]
    vocab_w = jnp.concatenate([half_w, fetch(half_w, "c", 1)]).reshape(-1, width)
    vocab_b = jnp.concatenate([half_b, fetch(half_b, "c", 1)]).reshape(-1).astype(F32)
    start = jnp.stack(
        [
            (((at["y"] * NC + (at["c"] + kc) % NC) * NZ + at["z"]) * NX + (at["x"] + kx) % NX)
            * per
            for kc in range(NC)
            for kx in range(NX)
        ]
    )
    column = (start[:, None] + jnp.arange(per, dtype=jnp.int32)[None, :]).reshape(-1)

    flat_labels = mask_labels.reshape(micro, -1)
    counts = jnp.sum((flat_labels >= 0).astype(F32), axis=1)
    norms = 1.0 / (counts * micro)
    slots = mask_labels.shape[-1]
    peers = NZ * NX
    grid = mask_labels.reshape(micro, NY, NC, peers, NZ, NX, slots)
    grid = lax.dynamic_index_in_dim(grid, at["c"], 2, False)
    grid = lax.dynamic_index_in_dim(grid, at["x"], 4, False)
    grid = grid.transpose(1, 3, 0, 2, 4).reshape(NY, NZ, -1)
    grid = jnp.concatenate([grid, grid], axis=0)
    grid = lax.dynamic_slice_in_dim(grid, at["y"], NY, 0)
    grid = jnp.concatenate([grid, grid], axis=1)
    grid = lax.dynamic_slice_in_dim(grid, at["z"], NZ, 1)
    labels = grid.reshape(-1)
    rows = micro * peers * slots
    row_norm = jnp.broadcast_to(norms[None, :, None], (NY * NZ, micro, peers * slots)).reshape(-1)
    live = (labels >= 0).astype(F32)
    row_weight = live * row_norm
    positions = mask_pos.reshape(micro, -1)
    shifted = jnp.where(
        positions >= 0, positions + block * jnp.arange(micro, dtype=jnp.int32)[:, None], -1
    ).reshape(-1)
    select = (shifted[:, None] == jnp.arange(tokens, dtype=jnp.int32)[None, :]).astype(BF)

    x = hidden_in.reshape(tokens, width)
    united = matmul(x, qkv_full)

    def split(values):
        return values.astype(BF).reshape(micro, block, heads, HEAD_DIM)

    query = split(united[:, :width] + b_query)
    keys = split(united[:, width : 2 * width])
    values = split(united[:, 2 * width :] + b_value)
    allowed = (segments[:, :, None] == segments[:, None, :])[:, None]
    raw = jnp.einsum("mqhd,mkhd->mhqk", query, keys, preferred_element_type=F32)
    scores = jnp.where(allowed, raw * factor, MASKED)
    expo = jnp.exp(scores - jnp.max(scores, axis=-1, keepdims=True))
    probs = expo / jnp.sum(expo, axis=-1, keepdims=True)
    weights = probs.astype(BF)
    attended = (
        jnp.einsum("mhqk,mkhd->mqhd", weights, values, preferred_element_type=F32)
        .reshape(tokens, width)
        .astype(BF)
    )
    branch = matmul(attended, attn_full) + b_attn
    first, normed1, inverse1 = layer_norm(x.astype(F32) + branch, attn_gain, attn_shift)
    first_low = first.astype(BF)
    pre = matmul(first_low, expand_full) + b_expand
    act = gelu_value(pre).astype(BF)
    second = first + matmul(act, shrink_full) + b_shrink
    settled, normed2, inverse2 = layer_norm(second, ffn_gain, ffn_shift)
    settled_low = settled.astype(BF)

    picked = matmul(select, settled_low).astype(BF)
    dense_pre = matmul(picked, dense_full) + b_dense
    head_val, normed3, inverse3 = layer_norm(gelu_value(dense_pre), dense_gain, dense_shift)
    head_out = head_val.astype(BF)
    spread = jnp.concatenate([fetch_yz(head_out, a, b) for a in range(NY) for b in range(NZ)])
    logits = matmul_nt(spread, vocab_w) + vocab_b
    hit = labels[:, None] == column[None, :]
    top = jnp.max(logits, axis=1)
    expl = jnp.exp(logits - top[:, None])
    part_sum = jnp.sum(expl, axis=1)
    label_logit = jnp.sum(jnp.where(hit, logits, 0.0), axis=1)
    stats = jnp.stack([top, part_sum, label_logit])
    seen = [stats]
    for a in range(NY):
        for b in range(NZ):
            if (a, b) != (0, 0):
                there = fetch_yz(stats, a, b).reshape(3, NY, NZ, rows)
                there = jnp.roll(there, (a, b), axis=(1, 2))
                seen.append(there.reshape(3, -1))
    top_all = functools.reduce(jnp.maximum, [s[0] for s in seen])
    sum_all = sum(s[1] * jnp.exp(s[0] - top_all) for s in seen)
    label_all = sum(s[2] for s in seen)
    log_sum = top_all + jnp.log(sum_all)
    scale = loss_scale * row_weight
    dlogits = (
        (scale * jnp.exp(top - log_sum))[:, None] * expl
        - jnp.where(hit, scale[:, None], 0.0)
    ).astype(BF)
    part = matmul(dlogits, vocab_w).astype(BF).reshape(NY, NZ, rows, width)
    row_grad = total(
        [give_yz(part[a, b], a, b) for a in range(NY) for b in range(NZ)]
    )
    loss_own = jnp.sum((row_weight * (log_sum - label_all))[:rows])
    loss = sum_everywhere(jnp.broadcast_to(loss_own, (8, 128)))[0, 0]
    grad_w = matmul_tn(dlogits, spread).astype(BF).reshape(NC, NX, per, width)
    grad_b = column_sum(dlogits).reshape(NC, NX, per)
    grad_w = (grad_w[0].astype(F32) + give(grad_w[1], "c", 1).astype(F32)).astype(BF)
    grad_b = grad_b[0] + give(grad_b[1], "c", 1)
    g_vocab = total([grad_w[0]] + [give(grad_w[k], "x", k) for k in (1, 2, 3)]).T
    g_vocab_bias = total([grad_b[0]] + [give(grad_b[k], "x", k) for k in (1, 2, 3)])

    g_dense_gain = column_sum(row_grad * normed3)
    g_dense_shift = column_sum(row_grad)
    ddense = (norm_back(row_grad, normed3, inverse3, dense_gain) * gelu_slope(dense_pre)).astype(BF)
    g_dense = scatter_sum(matmul_tn(picked, ddense), ("z", "y"))
    g_dense_bias = column_sum(ddense)
    drows = matmul_nt(ddense, dense_full).astype(BF)

    dout = out_grad.reshape(tokens, width).astype(F32) + matmul_tn(select, drows)
    g_ffn_gain = column_sum(dout * normed2)
    g_ffn_shift = column_sum(dout)
    dsecond = norm_back(dout, normed2, inverse2, ffn_gain)
    dffn = dsecond.astype(BF)
    g_shrink = scatter_sum(matmul_tn(act, dffn), ("y", "z"))
    g_shrink_bias = column_sum(dffn)
    dpre = (matmul_nt(dffn, shrink_full) * gelu_slope(pre)).astype(BF)
    g_expand = scatter_sum(matmul_tn(first_low, dpre), ("z", "y"))
    g_expand_bias = column_sum(dpre)
    dfirst = dsecond + matmul_nt(dpre, expand_full)
    g_attn_gain = column_sum(dfirst * normed1)
    g_attn_shift = column_sum(dfirst)
    dresidual = norm_back(dfirst, normed1, inverse1, attn_gain)
    dbranch = dresidual.astype(BF)
    g_attn = scatter_sum(matmul_tn(attended, dbranch), ("z", "y"))
    g_attn_bias = column_sum(dbranch)
    dattended = matmul_nt(dbranch, attn_full).astype(BF).reshape(micro, block, heads, HEAD_DIM)
    dprobs = jnp.einsum("mqhd,mkhd->mhqk", dattended, values, preferred_element_type=F32)
    inner = jnp.sum(probs * dprobs, axis=-1, keepdims=True)
    dscores = (probs * (dprobs - inner)).astype(BF)

    def merge(array):
        return array.astype(BF).reshape(tokens, width)

    dquery = merge(
        jnp.einsum("mhqk,mkhd->mqhd", dscores, keys, preferred_element_type=F32) * factor
    )
    dkeys = merge(
        jnp.einsum("mhqk,mqhd->mkhd", dscores, query, preferred_element_type=F32) * factor
    )
    dvalues = merge(
        jnp.einsum("mhqk,mqhd->mkhd", weights, dattended, preferred_element_type=F32)
    )
    dfused = jnp.concatenate([dquery, dkeys, dvalues], axis=1)
    g_qkv = scatter_sum(matmul_tn(x, dfused), ("y", "z"))
    g_query = column_sum(dquery)
    g_value = column_sum(dvalues)
    dinput = dresidual + matmul_nt(dfused, qkv_full)

    sums = jnp.stack(
        [
            g_query,
            g_value,
            g_attn_bias,
            g_attn_gain,
            g_attn_shift,
            g_shrink_bias,
            g_ffn_gain,
            g_ffn_shift,
            g_dense_bias,
            g_dense_gain,
            g_dense_shift,
        ],
        axis=1,
    )
    sums = jnp.concatenate([sums, g_expand_bias.reshape(width, -1)], axis=1)
    sums = jnp.pad(sums, ((0, 0), (0, 128 - sums.shape[1])))
    sums = scatter_sum(sums, ("z", "y"))
    return (
        settled_low.reshape(hidden_in.shape),
        loss,
        dinput.reshape(hidden_in.shape),
        g_qkv,
        sums[:, 0],
        sums[:, 1],
        g_attn,
        sums[:, 2],
        sums[:, 3],
        sums[:, 4],
        g_expand,
        sums[:, 11:15].reshape(-1),
        g_shrink,
        sums[:, 5],
        sums[:, 6],
        sums[:, 7],
        g_dense,
        sums[:, 8],
        sums[:, 9],
        sums[:, 10],
        g_vocab,
        g_vocab_bias,
    )


def solution(mesh):
    split = Mesh(mesh.devices.reshape(NY, NC, NZ, NX), EVERY)
    whole, one = P(), P(EVERY)
    tokens3 = P(None, EVERY, None)
    matrix = P(EVERY, None)
    in_specs = (
        tokens3,
        tokens3,
        P(None, EVERY),
        P(None, EVERY, None, None),
        whole,
        whole,
        matrix,
        one,
        one,
        matrix,
        one,
        one,
        one,
        matrix,
        one,
        matrix,
        one,
        one,
        one,
        matrix,
        one,
        one,
        one,
        P(None, EVERY),
        one,
    )
    out_specs = (
        tokens3,
        whole,
        tokens3,
        matrix,
        one,
        one,
        matrix,
        one,
        one,
        one,
        matrix,
        one,
        matrix,
        one,
        one,
        one,
        matrix,
        one,
        one,
        one,
        P(None, EVERY),
        one,
    )
    return jax.shard_map(body, mesh=split, in_specs=in_specs, out_specs=out_specs, check_vma=False)
```

```python
import jax
import jax.numpy as jnp
from jax import lax
from jax.sharding import Mesh
from jax.sharding import PartitionSpec as P

HEAD_DIM = 64
EPS = 1e-05
HALF_ROOT = 0.7071067811865476
NORMAL_PEAK = 0.3989422804014327
MASKED = -1e30

BF = jnp.bfloat16
F32 = jnp.float32
NY, NC, NZ, NX = 4, 2, 4, 4
SIZES = {"y": NY, "c": NC, "z": NZ, "x": NX}
EVERY = ("y", "c", "z", "x")


def fetch(array, axis, k):
    n = SIZES[axis]
    return lax.ppermute(array, axis, [((i + k) % n, i) for i in range(n)])


def give(array, axis, k):
    n = SIZES[axis]
    return lax.ppermute(array, axis, [(i, (i + k) % n) for i in range(n)])


def in_order(pieces, index):
    n = len(pieces)
    twice = jnp.stack(pieces + pieces)
    return lax.dynamic_slice_in_dim(twice, (n - index) % n, n, 0)


def gather_x(shard):
    pieces = [shard] + [fetch(shard, "x", k) for k in (1, 2, 3)]
    return in_order(pieces, lax.axis_index("x"))


def swap(array, axes):
    return lax.all_to_all(array, axes, 0, 0, tiled=True)


def scatter_sum(grads):
    n = grads[0].shape[1]
    rows = [grad.shape[0] // 128 for grad in grads]
    core = lax.axis_index("c")

    def half(c):
        cut = [
            lax.dynamic_index_in_dim(
                grad.astype(BF).reshape(NY, NC, NZ, NX * r, n), c, 1, False
            ).reshape(NY * NZ, NX * r, n)
            for grad, r in zip(grads, rows)
        ]
        return cut[0] if len(cut) == 1 else jnp.concatenate(cut, axis=1)

    got = give(half(1 - core), "c", 1)
    mine = (half(core).astype(F32) + got.astype(F32)).astype(BF)
    mine = jnp.sum(swap(mine, ("y", "z")).astype(F32), axis=0).astype(BF)
    parts, start = [], 0
    for r in rows:
        parts.append(mine[start : start + NX * r].reshape(NX, r, n))
        start += NX * r
    mine = parts[0] if len(parts) == 1 else jnp.concatenate(parts, axis=1)
    return jnp.sum(swap(mine, "x").astype(F32), axis=0)


def total(parts):
    out = parts[0].astype(F32)
    for part in parts[1:]:
        out = out + part.astype(F32)
    return out


def three(value):
    high = lax.reduce_precision(value, 8, 7)
    rest = value - high
    middle = lax.reduce_precision(rest, 8, 7)
    return [high, middle, lax.reduce_precision(rest - middle, 8, 7)]


def gelu_value(values):
    return 0.5 * values * (1.0 + lax.erf(values * HALF_ROOT))


def gelu_slope(values):
    return 0.5 * (1.0 + lax.erf(values * HALF_ROOT)) + values * NORMAL_PEAK * jnp.exp(
        -0.5 * values * values
    )


def layer_norm(values, gain, shift):
    center = values - jnp.mean(values, axis=-1, keepdims=True)
    inverse = lax.rsqrt(jnp.mean(center * center, axis=-1, keepdims=True) + EPS)
    normed = center * inverse
    return (normed * gain + shift, normed, inverse)


def norm_back(grad, normed, inverse, gain):
    scaled = grad * gain
    inner = (
        scaled
        - jnp.mean(scaled, axis=-1, keepdims=True)
        - normed * jnp.mean(scaled * normed, axis=-1, keepdims=True)
    )
    return inner * inverse


def column_sum(values):
    return jnp.sum(values, axis=0, dtype=F32)


def matmul(left, right):
    return jnp.dot(left, right, preferred_element_type=F32)


def matmul_tn(left, right):
    return lax.dot_general(left, right, (((0,), (0,)), ((), ())), preferred_element_type=F32)


def matmul_nt(left, right):
    return lax.dot_general(left, right, (((1,), (1,)), ((), ())), preferred_element_type=F32)


def body(
    hidden_in,
    out_grad,
    segments,
    mask_pos,
    mask_labels,
    loss_scale,
    w_qkv,
    b_query,
    b_value,
    w_attn,
    b_attn,
    attn_gain,
    attn_shift,
    w_expand,
    b_expand,
    w_shrink,
    b_shrink,
    ffn_gain,
    ffn_shift,
    w_dense,
    b_dense,
    dense_gain,
    dense_shift,
    w_vocab,
    b_vocab,
):
    micro, block, width = hidden_in.shape
    tokens = micro * block
    heads = width // HEAD_DIM
    factor = HEAD_DIM ** (-0.5)
    at = {axis: lax.axis_index(axis) for axis in EVERY}
    vectors = (
        b_query,
        b_value,
        b_attn,
        attn_gain,
        attn_shift,
        b_shrink,
        ffn_gain,
        ffn_shift,
        b_dense,
        dense_gain,
        dense_shift,
    )
    small = jnp.concatenate(
        [jnp.stack(vectors, axis=1), b_expand.reshape(w_qkv.shape[0], -1)], axis=1
    )
    small = jnp.pad(small, ((0, 0), (0, 128 - small.shape[1])))
    fused = jnp.concatenate([w_qkv, small, w_attn, w_expand, w_dense], axis=1)
    fused = gather_x(fused).reshape(-1, fused.shape[1])
    tall = gather_x(w_shrink)
    tall = tall.transpose(1, 0, 2).reshape(fused.shape[0], -1)
    layer = lax.all_gather(
        jnp.concatenate([fused, tall], axis=1), ("y", "c", "z"), axis=0, tiled=True
    )
    ends = [3 * width, 128, width, w_expand.shape[1], width]
    ends = [sum(ends[: i + 1]) for i in range(len(ends))]
    qkv_full = layer[:, : ends[0]]
    vec_full = layer[:, ends[0] : ends[1]]
    attn_full = layer[:, ends[1] : ends[2]]
    expand_full = layer[:, ends[2] : ends[3]]
    dense_full = layer[:, ends[3] : ends[4]]
    shrink_full = (
        layer[:, ends[4] :]
        .reshape(NY * NC * NZ, -1, NX, width)
        .transpose(0, 2, 1, 3)
        .reshape(-1, width)
    )
    rows_of = vec_full.T.astype(F32)
    (
        b_query,
        b_value,
        b_attn,
        attn_gain,
        attn_shift,
        b_shrink,
        ffn_gain,
        ffn_shift,
        b_dense,
        dense_gain,
        dense_shift,
    ) = (rows_of[i] for i in range(len(vectors)))
    b_expand = vec_full[:, 11:15].astype(F32).reshape(-1)

    own_w = w_vocab.T
    piece_w = [own_w] + [fetch(own_w, "x", k) for k in (1, 2, 3)]
    piece_b = [b_vocab] + [fetch(b_vocab, "x", k) for k in (1, 2, 3)]
    half_w = jnp.stack(piece_w)
    half_b = jnp.stack(piece_b)
    per = own_w.shape[0]
    vocab_w = jnp.concatenate([half_w, fetch(half_w, "c", 1)]).reshape(-1, width)
    vocab_b = jnp.concatenate([half_b, fetch(half_b, "c", 1)]).reshape(-1).astype(F32)
    start = jnp.stack(
        [
            (((at["y"] * NC + (at["c"] + kc) % NC) * NZ + at["z"]) * NX + (at["x"] + kx) % NX)
            * per
            for kc in range(NC)
            for kx in range(NX)
        ]
    )
    column = (start[:, None] + jnp.arange(per, dtype=jnp.int32)[None, :]).reshape(-1)

    flat_labels = mask_labels.reshape(micro, -1)
    counts = jnp.sum((flat_labels >= 0).astype(F32), axis=1)
    norms = 1.0 / (counts * micro)
    slots = mask_labels.shape[-1]
    peers = NZ * NX
    grid = mask_labels.reshape(micro, NY, NC, peers, NZ, NX, slots)
    grid = lax.dynamic_index_in_dim(grid, at["c"], 2, False)
    grid = lax.dynamic_index_in_dim(grid, at["x"], 4, False)
    labels = grid.transpose(1, 3, 0, 2, 4).reshape(-1)
    rows = micro * peers * slots
    row_norm = jnp.broadcast_to(norms[None, :, None], (NY * NZ, micro, peers * slots)).reshape(-1)
    live = (labels >= 0).astype(F32)
    row_weight = live * row_norm
    hit = labels[:, None] == column[None, :]
    scale = loss_scale * row_weight
    own_first = (at["y"] * NZ + at["z"]) * rows
    own_weight = lax.dynamic_slice_in_dim(row_weight, own_first, rows)
    label_w = matmul(hit.astype(BF), vocab_w)
    label_b = jnp.sum(jnp.where(hit, vocab_b, 0.0), axis=1, keepdims=True)
    label_w = jnp.concatenate([label_w, jnp.pad(label_b, ((0, 0), (0, 127)))], axis=1)
    label_w = swap(label_w.astype(BF).reshape(NY * NZ, rows, -1), ("y", "z"))
    label_w = jnp.sum(label_w.astype(F32), axis=0)
    label_w, label_b = label_w[:, :width], label_w[:, width]
    positions = mask_pos.reshape(micro, -1)
    shifted = jnp.where(
        positions >= 0, positions + block * jnp.arange(micro, dtype=jnp.int32)[:, None], -1
    ).reshape(-1)
    select = (shifted[:, None] == jnp.arange(tokens, dtype=jnp.int32)[None, :]).astype(BF)

    x = hidden_in.reshape(tokens, width)
    united = matmul(x, qkv_full)

    def split(values):
        return values.astype(BF).reshape(micro, block, heads, HEAD_DIM)

    query = split(united[:, :width] + b_query)
    keys = split(united[:, width : 2 * width])
    values = split(united[:, 2 * width :] + b_value)
    allowed = (segments[:, :, None] == segments[:, None, :])[:, None]
    raw = jnp.einsum("mqhd,mkhd->mhqk", query, keys, preferred_element_type=F32)
    scores = jnp.where(allowed, raw * factor, MASKED)
    expo = jnp.exp(scores - jnp.max(scores, axis=-1, keepdims=True))
    probs = expo / jnp.sum(expo, axis=-1, keepdims=True)
    weights = probs.astype(BF)
    attended = (
        jnp.einsum("mhqk,mkhd->mqhd", weights, values, preferred_element_type=F32)
        .reshape(tokens, width)
        .astype(BF)
    )
    branch = matmul(attended, attn_full) + b_attn
    first, normed1, inverse1 = layer_norm(x.astype(F32) + branch, attn_gain, attn_shift)
    first_low = first.astype(BF)
    pre = matmul(first_low, expand_full) + b_expand
    act = gelu_value(pre).astype(BF)
    second = first + matmul(act, shrink_full) + b_shrink
    settled, normed2, inverse2 = layer_norm(second, ffn_gain, ffn_shift)
    settled_low = settled.astype(BF)

    picked = matmul(select, settled_low).astype(BF)
    dense_pre = matmul(picked, dense_full) + b_dense
    head_val, normed3, inverse3 = layer_norm(gelu_value(dense_pre), dense_gain, dense_shift)
    head_out = head_val.astype(BF)
    spread = lax.all_gather(head_out, ("y", "z"), axis=0, tiled=True)
    logits = matmul_nt(spread, vocab_w) + vocab_b
    top = jnp.max(logits, axis=1)
    expl = jnp.exp(logits - top[:, None])
    part_sum = jnp.sum(expl, axis=1)
    part = matmul(jnp.where(hit, 0.0, expl).astype(BF), vocab_w)
    stats = jnp.stack(three(top) + three(part_sum), axis=1)
    stats = jnp.pad(stats, ((0, 0), (0, 128 - stats.shape[1])))
    part = jnp.concatenate([part, stats], axis=1).astype(BF).reshape(NY * NZ, rows, -1)
    part = swap(part, ("y", "z")).astype(F32)
    stats = part[:, :, width : width + 6]
    tops = stats[:, :, 0] + stats[:, :, 1] + stats[:, :, 2]
    sums = stats[:, :, 3] + stats[:, :, 4] + stats[:, :, 5]
    top_all = jnp.max(tops, axis=0)
    share = jnp.exp(tops - top_all)
    sum_all = jnp.sum(sums * share, axis=0)
    log_sum = top_all + jnp.log(sum_all)
    label_logit = jnp.sum(head_out.astype(F32) * label_w, axis=1) + label_b
    mixed = jnp.sum((share / sum_all)[:, :, None] * part[:, :, :width], axis=0)
    row_grad = (loss_scale * own_weight)[:, None] * (
        mixed + (jnp.exp(label_logit - log_sum) - 1.0)[:, None] * label_w
    )
    loss_own = jnp.sum(own_weight * (log_sum - label_logit))
    told = jnp.concatenate([log_sum, loss_own[None], jnp.zeros(128 - rows - 1, F32)])
    told = lax.all_gather(told, ("y", "z"))
    log_sums = told[:, :rows].reshape(-1)
    loss = jnp.sum(lax.all_gather(jnp.sum(told[:, rows]), ("c", "x")))
    dlogits = (
        (scale * jnp.exp(top - log_sums))[:, None] * expl
        - jnp.where(hit, scale[:, None], 0.0)
    ).astype(BF)
    grad_w = matmul_tn(dlogits, spread).astype(BF).reshape(NC, NX, per, width)
    grad_b = column_sum(dlogits).reshape(NC, NX, per)
    grad_w = (grad_w[0].astype(F32) + give(grad_w[1], "c", 1).astype(F32)).astype(BF)
    grad_b = grad_b[0] + give(grad_b[1], "c", 1)
    g_vocab = total([grad_w[0]] + [give(grad_w[k], "x", k) for k in (1, 2, 3)]).T
    g_vocab_bias = total([grad_b[0]] + [give(grad_b[k], "x", k) for k in (1, 2, 3)])

    g_dense_gain = column_sum(row_grad * normed3)
    g_dense_shift = column_sum(row_grad)
    ddense = (norm_back(row_grad, normed3, inverse3, dense_gain) * gelu_slope(dense_pre)).astype(BF)
    g_dense = matmul_tn(picked, ddense)
    g_dense_bias = column_sum(ddense)
    drows = matmul_nt(ddense, dense_full).astype(BF)

    dout = out_grad.reshape(tokens, width).astype(F32) + matmul_tn(select, drows)
    g_ffn_gain = column_sum(dout * normed2)
    g_ffn_shift = column_sum(dout)
    dsecond = norm_back(dout, normed2, inverse2, ffn_gain)
    dffn = dsecond.astype(BF)
    g_shrink = matmul_tn(act, dffn)
    g_both = scatter_sum([g_shrink, g_dense])
    g_shrink, g_dense = g_both[: w_shrink.shape[0]], g_both[w_shrink.shape[0] :]
    g_shrink_bias = column_sum(dffn)
    dpre = (matmul_nt(dffn, shrink_full) * gelu_slope(pre)).astype(BF)
    g_expand = scatter_sum([matmul_tn(first_low, dpre)])
    g_expand_bias = column_sum(dpre)
    dfirst = dsecond + matmul_nt(dpre, expand_full)
    g_attn_gain = column_sum(dfirst * normed1)
    g_attn_shift = column_sum(dfirst)
    dresidual = norm_back(dfirst, normed1, inverse1, attn_gain)
    dbranch = dresidual.astype(BF)
    g_attn = matmul_tn(attended, dbranch)
    g_attn_bias = column_sum(dbranch)
    dattended = matmul_nt(dbranch, attn_full).astype(BF).reshape(micro, block, heads, HEAD_DIM)
    dprobs = jnp.einsum("mqhd,mkhd->mhqk", dattended, values, preferred_element_type=F32)
    inner = jnp.sum(probs * dprobs, axis=-1, keepdims=True)
    dscores = (probs * (dprobs - inner)).astype(BF)

    def merge(array):
        return array.astype(BF).reshape(tokens, width)

    dquery = merge(
        jnp.einsum("mhqk,mkhd->mqhd", dscores, keys, preferred_element_type=F32) * factor
    )
    dkeys = merge(
        jnp.einsum("mhqk,mqhd->mkhd", dscores, query, preferred_element_type=F32) * factor
    )
    dvalues = merge(
        jnp.einsum("mhqk,mqhd->mkhd", weights, dattended, preferred_element_type=F32)
    )
    dfused = jnp.concatenate([dquery, dkeys, dvalues], axis=1)
    g_qkv = matmul_tn(x, dfused)
    g_query = column_sum(dquery)
    g_value = column_sum(dvalues)
    dinput = dresidual + matmul_nt(dfused, qkv_full)

    sums = jnp.stack(
        [
            g_query,
            g_value,
            g_attn_bias,
            g_attn_gain,
            g_attn_shift,
            g_shrink_bias,
            g_ffn_gain,
            g_ffn_shift,
            g_dense_bias,
            g_dense_gain,
            g_dense_shift,
        ],
        axis=1,
    )
    sums = jnp.concatenate([sums, g_expand_bias.reshape(width, -1)], axis=1)
    sums = jnp.pad(sums, ((0, 0), (0, 128 - sums.shape[1])))
    last = scatter_sum([jnp.concatenate([g_qkv.astype(BF), g_attn.astype(BF), sums.astype(BF)], axis=1)])
    g_qkv, g_attn, sums = last[:, : 3 * width], last[:, 3 * width : 4 * width], last[:, 4 * width :]
    return (
        settled_low.reshape(hidden_in.shape),
        loss,
        dinput.reshape(hidden_in.shape),
        g_qkv,
        sums[:, 0],
        sums[:, 1],
        g_attn,
        sums[:, 2],
        sums[:, 3],
        sums[:, 4],
        g_expand,
        sums[:, 11:15].reshape(-1),
        g_shrink,
        sums[:, 5],
        sums[:, 6],
        sums[:, 7],
        g_dense,
        sums[:, 8],
        sums[:, 9],
        sums[:, 10],
        g_vocab,
        g_vocab_bias,
    )


def solution(mesh):
    split = Mesh(mesh.devices.reshape(NY, NC, NZ, NX), EVERY)
    whole, one = P(), P(EVERY)
    tokens3 = P(None, EVERY, None)
    matrix = P(EVERY, None)
    in_specs = (
        tokens3,
        tokens3,
        P(None, EVERY),
        P(None, EVERY, None, None),
        whole,
        whole,
        matrix,
        one,
        one,
        matrix,
        one,
        one,
        one,
        matrix,
        one,
        matrix,
        one,
        one,
        one,
        matrix,
        one,
        one,
        one,
        P(None, EVERY),
        one,
    )
    out_specs = (
        tokens3,
        whole,
        tokens3,
        matrix,
        one,
        one,
        matrix,
        one,
        one,
        one,
        matrix,
        one,
        matrix,
        one,
        one,
        one,
        matrix,
        one,
        one,
        one,
        P(None, EVERY),
        one,
    )
    return jax.shard_map(body, mesh=split, in_specs=in_specs, out_specs=out_specs, check_vma=False)
```

```python
import jax
import jax.numpy as jnp
from jax import lax
from jax.sharding import Mesh
from jax.sharding import PartitionSpec as P

HEAD_DIM = 64
EPS = 1e-05
HALF_ROOT = 0.7071067811865476
NORMAL_PEAK = 0.3989422804014327
MASKED = -1e30

BF = jnp.bfloat16
F32 = jnp.float32
NY, NC, NZ, NX = 4, 2, 4, 4
SIZES = {"y": NY, "c": NC, "z": NZ, "x": NX}
EVERY = ("y", "c", "z", "x")


def fetch(array, axis, k):
    n = SIZES[axis]
    return lax.ppermute(array, axis, [((i + k) % n, i) for i in range(n)])


def give(array, axis, k):
    n = SIZES[axis]
    return lax.ppermute(array, axis, [(i, (i + k) % n) for i in range(n)])


def in_order(pieces, index):
    n = len(pieces)
    twice = jnp.stack(pieces + pieces)
    return lax.dynamic_slice_in_dim(twice, (n - index) % n, n, 0)


def gather_x(shard):
    pieces = [shard] + [fetch(shard, "x", k) for k in (1, 2, 3)]
    return in_order(pieces, lax.axis_index("x"))


def swap(array, axes):
    return lax.all_to_all(array, axes, 0, 0, tiled=True)


def blocks(grad):
    return grad.astype(BF).reshape(NY, NC, NZ, -1, grad.shape[1])


def half(grads, core, axis):
    cut = [lax.dynamic_index_in_dim(grad, core, 1, False) for grad in grads]
    cut = [part.reshape((NY * NZ,) + part.shape[2:]) for part in cut]
    return cut[0] if len(cut) == 1 else jnp.concatenate(cut, axis=axis)


def sum_cores(grads, axis):
    core = lax.axis_index("c")
    return half(grads, core, axis), give(half(grads, 1 - core, axis), "c", 1)


def add_cores(pair):
    return (pair[0].astype(F32) + pair[1].astype(F32)).astype(BF)


def sum_yz(mine):
    return jnp.sum(swap(mine, ("y", "z")).astype(F32), axis=0).astype(BF)


def sum_x(mine):
    return jnp.sum(swap(mine, "x").astype(F32), axis=0)


def split_three(value):
    return jnp.pad(jnp.stack(three(value)), (0, 765)).astype(BF)


def after(*arrays):
    return lax.optimization_barrier(arrays)


def total(parts):
    out = parts[0].astype(F32)
    for part in parts[1:]:
        out = out + part.astype(F32)
    return out


def three(value):
    high = lax.reduce_precision(value, 8, 7)
    rest = value - high
    middle = lax.reduce_precision(rest, 8, 7)
    return [high, middle, lax.reduce_precision(rest - middle, 8, 7)]


def gelu_value(values):
    return 0.5 * values * (1.0 + lax.erf(values * HALF_ROOT))


def gelu_slope(values):
    return 0.5 * (1.0 + lax.erf(values * HALF_ROOT)) + values * NORMAL_PEAK * jnp.exp(
        -0.5 * values * values
    )


def layer_norm(values, gain, shift):
    center = values - jnp.mean(values, axis=-1, keepdims=True)
    inverse = lax.rsqrt(jnp.mean(center * center, axis=-1, keepdims=True) + EPS)
    normed = center * inverse
    return (normed * gain + shift, normed, inverse)


def norm_back(grad, normed, inverse, gain):
    scaled = grad * gain
    inner = (
        scaled
        - jnp.mean(scaled, axis=-1, keepdims=True)
        - normed * jnp.mean(scaled * normed, axis=-1, keepdims=True)
    )
    return inner * inverse


def column_sum(values):
    return jnp.sum(values, axis=0, dtype=F32)


def matmul(left, right):
    return jnp.dot(left, right, preferred_element_type=F32)


def matmul_tn(left, right):
    return lax.dot_general(left, right, (((0,), (0,)), ((), ())), preferred_element_type=F32)


def matmul_nt(left, right):
    return lax.dot_general(left, right, (((1,), (1,)), ((), ())), preferred_element_type=F32)


def body(
    hidden_in,
    out_grad,
    segments,
    mask_pos,
    mask_labels,
    loss_scale,
    w_qkv,
    b_query,
    b_value,
    w_attn,
    b_attn,
    attn_gain,
    attn_shift,
    w_expand,
    b_expand,
    w_shrink,
    b_shrink,
    ffn_gain,
    ffn_shift,
    w_dense,
    b_dense,
    dense_gain,
    dense_shift,
    w_vocab,
    b_vocab,
):
    micro, block, width = hidden_in.shape
    tokens = micro * block
    heads = width // HEAD_DIM
    factor = HEAD_DIM ** (-0.5)
    at = {axis: lax.axis_index(axis) for axis in EVERY}
    vectors = (
        b_query,
        b_value,
        b_attn,
        attn_gain,
        attn_shift,
        b_shrink,
        ffn_gain,
        ffn_shift,
        b_dense,
        dense_gain,
        dense_shift,
    )
    small = after(jnp.stack(vectors))[0].T
    small = jnp.concatenate([small, b_expand.reshape(w_qkv.shape[0], -1)], axis=1)
    small = jnp.pad(small, ((0, 0), (0, 128 - small.shape[1])))
    fused = jnp.concatenate([w_qkv, small, w_attn, w_expand, w_dense], axis=1)
    fused = gather_x(fused).reshape(-1, fused.shape[1])
    tall = gather_x(w_shrink)
    tall = tall.transpose(1, 0, 2).reshape(fused.shape[0], -1)
    layer = lax.all_gather(
        jnp.concatenate([fused, tall], axis=1), ("y", "c", "z"), axis=0, tiled=True
    )
    layer, w_vocab = after(layer, w_vocab)
    ends = [3 * width, 128, width, w_expand.shape[1], width]
    ends = [sum(ends[: i + 1]) for i in range(len(ends))]
    qkv_full = layer[:, : ends[0]]
    vec_full = layer[:, ends[0] : ends[1]]
    attn_full = layer[:, ends[1] : ends[2]]
    expand_full = layer[:, ends[2] : ends[3]]
    dense_full = layer[:, ends[3] : ends[4]]
    shrink_full = jnp.stack(
        [
            layer[:, ends[4] + k * width : ends[4] + (k + 1) * width].reshape(
                NY * NC * NZ, -1, width
            )
            for k in range(NX)
        ],
        axis=1,
    ).reshape(-1, width)
    rows_of = vec_full.T.astype(F32)
    (
        b_query,
        b_value,
        b_attn,
        attn_gain,
        attn_shift,
        b_shrink,
        ffn_gain,
        ffn_shift,
        b_dense,
        dense_gain,
        dense_shift,
    ) = (rows_of[i] for i in range(len(vectors)))
    b_expand = vec_full[:, 11:15].astype(F32).reshape(-1)

    own_w = w_vocab.T
    piece_w = [own_w] + [fetch(own_w, "x", k) for k in (1, 2, 3)]
    piece_b = [b_vocab] + [fetch(b_vocab, "x", k) for k in (1, 2, 3)]
    half_w = jnp.stack(piece_w)
    half_b = jnp.stack(piece_b)
    per = own_w.shape[0]
    vocab_w = jnp.concatenate([half_w, fetch(half_w, "c", 1)]).reshape(-1, width)
    vocab_b = jnp.concatenate([half_b, fetch(half_b, "c", 1)]).reshape(-1).astype(F32)
    start = jnp.stack(
        [
            (((at["y"] * NC + (at["c"] + kc) % NC) * NZ + at["z"]) * NX + (at["x"] + kx) % NX)
            * per
            for kc in range(NC)
            for kx in range(NX)
        ]
    )
    column = (start[:, None] + jnp.arange(per, dtype=jnp.int32)[None, :]).reshape(-1)

    flat_labels = mask_labels.reshape(micro, -1)
    counts = jnp.sum((flat_labels >= 0).astype(F32), axis=1)
    norms = 1.0 / (counts * micro)
    slots = mask_labels.shape[-1]
    peers = NZ * NX
    grid = mask_labels.reshape(micro, NY, NC, peers, NZ, NX, slots)
    grid = lax.dynamic_index_in_dim(grid, at["c"], 2, False)
    grid = lax.dynamic_index_in_dim(grid, at["x"], 4, False)
    labels = grid.transpose(1, 3, 0, 2, 4).reshape(-1)
    rows = micro * peers * slots
    row_norm = jnp.broadcast_to(norms[None, :, None], (NY * NZ, micro, peers * slots)).reshape(-1)
    live = (labels >= 0).astype(F32)
    row_weight = live * row_norm
    hit = labels[:, None] == column[None, :]
    scale = loss_scale * row_weight
    own_first = (at["y"] * NZ + at["z"]) * rows
    own_weight = lax.dynamic_slice_in_dim(row_weight, own_first, rows)
    positions = mask_pos.reshape(micro, -1)
    shifted = jnp.where(
        positions >= 0, positions + block * jnp.arange(micro, dtype=jnp.int32)[:, None], -1
    ).reshape(-1)
    select = (shifted[:, None] == jnp.arange(tokens, dtype=jnp.int32)[None, :]).astype(BF)

    x = hidden_in.reshape(tokens, width)
    united = matmul(x, qkv_full)

    def split(values):
        return values.astype(BF).reshape(micro, block, heads, HEAD_DIM)

    query = split(united[:, :width] + b_query)
    keys = split(united[:, width : 2 * width])
    values = split(united[:, 2 * width :] + b_value)
    allowed = (segments[:, :, None] == segments[:, None, :])[:, None]
    raw = jnp.einsum("mqhd,mkhd->mhqk", query, keys, preferred_element_type=F32)
    scores = jnp.where(allowed, raw * factor, MASKED)
    expo = jnp.exp(scores - jnp.max(scores, axis=-1, keepdims=True))
    probs = expo / jnp.sum(expo, axis=-1, keepdims=True)
    weights = probs.astype(BF)
    attended = (
        jnp.einsum("mhqk,mkhd->mqhd", weights, values, preferred_element_type=F32)
        .reshape(tokens, width)
        .astype(BF)
    )
    branch = matmul(attended, attn_full) + b_attn
    first, normed1, inverse1 = layer_norm(x.astype(F32) + branch, attn_gain, attn_shift)
    first_low = first.astype(BF)
    pre = matmul(first_low, expand_full) + b_expand
    act = gelu_value(pre).astype(BF)
    second = first + matmul(act, shrink_full) + b_shrink
    settled, normed2, inverse2 = layer_norm(second, ffn_gain, ffn_shift)
    settled_low = settled.astype(BF)

    picked = matmul(select, settled_low).astype(BF)
    dense_pre = matmul(picked, dense_full) + b_dense
    head_val, normed3, inverse3 = layer_norm(gelu_value(dense_pre), dense_gain, dense_shift)
    head_out = head_val.astype(BF)
    head_out, vocab_w = after(head_out, vocab_w)
    spread = swap(
        jnp.broadcast_to(head_out, (NY * NZ,) + head_out.shape), ("y", "z")
    ).reshape(-1, width)
    label_w = matmul(hit.astype(BF), vocab_w)
    label_b = jnp.sum(jnp.where(hit, vocab_b, 0.0), axis=1, keepdims=True)
    label_w = jnp.concatenate([label_w, jnp.pad(label_b, ((0, 0), (0, 127)))], axis=1)
    spread, label_w = after(spread, label_w.astype(BF).reshape(NY * NZ, rows, -1))
    label_w = swap(label_w, ("y", "z"))
    label_w = jnp.sum(label_w.astype(F32), axis=0)
    label_w, label_b = label_w[:, :width], label_w[:, width]
    logits = matmul_nt(spread, vocab_w) + vocab_b
    top = jnp.max(logits, axis=1)
    expl = jnp.exp(logits - top[:, None])
    part_sum = jnp.sum(expl, axis=1)
    other = jnp.where(hit, 0.0, expl).astype(BF)
    other, label_w, label_b = after(other, label_w, label_b)
    part = matmul(other, vocab_w).astype(BF).reshape(NY * NZ, rows, width)
    stats = jnp.stack(three(top) + three(part_sum)).astype(BF)
    stats = jnp.concatenate([stats[:, :width], stats[:, width:].reshape(2, width)])
    stats = jnp.broadcast_to(stats, (NY * NZ,) + stats.shape)
    part = swap(jnp.concatenate([part, stats], axis=1), ("y", "z"))
    stats = part[:, rows:]
    stats = jnp.concatenate(
        [stats[:, :6], stats[:, 6:].reshape(NY * NZ, 6, NY * NZ * rows - width)], axis=2
    ).astype(F32)
    tops = stats[:, 0] + stats[:, 1] + stats[:, 2]
    sums = stats[:, 3] + stats[:, 4] + stats[:, 5]
    top_all = jnp.max(tops, axis=0)
    shares = jnp.exp(tops - top_all)
    sum_all = jnp.sum(sums * shares, axis=0)
    log_sums = top_all + jnp.log(sum_all)
    log_sum = lax.dynamic_slice_in_dim(log_sums, own_first, rows)
    share = lax.dynamic_slice_in_dim(shares / sum_all, own_first, rows, 1)
    label_logit = jnp.sum(head_out.astype(F32) * label_w, axis=1) + label_b
    mixed = jnp.sum(share[:, :, None] * part[:, :rows].astype(F32), axis=0)
    row_grad = (loss_scale * own_weight)[:, None] * (
        mixed + (jnp.exp(label_logit - log_sum) - 1.0)[:, None] * label_w
    )
    loss_own = jnp.sum(own_weight * (log_sum - label_logit))
    dlogits = (
        (scale * jnp.exp(top - log_sums))[:, None] * expl
        - jnp.where(hit, scale[:, None], 0.0)
    ).astype(BF)
    grad_w = matmul_tn(dlogits, spread).astype(BF).reshape(NC, NX, per, width)
    grad_b = column_sum(dlogits).reshape(NC, NX, per)
    grad_w = (grad_w[0].astype(F32) + give(grad_w[1], "c", 1).astype(F32)).astype(BF)
    grad_b = grad_b[0] + give(grad_b[1], "c", 1)
    g_vocab = total([grad_w[0]] + [give(grad_w[k], "x", k) for k in (1, 2, 3)]).T
    g_vocab_bias = total([grad_b[0]] + [give(grad_b[k], "x", k) for k in (1, 2, 3)])

    g_dense_gain = column_sum(row_grad * normed3)
    g_dense_shift = column_sum(row_grad)
    ddense = (norm_back(row_grad, normed3, inverse3, dense_gain) * gelu_slope(dense_pre)).astype(BF)
    g_dense = matmul_tn(picked, ddense)
    g_dense_bias = column_sum(ddense)
    drows = matmul_nt(ddense, dense_full).astype(BF)

    dout = out_grad.reshape(tokens, width).astype(F32) + matmul_tn(select, drows)
    g_ffn_gain = column_sum(dout * normed2)
    g_ffn_shift = column_sum(dout)
    dsecond = norm_back(dout, normed2, inverse2, ffn_gain)
    dffn = dsecond.astype(BF)
    g_shrink = matmul_tn(act, dffn)
    loss_row = jnp.where(
        (jnp.arange(NC) == at["c"])[None, :, None, None, None], split_three(loss_own), 0.0
    ).astype(BF)
    loss_row = jnp.broadcast_to(loss_row, (NY, NC, NZ, 8, width))
    tall_pair = sum_cores([blocks(g_shrink), blocks(g_dense), loss_row], 1)
    g_shrink_bias = column_sum(dffn)
    dpre = (matmul_nt(dffn, shrink_full) * gelu_slope(pre)).astype(BF)
    g_expand = matmul_tn(first_low, dpre)
    wide_pair = sum_cores([blocks(g_expand)], 2)
    g_expand_bias = column_sum(dpre)
    dfirst = dsecond + matmul_nt(dpre, expand_full)
    g_attn_gain = column_sum(dfirst * normed1)
    g_attn_shift = column_sum(dfirst)
    dresidual = norm_back(dfirst, normed1, inverse1, attn_gain)
    dbranch = dresidual.astype(BF)
    dbranch, got = after(dbranch, tall_pair[1])
    tall_sum = add_cores((tall_pair[0], got))
    tall_all = swap(tall_sum, ("y", "z")).astype(F32)
    tall_sum = jnp.sum(tall_all[:, :120], axis=0).astype(BF)
    loss_row = split_three(jnp.sum(tall_all[:, 120, :3]))
    g_attn = matmul_tn(attended, dbranch)
    g_attn_bias = column_sum(dbranch)
    dattended = matmul_nt(dbranch, attn_full).astype(BF).reshape(micro, block, heads, HEAD_DIM)
    dprobs = jnp.einsum("mqhd,mkhd->mhqk", dattended, values, preferred_element_type=F32)
    inner = jnp.sum(probs * dprobs, axis=-1, keepdims=True)
    dscores = (probs * (dprobs - inner)).astype(BF)

    def merge(array):
        return array.astype(BF).reshape(tokens, width)

    dquery = merge(
        jnp.einsum("mhqk,mkhd->mqhd", dscores, keys, preferred_element_type=F32) * factor
    )
    dkeys = merge(
        jnp.einsum("mhqk,mqhd->mkhd", dscores, query, preferred_element_type=F32) * factor
    )
    dvalues = merge(
        jnp.einsum("mhqk,mqhd->mkhd", weights, dattended, preferred_element_type=F32)
    )
    dfused = jnp.concatenate([dquery, dkeys, dvalues], axis=1)
    g_qkv = matmul_tn(x, dfused)
    g_query = column_sum(dquery)
    g_value = column_sum(dvalues)
    dinput = dresidual + matmul_nt(dfused, qkv_full)

    sums = jnp.stack(
        [
            g_query,
            g_value,
            g_attn_bias,
            g_attn_gain,
            g_attn_shift,
            g_shrink_bias,
            g_ffn_gain,
            g_ffn_shift,
            g_dense_bias,
            g_dense_gain,
            g_dense_shift,
        ],
        axis=1,
    )
    sums = jnp.concatenate([sums, g_expand_bias.reshape(width, -1)], axis=1)
    sums = jnp.pad(sums, ((0, 0), (0, 128 - sums.shape[1])))
    wide = sum_yz(add_cores(wide_pair))
    tall = sum_x(
        jnp.concatenate(
            [tall_sum[:96].reshape(NX, -1, width), jnp.broadcast_to(loss_row, (NX, 8, width))],
            axis=1,
        )
    )
    last_pair = sum_cores([blocks(g_qkv), blocks(g_attn), blocks(sums)], 2)
    last_pair, wide, tall = after(last_pair, wide, tall)
    last = sum_yz(add_cores(last_pair))
    last = jnp.concatenate([last, tall_sum[96:120], wide], axis=1)
    last = sum_x(last.reshape(NX, -1, last.shape[1]))
    ends = [3 * width, width, 128, width, w_expand.shape[1]]
    ends = [sum(ends[: i + 1]) for i in range(len(ends))]
    g_qkv = last[:, : ends[0]]
    g_attn = last[:, ends[0] : ends[1]]
    sums = last[:, ends[1] : ends[2]]
    g_dense = last[:, ends[2] : ends[3]]
    g_expand = last[:, ends[3] :]
    g_shrink = tall[:24]
    loss = jnp.full((8, 128), jnp.sum(tall[24, :3]))
    loss = (loss + give(loss, "c", 1))[0, 0]
    return (
        settled_low.reshape(hidden_in.shape),
        loss,
        dinput.reshape(hidden_in.shape),
        g_qkv,
        sums[:, 0],
        sums[:, 1],
        g_attn,
        sums[:, 2],
        sums[:, 3],
        sums[:, 4],
        g_expand,
        sums[:, 11:15].reshape(-1),
        g_shrink,
        sums[:, 5],
        sums[:, 6],
        sums[:, 7],
        g_dense,
        sums[:, 8],
        sums[:, 9],
        sums[:, 10],
        g_vocab,
        g_vocab_bias,
    )


def solution(mesh):
    split = Mesh(mesh.devices.reshape(NY, NC, NZ, NX), EVERY)
    whole, one = P(), P(EVERY)
    tokens3 = P(None, EVERY, None)
    matrix = P(EVERY, None)
    in_specs = (
        tokens3,
        tokens3,
        P(None, EVERY),
        P(None, EVERY, None, None),
        whole,
        whole,
        matrix,
        one,
        one,
        matrix,
        one,
        one,
        one,
        matrix,
        one,
        matrix,
        one,
        one,
        one,
        matrix,
        one,
        one,
        one,
        P(None, EVERY),
        one,
    )
    out_specs = (
        tokens3,
        whole,
        tokens3,
        matrix,
        one,
        one,
        matrix,
        one,
        one,
        one,
        matrix,
        one,
        matrix,
        one,
        one,
        one,
        matrix,
        one,
        one,
        one,
        P(None, EVERY),
        one,
    )
    return jax.shard_map(body, mesh=split, in_specs=in_specs, out_specs=out_specs, check_vma=False)
```

```python
import jax
import jax.numpy as jnp
from jax import lax
from jax.experimental import pallas as pl
from jax.experimental.pallas import tpu as pltpu
from jax.sharding import Mesh
from jax.sharding import PartitionSpec as P

HEAD_DIM = 64
EPS = 1e-05
HALF_ROOT = 0.7071067811865476
NORMAL_PEAK = 0.3989422804014327
MASKED = -1e30

BF = jnp.bfloat16
F32 = jnp.float32
NY, NC, NZ, NX = 4, 2, 4, 4
SIZES = {"y": NY, "c": NC, "z": NZ, "x": NX}
EVERY = ("y", "c", "z", "x")


def fetch(array, axis, k):
    n = SIZES[axis]
    return lax.ppermute(array, axis, [((i + k) % n, i) for i in range(n)])


def give(array, axis, k):
    n = SIZES[axis]
    return lax.ppermute(array, axis, [(i, (i + k) % n) for i in range(n)])


def in_order(pieces, index):
    n = len(pieces)
    twice = jnp.stack(pieces + pieces)
    return lax.dynamic_slice_in_dim(twice, (n - index) % n, n, 0)


def gather_x(shard):
    pieces = [shard] + [fetch(shard, "x", k) for k in (1, 2, 3)]
    return in_order(pieces, lax.axis_index("x"))


def swap(array, axes):
    return lax.all_to_all(array, axes, 0, 0, tiled=True)


def blocks(grad):
    return grad.astype(BF).reshape(NY, NC, NZ, -1, grad.shape[1])


def half(grads, core, axis):
    cut = [lax.dynamic_index_in_dim(grad, core, 1, False) for grad in grads]
    cut = [part.reshape((NY * NZ,) + part.shape[2:]) for part in cut]
    return cut[0] if len(cut) == 1 else jnp.concatenate(cut, axis=axis)


def sum_cores(grads, axis):
    core = lax.axis_index("c")
    return half(grads, core, axis), give(half(grads, 1 - core, axis), "c", 1)


def add_cores(pair):
    return (pair[0].astype(F32) + pair[1].astype(F32)).astype(BF)


def sum_yz(mine):
    return jnp.sum(swap(mine, ("y", "z")).astype(F32), axis=0).astype(BF)


def sum_x(mine):
    return jnp.sum(swap(mine, "x").astype(F32), axis=0)


def split_three(value):
    return jnp.pad(jnp.stack(three(value)), (0, 765)).astype(BF)


def after(*arrays):
    return lax.optimization_barrier(arrays)


def total(parts):
    out = parts[0].astype(F32)
    for part in parts[1:]:
        out = out + part.astype(F32)
    return out


def three(value):
    high = lax.reduce_precision(value, 8, 7)
    rest = value - high
    middle = lax.reduce_precision(rest, 8, 7)
    return [high, middle, lax.reduce_precision(rest - middle, 8, 7)]


def gelu_value(values):
    return 0.5 * values * (1.0 + lax.erf(values * HALF_ROOT))


def gelu_slope(values):
    return 0.5 * (1.0 + lax.erf(values * HALF_ROOT)) + values * NORMAL_PEAK * jnp.exp(
        -0.5 * values * values
    )


def layer_norm(values, gain, shift):
    center = values - jnp.mean(values, axis=-1, keepdims=True)
    inverse = lax.rsqrt(jnp.mean(center * center, axis=-1, keepdims=True) + EPS)
    normed = center * inverse
    return (normed * gain + shift, normed, inverse)


def norm_back(grad, normed, inverse, gain):
    scaled = grad * gain
    inner = (
        scaled
        - jnp.mean(scaled, axis=-1, keepdims=True)
        - normed * jnp.mean(scaled * normed, axis=-1, keepdims=True)
    )
    return inner * inverse


def column_sum(values):
    return jnp.sum(values, axis=0, dtype=F32)


def matmul(left, right):
    return jnp.dot(left, right, preferred_element_type=F32)


def matmul_tn(left, right):
    return lax.dot_general(left, right, (((0,), (0,)), ((), ())), preferred_element_type=F32)


def matmul_nt(left, right):
    return lax.dot_general(left, right, (((1,), (1,)), ((), ())), preferred_element_type=F32)


def dot_nn(left, right):
    return lax.dot_general(left, right, (((1,), (0,)), ((), ())), preferred_element_type=F32)


def dot_nt(left, right):
    return lax.dot_general(left, right, (((1,), (1,)), ((), ())), preferred_element_type=F32)


def dot_tn(left, right):
    return lax.dot_general(left, right, (((0,), (0,)), ((), ())), preferred_element_type=F32)


def attention_forward_kernel(
    x_ref,
    row_ref,
    col_ref,
    wq_ref,
    wk_ref,
    wv_ref,
    wa_ref,
    vec_ref,
    qkv_ref,
    probs_ref,
    attended_ref,
    first_ref,
    low_ref,
    normed_ref,
    inverse_ref,
):
    tokens, width = x_ref.shape
    pair = 2 * HEAD_DIM
    factor = HEAD_DIM ** (-0.5)
    x = x_ref[...]
    qkv_ref[:, :width] = (dot_nn(x, wq_ref[...]) + vec_ref[0:1]).astype(BF)
    qkv_ref[:, width : 2 * width] = dot_nn(x, wk_ref[...]).astype(BF)
    qkv_ref[:, 2 * width :] = (dot_nn(x, wv_ref[...]) + vec_ref[1:2]).astype(BF)
    allowed = row_ref[...] == col_ref[...]
    lower = lax.broadcasted_iota(jnp.int32, (tokens, pair), 1) < HEAD_DIM
    for h in range(width // pair):
        lanes = slice(h * pair, (h + 1) * pair)
        query = qkv_ref[:, lanes]
        keys = qkv_ref[:, width + h * pair : width + (h + 1) * pair]
        values = qkv_ref[:, 2 * width + h * pair : 2 * width + (h + 1) * pair]
        zero = jnp.zeros_like(query)
        outs = []
        for side in range(2):
            mine = jnp.where(lower, query, zero) if side == 0 else jnp.where(lower, zero, query)
            scores = jnp.where(allowed, dot_nt(mine, keys) * factor, MASKED)
            expo = jnp.exp(scores - jnp.max(scores, axis=1, keepdims=True))
            probs = (expo / jnp.sum(expo, axis=1, keepdims=True)).astype(BF)
            probs_ref[2 * h + side] = probs
            outs.append(dot_nn(probs, values))
        attended_ref[:, lanes] = jnp.where(lower, outs[0], outs[1]).astype(BF)
    branch = dot_nn(attended_ref[...], wa_ref[...]) + vec_ref[2:3]
    first, normed, inverse = layer_norm(x.astype(F32) + branch, vec_ref[3:4], vec_ref[4:5])
    first_ref[...] = first
    low_ref[...] = first.astype(BF)
    normed_ref[...] = normed
    inverse_ref[...] = inverse


def weight_spec(width, block):
    return pl.BlockSpec((width, width), lambda m: (0, block))


def attention_forward(x, segments, layer, first_block, vec):
    micro, block = segments.shape
    tokens, width = x.shape
    heads = width // HEAD_DIM
    here = lambda n: pl.BlockSpec((block, n), lambda m: (m, 0))
    return pl.pallas_call(
        attention_forward_kernel,
        grid=(micro,),
        in_specs=[
            here(width),
            pl.BlockSpec((None, 1, block), lambda m: (m, 0, 0)),
            pl.BlockSpec((None, block, 1), lambda m: (m, 0, 0)),
            weight_spec(width, first_block),
            weight_spec(width, first_block + 1),
            weight_spec(width, first_block + 2),
            weight_spec(width, first_block + 3),
            pl.BlockSpec(vec.shape, lambda m: (0, 0)),
        ],
        out_specs=[
            here(3 * width),
            pl.BlockSpec((None, heads, block, block), lambda m: (m, 0, 0, 0)),
            here(width),
            here(width),
            here(width),
            here(width),
            here(1),
        ],
        out_shape=[
            jax.ShapeDtypeStruct((tokens, 3 * width), BF),
            jax.ShapeDtypeStruct((micro, heads, block, block), BF),
            jax.ShapeDtypeStruct((tokens, width), BF),
            jax.ShapeDtypeStruct((tokens, width), F32),
            jax.ShapeDtypeStruct((tokens, width), BF),
            jax.ShapeDtypeStruct((tokens, width), F32),
            jax.ShapeDtypeStruct((tokens, 1), F32),
        ],
        compiler_params=pltpu.CompilerParams(vmem_limit_bytes=48 * 1024 * 1024),
        cost_estimate=pl.CostEstimate(
            flops=4_000_000_000, bytes_accessed=16_000_000, transcendentals=2_000_000
        ),
    )(x, segments[:, None, :], segments[:, :, None], layer, layer, layer, layer, vec)


def attention_backward_kernel(dbranch_ref, qkv_ref, probs_ref, wa_ref, out_ref, sum_ref):
    tokens, width = dbranch_ref.shape
    pair = 2 * HEAD_DIM
    factor = HEAD_DIM ** (-0.5)
    dattended = dot_nt(dbranch_ref[...], wa_ref[...]).astype(BF)
    lower = lax.broadcasted_iota(jnp.int32, (tokens, pair), 1) < HEAD_DIM
    for h in range(width // pair):
        lanes = slice(h * pair, (h + 1) * pair)
        query = qkv_ref[:, lanes]
        keys = qkv_ref[:, width + h * pair : width + (h + 1) * pair]
        values = qkv_ref[:, 2 * width + h * pair : 2 * width + (h + 1) * pair]
        grad = dattended[:, lanes]
        zero = jnp.zeros_like(grad)
        parts = []
        for side in range(2):
            mine = jnp.where(lower, grad, zero) if side == 0 else jnp.where(lower, zero, grad)
            low = probs_ref[2 * h + side]
            probs = low.astype(F32)
            dprobs = dot_nt(mine, values)
            inner = jnp.sum(probs * dprobs, axis=1, keepdims=True)
            dscores = (probs * (dprobs - inner)).astype(BF)
            parts.append(
                (dot_nn(dscores, keys) * factor, dot_tn(dscores, query) * factor, dot_tn(low, grad))
            )
        for i in range(3):
            start = i * width + h * pair
            out_ref[:, start : start + pair] = jnp.where(lower, parts[0][i], parts[1][i]).astype(BF)
    seen = jnp.sum(out_ref[...].astype(F32), axis=0, keepdims=True)

    @pl.when(pl.program_id(0) == 0)
    def _():
        sum_ref[...] = seen

    @pl.when(pl.program_id(0) > 0)
    def _():
        sum_ref[...] += seen


def attention_backward(dbranch, qkv, probs, layer, attn_block):
    micro, heads, block, _ = probs.shape
    tokens, width = dbranch.shape
    here = lambda n: pl.BlockSpec((block, n), lambda m: (m, 0))
    return pl.pallas_call(
        attention_backward_kernel,
        grid=(micro,),
        in_specs=[
            here(width),
            here(3 * width),
            pl.BlockSpec((None, heads, block, block), lambda m: (m, 0, 0, 0)),
            weight_spec(width, attn_block),
        ],
        out_specs=[here(3 * width), pl.BlockSpec((1, 3 * width), lambda m: (0, 0))],
        out_shape=[
            jax.ShapeDtypeStruct((tokens, 3 * width), BF),
            jax.ShapeDtypeStruct((1, 3 * width), F32),
        ],
        compiler_params=pltpu.CompilerParams(vmem_limit_bytes=48 * 1024 * 1024),
        cost_estimate=pl.CostEstimate(
            flops=3_000_000_000, bytes_accessed=10_000_000, transcendentals=0
        ),
    )(dbranch, qkv, probs, layer)


def body(
    hidden_in,
    out_grad,
    segments,
    mask_pos,
    mask_labels,
    loss_scale,
    w_qkv,
    b_query,
    b_value,
    w_attn,
    b_attn,
    attn_gain,
    attn_shift,
    w_expand,
    b_expand,
    w_shrink,
    b_shrink,
    ffn_gain,
    ffn_shift,
    w_dense,
    b_dense,
    dense_gain,
    dense_shift,
    w_vocab,
    b_vocab,
):
    micro, block, width = hidden_in.shape
    tokens = micro * block
    heads = width // HEAD_DIM
    factor = HEAD_DIM ** (-0.5)
    at = {axis: lax.axis_index(axis) for axis in EVERY}
    vectors = (
        b_query,
        b_value,
        b_attn,
        attn_gain,
        attn_shift,
        b_shrink,
        ffn_gain,
        ffn_shift,
        b_dense,
        dense_gain,
        dense_shift,
    )
    small = after(jnp.stack(vectors))[0].T
    small = jnp.concatenate([small, b_expand.reshape(w_qkv.shape[0], -1)], axis=1)
    small = jnp.pad(small, ((0, 0), (0, 128 - small.shape[1])))
    fused = jnp.concatenate([w_expand, w_qkv, w_attn, w_dense, small], axis=1)
    fused = gather_x(fused).reshape(-1, fused.shape[1])
    tall = gather_x(w_shrink)
    tall = tall.transpose(1, 0, 2).reshape(fused.shape[0], -1)
    layer = lax.all_gather(
        jnp.concatenate([tall, fused], axis=1), ("y", "c", "z"), axis=0, tiled=True
    )
    own_w = w_vocab.T
    piece_w = [own_w] + [fetch(own_w, "x", k) for k in (1, 2, 3)]
    piece_b = [b_vocab] + [fetch(b_vocab, "x", k) for k in (1, 2, 3)]
    half_w = jnp.stack(piece_w)
    half_b = jnp.stack(piece_b)
    per = own_w.shape[0]
    vocab_w = jnp.concatenate([half_w, fetch(half_w, "c", 1)]).reshape(-1, width)
    vocab_b = jnp.concatenate([half_b, fetch(half_b, "c", 1)]).reshape(-1).astype(F32)
    start = jnp.stack(
        [
            (((at["y"] * NC + (at["c"] + kc) % NC) * NZ + at["z"]) * NX + (at["x"] + kx) % NX)
            * per
            for kc in range(NC)
            for kx in range(NX)
        ]
    )
    column = (start[:, None] + jnp.arange(per, dtype=jnp.int32)[None, :]).reshape(-1)

    flat_labels = mask_labels.reshape(micro, -1)
    counts = jnp.sum((flat_labels >= 0).astype(F32), axis=1)
    norms = 1.0 / (counts * micro)
    slots = mask_labels.shape[-1]
    peers = NZ * NX
    grid = mask_labels.reshape(micro, NY, NC, peers, NZ, NX, slots)
    grid = lax.dynamic_index_in_dim(grid, at["c"], 2, False)
    grid = lax.dynamic_index_in_dim(grid, at["x"], 4, False)
    labels = grid.transpose(1, 3, 0, 2, 4).reshape(-1)
    rows = micro * peers * slots
    row_norm = jnp.broadcast_to(norms[None, :, None], (NY * NZ, micro, peers * slots)).reshape(-1)
    live = (labels >= 0).astype(F32)
    row_weight = live * row_norm
    hit = labels[:, None] == column[None, :]
    scale = loss_scale * row_weight
    own_first = (at["y"] * NZ + at["z"]) * rows
    own_weight = lax.dynamic_slice_in_dim(row_weight, own_first, rows)
    label_w = matmul(hit.astype(BF), vocab_w)
    label_b = jnp.sum(jnp.where(hit, vocab_b, 0.0), axis=1, keepdims=True)
    label_w = jnp.concatenate([label_w, jnp.pad(label_b, ((0, 0), (0, 127)))], axis=1)
    label_w = swap(label_w.astype(BF).reshape(NY * NZ, rows, -1), ("y", "z"))
    label_w = jnp.sum(label_w.astype(F32), axis=0)
    label_w, label_b = label_w[:, :width], label_w[:, width]
    positions = mask_pos.reshape(micro, -1)
    shifted = jnp.where(
        positions >= 0, positions + block * jnp.arange(micro, dtype=jnp.int32)[:, None], -1
    ).reshape(-1)
    select = (shifted[:, None] == jnp.arange(tokens, dtype=jnp.int32)[None, :]).astype(BF)

    layer, label_w, label_b, vocab_w, select = after(layer, label_w, label_b, vocab_w, select)
    ends = [NX * width, w_expand.shape[1], 3 * width, width, width, 128]
    ends = [sum(ends[: i + 1]) for i in range(len(ends))]
    expand_full = layer[:, ends[0] : ends[1]]
    qkv_full = layer[:, ends[1] : ends[2]]
    attn_block = ends[2] // width
    dense_full = layer[:, ends[3] : ends[4]]
    vec_full = layer[:, ends[4] :]
    shrink_full = jnp.stack(
        [
            layer[:, k * width : (k + 1) * width].reshape(
                NY * NC * NZ, -1, width
            )
            for k in range(NX)
        ],
        axis=1,
    ).reshape(-1, width)
    rows_of = vec_full[:, :16].T.astype(F32)
    (
        b_query,
        b_value,
        b_attn,
        attn_gain,
        attn_shift,
        b_shrink,
        ffn_gain,
        ffn_shift,
        b_dense,
        dense_gain,
        dense_shift,
    ) = (rows_of[i] for i in range(len(vectors)))
    b_expand = vec_full[:, 11:15].astype(F32).reshape(-1)

    x = hidden_in.reshape(tokens, width)
    qkv, probs, attended, first, first_low, normed1, inverse1 = attention_forward(
        x, segments, layer, attn_block - 3, rows_of
    )
    pre = matmul(first_low, expand_full) + b_expand
    act = gelu_value(pre).astype(BF)
    second = first + matmul(act, shrink_full) + b_shrink
    settled, normed2, inverse2 = layer_norm(second, ffn_gain, ffn_shift)
    settled_low = settled.astype(BF)

    picked = matmul(select, settled_low).astype(BF)
    dense_pre = matmul(picked, dense_full) + b_dense
    head_val, normed3, inverse3 = layer_norm(gelu_value(dense_pre), dense_gain, dense_shift)
    head_out = head_val.astype(BF)
    spread = swap(
        jnp.broadcast_to(head_out, (NY * NZ,) + head_out.shape), ("y", "z")
    ).reshape(-1, width)
    logits = matmul_nt(spread, vocab_w) + vocab_b
    top = jnp.max(logits, axis=1)
    expl = jnp.exp(logits - top[:, None])
    part_sum = jnp.sum(expl, axis=1)
    other = jnp.where(hit, 0.0, expl).astype(BF)
    part = matmul(other, vocab_w).astype(BF).reshape(NY * NZ, rows, width)
    stats = jnp.stack(three(top) + three(part_sum)).astype(BF)
    stats = jnp.concatenate([stats[:, :width], stats[:, width:].reshape(2, width)])
    stats = jnp.broadcast_to(stats, (NY * NZ,) + stats.shape)
    part = swap(jnp.concatenate([part, stats], axis=1), ("y", "z"))
    stats = part[:, rows:]
    stats = jnp.concatenate(
        [stats[:, :6], stats[:, 6:].reshape(NY * NZ, 6, NY * NZ * rows - width)], axis=2
    ).astype(F32)
    tops = stats[:, 0] + stats[:, 1] + stats[:, 2]
    sums = stats[:, 3] + stats[:, 4] + stats[:, 5]
    top_all = jnp.max(tops, axis=0)
    shares = jnp.exp(tops - top_all)
    sum_all = jnp.sum(sums * shares, axis=0)
    log_sums = top_all + jnp.log(sum_all)
    log_sum = lax.dynamic_slice_in_dim(log_sums, own_first, rows)
    share = lax.dynamic_slice_in_dim(shares / sum_all, own_first, rows, 1)
    label_logit = jnp.sum(head_out.astype(F32) * label_w, axis=1) + label_b
    mixed = jnp.sum(share[:, :, None] * part[:, :rows].astype(F32), axis=0)
    row_grad = (loss_scale * own_weight)[:, None] * (
        mixed + (jnp.exp(label_logit - log_sum) - 1.0)[:, None] * label_w
    )
    loss_own = jnp.sum(own_weight * (log_sum - label_logit))
    g_dense_gain = column_sum(row_grad * normed3)
    g_dense_shift = column_sum(row_grad)
    ddense = (norm_back(row_grad, normed3, inverse3, dense_gain) * gelu_slope(dense_pre)).astype(BF)
    g_dense = matmul_tn(picked, ddense)
    g_dense_bias = column_sum(ddense)
    drows = matmul_nt(ddense, dense_full).astype(BF)

    dout = out_grad.reshape(tokens, width).astype(F32) + matmul_tn(select, drows)
    g_ffn_gain = column_sum(dout * normed2)
    g_ffn_shift = column_sum(dout)
    dsecond = norm_back(dout, normed2, inverse2, ffn_gain)
    dffn = dsecond.astype(BF)
    g_shrink = matmul_tn(act, dffn)
    loss_row = jnp.where(
        (jnp.arange(NC) == at["c"])[None, :, None, None, None], split_three(loss_own), 0.0
    ).astype(BF)
    loss_row = jnp.broadcast_to(loss_row, (NY, NC, NZ, 8, width))
    tall_pair = sum_cores([blocks(g_shrink), blocks(g_dense), loss_row], 1)
    g_shrink_bias = column_sum(dffn)
    dpre = (matmul_nt(dffn, shrink_full) * gelu_slope(pre)).astype(BF)
    g_expand = matmul_tn(first_low, dpre)
    wide_pair = sum_cores([blocks(g_expand)], 2)
    g_expand_bias = column_sum(dpre)
    dpre, tall_mine = after(dpre, add_cores(tall_pair))
    dfirst = dsecond + matmul_nt(dpre, expand_full)
    g_attn_gain = column_sum(dfirst * normed1)
    g_attn_shift = column_sum(dfirst)
    dresidual = norm_back(dfirst, normed1, inverse1, attn_gain)
    dbranch = dresidual.astype(BF)
    tall_all = swap(tall_mine, ("y", "z")).astype(F32)
    tall_sum = jnp.sum(tall_all[:, :120], axis=0).astype(BF)
    loss_row = split_three(jnp.sum(tall_all[:, 120, :3]))
    g_attn = matmul_tn(attended, dbranch)
    g_attn_bias = column_sum(dbranch)
    dfused, fused_sum = attention_backward(dbranch, qkv, probs, layer, attn_block)
    dfused, got = after(dfused, wide_pair[1])
    wide_mine = add_cores((wide_pair[0], got))
    g_qkv = matmul_tn(x, dfused)
    g_query, g_value = fused_sum[0, :width], fused_sum[0, 2 * width :]
    dinput = dresidual + matmul_nt(dfused, qkv_full)

    late_sums, dfused = after(log_sums, dfused)
    dlogits = (
        (scale * jnp.exp(top - late_sums))[:, None] * expl
        - jnp.where(hit, scale[:, None], 0.0)
    ).astype(BF)
    grad_w = matmul_tn(dlogits, spread).astype(BF).reshape(NC, NX, per, width)
    grad_b = column_sum(dlogits).reshape(NC, NX, 1, per)
    grad_b = jnp.pad(grad_b, ((0, 0), (0, 0), (0, 7), (0, width - per))).astype(BF)
    grad_w = jnp.concatenate([grad_w, grad_b], axis=2)
    grad_w = (grad_w[0].astype(F32) + give(grad_w[1], "c", 1).astype(F32)).astype(BF)
    grad_w = total([grad_w[0]] + [give(grad_w[k], "x", k) for k in (1, 2, 3)])
    g_vocab, g_vocab_bias = grad_w[:per].T, grad_w[per, :per]

    sums = jnp.stack(
        [
            g_query,
            g_value,
            g_attn_bias,
            g_attn_gain,
            g_attn_shift,
            g_shrink_bias,
            g_ffn_gain,
            g_ffn_shift,
            g_dense_bias,
            g_dense_gain,
            g_dense_shift,
        ]
    )
    sums = jnp.concatenate([after(sums)[0].T, g_expand_bias.reshape(width, -1)], axis=1)
    sums = jnp.pad(sums, ((0, 0), (0, 128 - sums.shape[1])))
    wide = sum_yz(wide_mine)
    tall = sum_x(
        jnp.concatenate(
            [tall_sum[:96].reshape(NX, -1, width), jnp.broadcast_to(loss_row, (NX, 8, width))],
            axis=1,
        )
    )
    last_pair = sum_cores([blocks(g_qkv), blocks(g_attn), blocks(sums)], 2)
    last_pair, wide, tall = after(last_pair, wide, tall)
    last = sum_yz(add_cores(last_pair))
    last = jnp.concatenate([last, tall_sum[96:120], wide], axis=1)
    last = sum_x(last.reshape(NX, -1, last.shape[1]))
    ends = [3 * width, width, 128, width, w_expand.shape[1]]
    ends = [sum(ends[: i + 1]) for i in range(len(ends))]
    g_qkv = last[:, : ends[0]]
    g_attn = last[:, ends[0] : ends[1]]
    sums = last[:, ends[1] : ends[2]]
    g_dense = last[:, ends[2] : ends[3]]
    g_expand = last[:, ends[3] :]
    g_shrink = tall[:24]
    loss = jnp.full((8, 128), jnp.sum(tall[24, :3]))
    loss = (loss + give(loss, "c", 1))[0, 0]
    return (
        settled_low.reshape(hidden_in.shape),
        loss,
        dinput.reshape(hidden_in.shape),
        g_qkv,
        sums[:, 0],
        sums[:, 1],
        g_attn,
        sums[:, 2],
        sums[:, 3],
        sums[:, 4],
        g_expand,
        sums[:, 11:15].reshape(-1),
        g_shrink,
        sums[:, 5],
        sums[:, 6],
        sums[:, 7],
        g_dense,
        sums[:, 8],
        sums[:, 9],
        sums[:, 10],
        g_vocab,
        g_vocab_bias,
    )


def solution(mesh):
    split = Mesh(mesh.devices.reshape(NY, NC, NZ, NX), EVERY)
    whole, one = P(), P(EVERY)
    tokens3 = P(None, EVERY, None)
    matrix = P(EVERY, None)
    in_specs = (
        tokens3,
        tokens3,
        P(None, EVERY),
        P(None, EVERY, None, None),
        whole,
        whole,
        matrix,
        one,
        one,
        matrix,
        one,
        one,
        one,
        matrix,
        one,
        matrix,
        one,
        one,
        one,
        matrix,
        one,
        one,
        one,
        P(None, EVERY),
        one,
    )
    out_specs = (
        tokens3,
        whole,
        tokens3,
        matrix,
        one,
        one,
        matrix,
        one,
        one,
        one,
        matrix,
        one,
        matrix,
        one,
        one,
        one,
        matrix,
        one,
        one,
        one,
        P(None, EVERY),
        one,
    )
    return jax.shard_map(body, mesh=split, in_specs=in_specs, out_specs=out_specs, check_vma=False)
```

```python
import jax
import jax.numpy as jnp
from jax import lax
from jax.experimental import pallas as pl
from jax.experimental.pallas import tpu as pltpu
from jax.sharding import Mesh
from jax.sharding import PartitionSpec as P

HEAD_DIM = 64
EPS = 1e-05
HALF_ROOT = 0.7071067811865476
NORMAL_PEAK = 0.3989422804014327
MASKED = -1e30

BF = jnp.bfloat16
F32 = jnp.float32
NY, NC, NZ, NX = 4, 2, 4, 4
SIZES = {"y": NY, "c": NC, "z": NZ, "x": NX}
EVERY = ("y", "c", "z", "x")


def fetch(array, axis, k):
    n = SIZES[axis]
    return lax.ppermute(array, axis, [((i + k) % n, i) for i in range(n)])


def give(array, axis, k):
    n = SIZES[axis]
    return lax.ppermute(array, axis, [(i, (i + k) % n) for i in range(n)])


def in_order(pieces, index):
    n = len(pieces)
    twice = jnp.stack(pieces + pieces)
    return lax.dynamic_slice_in_dim(twice, (n - index) % n, n, 0)


def gather_x(shard):
    pieces = [shard] + [fetch(shard, "x", k) for k in (1, 2, 3)]
    return in_order(pieces, lax.axis_index("x"))


def swap(array, axes):
    return lax.all_to_all(array, axes, 0, 0, tiled=True)


def blocks(grad):
    return grad.astype(BF).reshape(NY, NC, NZ, -1, grad.shape[1])


def half(grads, core, axis):
    cut = [lax.dynamic_index_in_dim(grad, core, 1, False) for grad in grads]
    cut = [part.reshape((NY * NZ,) + part.shape[2:]) for part in cut]
    return cut[0] if len(cut) == 1 else jnp.concatenate(cut, axis=axis)


def sum_cores(grads, axis):
    core = lax.axis_index("c")
    return half(grads, core, axis), give(half(grads, 1 - core, axis), "c", 1)


def add_cores(pair):
    return (pair[0].astype(F32) + pair[1].astype(F32)).astype(BF)


def sum_yz(mine):
    return jnp.sum(swap(mine, ("y", "z")).astype(F32), axis=0).astype(BF)


def sum_x(mine):
    return jnp.sum(swap(mine, "x").astype(F32), axis=0)


def split_three(value):
    return jnp.pad(jnp.stack(three(value)), (0, 765)).astype(BF)


def after(*arrays):
    return lax.optimization_barrier(arrays)


def total(parts):
    out = parts[0].astype(F32)
    for part in parts[1:]:
        out = out + part.astype(F32)
    return out


def three(value):
    high = lax.reduce_precision(value, 8, 7)
    rest = value - high
    middle = lax.reduce_precision(rest, 8, 7)
    return [high, middle, lax.reduce_precision(rest - middle, 8, 7)]


def gelu_value(values):
    return 0.5 * values * (1.0 + lax.erf(values * HALF_ROOT))


def gelu_slope(values):
    return 0.5 * (1.0 + lax.erf(values * HALF_ROOT)) + values * NORMAL_PEAK * jnp.exp(
        -0.5 * values * values
    )


def layer_norm(values, gain, shift):
    center = values - jnp.mean(values, axis=-1, keepdims=True)
    inverse = lax.rsqrt(jnp.mean(center * center, axis=-1, keepdims=True) + EPS)
    normed = center * inverse
    return (normed * gain + shift, normed, inverse)


def norm_back(grad, normed, inverse, gain):
    scaled = grad * gain
    inner = (
        scaled
        - jnp.mean(scaled, axis=-1, keepdims=True)
        - normed * jnp.mean(scaled * normed, axis=-1, keepdims=True)
    )
    return inner * inverse


def column_sum(values):
    return jnp.sum(values, axis=0, dtype=F32)


def matmul(left, right):
    return jnp.dot(left, right, preferred_element_type=F32)


def matmul_tn(left, right):
    return lax.dot_general(left, right, (((0,), (0,)), ((), ())), preferred_element_type=F32)


def matmul_nt(left, right):
    return lax.dot_general(left, right, (((1,), (1,)), ((), ())), preferred_element_type=F32)


def dot_nn(left, right):
    return lax.dot_general(left, right, (((1,), (0,)), ((), ())), preferred_element_type=F32)


def dot_nt(left, right):
    return lax.dot_general(left, right, (((1,), (1,)), ((), ())), preferred_element_type=F32)


def dot_tn(left, right):
    return lax.dot_general(left, right, (((0,), (0,)), ((), ())), preferred_element_type=F32)


def attention_forward_kernel(
    x_ref,
    row_ref,
    col_ref,
    wq_ref,
    wk_ref,
    wv_ref,
    wa_ref,
    vec_ref,
    qkv_ref,
    probs_ref,
    attended_ref,
    first_ref,
    low_ref,
    normed_ref,
    inverse_ref,
):
    tokens, width = x_ref.shape
    pair = 2 * HEAD_DIM
    factor = HEAD_DIM ** (-0.5)
    x = x_ref[...]
    qkv_ref[:, :width] = (dot_nn(x, wq_ref[...]) + vec_ref[0:1]).astype(BF)
    qkv_ref[:, width : 2 * width] = dot_nn(x, wk_ref[...]).astype(BF)
    qkv_ref[:, 2 * width :] = (dot_nn(x, wv_ref[...]) + vec_ref[1:2]).astype(BF)
    allowed = row_ref[...] == col_ref[...]
    lower = lax.broadcasted_iota(jnp.int32, (tokens, pair), 1) < HEAD_DIM
    for h in range(width // pair):
        lanes = slice(h * pair, (h + 1) * pair)
        query = qkv_ref[:, lanes]
        keys = qkv_ref[:, width + h * pair : width + (h + 1) * pair]
        values = qkv_ref[:, 2 * width + h * pair : 2 * width + (h + 1) * pair]
        zero = jnp.zeros_like(query)
        outs = []
        for side in range(2):
            mine = jnp.where(lower, query, zero) if side == 0 else jnp.where(lower, zero, query)
            scores = jnp.where(allowed, dot_nt(mine, keys) * factor, MASKED)
            expo = jnp.exp(scores - jnp.max(scores, axis=1, keepdims=True))
            probs = (expo / jnp.sum(expo, axis=1, keepdims=True)).astype(BF)
            probs_ref[2 * h + side] = probs
            outs.append(dot_nn(probs, values))
        attended_ref[:, lanes] = jnp.where(lower, outs[0], outs[1]).astype(BF)
    branch = dot_nn(attended_ref[...], wa_ref[...]) + vec_ref[2:3]
    first, normed, inverse = layer_norm(x.astype(F32) + branch, vec_ref[3:4], vec_ref[4:5])
    first_ref[...] = first
    low_ref[...] = first.astype(BF)
    normed_ref[...] = normed
    inverse_ref[...] = inverse


def weight_spec(width, block):
    return pl.BlockSpec((width, width), lambda m: (0, block))


def attention_forward(x, segments, layer, first_block, vec):
    micro, block = segments.shape
    tokens, width = x.shape
    heads = width // HEAD_DIM
    here = lambda n: pl.BlockSpec((block, n), lambda m: (m, 0))
    return pl.pallas_call(
        attention_forward_kernel,
        grid=(micro,),
        in_specs=[
            here(width),
            pl.BlockSpec((None, 1, block), lambda m: (m, 0, 0)),
            pl.BlockSpec((None, block, 1), lambda m: (m, 0, 0)),
            weight_spec(width, first_block),
            weight_spec(width, first_block + 1),
            weight_spec(width, first_block + 2),
            weight_spec(width, first_block + 3),
            pl.BlockSpec(vec.shape, lambda m: (0, 0)),
        ],
        out_specs=[
            here(3 * width),
            pl.BlockSpec((None, heads, block, block), lambda m: (m, 0, 0, 0)),
            here(width),
            here(width),
            here(width),
            here(width),
            here(1),
        ],
        out_shape=[
            jax.ShapeDtypeStruct((tokens, 3 * width), BF),
            jax.ShapeDtypeStruct((micro, heads, block, block), BF),
            jax.ShapeDtypeStruct((tokens, width), BF),
            jax.ShapeDtypeStruct((tokens, width), F32),
            jax.ShapeDtypeStruct((tokens, width), BF),
            jax.ShapeDtypeStruct((tokens, width), F32),
            jax.ShapeDtypeStruct((tokens, 1), F32),
        ],
        compiler_params=pltpu.CompilerParams(vmem_limit_bytes=48 * 1024 * 1024),
        cost_estimate=pl.CostEstimate(
            flops=4_000_000_000, bytes_accessed=16_000_000, transcendentals=2_000_000
        ),
    )(x, segments[:, None, :], segments[:, :, None], layer, layer, layer, layer, vec)


def attention_backward_kernel(dbranch_ref, qkv_ref, probs_ref, wa_ref, out_ref, sum_ref):
    tokens, width = dbranch_ref.shape
    pair = 2 * HEAD_DIM
    factor = HEAD_DIM ** (-0.5)
    dattended = dot_nt(dbranch_ref[...], wa_ref[...]).astype(BF)
    lower = lax.broadcasted_iota(jnp.int32, (tokens, pair), 1) < HEAD_DIM
    for h in range(width // pair):
        lanes = slice(h * pair, (h + 1) * pair)
        query = qkv_ref[:, lanes]
        keys = qkv_ref[:, width + h * pair : width + (h + 1) * pair]
        values = qkv_ref[:, 2 * width + h * pair : 2 * width + (h + 1) * pair]
        grad = dattended[:, lanes]
        zero = jnp.zeros_like(grad)
        parts = []
        for side in range(2):
            mine = jnp.where(lower, grad, zero) if side == 0 else jnp.where(lower, zero, grad)
            low = probs_ref[2 * h + side]
            probs = low.astype(F32)
            dprobs = dot_nt(mine, values)
            inner = jnp.sum(probs * dprobs, axis=1, keepdims=True)
            dscores = (probs * (dprobs - inner)).astype(BF)
            parts.append(
                (dot_nn(dscores, keys) * factor, dot_tn(dscores, query) * factor, dot_tn(low, grad))
            )
        for i in range(3):
            start = i * width + h * pair
            out_ref[:, start : start + pair] = jnp.where(lower, parts[0][i], parts[1][i]).astype(BF)
    seen = jnp.sum(out_ref[...].astype(F32), axis=0, keepdims=True)

    @pl.when(pl.program_id(0) == 0)
    def _():
        sum_ref[...] = seen

    @pl.when(pl.program_id(0) > 0)
    def _():
        sum_ref[...] += seen


def attention_backward(dbranch, qkv, probs, layer, attn_block):
    micro, heads, block, _ = probs.shape
    tokens, width = dbranch.shape
    here = lambda n: pl.BlockSpec((block, n), lambda m: (m, 0))
    return pl.pallas_call(
        attention_backward_kernel,
        grid=(micro,),
        in_specs=[
            here(width),
            here(3 * width),
            pl.BlockSpec((None, heads, block, block), lambda m: (m, 0, 0, 0)),
            weight_spec(width, attn_block),
        ],
        out_specs=[here(3 * width), pl.BlockSpec((1, 3 * width), lambda m: (0, 0))],
        out_shape=[
            jax.ShapeDtypeStruct((tokens, 3 * width), BF),
            jax.ShapeDtypeStruct((1, 3 * width), F32),
        ],
        compiler_params=pltpu.CompilerParams(vmem_limit_bytes=48 * 1024 * 1024),
        cost_estimate=pl.CostEstimate(
            flops=3_000_000_000, bytes_accessed=10_000_000, transcendentals=0
        ),
    )(dbranch, qkv, probs, layer)


def body(
    hidden_in,
    out_grad,
    segments,
    mask_pos,
    mask_labels,
    loss_scale,
    w_qkv,
    b_query,
    b_value,
    w_attn,
    b_attn,
    attn_gain,
    attn_shift,
    w_expand,
    b_expand,
    w_shrink,
    b_shrink,
    ffn_gain,
    ffn_shift,
    w_dense,
    b_dense,
    dense_gain,
    dense_shift,
    w_vocab,
    b_vocab,
):
    micro, block, width = hidden_in.shape
    tokens = micro * block
    heads = width // HEAD_DIM
    factor = HEAD_DIM ** (-0.5)
    at = {axis: lax.axis_index(axis) for axis in EVERY}
    vectors = (
        b_query,
        b_value,
        b_attn,
        attn_gain,
        attn_shift,
        b_shrink,
        ffn_gain,
        ffn_shift,
        b_dense,
        dense_gain,
        dense_shift,
    )
    small = after(jnp.stack(vectors))[0].T
    small = jnp.concatenate([small, b_expand.reshape(w_qkv.shape[0], -1)], axis=1)
    small = jnp.pad(small, ((0, 0), (0, 128 - small.shape[1])))
    fused = jnp.concatenate([w_expand, w_qkv, w_attn, w_dense, small], axis=1)
    fused = gather_x(fused).reshape(-1, fused.shape[1])
    tall = gather_x(w_shrink)
    tall = tall.transpose(1, 0, 2).reshape(fused.shape[0], -1)
    layer = lax.all_gather(
        jnp.concatenate([tall, fused], axis=1), ("y", "c", "z"), axis=0, tiled=True
    )
    own_w = w_vocab.T
    piece_w = [own_w] + [fetch(own_w, "x", k) for k in (1, 2, 3)]
    piece_b = [b_vocab] + [fetch(b_vocab, "x", k) for k in (1, 2, 3)]
    half_w = jnp.stack(piece_w)
    half_b = jnp.stack(piece_b)
    per = own_w.shape[0]
    vocab_w = jnp.concatenate([half_w, fetch(half_w, "c", 1)]).reshape(-1, width)
    vocab_b = jnp.concatenate([half_b, fetch(half_b, "c", 1)]).reshape(-1).astype(F32)
    start = jnp.stack(
        [
            (((at["y"] * NC + (at["c"] + kc) % NC) * NZ + at["z"]) * NX + (at["x"] + kx) % NX)
            * per
            for kc in range(NC)
            for kx in range(NX)
        ]
    )
    column = (start[:, None] + jnp.arange(per, dtype=jnp.int32)[None, :]).reshape(-1)

    flat_labels = mask_labels.reshape(micro, -1)
    counts = jnp.sum((flat_labels >= 0).astype(F32), axis=1)
    norms = 1.0 / (counts * micro)
    slots = mask_labels.shape[-1]
    peers = NZ * NX
    grid = mask_labels.reshape(micro, NY, NC, peers, NZ, NX, slots)
    grid = lax.dynamic_index_in_dim(grid, at["c"], 2, False)
    grid = lax.dynamic_index_in_dim(grid, at["x"], 4, False)
    labels = grid.transpose(1, 3, 0, 2, 4).reshape(-1)
    rows = micro * peers * slots
    row_norm = jnp.broadcast_to(norms[None, :, None], (NY * NZ, micro, peers * slots)).reshape(-1)
    live = (labels >= 0).astype(F32)
    row_weight = live * row_norm
    hit = labels[:, None] == column[None, :]
    scale = loss_scale * row_weight
    own_first = (at["y"] * NZ + at["z"]) * rows
    own_weight = lax.dynamic_slice_in_dim(row_weight, own_first, rows)
    label_w = matmul(hit.astype(BF), vocab_w)
    label_b = jnp.sum(jnp.where(hit, vocab_b, 0.0), axis=1, keepdims=True)
    label_w = jnp.concatenate([label_w, jnp.pad(label_b, ((0, 0), (0, 127)))], axis=1)
    label_w = label_w.astype(BF).reshape(NY * NZ, rows, -1)
    positions = mask_pos.reshape(micro, -1)
    shifted = jnp.where(
        positions >= 0, positions + block * jnp.arange(micro, dtype=jnp.int32)[:, None], -1
    ).reshape(-1)
    select = (shifted[:, None] == jnp.arange(tokens, dtype=jnp.int32)[None, :]).astype(BF)

    layer, label_w, vocab_w, select = after(layer, label_w, vocab_w, select)
    label_w = swap(label_w, ("y", "z"))
    ends = [NX * width, w_expand.shape[1], 3 * width, width, width, 128]
    ends = [sum(ends[: i + 1]) for i in range(len(ends))]
    expand_full = layer[:, ends[0] : ends[1]]
    qkv_full = layer[:, ends[1] : ends[2]]
    attn_block = ends[2] // width
    dense_full = layer[:, ends[3] : ends[4]]
    vec_full = layer[:, ends[4] :]
    shrink_full = jnp.stack(
        [
            layer[:, k * width : (k + 1) * width].reshape(
                NY * NC * NZ, -1, width
            )
            for k in range(NX)
        ],
        axis=1,
    ).reshape(-1, width)
    rows_of = vec_full[:, :16].T.astype(F32)
    (
        b_query,
        b_value,
        b_attn,
        attn_gain,
        attn_shift,
        b_shrink,
        ffn_gain,
        ffn_shift,
        b_dense,
        dense_gain,
        dense_shift,
    ) = (rows_of[i] for i in range(len(vectors)))
    b_expand = vec_full[:, 11:15].astype(F32).reshape(-1)

    x = hidden_in.reshape(tokens, width)
    qkv, probs, attended, first, first_low, normed1, inverse1 = attention_forward(
        x, segments, layer, attn_block - 3, rows_of
    )
    pre = matmul(first_low, expand_full) + b_expand
    act = gelu_value(pre).astype(BF)
    second = first + matmul(act, shrink_full) + b_shrink
    settled, normed2, inverse2 = layer_norm(second, ffn_gain, ffn_shift)
    settled_low = settled.astype(BF)

    select, label_w = after(select, label_w)
    label_w = jnp.sum(label_w.astype(F32), axis=0)
    label_w, label_b = label_w[:, :width], label_w[:, width]
    picked = matmul(select, settled_low).astype(BF)
    dense_pre = matmul(picked, dense_full) + b_dense
    head_val, normed3, inverse3 = layer_norm(gelu_value(dense_pre), dense_gain, dense_shift)
    head_out = head_val.astype(BF)
    spread = swap(
        jnp.broadcast_to(head_out, (NY * NZ,) + head_out.shape), ("y", "z")
    ).reshape(-1, width)
    logits = matmul_nt(spread, vocab_w) + vocab_b
    top = jnp.max(logits, axis=1)
    expl = jnp.exp(logits - top[:, None])
    part_sum = jnp.sum(expl, axis=1)
    other = jnp.where(hit, 0.0, expl).astype(BF)
    part = matmul(other, vocab_w).astype(BF).reshape(NY * NZ, rows, width)
    stats = jnp.stack(three(top) + three(part_sum)).astype(BF)
    stats = jnp.concatenate([stats[:, :width], stats[:, width:].reshape(2, width)])
    stats = jnp.broadcast_to(stats, (NY * NZ,) + stats.shape)
    part = swap(jnp.concatenate([part, stats], axis=1), ("y", "z"))
    stats = part[:, rows:]
    stats = jnp.concatenate(
        [stats[:, :6], stats[:, 6:].reshape(NY * NZ, 6, NY * NZ * rows - width)], axis=2
    ).astype(F32)
    tops = stats[:, 0] + stats[:, 1] + stats[:, 2]
    sums = stats[:, 3] + stats[:, 4] + stats[:, 5]
    top_all = jnp.max(tops, axis=0)
    shares = jnp.exp(tops - top_all)
    sum_all = jnp.sum(sums * shares, axis=0)
    log_sums = top_all + jnp.log(sum_all)
    log_sum = lax.dynamic_slice_in_dim(log_sums, own_first, rows)
    share = lax.dynamic_slice_in_dim(shares / sum_all, own_first, rows, 1)
    label_logit = jnp.sum(head_out.astype(F32) * label_w, axis=1) + label_b
    mixed = jnp.sum(share[:, :, None] * part[:, :rows].astype(F32), axis=0)
    row_grad = (loss_scale * own_weight)[:, None] * (
        mixed + (jnp.exp(label_logit - log_sum) - 1.0)[:, None] * label_w
    )
    loss_own = jnp.sum(own_weight * (log_sum - label_logit))
    g_dense_gain = column_sum(row_grad * normed3)
    g_dense_shift = column_sum(row_grad)
    ddense = (norm_back(row_grad, normed3, inverse3, dense_gain) * gelu_slope(dense_pre)).astype(BF)
    g_dense = matmul_tn(picked, ddense)
    g_dense_bias = column_sum(ddense)
    drows = matmul_nt(ddense, dense_full).astype(BF)

    dout = out_grad.reshape(tokens, width).astype(F32) + matmul_tn(select, drows)
    g_ffn_gain = column_sum(dout * normed2)
    g_ffn_shift = column_sum(dout)
    dsecond = norm_back(dout, normed2, inverse2, ffn_gain)
    dffn = dsecond.astype(BF)
    g_shrink = matmul_tn(act, dffn)
    loss_row = jnp.where(
        (jnp.arange(NC) == at["c"])[None, :, None, None, None], split_three(loss_own), 0.0
    ).astype(BF)
    loss_row = jnp.broadcast_to(loss_row, (NY, NC, NZ, 8, width))
    tall_pair = sum_cores([blocks(g_shrink), blocks(g_dense), loss_row], 1)
    g_shrink_bias = column_sum(dffn)
    dpre = (matmul_nt(dffn, shrink_full) * gelu_slope(pre)).astype(BF)
    dpre, tall_mine = after(dpre, add_cores(tall_pair))
    g_expand = matmul_tn(first_low, dpre)
    wide_pair = sum_cores([blocks(g_expand)], 2)
    g_expand_bias = column_sum(dpre)
    dfirst = dsecond + matmul_nt(dpre, expand_full)
    g_attn_gain = column_sum(dfirst * normed1)
    g_attn_shift = column_sum(dfirst)
    dresidual = norm_back(dfirst, normed1, inverse1, attn_gain)
    dbranch = dresidual.astype(BF)
    tall_all = swap(tall_mine, ("y", "z"))
    g_attn = matmul_tn(attended, dbranch)
    g_attn_bias = column_sum(dbranch)
    dfused, fused_sum = attention_backward(dbranch, qkv, probs, layer, attn_block)
    dfused, got, tall_all = after(dfused, wide_pair[1], tall_all)
    wide_mine = add_cores((wide_pair[0], got))
    g_qkv = matmul_tn(x, dfused)
    g_query, g_value = fused_sum[0, :width], fused_sum[0, 2 * width :]
    dinput = dresidual + matmul_nt(dfused, qkv_full)

    late_sums, dfused = after(log_sums, dfused)
    dlogits = (
        (scale * jnp.exp(top - late_sums))[:, None] * expl
        - jnp.where(hit, scale[:, None], 0.0)
    ).astype(BF)
    grad_w = matmul_tn(dlogits, spread).astype(BF).reshape(NC, NX, per, width)
    grad_b = column_sum(dlogits).reshape(NC, NX, 1, per)
    grad_b = jnp.pad(grad_b, ((0, 0), (0, 0), (0, 7), (0, width - per))).astype(BF)
    grad_w = jnp.concatenate([grad_w, grad_b], axis=2)
    grad_w = (grad_w[0].astype(F32) + give(grad_w[1], "c", 1).astype(F32)).astype(BF)
    grad_w = total([grad_w[0]] + [give(grad_w[k], "x", k) for k in (1, 2, 3)])
    g_vocab, g_vocab_bias = grad_w[:per].T, grad_w[per, :per]

    sums = jnp.stack(
        [
            g_query,
            g_value,
            g_attn_bias,
            g_attn_gain,
            g_attn_shift,
            g_shrink_bias,
            g_ffn_gain,
            g_ffn_shift,
            g_dense_bias,
            g_dense_gain,
            g_dense_shift,
        ]
    )
    sums = jnp.concatenate([after(sums)[0].T, g_expand_bias.reshape(width, -1)], axis=1)
    sums = jnp.pad(sums, ((0, 0), (0, 128 - sums.shape[1])))
    wide = sum_yz(wide_mine)
    last_pair = sum_cores([blocks(g_qkv), blocks(g_attn), blocks(sums)], 2)
    last_pair, wide, tall_all = after(last_pair, wide, tall_all)
    tall = jnp.sum(tall_all[:, :120].astype(F32), axis=0).astype(BF)
    loss_row = split_three(jnp.sum(tall_all[:, 120, :3].astype(F32)))[:128]
    tall_low = tall[:96].reshape(NX, 4, 6, width).transpose(0, 2, 1, 3).reshape(NX, 6, 4 * width)
    early = jnp.concatenate(
        [
            wide.reshape(NX, 6, -1),
            tall_low,
            tall[96:].reshape(NX, 6, width),
            jnp.broadcast_to(loss_row, (NX, 6, 128)),
        ],
        axis=2,
    )
    last = sum_yz(add_cores(last_pair))
    last = sum_x(jnp.concatenate([early, last.reshape(NX, 6, -1)], axis=2))
    ends = [w_expand.shape[1], 4 * width, width, 128, 3 * width, width, 128]
    ends = [sum(ends[: i + 1]) for i in range(len(ends))]
    g_expand = last[:, : ends[0]]
    g_shrink = last[:, ends[0] : ends[1]].reshape(6, 4, width).transpose(1, 0, 2).reshape(24, width)
    g_dense = last[:, ends[1] : ends[2]]
    loss = jnp.full((8, 128), jnp.sum(last[0, ends[2] : ends[2] + 3]))
    loss = (loss + give(loss, "c", 1))[0, 0]
    g_qkv = last[:, ends[3] : ends[4]]
    g_attn = last[:, ends[4] : ends[5]]
    sums = last[:, ends[5] :]
    return (
        settled_low.reshape(hidden_in.shape),
        loss,
        dinput.reshape(hidden_in.shape),
        g_qkv,
        sums[:, 0],
        sums[:, 1],
        g_attn,
        sums[:, 2],
        sums[:, 3],
        sums[:, 4],
        g_expand,
        sums[:, 11:15].reshape(-1),
        g_shrink,
        sums[:, 5],
        sums[:, 6],
        sums[:, 7],
        g_dense,
        sums[:, 8],
        sums[:, 9],
        sums[:, 10],
        g_vocab,
        g_vocab_bias,
    )


def solution(mesh):
    split = Mesh(mesh.devices.reshape(NY, NC, NZ, NX), EVERY)
    whole, one = P(), P(EVERY)
    tokens3 = P(None, EVERY, None)
    matrix = P(EVERY, None)
    in_specs = (
        tokens3,
        tokens3,
        P(None, EVERY),
        P(None, EVERY, None, None),
        whole,
        whole,
        matrix,
        one,
        one,
        matrix,
        one,
        one,
        one,
        matrix,
        one,
        matrix,
        one,
        one,
        one,
        matrix,
        one,
        one,
        one,
        P(None, EVERY),
        one,
    )
    out_specs = (
        tokens3,
        whole,
        tokens3,
        matrix,
        one,
        one,
        matrix,
        one,
        one,
        one,
        matrix,
        one,
        matrix,
        one,
        one,
        one,
        matrix,
        one,
        one,
        one,
        P(None, EVERY),
        one,
    )
    return jax.shard_map(body, mesh=split, in_specs=in_specs, out_specs=out_specs, check_vma=False)
```

```python
import jax
import jax.numpy as jnp
from jax import lax
from jax.experimental import pallas as pl
from jax.experimental.pallas import tpu as pltpu
from jax.sharding import Mesh
from jax.sharding import PartitionSpec as P

HEAD_DIM = 64
EPS = 1e-05
HALF_ROOT = 0.7071067811865476
NORMAL_PEAK = 0.3989422804014327
MASKED = -1e30

BF = jnp.bfloat16
F32 = jnp.float32
NY, NC, NZ, NX = 4, 2, 4, 4
SIZES = {"y": NY, "c": NC, "z": NZ, "x": NX}
EVERY = ("y", "c", "z", "x")


def fetch(array, axis, k):
    n = SIZES[axis]
    return lax.ppermute(array, axis, [((i + k) % n, i) for i in range(n)])


def give(array, axis, k):
    n = SIZES[axis]
    return lax.ppermute(array, axis, [(i, (i + k) % n) for i in range(n)])


def in_order(pieces, index):
    n = len(pieces)
    twice = jnp.stack(pieces + pieces)
    return lax.dynamic_slice_in_dim(twice, (n - index) % n, n, 0)


def gather_x(shard):
    pieces = [shard] + [fetch(shard, "x", k) for k in (1, 2, 3)]
    return in_order(pieces, lax.axis_index("x"))


def swap(array, axes):
    return lax.all_to_all(array, axes, 0, 0, tiled=True)


def blocks(grad):
    return grad.astype(BF).reshape(NY, NC, NZ, -1, grad.shape[1])


def half(grads, core, axis):
    cut = [lax.dynamic_index_in_dim(grad, core, 1, False) for grad in grads]
    cut = [part.reshape((NY * NZ,) + part.shape[2:]) for part in cut]
    return cut[0] if len(cut) == 1 else jnp.concatenate(cut, axis=axis)


def sum_cores(grads, axis):
    core = lax.axis_index("c")
    return half(grads, core, axis), give(half(grads, 1 - core, axis), "c", 1)


def add_cores(pair):
    return (pair[0].astype(F32) + pair[1].astype(F32)).astype(BF)


def sum_yz(mine):
    return jnp.sum(swap(mine, ("y", "z")).astype(F32), axis=0).astype(BF)


def sum_x(mine):
    return jnp.sum(swap(mine, "x").astype(F32), axis=0)


def split_three(value):
    return jnp.pad(jnp.stack(three(value)), (0, 765)).astype(BF)


def after(*arrays):
    return lax.optimization_barrier(arrays)


def total(parts):
    out = parts[0].astype(F32)
    for part in parts[1:]:
        out = out + part.astype(F32)
    return out


def three(value):
    high = lax.reduce_precision(value, 8, 7)
    rest = value - high
    middle = lax.reduce_precision(rest, 8, 7)
    return [high, middle, lax.reduce_precision(rest - middle, 8, 7)]


def gelu_value(values):
    return 0.5 * values * (1.0 + lax.erf(values * HALF_ROOT))


def gelu_slope(values):
    return 0.5 * (1.0 + lax.erf(values * HALF_ROOT)) + values * NORMAL_PEAK * jnp.exp(
        -0.5 * values * values
    )


def layer_norm(values, gain, shift):
    center = values - jnp.mean(values, axis=-1, keepdims=True)
    inverse = lax.rsqrt(jnp.mean(center * center, axis=-1, keepdims=True) + EPS)
    normed = center * inverse
    return (normed * gain + shift, normed, inverse)


def norm_back(grad, normed, inverse, gain):
    scaled = grad * gain
    inner = (
        scaled
        - jnp.mean(scaled, axis=-1, keepdims=True)
        - normed * jnp.mean(scaled * normed, axis=-1, keepdims=True)
    )
    return inner * inverse


def column_sum(values):
    return jnp.sum(values, axis=0, dtype=F32)


def matmul(left, right):
    return jnp.dot(left, right, preferred_element_type=F32)


def matmul_tn(left, right):
    return lax.dot_general(left, right, (((0,), (0,)), ((), ())), preferred_element_type=F32)


def matmul_nt(left, right):
    return lax.dot_general(left, right, (((1,), (1,)), ((), ())), preferred_element_type=F32)


def dot_nn(left, right):
    return lax.dot_general(left, right, (((1,), (0,)), ((), ())), preferred_element_type=F32)


def dot_nt(left, right):
    return lax.dot_general(left, right, (((1,), (1,)), ((), ())), preferred_element_type=F32)


def dot_tn(left, right):
    return lax.dot_general(left, right, (((0,), (0,)), ((), ())), preferred_element_type=F32)


def attention_forward_kernel(
    x_ref,
    row_ref,
    col_ref,
    wq_ref,
    wk_ref,
    wv_ref,
    wa_ref,
    vec_ref,
    qkv_ref,
    probs_ref,
    attended_ref,
    first_ref,
    low_ref,
    normed_ref,
    inverse_ref,
):
    tokens, width = x_ref.shape
    pair = 2 * HEAD_DIM
    factor = HEAD_DIM ** (-0.5)
    x = x_ref[...]
    qkv_ref[:, :width] = (dot_nn(x, wq_ref[...]) + vec_ref[0:1]).astype(BF)
    qkv_ref[:, width : 2 * width] = dot_nn(x, wk_ref[...]).astype(BF)
    qkv_ref[:, 2 * width :] = (dot_nn(x, wv_ref[...]) + vec_ref[1:2]).astype(BF)
    allowed = row_ref[...] == col_ref[...]
    lower = lax.broadcasted_iota(jnp.int32, (tokens, pair), 1) < HEAD_DIM
    for h in range(width // pair):
        lanes = slice(h * pair, (h + 1) * pair)
        query = qkv_ref[:, lanes]
        keys = qkv_ref[:, width + h * pair : width + (h + 1) * pair]
        values = qkv_ref[:, 2 * width + h * pair : 2 * width + (h + 1) * pair]
        zero = jnp.zeros_like(query)
        outs = []
        for side in range(2):
            mine = jnp.where(lower, query, zero) if side == 0 else jnp.where(lower, zero, query)
            scores = jnp.where(allowed, dot_nt(mine, keys) * factor, MASKED)
            expo = jnp.exp(scores - jnp.max(scores, axis=1, keepdims=True))
            probs = (expo / jnp.sum(expo, axis=1, keepdims=True)).astype(BF)
            probs_ref[2 * h + side] = probs
            outs.append(dot_nn(probs, values))
        attended_ref[:, lanes] = jnp.where(lower, outs[0], outs[1]).astype(BF)
    branch = dot_nn(attended_ref[...], wa_ref[...]) + vec_ref[2:3]
    first, normed, inverse = layer_norm(x.astype(F32) + branch, vec_ref[3:4], vec_ref[4:5])
    first_ref[...] = first
    low_ref[...] = first.astype(BF)
    normed_ref[...] = normed
    inverse_ref[...] = inverse


def weight_spec(width, block):
    return pl.BlockSpec((width, width), lambda m: (0, block))


def attention_forward(x, segments, layer, first_block, vec):
    micro, block = segments.shape
    tokens, width = x.shape
    heads = width // HEAD_DIM
    here = lambda n: pl.BlockSpec((block, n), lambda m: (m, 0))
    return pl.pallas_call(
        attention_forward_kernel,
        grid=(micro,),
        in_specs=[
            here(width),
            pl.BlockSpec((None, 1, block), lambda m: (m, 0, 0)),
            pl.BlockSpec((None, block, 1), lambda m: (m, 0, 0)),
            weight_spec(width, first_block),
            weight_spec(width, first_block + 1),
            weight_spec(width, first_block + 2),
            weight_spec(width, first_block + 3),
            pl.BlockSpec(vec.shape, lambda m: (0, 0)),
        ],
        out_specs=[
            here(3 * width),
            pl.BlockSpec((None, heads, block, block), lambda m: (m, 0, 0, 0)),
            here(width),
            here(width),
            here(width),
            here(width),
            here(1),
        ],
        out_shape=[
            jax.ShapeDtypeStruct((tokens, 3 * width), BF),
            jax.ShapeDtypeStruct((micro, heads, block, block), BF),
            jax.ShapeDtypeStruct((tokens, width), BF),
            jax.ShapeDtypeStruct((tokens, width), F32),
            jax.ShapeDtypeStruct((tokens, width), BF),
            jax.ShapeDtypeStruct((tokens, width), F32),
            jax.ShapeDtypeStruct((tokens, 1), F32),
        ],
        compiler_params=pltpu.CompilerParams(vmem_limit_bytes=48 * 1024 * 1024),
        cost_estimate=pl.CostEstimate(
            flops=4_000_000_000, bytes_accessed=16_000_000, transcendentals=2_000_000
        ),
    )(x, segments[:, None, :], segments[:, :, None], layer, layer, layer, layer, vec)


def attention_backward_kernel(dbranch_ref, qkv_ref, probs_ref, wa_ref, out_ref, sum_ref):
    tokens, width = dbranch_ref.shape
    pair = 2 * HEAD_DIM
    factor = HEAD_DIM ** (-0.5)
    dattended = dot_nt(dbranch_ref[...], wa_ref[...]).astype(BF)
    lower = lax.broadcasted_iota(jnp.int32, (tokens, pair), 1) < HEAD_DIM
    for h in range(width // pair):
        lanes = slice(h * pair, (h + 1) * pair)
        query = qkv_ref[:, lanes]
        keys = qkv_ref[:, width + h * pair : width + (h + 1) * pair]
        values = qkv_ref[:, 2 * width + h * pair : 2 * width + (h + 1) * pair]
        grad = dattended[:, lanes]
        zero = jnp.zeros_like(grad)
        parts = []
        for side in range(2):
            mine = jnp.where(lower, grad, zero) if side == 0 else jnp.where(lower, zero, grad)
            low = probs_ref[2 * h + side]
            probs = low.astype(F32)
            dprobs = dot_nt(mine, values)
            inner = jnp.sum(probs * dprobs, axis=1, keepdims=True)
            dscores = (probs * (dprobs - inner)).astype(BF)
            parts.append(
                (dot_nn(dscores, keys) * factor, dot_tn(dscores, query) * factor, dot_tn(low, grad))
            )
        for i in range(3):
            start = i * width + h * pair
            out_ref[:, start : start + pair] = jnp.where(lower, parts[0][i], parts[1][i]).astype(BF)
    seen = jnp.sum(out_ref[...].astype(F32), axis=0, keepdims=True)

    @pl.when(pl.program_id(0) == 0)
    def _():
        sum_ref[...] = seen

    @pl.when(pl.program_id(0) > 0)
    def _():
        sum_ref[...] += seen


def attention_backward(dbranch, qkv, probs, layer, attn_block):
    micro, heads, block, _ = probs.shape
    tokens, width = dbranch.shape
    here = lambda n: pl.BlockSpec((block, n), lambda m: (m, 0))
    return pl.pallas_call(
        attention_backward_kernel,
        grid=(micro,),
        in_specs=[
            here(width),
            here(3 * width),
            pl.BlockSpec((None, heads, block, block), lambda m: (m, 0, 0, 0)),
            weight_spec(width, attn_block),
        ],
        out_specs=[here(3 * width), pl.BlockSpec((1, 3 * width), lambda m: (0, 0))],
        out_shape=[
            jax.ShapeDtypeStruct((tokens, 3 * width), BF),
            jax.ShapeDtypeStruct((1, 3 * width), F32),
        ],
        compiler_params=pltpu.CompilerParams(vmem_limit_bytes=48 * 1024 * 1024),
        cost_estimate=pl.CostEstimate(
            flops=1000, bytes_accessed=1000, transcendentals=0
        ),
    )(dbranch, qkv, probs, layer)


LIMIT = 56 * 1024 * 1024


def whole_spec(array):
    return pl.BlockSpec(array.shape, lambda *_: (0,) * len(array.shape))


def call(kernel, grid, ins, in_specs, outs, out_specs, scratch, flops, size):
    return pl.pallas_call(
        kernel,
        grid=grid,
        in_specs=in_specs,
        out_specs=out_specs,
        out_shape=[jax.ShapeDtypeStruct(shape, kind) for shape, kind in outs],
        scratch_shapes=scratch,
        compiler_params=pltpu.CompilerParams(vmem_limit_bytes=LIMIT),
        cost_estimate=pl.CostEstimate(flops=flops, bytes_accessed=size, transcendentals=0),
    )(*ins)


def low_three(value):
    high = value.astype(BF).astype(F32)
    middle = (value - high).astype(BF).astype(F32)
    rest = (value - high - middle).astype(BF).astype(F32)
    return [high, middle, rest]


def logits_kernel(
    spread_ref, w_ref, b_ref, column_ref, label_ref, expl_ref, stat_ref, part_ref, flat_ref, logits_ref
):
    step = pl.program_id(0)
    count, width = spread_ref.shape
    peers, high, _ = part_ref.shape
    rows = high - 16
    spread = spread_ref[...]
    entries = w_ref.shape[0]
    chunks = [slice(i, i + entries // 5) for i in range(0, entries, entries // 5)]
    peak = None
    for cut in chunks:
        logits = dot_nt(spread, w_ref[cut, :]) + b_ref[:, cut]
        logits_ref[:, cut] = logits
        most = jnp.max(logits, axis=1, keepdims=True)
        peak = most if peak is None else jnp.maximum(peak, most)
    top = peak
    sums = jnp.zeros((count, 1), F32)
    label = jnp.zeros((count, 1), F32)
    part = jnp.zeros((count, width), F32)
    for cut in chunks:
        expl = jnp.exp(logits_ref[:, cut] - top)
        sums += jnp.sum(expl, axis=1, keepdims=True)
        hit = label_ref[...] == column_ref[:, cut]
        rest = jnp.where(hit, 0.0, expl)
        label += jnp.sum(expl - rest, axis=1, keepdims=True)
        other = rest.astype(BF)
        expl_ref[:, cut] = other
        part += dot_nn(other, w_ref[cut, :])
    part = part.astype(BF)
    for i in range(count // rows):
        part_ref[step * (count // rows) + i, 0:rows, :] = part[i * rows : (i + 1) * rows]
    lane = lax.broadcasted_iota(jnp.int32, (count, 128), 1)
    stat = jnp.where(lane == 0, top, jnp.where(lane == 1, label, 0.0))
    stat_ref[...] = stat
    parts = jnp.zeros((count, 128), F32)
    for i, value in enumerate(low_three(top) + low_three(sums)):
        parts = jnp.where(lane == i, value, parts)
    flat_ref[step] = parts.T[0:8]

    @pl.when(step == pl.num_programs(0) - 1)
    def _():
        told = jnp.concatenate([flat_ref[i] for i in range(flat_ref.shape[0])], axis=1)
        rest = told.shape[1] - width
        last = jnp.concatenate([told[:, width:], jnp.zeros((8, width - rest), F32)], axis=1)
        told = jnp.concatenate([told[:, :width], last], axis=0).astype(BF)
        for i in range(peers):
            part_ref[i, rows:, :] = told


def logits_call(spread, vocab_w, vocab_b, column, labels, rows):
    count, width = spread.shape
    entries = vocab_w.shape[0]
    block = count // 2
    here = lambda n: pl.BlockSpec((block, n), lambda i: (i, 0))
    ins = (spread, vocab_w, vocab_b[None, :], column[None, :], labels)
    specs = [here(width)] + [whole_spec(a) for a in ins[1:4]] + [here(1)]
    part = (count // rows, rows + 16, width)
    return call(
        logits_kernel,
        (2,),
        ins,
        specs,
        [((count, entries), BF), ((count, 128), F32), (part, BF)],
        [here(entries), here(128), pl.BlockSpec(part, lambda i: (0, 0, 0))],
        [pltpu.VMEM((2, 8, block), F32), pltpu.VMEM((block, entries), F32)],
        10_000_000_000,
        20_000_000,
    )


def decoder_kernel(
    expl_ref, spread_ref, column_ref, label_ref, scale_ref, stat_ref, lse_ref, out_ref
):
    count, width = spread_ref.shape
    lse = jnp.broadcast_to(lse_ref[...], (8, count)).T[:, 0:1]
    share = jnp.exp(stat_ref[:, 0:1] - lse)
    scale = scale_ref[...]
    hit = label_ref[...] == column_ref[...]
    other = (scale * share) * expl_ref[...].astype(F32)
    dlogits = jnp.where(hit, scale * (stat_ref[:, 1:2] * share - 1.0), other).astype(BF)
    out_ref[:, :width] = dot_tn(dlogits, spread_ref[...]).astype(BF)
    ones = jnp.ones((count, out_ref.shape[1] - width), BF)
    out_ref[:, width:] = dot_tn(dlogits, ones).astype(BF)


def decoder_call(expl, spread, column, labels, scale, stat, lse):
    count, width = spread.shape
    entries = expl.shape[1]
    block = entries // 5
    ins = (expl, spread, column[None, :], labels, scale, stat, lse)
    return call(
        decoder_kernel,
        (5,),
        ins,
        [
            pl.BlockSpec((count, block), lambda j: (0, j)),
            whole_spec(spread),
            pl.BlockSpec((1, block), lambda j: (0, j)),
        ]
        + [whole_spec(a) for a in ins[3:]],
        [((entries, width + 128), BF)],
        [pl.BlockSpec((block, width + 128), lambda j: (j, 0))],
        [],
        1000,
        1000,
    )[0]


def merge_kernel(
    own_ref,
    part_ref,
    head_ref,
    label_ref,
    scalar_ref,
    normed3_ref,
    slope3_ref,
    vec_ref,
    picked_ref,
    dense_ref,
    select_ref,
    grad_ref,
    normed2_ref,
    inverse2_ref,
    lse_ref,
    loss_ref,
    g_dense_ref,
    dsecond_ref,
    dffn_ref,
    sums_ref,
):
    peers, high, width = part_ref.shape
    rows = high - 16
    tail = peers * rows - width

    def told(i):
        first = part_ref[:, rows : rows + 8, :].astype(F32)[:, i]
        rest = part_ref[:, rows + 8 :, :].astype(F32)[:, i, :tail]
        return jnp.concatenate([first, rest], axis=1)

    tops = told(0) + told(1) + told(2)
    sums = told(3) + told(4) + told(5)
    top = jnp.max(tops, axis=0, keepdims=True)
    share = jnp.exp(tops - top)
    total_sum = jnp.sum(sums * share, axis=0, keepdims=True)
    lse = top + jnp.log(total_sum)
    share = share / total_sum
    lse_ref[...] = lse
    mine = own_ref[0] + lax.broadcasted_iota(jnp.int32, (rows, peers * rows), 0)
    mine = mine == lax.broadcasted_iota(jnp.int32, (rows, peers * rows), 1)
    own_lse = jnp.sum(jnp.where(mine, lse, 0.0), axis=1, keepdims=True)
    mixed = jnp.zeros((rows, width), F32)
    for i in range(peers):
        weight = jnp.sum(jnp.where(mine, share[i : i + 1], 0.0), axis=1, keepdims=True)
        mixed += weight * part_ref[i, 0:rows, :].astype(F32)
    label = label_ref[...]
    label_logit = jnp.sum(head_ref[...].astype(F32) * label, axis=1, keepdims=True)
    label_logit += scalar_ref[:, 0:1]
    grad = scalar_ref[:, 2:3] * (mixed + (jnp.exp(label_logit - own_lse) - 1.0) * label)
    loss_ref[...] = jnp.zeros(loss_ref.shape, F32) + jnp.sum(
        scalar_ref[:, 1:2] * (own_lse - label_logit)
    )
    normed3 = normed3_ref[...]
    ddense = norm_back(grad, normed3, scalar_ref[:, 3:4], vec_ref[9:10]) * slope3_ref[...]
    low = ddense.astype(BF)
    column = lambda v: jnp.sum(v, axis=0, keepdims=True)
    g_dense_ref[...] = dot_tn(picked_ref[...], low)
    drows = dot_nt(low, dense_ref[...]).astype(BF)
    dout = grad_ref[...].astype(F32) + dot_tn(select_ref[...], drows)
    normed2 = normed2_ref[...]
    dsecond = norm_back(dout, normed2, inverse2_ref[...], vec_ref[6:7])
    dffn = dsecond.astype(BF)
    dsecond_ref[...] = dsecond
    dffn_ref[...] = dffn
    parts = [
        column(low.astype(F32)),
        column(grad * normed3),
        column(grad),
        column(dout * normed2),
        column(dout),
        column(dffn.astype(F32)),
    ]
    for i, value in enumerate(parts):
        sums_ref[i : i + 1] = value


def merge_call(own, *arrays, layer, dense_block):
    part, head = arrays[0], arrays[1]
    width = head.shape[1]
    tokens = arrays[-1].shape[0]
    count = part.shape[0] * (part.shape[1] - 16)
    ins = list(arrays)
    ins.insert(8, layer)
    specs = [whole_spec(a) for a in arrays]
    specs.insert(8, pl.BlockSpec((width, width), lambda *_: (0, dense_block)))
    outs = [
        ((1, count), F32),
        ((8, 128), F32),
        ((width, width), F32),
        ((tokens, width), F32),
        ((tokens, width), BF),
        ((8, width), F32),
    ]
    return call(
        merge_kernel,
        (1,),
        [own] + ins,
        [pl.BlockSpec(memory_space=pltpu.SMEM)] + specs,
        outs,
        [pl.BlockSpec(shape, lambda *_: (0, 0)) for shape, _ in outs],
        [],
        300_000_000,
        10_000_000,
    )


def keep_halves(core, block, here, away):
    for c in range(NC):

        @pl.when(core == c)
        def _():
            here(block(c))

        @pl.when(core != c)
        def _():
            away(block(c))


def shrink_kernel(core_ref, act_ref, dffn_ref, dense_ref, loss_ref, here_ref, away_ref):
    width = dffn_ref.shape[1]
    grad = dot_tn(act_ref[...], dffn_ref[...])
    core = core_ref[0]
    spot = lax.broadcasted_iota(jnp.int32, (8, width), 1)
    first = lax.broadcasted_iota(jnp.int32, (8, width), 0) == 0
    told = jnp.zeros((8, width), F32)
    for i, value in enumerate(low_three(loss_ref[0:1, 0:1])):
        told = jnp.where(first & (spot == i + 3 * core), value, told)

    def put(ref, extra):
        def store(block):
            tall, dense = block
            for z in range(NZ):
                ref[z, 0:96, :] = tall[z * 96 : (z + 1) * 96].astype(BF)
                ref[z, 96:128, :] = jnp.concatenate(
                    [dense[z * 24 : (z + 1) * 24], extra], axis=0
                ).astype(BF)

        return store

    def block(c):
        tall = grad[c * width // 2 : (c + 1) * width // 2]
        return tall, dense_ref[c * 96 : (c + 1) * 96, :]

    keep_halves(core, block, put(here_ref, told), put(away_ref, told))


def shrink_call(core, act, dffn, g_dense, loss):
    tokens, width = dffn.shape
    out = ((NY * NZ, 128, width), BF)
    half_spec = pl.BlockSpec((NZ, 128, width), lambda y: (y, 0, 0))
    return call(
        shrink_kernel,
        (NY,),
        (core, act, dffn, g_dense, loss),
        [
            pl.BlockSpec(memory_space=pltpu.SMEM),
            pl.BlockSpec((tokens, width), lambda y: (0, y)),
            whole_spec(dffn),
            pl.BlockSpec((width // NY, width), lambda y: (y, 0)),
            whole_spec(loss),
        ],
        [out, out],
        [half_spec, half_spec],
        [],
        1000,
        1000,
    )


def put_wide(grad, core, here_ref, away_ref, lanes):
    def block(c):
        return [grad[96 * (NC * y + c) : 96 * (NC * y + c) + 96] for y in range(NY)]

    def put(ref):
        def store(parts):
            for y, part in enumerate(parts):
                ref[y * NZ : (y + 1) * NZ, :, lanes] = part.reshape(NZ, 24, -1).astype(BF)

        return store

    keep_halves(core, block, put(here_ref), put(away_ref))


def feed_back_kernel(
    core_ref,
    dffn_ref,
    shrink_ref,
    slope_ref,
    low_ref,
    expand_ref,
    dsecond_ref,
    normed_ref,
    inverse_ref,
    vec_ref,
    here_ref,
    away_ref,
    bias_ref,
    dresidual_ref,
    dbranch_ref,
    sums_ref,
    total_ref,
):
    step = pl.program_id(0)
    dpre = (dot_nt(dffn_ref[...], shrink_ref[...]) * slope_ref[...].astype(F32)).astype(BF)
    bias_ref[...] = jnp.sum(dpre.astype(F32), axis=0, keepdims=True)
    more = dot_nt(dpre, expand_ref[...])

    @pl.when(step == 0)
    def _():
        total_ref[...] = dsecond_ref[...] + more

    @pl.when(step > 0)
    def _():
        total_ref[...] += more

    put_wide(dot_tn(low_ref[...], dpre), core_ref[0], here_ref, away_ref, slice(None))

    @pl.when(step == pl.num_programs(0) - 1)
    def _():
        dfirst = total_ref[...]
        normed = normed_ref[...]
        dresidual = norm_back(dfirst, normed, inverse_ref[...], vec_ref[3:4])
        dbranch = dresidual.astype(BF)
        dresidual_ref[...] = dresidual
        dbranch_ref[...] = dbranch
        sums_ref[0:1] = jnp.sum(dfirst * normed, axis=0, keepdims=True)
        sums_ref[1:2] = jnp.sum(dfirst, axis=0, keepdims=True)
        sums_ref[2:3] = jnp.sum(dbranch.astype(F32), axis=0, keepdims=True)


def feed_back_call(core, dffn, shrink, slope, low, layer, expand_block, dsecond, normed, inverse, vec):
    tokens, width = dffn.shape
    wide = slope.shape[1]
    half = ((NY * NZ, 24, wide), BF)
    half_spec = pl.BlockSpec((NY * NZ, 24, width), lambda j: (0, 0, j))
    outs = [
        half,
        half,
        ((1, wide), F32),
        ((tokens, width), F32),
        ((tokens, width), BF),
        ((8, width), F32),
    ]
    return call(
        feed_back_kernel,
        (wide // width,),
        (core, dffn, shrink, slope, low, layer, dsecond, normed, inverse, vec),
        [
            pl.BlockSpec(memory_space=pltpu.SMEM),
            whole_spec(dffn),
            pl.BlockSpec((width, width), lambda j: (j, 0)),
            pl.BlockSpec((tokens, width), lambda j: (0, j)),
            whole_spec(low),
            pl.BlockSpec((width, width), lambda j: (0, expand_block + j)),
            whole_spec(dsecond),
            whole_spec(normed),
            whole_spec(inverse),
            whole_spec(vec),
        ],
        outs,
        [
            half_spec,
            half_spec,
            pl.BlockSpec((1, width), lambda j: (0, j)),
            pl.BlockSpec((tokens, width), lambda j: (0, 0)),
            pl.BlockSpec((tokens, width), lambda j: (0, 0)),
            pl.BlockSpec((8, width), lambda j: (0, 0)),
        ],
        [pltpu.VMEM((tokens, width), F32)],
        1000,
        1000,
    )


def last_kernel(core_ref, x_ref, dfused_ref, attended_ref, dbranch_ref, sums_ref, here_ref, away_ref):
    width = x_ref.shape[1]
    core = core_ref[0]
    for i in range(4):
        lanes = slice(i * width, (i + 1) * width)
        if i < 3:
            grad = dot_tn(x_ref[...], dfused_ref[:, lanes])
        else:
            grad = dot_tn(attended_ref[...], dbranch_ref[...])
        put_wide(grad, core, here_ref, away_ref, lanes)
    put_wide(sums_ref[...], core, here_ref, away_ref, slice(4 * width, 4 * width + 128))


def last_call(core, x, dfused, attended, dbranch, sums):
    width = x.shape[1]
    out = ((NY * NZ, 24, 4 * width + 128), BF)
    ins = (x, dfused, attended, dbranch, sums)
    half_spec = pl.BlockSpec(out[0], lambda *_: (0, 0, 0))
    return call(
        last_kernel,
        (1,),
        (core,) + ins,
        [pl.BlockSpec(memory_space=pltpu.SMEM)] + [whole_spec(a) for a in ins],
        [out, out],
        [half_spec, half_spec],
        [],
        1000,
        1000,
    )


def tall_kernel(in_ref, out_ref):
    blocks_, rows, width = out_ref.shape
    out_ref[...] = in_ref[...].astype(F32).reshape(blocks_, rows, width).astype(BF)


def tall_call(layer, width):
    places = NY * NC * NZ
    rows = layer.shape[0] // places
    return call(
        tall_kernel,
        (2, NX),
        (layer,),
        [pl.BlockSpec((layer.shape[0] // 2, width), lambda j, k: (j, k))],
        [((places, NX, rows, width), BF)],
        [pl.BlockSpec((places // 2, None, rows, width), lambda j, k: (j, k, 0, 0))],
        [],
        1000,
        1000,
    )[0].reshape(-1, width)


def body(
    hidden_in,
    out_grad,
    segments,
    mask_pos,
    mask_labels,
    loss_scale,
    w_qkv,
    b_query,
    b_value,
    w_attn,
    b_attn,
    attn_gain,
    attn_shift,
    w_expand,
    b_expand,
    w_shrink,
    b_shrink,
    ffn_gain,
    ffn_shift,
    w_dense,
    b_dense,
    dense_gain,
    dense_shift,
    w_vocab,
    b_vocab,
):
    micro, block, width = hidden_in.shape
    tokens = micro * block
    heads = width // HEAD_DIM
    factor = HEAD_DIM ** (-0.5)
    at = {axis: lax.axis_index(axis) for axis in EVERY}
    core = at["c"].astype(jnp.int32)[None]

    vectors = (
        b_query,
        b_value,
        b_attn,
        attn_gain,
        attn_shift,
        b_shrink,
        ffn_gain,
        ffn_shift,
        b_dense,
        dense_gain,
        dense_shift,
    )
    small = after(jnp.stack(vectors))[0].T
    small = jnp.concatenate([small, b_expand.reshape(w_qkv.shape[0], -1)], axis=1)
    small = jnp.pad(small, ((0, 0), (0, 128 - small.shape[1])))
    fused = jnp.concatenate([w_expand, w_qkv, w_attn, w_dense, small], axis=1)
    fused = gather_x(fused).reshape(-1, fused.shape[1])
    tall = gather_x(w_shrink)
    tall = tall.transpose(1, 0, 2).reshape(fused.shape[0], -1)
    layer = lax.all_gather(
        jnp.concatenate([tall, fused], axis=1), ("y", "c", "z"), axis=0, tiled=True
    )
    own_w = w_vocab.T
    piece_w = [own_w] + [fetch(own_w, "x", k) for k in (1, 2, 3)]
    piece_b = [b_vocab] + [fetch(b_vocab, "x", k) for k in (1, 2, 3)]
    half_w = jnp.stack(piece_w)
    half_b = jnp.stack(piece_b)
    per = own_w.shape[0]
    vocab_w = jnp.concatenate([half_w, fetch(half_w, "c", 1)]).reshape(-1, width)
    vocab_b = jnp.concatenate([half_b, fetch(half_b, "c", 1)]).reshape(-1).astype(F32)
    start = jnp.stack(
        [
            (((at["y"] * NC + (at["c"] + kc) % NC) * NZ + at["z"]) * NX + (at["x"] + kx) % NX)
            * per
            for kc in range(NC)
            for kx in range(NX)
        ]
    )
    column = (start[:, None] + jnp.arange(per, dtype=jnp.int32)[None, :]).reshape(-1)

    flat_labels = mask_labels.reshape(micro, -1)
    counts = jnp.sum((flat_labels >= 0).astype(F32), axis=1)
    norms = 1.0 / (counts * micro)
    slots = mask_labels.shape[-1]
    peers = NZ * NX
    grid = mask_labels.reshape(micro, NY, NC, peers, NZ, NX, slots)
    grid = lax.dynamic_index_in_dim(grid, at["c"], 2, False)
    grid = lax.dynamic_index_in_dim(grid, at["x"], 4, False)
    labels = grid.transpose(1, 3, 0, 2, 4).reshape(-1)
    rows = micro * peers * slots
    row_norm = jnp.broadcast_to(norms[None, :, None], (NY * NZ, micro, peers * slots)).reshape(-1)
    live = (labels >= 0).astype(F32)
    row_weight = live * row_norm
    hit = labels[:, None] == column[None, :]
    scale = loss_scale * row_weight
    own_first = (at["y"] * NZ + at["z"]) * rows
    own_weight = lax.dynamic_slice_in_dim(row_weight, own_first, rows)
    label_w = matmul(hit.astype(BF), vocab_w)
    label_b = jnp.sum(jnp.where(hit, vocab_b, 0.0), axis=1, keepdims=True)
    label_w = jnp.concatenate([label_w, jnp.pad(label_b, ((0, 0), (0, 127)))], axis=1)
    label_w = label_w.astype(BF).reshape(NY * NZ, rows, -1)
    positions = mask_pos.reshape(micro, -1)
    shifted = jnp.where(
        positions >= 0, positions + block * jnp.arange(micro, dtype=jnp.int32)[:, None], -1
    ).reshape(-1)
    select = (shifted[:, None] == jnp.arange(tokens, dtype=jnp.int32)[None, :]).astype(BF)

    scale, labels = scale[:, None], labels[:, None]
    layer, label_w, vocab_w, select, scale, labels = after(
        layer, label_w, vocab_w, select, scale, labels
    )
    label_w = swap(label_w, ("y", "z"))
    ends = [NX * width, w_expand.shape[1], 3 * width, width, width, 128]
    ends = [sum(ends[: i + 1]) for i in range(len(ends))]
    expand_full = layer[:, ends[0] : ends[1]]
    qkv_full = layer[:, ends[1] : ends[2]]
    attn_block = ends[2] // width
    dense_full = layer[:, ends[3] : ends[4]]
    vec_full = layer[:, ends[4] :]
    shrink_full = tall_call(layer, width)
    rows_of = vec_full[:, :16].T.astype(F32)
    (
        b_query,
        b_value,
        b_attn,
        attn_gain,
        attn_shift,
        b_shrink,
        ffn_gain,
        ffn_shift,
        b_dense,
        dense_gain,
        dense_shift,
    ) = (rows_of[i] for i in range(len(vectors)))
    b_expand = vec_full[:, 11:15].astype(F32).reshape(-1)

    x = hidden_in.reshape(tokens, width)
    qkv, probs, attended, first, first_low, normed1, inverse1 = attention_forward(
        x, segments, layer, attn_block - 3, rows_of
    )
    pre = matmul(first_low, expand_full) + b_expand
    act = gelu_value(pre).astype(BF)
    slope = gelu_slope(pre).astype(BF)
    second = first + matmul(act, shrink_full) + b_shrink
    settled, normed2, inverse2 = layer_norm(second, ffn_gain, ffn_shift)
    settled_low = settled.astype(BF)

    select, label_w = after(select, label_w)
    label_w = jnp.sum(label_w.astype(F32), axis=0)
    label_w, label_b = label_w[:, :width], label_w[:, width]
    picked = matmul(select, settled_low).astype(BF)
    dense_pre = matmul(picked, dense_full) + b_dense
    head_val, normed3, inverse3 = layer_norm(gelu_value(dense_pre), dense_gain, dense_shift)
    head_out = head_val.astype(BF)
    spread = swap(
        jnp.broadcast_to(head_out, (NY * NZ,) + head_out.shape), ("y", "z")
    ).reshape(-1, width)
    expl, stat, part = logits_call(spread, vocab_w, vocab_b, column, labels, rows)
    part = swap(part, ("y", "z"))
    scalars = jnp.stack(
        [label_b, own_weight, loss_scale * own_weight, inverse3[:, 0]], axis=1
    )
    lse, loss_own, g_dense, dsecond, dffn, sums_a = merge_call(
        own_first.astype(jnp.int32)[None],
        part,
        head_out,
        label_w,
        jnp.pad(scalars, ((0, 0), (0, 124))),
        normed3,
        gelu_slope(dense_pre),
        rows_of,
        picked,
        select,
        out_grad.reshape(tokens, width),
        normed2,
        inverse2,
        layer=layer,
        dense_block=attn_block + 1,
    )

    tall_pair = shrink_call(core, act, dffn, g_dense, loss_own)
    tall_here, tall_away, dffn = after(*tall_pair, dffn)
    tall_pair = (tall_here, give(tall_away, "c", 1))
    wide_here, wide_away, g_expand_bias, dresidual, dbranch, sums_b = feed_back_call(
        core, dffn, shrink_full, slope, first_low, layer, 4, dsecond, normed1, inverse1, rows_of
    )
    wide_pair = (wide_here, give(wide_away, "c", 1))
    dbranch, tall_mine = after(dbranch, add_cores(tall_pair))
    tall_all = swap(tall_mine, ("y", "z"))
    dfused, fused_sum = attention_backward(dbranch, qkv, probs, layer, attn_block)

    sums = jnp.stack(
        [
            fused_sum[0, :width],
            fused_sum[0, 2 * width :],
            sums_b[2],
            sums_b[0],
            sums_b[1],
            sums_a[5],
            sums_a[3],
            sums_a[4],
            sums_a[0],
            sums_a[1],
            sums_a[2],
        ]
    )
    sums = jnp.concatenate([after(sums)[0].T, g_expand_bias.reshape(width, -1)], axis=1)
    sums = jnp.pad(sums, ((0, 0), (0, 128 - sums.shape[1])))
    last_here, last_away = last_call(core, x, dfused, attended, dbranch, sums)
    last_away, tall_all = after(last_away, tall_all)
    last_pair = (last_here, give(last_away, "c", 1))
    wide_mine, tall_all = after(add_cores(wide_pair), tall_all)
    wide_all = swap(wide_mine, ("y", "z"))
    last_mine, wide_all = after(add_cores(last_pair), wide_all)
    last_all = swap(last_mine, ("y", "z"))

    lse, wide_mine = after(lse, wide_mine)
    grad_w = decoder_call(expl, spread, column, labels, scale, stat, lse)
    grad_w = grad_w.reshape(NC, NX, per, -1)
    grad_w, grad_away, wide_all = after(grad_w[0], grad_w[1], wide_all)
    grad_w = add_cores((grad_w, give(grad_away, "c", 1)))
    grad_w = total([grad_w[0]] + [give(grad_w[k], "x", k) for k in (1, 2, 3)])

    dinput = dresidual + matmul_nt(dfused, qkv_full)
    tall = jnp.sum(tall_all[:, :120].astype(F32), axis=0).astype(BF)
    loss_row = split_three(jnp.sum(tall_all[:, 120, :6].astype(F32)))[:128]
    tall_low = tall[:96].reshape(NX, 4, 6, width).transpose(0, 2, 1, 3).reshape(NX, 6, 4 * width)
    early = jnp.concatenate(
        [
            tall_low,
            tall[96:].reshape(NX, 6, width),
            jnp.broadcast_to(loss_row, (NX, 6, 128)),
        ],
        axis=2,
    )
    wide = jnp.sum(wide_all.astype(F32), axis=0).astype(BF)
    last_all, grad_w = after(last_all, grad_w)
    g_vocab, g_vocab_bias = grad_w[:, :width].T, grad_w[:, width]
    last = jnp.sum(last_all.astype(F32), axis=0).astype(BF)
    last = sum_x(
        jnp.concatenate([early, wide.reshape(NX, 6, -1), last.reshape(NX, 6, -1)], axis=2)
    )
    ends = [4 * width, width, 128, w_expand.shape[1], 3 * width, width, 128]
    ends = [sum(ends[: i + 1]) for i in range(len(ends))]
    g_shrink = last[:, : ends[0]].reshape(6, 4, width).transpose(1, 0, 2).reshape(24, width)
    g_dense = last[:, ends[0] : ends[1]]
    loss = jnp.sum(last[0, ends[1] : ends[1] + 3])
    g_expand = last[:, ends[2] : ends[3]]
    g_qkv = last[:, ends[3] : ends[4]]
    g_attn = last[:, ends[4] : ends[5]]
    sums = last[:, ends[5] :]
    return (
        settled_low.reshape(hidden_in.shape),
        loss,
        dinput.reshape(hidden_in.shape),
        g_qkv,
        sums[:, 0],
        sums[:, 1],
        g_attn,
        sums[:, 2],
        sums[:, 3],
        sums[:, 4],
        g_expand,
        sums[:, 11:15].reshape(-1),
        g_shrink,
        sums[:, 5],
        sums[:, 6],
        sums[:, 7],
        g_dense,
        sums[:, 8],
        sums[:, 9],
        sums[:, 10],
        g_vocab,
        g_vocab_bias,
    )


def solution(mesh):
    split = Mesh(mesh.devices.reshape(NY, NC, NZ, NX), EVERY)
    whole, one = P(), P(EVERY)
    tokens3 = P(None, EVERY, None)
    matrix = P(EVERY, None)
    in_specs = (
        tokens3,
        tokens3,
        P(None, EVERY),
        P(None, EVERY, None, None),
        whole,
        whole,
        matrix,
        one,
        one,
        matrix,
        one,
        one,
        one,
        matrix,
        one,
        matrix,
        one,
        one,
        one,
        matrix,
        one,
        one,
        one,
        P(None, EVERY),
        one,
    )
    out_specs = (
        tokens3,
        whole,
        tokens3,
        matrix,
        one,
        one,
        matrix,
        one,
        one,
        one,
        matrix,
        one,
        matrix,
        one,
        one,
        one,
        matrix,
        one,
        one,
        one,
        P(None, EVERY),
        one,
    )
    return jax.shard_map(body, mesh=split, in_specs=in_specs, out_specs=out_specs, check_vma=False)
```

```python
import functools

import jax
import jax.numpy as jnp
from jax import lax
from jax.experimental import pallas as pl
from jax.experimental.pallas import tpu as pltpu
from jax.sharding import Mesh
from jax.sharding import PartitionSpec as P

HEAD_DIM = 64
EPS = 1e-05
HALF_ROOT = 0.7071067811865476
NORMAL_PEAK = 0.3989422804014327
MASKED = -1e30

BF = jnp.bfloat16
F32 = jnp.float32
NY, NC, NZ, NX = 4, 2, 4, 4
SIZES = {"y": NY, "c": NC, "z": NZ, "x": NX}
EVERY = ("y", "c", "z", "x")


def fetch(array, axis, k):
    n = SIZES[axis]
    return lax.ppermute(array, axis, [((i + k) % n, i) for i in range(n)])


def give(array, axis, k):
    n = SIZES[axis]
    return lax.ppermute(array, axis, [(i, (i + k) % n) for i in range(n)])


def in_order(pieces, index):
    n = len(pieces)
    twice = jnp.stack(pieces + pieces)
    return lax.dynamic_slice_in_dim(twice, (n - index) % n, n, 0)


def gather_x(shard):
    pieces = [shard] + [fetch(shard, "x", k) for k in (1, 2, 3)]
    return in_order(pieces, lax.axis_index("x"))


def swap(array, axes):
    return lax.all_to_all(array, axes, 0, 0, tiled=True)


def blocks(grad):
    return grad.astype(BF).reshape(NY, NC, NZ, -1, grad.shape[1])


def half(grads, core, axis):
    cut = [lax.dynamic_index_in_dim(grad, core, 1, False) for grad in grads]
    cut = [part.reshape((NY * NZ,) + part.shape[2:]) for part in cut]
    return cut[0] if len(cut) == 1 else jnp.concatenate(cut, axis=axis)


def sum_cores(grads, axis):
    core = lax.axis_index("c")
    return half(grads, core, axis), give(half(grads, 1 - core, axis), "c", 1)


def add_cores(pair):
    return (pair[0].astype(F32) + pair[1].astype(F32)).astype(BF)


def sum_yz(mine):
    return jnp.sum(swap(mine, ("y", "z")).astype(F32), axis=0).astype(BF)


def sum_x(mine):
    return jnp.sum(swap(mine, "x").astype(F32), axis=0)


def split_three(value):
    return jnp.pad(jnp.stack(three(value)), (0, 765)).astype(BF)


def after(*arrays):
    return lax.optimization_barrier(arrays)


def total(parts):
    out = parts[0].astype(F32)
    for part in parts[1:]:
        out = out + part.astype(F32)
    return out


def three(value):
    high = lax.reduce_precision(value, 8, 7)
    rest = value - high
    middle = lax.reduce_precision(rest, 8, 7)
    return [high, middle, lax.reduce_precision(rest - middle, 8, 7)]


def gelu_value(values):
    return 0.5 * values * (1.0 + lax.erf(values * HALF_ROOT))


def gelu_slope(values):
    return 0.5 * (1.0 + lax.erf(values * HALF_ROOT)) + values * NORMAL_PEAK * jnp.exp(
        -0.5 * values * values
    )


def layer_norm(values, gain, shift):
    center = values - jnp.mean(values, axis=-1, keepdims=True)
    inverse = lax.rsqrt(jnp.mean(center * center, axis=-1, keepdims=True) + EPS)
    normed = center * inverse
    return (normed * gain + shift, normed, inverse)


def norm_back(grad, normed, inverse, gain):
    scaled = grad * gain
    inner = (
        scaled
        - jnp.mean(scaled, axis=-1, keepdims=True)
        - normed * jnp.mean(scaled * normed, axis=-1, keepdims=True)
    )
    return inner * inverse


def column_sum(values):
    return jnp.sum(values, axis=0, dtype=F32)


def matmul(left, right):
    return jnp.dot(left, right, preferred_element_type=F32)


def matmul_tn(left, right):
    return lax.dot_general(left, right, (((0,), (0,)), ((), ())), preferred_element_type=F32)


def matmul_nt(left, right):
    return lax.dot_general(left, right, (((1,), (1,)), ((), ())), preferred_element_type=F32)


def dot_nn(left, right):
    return lax.dot_general(left, right, (((1,), (0,)), ((), ())), preferred_element_type=F32)


def dot_nt(left, right):
    return lax.dot_general(left, right, (((1,), (1,)), ((), ())), preferred_element_type=F32)


def dot_tn(left, right):
    return lax.dot_general(left, right, (((0,), (0,)), ((), ())), preferred_element_type=F32)


def attention_forward_kernel(
    x_ref,
    row_ref,
    col_ref,
    wq_ref,
    wk_ref,
    wv_ref,
    wa_ref,
    vec_ref,
    qkv_ref,
    probs_ref,
    attended_ref,
    first_ref,
    low_ref,
    normed_ref,
    inverse_ref,
):
    tokens, width = x_ref.shape
    pair = 2 * HEAD_DIM
    factor = HEAD_DIM ** (-0.5)
    x = x_ref[...]
    qkv_ref[:, :width] = (dot_nn(x, wq_ref[...]) + vec_ref[0:1]).astype(BF)
    qkv_ref[:, width : 2 * width] = dot_nn(x, wk_ref[...]).astype(BF)
    qkv_ref[:, 2 * width :] = (dot_nn(x, wv_ref[...]) + vec_ref[1:2]).astype(BF)
    allowed = row_ref[...] == col_ref[...]
    lower = lax.broadcasted_iota(jnp.int32, (tokens, pair), 1) < HEAD_DIM
    for h in range(width // pair):
        lanes = slice(h * pair, (h + 1) * pair)
        query = qkv_ref[:, lanes]
        keys = qkv_ref[:, width + h * pair : width + (h + 1) * pair]
        values = qkv_ref[:, 2 * width + h * pair : 2 * width + (h + 1) * pair]
        zero = jnp.zeros_like(query)
        outs = []
        for side in range(2):
            mine = jnp.where(lower, query, zero) if side == 0 else jnp.where(lower, zero, query)
            scores = jnp.where(allowed, dot_nt(mine, keys) * factor, MASKED)
            expo = jnp.exp(scores - jnp.max(scores, axis=1, keepdims=True))
            probs = (expo / jnp.sum(expo, axis=1, keepdims=True)).astype(BF)
            probs_ref[2 * h + side] = probs
            outs.append(dot_nn(probs, values))
        attended_ref[:, lanes] = jnp.where(lower, outs[0], outs[1]).astype(BF)
    branch = dot_nn(attended_ref[...], wa_ref[...]) + vec_ref[2:3]
    first, normed, inverse = layer_norm(x.astype(F32) + branch, vec_ref[3:4], vec_ref[4:5])
    first_ref[...] = first
    low_ref[...] = first.astype(BF)
    normed_ref[...] = normed
    inverse_ref[...] = inverse


def weight_spec(width, block):
    return pl.BlockSpec((width, width), lambda m: (0, block))


def attention_forward(x, segments, layer, first_block, vec):
    micro, block = segments.shape
    tokens, width = x.shape
    heads = width // HEAD_DIM
    here = lambda n: pl.BlockSpec((block, n), lambda m: (m, 0))
    return pl.pallas_call(
        attention_forward_kernel,
        grid=(micro,),
        in_specs=[
            here(width),
            pl.BlockSpec((None, 1, block), lambda m: (m, 0, 0)),
            pl.BlockSpec((None, block, 1), lambda m: (m, 0, 0)),
            weight_spec(width, first_block),
            weight_spec(width, first_block + 1),
            weight_spec(width, first_block + 2),
            weight_spec(width, first_block + 3),
            pl.BlockSpec(vec.shape, lambda m: (0, 0)),
        ],
        out_specs=[
            here(3 * width),
            pl.BlockSpec((None, heads, block, block), lambda m: (m, 0, 0, 0)),
            here(width),
            here(width),
            here(width),
            here(width),
            here(1),
        ],
        out_shape=[
            jax.ShapeDtypeStruct((tokens, 3 * width), BF),
            jax.ShapeDtypeStruct((micro, heads, block, block), BF),
            jax.ShapeDtypeStruct((tokens, width), BF),
            jax.ShapeDtypeStruct((tokens, width), F32),
            jax.ShapeDtypeStruct((tokens, width), BF),
            jax.ShapeDtypeStruct((tokens, width), F32),
            jax.ShapeDtypeStruct((tokens, 1), F32),
        ],
        compiler_params=pltpu.CompilerParams(vmem_limit_bytes=48 * 1024 * 1024),
        cost_estimate=pl.CostEstimate(
            flops=4_000_000_000, bytes_accessed=16_000_000, transcendentals=2_000_000
        ),
    )(x, segments[:, None, :], segments[:, :, None], layer, layer, layer, layer, vec)


def attention_backward_kernel(dbranch_ref, qkv_ref, probs_ref, wa_ref, out_ref, sum_ref):
    tokens, width = dbranch_ref.shape
    pair = 2 * HEAD_DIM
    factor = HEAD_DIM ** (-0.5)
    dattended = dot_nt(dbranch_ref[...], wa_ref[...]).astype(BF)
    lower = lax.broadcasted_iota(jnp.int32, (tokens, pair), 1) < HEAD_DIM
    for h in range(width // pair):
        lanes = slice(h * pair, (h + 1) * pair)
        query = qkv_ref[:, lanes]
        keys = qkv_ref[:, width + h * pair : width + (h + 1) * pair]
        values = qkv_ref[:, 2 * width + h * pair : 2 * width + (h + 1) * pair]
        grad = dattended[:, lanes]
        zero = jnp.zeros_like(grad)
        parts = []
        for side in range(2):
            mine = jnp.where(lower, grad, zero) if side == 0 else jnp.where(lower, zero, grad)
            low = probs_ref[2 * h + side]
            probs = low.astype(F32)
            dprobs = dot_nt(mine, values)
            inner = jnp.sum(probs * dprobs, axis=1, keepdims=True)
            dscores = (probs * (dprobs - inner)).astype(BF)
            parts.append(
                (dot_nn(dscores, keys) * factor, dot_tn(dscores, query) * factor, dot_tn(low, grad))
            )
        for i in range(3):
            start = i * width + h * pair
            out_ref[:, start : start + pair] = jnp.where(lower, parts[0][i], parts[1][i]).astype(BF)
    seen = jnp.sum(out_ref[...].astype(F32), axis=0, keepdims=True)

    @pl.when(pl.program_id(0) == 0)
    def _():
        sum_ref[...] = seen

    @pl.when(pl.program_id(0) > 0)
    def _():
        sum_ref[...] += seen


def attention_backward(dbranch, qkv, probs, layer, attn_block):
    micro, heads, block, _ = probs.shape
    tokens, width = dbranch.shape
    here = lambda n: pl.BlockSpec((block, n), lambda m: (m, 0))
    return pl.pallas_call(
        attention_backward_kernel,
        grid=(micro,),
        in_specs=[
            here(width),
            here(3 * width),
            pl.BlockSpec((None, heads, block, block), lambda m: (m, 0, 0, 0)),
            weight_spec(width, attn_block),
        ],
        out_specs=[here(3 * width), pl.BlockSpec((1, 3 * width), lambda m: (0, 0))],
        out_shape=[
            jax.ShapeDtypeStruct((tokens, 3 * width), BF),
            jax.ShapeDtypeStruct((1, 3 * width), F32),
        ],
        compiler_params=pltpu.CompilerParams(vmem_limit_bytes=48 * 1024 * 1024),
        cost_estimate=pl.CostEstimate(
            flops=1000, bytes_accessed=1000, transcendentals=0
        ),
    )(dbranch, qkv, probs, layer)


LIMIT = 56 * 1024 * 1024


def whole_spec(array):
    return pl.BlockSpec(array.shape, lambda *_: (0,) * len(array.shape))


def call(kernel, grid, ins, in_specs, outs, out_specs, scratch, flops, size):
    return pl.pallas_call(
        kernel,
        grid=grid,
        in_specs=in_specs,
        out_specs=out_specs,
        out_shape=[jax.ShapeDtypeStruct(shape, kind) for shape, kind in outs],
        scratch_shapes=scratch,
        compiler_params=pltpu.CompilerParams(vmem_limit_bytes=LIMIT),
        cost_estimate=pl.CostEstimate(flops=flops, bytes_accessed=size, transcendentals=0),
    )(*ins)


def low_three(value):
    high = value.astype(BF).astype(F32)
    middle = (value - high).astype(BF).astype(F32)
    rest = (value - high - middle).astype(BF).astype(F32)
    return [high, middle, rest]


def logits_kernel(
    spread_ref, w_ref, b_ref, column_ref, label_ref, expl_ref, stat_ref, part_ref, flat_ref, logits_ref
):
    step = pl.program_id(0)
    count, width = spread_ref.shape
    peers, high, _ = part_ref.shape
    rows = high - 16
    spread = spread_ref[...]
    entries = w_ref.shape[0]
    chunks = [slice(i, i + entries // 5) for i in range(0, entries, entries // 5)]
    peak = None
    for cut in chunks:
        logits = dot_nt(spread, w_ref[cut, :]) + b_ref[:, cut]
        logits_ref[:, cut] = logits
        most = jnp.max(logits, axis=1, keepdims=True)
        peak = most if peak is None else jnp.maximum(peak, most)
    top = peak
    sums = jnp.zeros((count, 1), F32)
    label = jnp.zeros((count, 1), F32)
    part = jnp.zeros((count, width), F32)
    for cut in chunks:
        expl = jnp.exp(logits_ref[:, cut] - top)
        sums += jnp.sum(expl, axis=1, keepdims=True)
        hit = label_ref[...] == column_ref[:, cut]
        rest = jnp.where(hit, 0.0, expl)
        label += jnp.sum(expl - rest, axis=1, keepdims=True)
        other = rest.astype(BF)
        expl_ref[:, cut] = other
        part += dot_nn(other, w_ref[cut, :])
    part = part.astype(BF)
    for i in range(count // rows):
        part_ref[step * (count // rows) + i, 0:rows, :] = part[i * rows : (i + 1) * rows]
    lane = lax.broadcasted_iota(jnp.int32, (count, 128), 1)
    stat = jnp.where(lane == 0, top, jnp.where(lane == 1, label, 0.0))
    stat_ref[...] = stat
    parts = jnp.zeros((count, 128), F32)
    for i, value in enumerate(low_three(top) + low_three(sums)):
        parts = jnp.where(lane == i, value, parts)
    flat_ref[step] = parts.T[0:8]

    @pl.when(step == pl.num_programs(0) - 1)
    def _():
        told = jnp.concatenate([flat_ref[i] for i in range(flat_ref.shape[0])], axis=1)
        rest = told.shape[1] - width
        last = jnp.concatenate([told[:, width:], jnp.zeros((8, width - rest), F32)], axis=1)
        told = jnp.concatenate([told[:, :width], last], axis=0).astype(BF)
        for i in range(peers):
            part_ref[i, rows:, :] = told


def logits_call(spread, vocab_w, vocab_b, column, labels, rows):
    count, width = spread.shape
    entries = vocab_w.shape[0]
    block = count // 2
    here = lambda n: pl.BlockSpec((block, n), lambda i: (i, 0))
    ins = (spread, vocab_w, vocab_b[None, :], column[None, :], labels)
    specs = [here(width)] + [whole_spec(a) for a in ins[1:4]] + [here(1)]
    part = (count // rows, rows + 16, width)
    return call(
        logits_kernel,
        (2,),
        ins,
        specs,
        [((count, entries), BF), ((count, 128), F32), (part, BF)],
        [here(entries), here(128), pl.BlockSpec(part, lambda i: (0, 0, 0))],
        [pltpu.VMEM((2, 8, block), F32), pltpu.VMEM((block, entries), F32)],
        10_000_000_000,
        20_000_000,
    )


def decoder_kernel(
    expl_ref, spread_ref, column_ref, label_ref, scale_ref, stat_ref, lse_ref, out_ref, sum_ref
):
    count = spread_ref.shape[0]
    lse = jnp.broadcast_to(lse_ref[...], (8, count)).T[:, 0:1]
    share = jnp.exp(stat_ref[:, 0:1] - lse)
    scale = scale_ref[...]
    hit = label_ref[...] == column_ref[...]
    other = (scale * share) * expl_ref[...].astype(F32)
    dlogits = jnp.where(hit, scale * (stat_ref[:, 1:2] * share - 1.0), other).astype(BF)
    out_ref[...] = dot_tn(dlogits, spread_ref[...]).astype(BF)
    sum_ref[...] = jnp.sum(dlogits.astype(F32), axis=0, keepdims=True)


def decoder_call(expl, spread, column, labels, scale, stat, lse):
    count, width = spread.shape
    entries = expl.shape[1]
    block = entries // 5
    ins = (expl, spread, column[None, :], labels, scale, stat, lse)
    return call(
        decoder_kernel,
        (5,),
        ins,
        [
            pl.BlockSpec((count, block), lambda j: (0, j)),
            whole_spec(spread),
            pl.BlockSpec((1, block), lambda j: (0, j)),
        ]
        + [whole_spec(a) for a in ins[3:]],
        [((entries, width), BF), ((1, entries), F32)],
        [
            pl.BlockSpec((block, width), lambda j: (j, 0)),
            pl.BlockSpec((1, block), lambda j: (0, j)),
        ],
        [],
        1000,
        1000,
    )


def merge_kernel(
    own_ref,
    part_ref,
    head_ref,
    label_ref,
    scalar_ref,
    normed3_ref,
    slope3_ref,
    vec_ref,
    picked_ref,
    dense_ref,
    select_ref,
    grad_ref,
    normed2_ref,
    inverse2_ref,
    lse_ref,
    loss_ref,
    g_dense_ref,
    dsecond_ref,
    dffn_ref,
    sums_ref,
):
    peers, high, width = part_ref.shape
    rows = high - 16
    tail = peers * rows - width

    def told(i):
        first = part_ref[:, rows : rows + 8, :].astype(F32)[:, i]
        rest = part_ref[:, rows + 8 :, :].astype(F32)[:, i, :tail]
        return jnp.concatenate([first, rest], axis=1)

    tops = told(0) + told(1) + told(2)
    sums = told(3) + told(4) + told(5)
    top = jnp.max(tops, axis=0, keepdims=True)
    share = jnp.exp(tops - top)
    total_sum = jnp.sum(sums * share, axis=0, keepdims=True)
    lse = top + jnp.log(total_sum)
    share = share / total_sum
    lse_ref[...] = lse
    mine = own_ref[0] + lax.broadcasted_iota(jnp.int32, (rows, peers * rows), 0)
    mine = mine == lax.broadcasted_iota(jnp.int32, (rows, peers * rows), 1)
    own_lse = jnp.sum(jnp.where(mine, lse, 0.0), axis=1, keepdims=True)
    mixed = jnp.zeros((rows, width), F32)
    for i in range(peers):
        weight = jnp.sum(jnp.where(mine, share[i : i + 1], 0.0), axis=1, keepdims=True)
        mixed += weight * part_ref[i, 0:rows, :].astype(F32)
    label = label_ref[...]
    label_logit = jnp.sum(head_ref[...].astype(F32) * label, axis=1, keepdims=True)
    label_logit += scalar_ref[:, 0:1]
    grad = scalar_ref[:, 2:3] * (mixed + (jnp.exp(label_logit - own_lse) - 1.0) * label)
    loss_ref[...] = jnp.zeros(loss_ref.shape, F32) + jnp.sum(
        scalar_ref[:, 1:2] * (own_lse - label_logit)
    )
    normed3 = normed3_ref[...]
    ddense = norm_back(grad, normed3, scalar_ref[:, 3:4], vec_ref[9:10]) * slope3_ref[...]
    low = ddense.astype(BF)
    column = lambda v: jnp.sum(v, axis=0, keepdims=True)
    g_dense_ref[...] = dot_tn(picked_ref[...], low)
    drows = dot_nt(low, dense_ref[...]).astype(BF)
    dout = grad_ref[...].astype(F32) + dot_tn(select_ref[...], drows)
    normed2 = normed2_ref[...]
    dsecond = norm_back(dout, normed2, inverse2_ref[...], vec_ref[6:7])
    dffn = dsecond.astype(BF)
    dsecond_ref[...] = dsecond
    dffn_ref[...] = dffn
    parts = [
        column(low.astype(F32)),
        column(grad * normed3),
        column(grad),
        column(dout * normed2),
        column(dout),
        column(dffn.astype(F32)),
    ]
    for i, value in enumerate(parts):
        sums_ref[i : i + 1] = value


def merge_call(own, *arrays, layer, dense_block):
    part, head = arrays[0], arrays[1]
    width = head.shape[1]
    tokens = arrays[-1].shape[0]
    count = part.shape[0] * (part.shape[1] - 16)
    ins = list(arrays)
    ins.insert(8, layer)
    specs = [whole_spec(a) for a in arrays]
    specs.insert(8, pl.BlockSpec((width, width), lambda *_: (0, dense_block)))
    outs = [
        ((1, count), F32),
        ((8, 128), F32),
        ((width, width), F32),
        ((tokens, width), F32),
        ((tokens, width), BF),
        ((8, width), F32),
    ]
    return call(
        merge_kernel,
        (1,),
        [own] + ins,
        [pl.BlockSpec(memory_space=pltpu.SMEM)] + specs,
        outs,
        [pl.BlockSpec(shape, lambda *_: (0, 0)) for shape, _ in outs],
        [],
        300_000_000,
        10_000_000,
    )


def keep_halves(core, block, here, away):
    for c in range(NC):

        @pl.when(core == c)
        def _():
            here(block(c))

        @pl.when(core != c)
        def _():
            away(block(c))


def shrink_kernel(core_ref, act_ref, dffn_ref, dense_ref, loss_ref, here_ref, away_ref):
    width = dffn_ref.shape[1]
    grad = dot_tn(act_ref[...], dffn_ref[...])
    core = core_ref[0]
    spot = lax.broadcasted_iota(jnp.int32, (8, width), 1)
    first = lax.broadcasted_iota(jnp.int32, (8, width), 0) == 0
    told = jnp.zeros((8, width), F32)
    for i, value in enumerate(low_three(loss_ref[0:1, 0:1])):
        told = jnp.where(first & (spot == i + 3 * core), value, told)

    def put(ref, extra):
        def store(block):
            tall, dense = block
            for z in range(NZ):
                ref[z, 0:96, :] = tall[z * 96 : (z + 1) * 96].astype(BF)
                ref[z, 96:128, :] = jnp.concatenate(
                    [dense[z * 24 : (z + 1) * 24], extra], axis=0
                ).astype(BF)

        return store

    def block(c):
        tall = grad[c * width // 2 : (c + 1) * width // 2]
        return tall, dense_ref[c * 96 : (c + 1) * 96, :]

    keep_halves(core, block, put(here_ref, told), put(away_ref, told))


def shrink_call(core, act, dffn, g_dense, loss):
    tokens, width = dffn.shape
    out = ((NY * NZ, 128, width), BF)
    half_spec = pl.BlockSpec((NZ, 128, width), lambda y: (y, 0, 0))
    return call(
        shrink_kernel,
        (NY,),
        (core, act, dffn, g_dense, loss),
        [
            pl.BlockSpec(memory_space=pltpu.SMEM),
            pl.BlockSpec((tokens, width), lambda y: (0, y)),
            whole_spec(dffn),
            pl.BlockSpec((width // NY, width), lambda y: (y, 0)),
            whole_spec(loss),
        ],
        [out, out],
        [half_spec, half_spec],
        [],
        1000,
        1000,
    )


def put_wide(grad, core, here_ref, away_ref, lanes):
    def block(c):
        return [grad[96 * (NC * y + c) : 96 * (NC * y + c) + 96] for y in range(NY)]

    def put(ref):
        def store(parts):
            for y, part in enumerate(parts):
                ref[y * NZ : (y + 1) * NZ, :, lanes] = part.reshape(NZ, 24, -1).astype(BF)

        return store

    keep_halves(core, block, put(here_ref), put(away_ref))


def feed_back_kernel(closing, core_ref, *refs):
    dffn_ref, shrink_ref, slope_ref, low_ref, expand_ref, before_ref = refs[:6]
    if closing:
        normed_ref, inverse_ref, vec_ref = refs[6:9]
        here_ref, away_ref, bias_ref, dresidual_ref, dbranch_ref, sums_ref, total_ref = refs[11:]
    else:
        here_ref, away_ref, bias_ref, total_ref = refs[6:]
    step = pl.program_id(0)
    dpre = (dot_nt(dffn_ref[...], shrink_ref[...]) * slope_ref[...].astype(F32)).astype(BF)
    bias_ref[...] = jnp.sum(dpre.astype(F32), axis=0, keepdims=True)
    more = dot_nt(dpre, expand_ref[...])

    @pl.when(step == 0)
    def _():
        total_ref[...] = before_ref[...] + more

    @pl.when(step > 0)
    def _():
        total_ref[...] += more

    put_wide(dot_tn(low_ref[...], dpre), core_ref[0], here_ref, away_ref, slice(None))
    if not closing:
        return

    @pl.when(step == pl.num_programs(0) - 1)
    def _():
        dfirst = total_ref[...]
        normed = normed_ref[...]
        dresidual = norm_back(dfirst, normed, inverse_ref[...], vec_ref[3:4])
        dbranch = dresidual.astype(BF)
        dresidual_ref[...] = dresidual
        dbranch_ref[...] = dbranch
        sums_ref[0:1] = jnp.sum(dfirst * normed, axis=0, keepdims=True)
        sums_ref[1:2] = jnp.sum(dfirst, axis=0, keepdims=True)
        sums_ref[2:3] = jnp.sum(dbranch.astype(F32), axis=0, keepdims=True)


def feed_back_call(core, dffn, shrink, slope, low, layer, expand_block, before, rest=None):
    tokens, width = dffn.shape
    wide = slope.shape[1]
    steps = wide // width // 2
    closing = rest is not None
    at = steps if closing else 0
    half = ((NY * NZ, 24, wide), BF)
    half_spec = pl.BlockSpec((NY * NZ, 24, width), lambda j: (0, 0, at + j))
    flat = pl.BlockSpec((tokens, width), lambda j: (0, 0))
    outs = [half, half, ((1, wide // 2), F32), ((tokens, width), F32)]
    out_specs = [half_spec, half_spec, pl.BlockSpec((1, width), lambda j: (0, j)), flat]
    ins = [core, dffn, shrink, slope, low, layer, before]
    in_specs = [
        pl.BlockSpec(memory_space=pltpu.SMEM),
        whole_spec(dffn),
        pl.BlockSpec((width, width), lambda j: (at + j, 0)),
        pl.BlockSpec((tokens, width), lambda j: (0, at + j)),
        whole_spec(low),
        pl.BlockSpec((width, width), lambda j: (0, expand_block + at + j)),
        whole_spec(before),
    ]
    if closing:
        outs += [((tokens, width), BF), ((8, width), F32)]
        out_specs += [flat, pl.BlockSpec((8, width), lambda j: (0, 0))]
        ins += rest
        in_specs += [whole_spec(a) for a in rest[:3]] + [pl.BlockSpec(memory_space=pl.ANY)] * 2
    return pl.pallas_call(
        functools.partial(feed_back_kernel, closing),
        grid=(steps,),
        in_specs=in_specs,
        out_specs=out_specs,
        out_shape=[jax.ShapeDtypeStruct(shape, kind) for shape, kind in outs],
        scratch_shapes=[pltpu.VMEM((tokens, width), F32)] if closing else [],
        input_output_aliases={10: 0, 11: 1} if closing else {},
        compiler_params=pltpu.CompilerParams(vmem_limit_bytes=LIMIT),
        cost_estimate=pl.CostEstimate(flops=1000, bytes_accessed=1000, transcendentals=0),
    )(*ins)


def last_kernel(core_ref, x_ref, dfused_ref, attended_ref, dbranch_ref, sums_ref, here_ref, away_ref):
    width = x_ref.shape[1]
    core = core_ref[0]
    for i in range(4):
        lanes = slice(i * width, (i + 1) * width)
        if i < 3:
            grad = dot_tn(x_ref[...], dfused_ref[:, lanes])
        else:
            grad = dot_tn(attended_ref[...], dbranch_ref[...])
        put_wide(grad, core, here_ref, away_ref, lanes)
    put_wide(sums_ref[...], core, here_ref, away_ref, slice(4 * width, 4 * width + 128))


def last_call(core, x, dfused, attended, dbranch, sums):
    width = x.shape[1]
    out = ((NY * NZ, 24, 4 * width + 128), BF)
    ins = (x, dfused, attended, dbranch, sums)
    half_spec = pl.BlockSpec(out[0], lambda *_: (0, 0, 0))
    return call(
        last_kernel,
        (1,),
        (core,) + ins,
        [pl.BlockSpec(memory_space=pltpu.SMEM)] + [whole_spec(a) for a in ins],
        [out, out],
        [half_spec, half_spec],
        [],
        1000,
        1000,
    )


def tall_kernel(in_ref, out_ref):
    blocks_, rows, width = out_ref.shape
    out_ref[...] = in_ref[...].astype(F32).reshape(blocks_, rows, width).astype(BF)


def tall_call(layer, width):
    places = NY * NC * NZ
    rows = layer.shape[0] // places
    return call(
        tall_kernel,
        (2, NX),
        (layer,),
        [pl.BlockSpec((layer.shape[0] // 2, width), lambda j, k: (j, k))],
        [((places, NX, rows, width), BF)],
        [pl.BlockSpec((places // 2, None, rows, width), lambda j, k: (j, k, 0, 0))],
        [],
        1000,
        1000,
    )[0].reshape(-1, width)


def body(
    hidden_in,
    out_grad,
    segments,
    mask_pos,
    mask_labels,
    loss_scale,
    w_qkv,
    b_query,
    b_value,
    w_attn,
    b_attn,
    attn_gain,
    attn_shift,
    w_expand,
    b_expand,
    w_shrink,
    b_shrink,
    ffn_gain,
    ffn_shift,
    w_dense,
    b_dense,
    dense_gain,
    dense_shift,
    w_vocab,
    b_vocab,
):
    micro, block, width = hidden_in.shape
    tokens = micro * block
    heads = width // HEAD_DIM
    factor = HEAD_DIM ** (-0.5)
    at = {axis: lax.axis_index(axis) for axis in EVERY}
    core = at["c"].astype(jnp.int32)[None]

    vectors = (
        b_query,
        b_value,
        b_attn,
        attn_gain,
        attn_shift,
        b_shrink,
        ffn_gain,
        ffn_shift,
        b_dense,
        dense_gain,
        dense_shift,
    )
    small = after(jnp.stack(vectors))[0].T
    small = jnp.concatenate([small, b_expand.reshape(w_qkv.shape[0], -1)], axis=1)
    small = jnp.pad(small, ((0, 0), (0, 128 - small.shape[1])))
    fused = jnp.concatenate([w_expand, w_qkv, w_attn, w_dense, small], axis=1)
    fused = gather_x(fused).reshape(-1, fused.shape[1])
    tall = gather_x(w_shrink)
    tall = tall.transpose(1, 0, 2).reshape(fused.shape[0], -1)
    layer = lax.all_gather(
        jnp.concatenate([tall, fused], axis=1), ("y", "c", "z"), axis=0, tiled=True
    )
    own_w = w_vocab.T
    piece_w = [own_w] + [fetch(own_w, "x", k) for k in (1, 2, 3)]
    piece_b = [b_vocab] + [fetch(b_vocab, "x", k) for k in (1, 2, 3)]
    half_w = jnp.stack(piece_w)
    half_b = jnp.stack(piece_b)
    per = own_w.shape[0]
    vocab_w = jnp.concatenate([half_w, fetch(half_w, "c", 1)]).reshape(-1, width)
    vocab_b = jnp.concatenate([half_b, fetch(half_b, "c", 1)]).reshape(-1).astype(F32)
    start = jnp.stack(
        [
            (((at["y"] * NC + (at["c"] + kc) % NC) * NZ + at["z"]) * NX + (at["x"] + kx) % NX)
            * per
            for kc in range(NC)
            for kx in range(NX)
        ]
    )
    column = (start[:, None] + jnp.arange(per, dtype=jnp.int32)[None, :]).reshape(-1)

    flat_labels = mask_labels.reshape(micro, -1)
    counts = jnp.sum((flat_labels >= 0).astype(F32), axis=1)
    norms = 1.0 / (counts * micro)
    slots = mask_labels.shape[-1]
    peers = NZ * NX
    grid = mask_labels.reshape(micro, NY, NC, peers, NZ, NX, slots)
    grid = lax.dynamic_index_in_dim(grid, at["c"], 2, False)
    grid = lax.dynamic_index_in_dim(grid, at["x"], 4, False)
    labels = grid.transpose(1, 3, 0, 2, 4).reshape(-1)
    rows = micro * peers * slots
    row_norm = jnp.broadcast_to(norms[None, :, None], (NY * NZ, micro, peers * slots)).reshape(-1)
    live = (labels >= 0).astype(F32)
    row_weight = live * row_norm
    hit = labels[:, None] == column[None, :]
    scale = loss_scale * row_weight
    own_first = (at["y"] * NZ + at["z"]) * rows
    own_weight = lax.dynamic_slice_in_dim(row_weight, own_first, rows)
    label_w = matmul(hit.astype(BF), vocab_w)
    label_b = jnp.sum(jnp.where(hit, vocab_b, 0.0), axis=1, keepdims=True)
    label_w = jnp.concatenate([label_w, jnp.pad(label_b, ((0, 0), (0, 127)))], axis=1)
    label_w = label_w.astype(BF).reshape(NY * NZ, rows, -1)
    positions = mask_pos.reshape(micro, -1)
    shifted = jnp.where(
        positions >= 0, positions + block * jnp.arange(micro, dtype=jnp.int32)[:, None], -1
    ).reshape(-1)
    select = (shifted[:, None] == jnp.arange(tokens, dtype=jnp.int32)[None, :]).astype(BF)

    scale, labels = scale[:, None], labels[:, None]
    layer, label_w, vocab_w, select, scale, labels = after(
        layer, label_w, vocab_w, select, scale, labels
    )
    label_w = swap(label_w, ("y", "z"))
    ends = [NX * width, w_expand.shape[1], 3 * width, width, width, 128]
    ends = [sum(ends[: i + 1]) for i in range(len(ends))]
    expand_full = layer[:, ends[0] : ends[1]]
    qkv_full = layer[:, ends[1] : ends[2]]
    attn_block = ends[2] // width
    dense_full = layer[:, ends[3] : ends[4]]
    vec_full = layer[:, ends[4] :]
    shrink_full = tall_call(layer, width)
    rows_of = vec_full[:, :16].T.astype(F32)
    (
        b_query,
        b_value,
        b_attn,
        attn_gain,
        attn_shift,
        b_shrink,
        ffn_gain,
        ffn_shift,
        b_dense,
        dense_gain,
        dense_shift,
    ) = (rows_of[i] for i in range(len(vectors)))
    b_expand = vec_full[:, 11:15].astype(F32).reshape(-1)

    x = hidden_in.reshape(tokens, width)
    qkv, probs, attended, first, first_low, normed1, inverse1 = attention_forward(
        x, segments, layer, attn_block - 3, rows_of
    )
    pre = matmul(first_low, expand_full) + b_expand
    act = gelu_value(pre).astype(BF)
    slope = gelu_slope(pre).astype(BF)
    second = first + matmul(act, shrink_full) + b_shrink
    settled, normed2, inverse2 = layer_norm(second, ffn_gain, ffn_shift)
    settled_low = settled.astype(BF)

    select, label_w = after(select, label_w)
    label_w = jnp.sum(label_w.astype(F32), axis=0)
    label_w, label_b = label_w[:, :width], label_w[:, width]
    picked = matmul(select, settled_low).astype(BF)
    dense_pre = matmul(picked, dense_full) + b_dense
    head_val, normed3, inverse3 = layer_norm(gelu_value(dense_pre), dense_gain, dense_shift)
    head_out = head_val.astype(BF)
    spread = swap(
        jnp.broadcast_to(head_out, (NY * NZ,) + head_out.shape), ("y", "z")
    ).reshape(-1, width)
    expl, stat, part = logits_call(spread, vocab_w, vocab_b, column, labels, rows)
    part = swap(part, ("y", "z"))
    scalars = jnp.stack(
        [label_b, own_weight, loss_scale * own_weight, inverse3[:, 0]], axis=1
    )
    lse, loss_own, g_dense, dsecond, dffn, sums_a = merge_call(
        own_first.astype(jnp.int32)[None],
        part,
        head_out,
        label_w,
        jnp.pad(scalars, ((0, 0), (0, 124))),
        normed3,
        gelu_slope(dense_pre),
        rows_of,
        picked,
        select,
        out_grad.reshape(tokens, width),
        normed2,
        inverse2,
        layer=layer,
        dense_block=attn_block + 1,
    )

    tall_pair = shrink_call(core, act, dffn, g_dense, loss_own)
    tall_here, tall_away, dffn = after(*tall_pair, dffn)
    tall_pair = (tall_here, give(tall_away, "c", 1))
    wide_here, wide_away, bias_low, half_first = feed_back_call(
        core, dffn, shrink_full, slope, first_low, layer, 4, dsecond
    )
    half_first, tall_mine = after(half_first, add_cores(tall_pair))
    wide_here, wide_away, bias_high, dresidual, dbranch, sums_b = feed_back_call(
        core,
        dffn,
        shrink_full,
        slope,
        first_low,
        layer,
        4,
        half_first,
        [normed1, inverse1, rows_of, wide_here, wide_away],
    )
    g_expand_bias = jnp.concatenate([bias_low, bias_high], axis=1)
    wide_pair = (wide_here, give(wide_away, "c", 1))
    tall_all = swap(tall_mine, ("y", "z"))
    dfused, fused_sum = attention_backward(dbranch, qkv, probs, layer, attn_block)

    sums = jnp.stack(
        [
            fused_sum[0, :width],
            fused_sum[0, 2 * width :],
            sums_b[2],
            sums_b[0],
            sums_b[1],
            sums_a[5],
            sums_a[3],
            sums_a[4],
            sums_a[0],
            sums_a[1],
            sums_a[2],
        ]
    )
    sums = jnp.concatenate([after(sums)[0].T, g_expand_bias.reshape(width, -1)], axis=1)
    sums = jnp.pad(sums, ((0, 0), (0, 128 - sums.shape[1])))
    last_here, last_away = last_call(core, x, dfused, attended, dbranch, sums)
    last_away, tall_all = after(last_away, tall_all)
    last_pair = (last_here, give(last_away, "c", 1))
    wide_mine, tall_all = after(add_cores(wide_pair), tall_all)
    wide_all = swap(wide_mine, ("y", "z"))
    last_mine, wide_all = after(add_cores(last_pair), wide_all)
    last_all = swap(last_mine, ("y", "z"))

    lse, wide_mine = after(lse, wide_mine)
    grad_w, grad_b = decoder_call(expl, spread, column, labels, scale, stat, lse)
    grad_b = grad_b.reshape(NC, NX, 1, per)
    grad_b = jnp.pad(grad_b, ((0, 0), (0, 0), (0, 7), (0, width - per))).astype(BF)
    grad_w = grad_w.reshape(NC, NX, per, width)
    grad_w, grad_away = (jnp.concatenate([grad_w[i], grad_b[i]], axis=1) for i in range(NC))
    grad_w, grad_away, wide_all = after(grad_w, grad_away, wide_all)
    grad_w = add_cores((grad_w, give(grad_away, "c", 1)))
    grad_w = total([grad_w[0]] + [give(grad_w[k], "x", k) for k in (1, 2, 3)])

    tall = jnp.sum(tall_all[:, :120].astype(F32), axis=0).astype(BF)
    loss_row = split_three(jnp.sum(tall_all[:, 120, :6].astype(F32)))[:128]
    tall_low = tall[:96].reshape(NX, 4, 6, width).transpose(0, 2, 1, 3).reshape(NX, 6, 4 * width)
    early = jnp.concatenate(
        [
            tall_low,
            tall[96:].reshape(NX, 6, width),
            jnp.broadcast_to(loss_row, (NX, 6, 128)),
        ],
        axis=2,
    )
    wide = jnp.sum(wide_all.astype(F32), axis=0).astype(BF)
    last_all, grad_w, dfused = after(last_all, grad_w, dfused)
    dinput = dresidual + matmul_nt(dfused, qkv_full)
    g_vocab, g_vocab_bias = grad_w[:per].T, grad_w[per, :per]
    last = jnp.sum(last_all.astype(F32), axis=0).astype(BF)
    last = sum_x(
        jnp.concatenate([early, wide.reshape(NX, 6, -1), last.reshape(NX, 6, -1)], axis=2)
    )
    ends = [4 * width, width, 128, w_expand.shape[1], 3 * width, width, 128]
    ends = [sum(ends[: i + 1]) for i in range(len(ends))]
    g_shrink = last[:, : ends[0]].reshape(6, 4, width).transpose(1, 0, 2).reshape(24, width)
    g_dense = last[:, ends[0] : ends[1]]
    loss = jnp.sum(last[0, ends[1] : ends[1] + 3])
    g_expand = last[:, ends[2] : ends[3]]
    g_qkv = last[:, ends[3] : ends[4]]
    g_attn = last[:, ends[4] : ends[5]]
    sums = last[:, ends[5] :]
    return (
        settled_low.reshape(hidden_in.shape),
        loss,
        dinput.reshape(hidden_in.shape),
        g_qkv,
        sums[:, 0],
        sums[:, 1],
        g_attn,
        sums[:, 2],
        sums[:, 3],
        sums[:, 4],
        g_expand,
        sums[:, 11:15].reshape(-1),
        g_shrink,
        sums[:, 5],
        sums[:, 6],
        sums[:, 7],
        g_dense,
        sums[:, 8],
        sums[:, 9],
        sums[:, 10],
        g_vocab,
        g_vocab_bias,
    )


def solution(mesh):
    split = Mesh(mesh.devices.reshape(NY, NC, NZ, NX), EVERY)
    whole, one = P(), P(EVERY)
    tokens3 = P(None, EVERY, None)
    matrix = P(EVERY, None)
    in_specs = (
        tokens3,
        tokens3,
        P(None, EVERY),
        P(None, EVERY, None, None),
        whole,
        whole,
        matrix,
        one,
        one,
        matrix,
        one,
        one,
        one,
        matrix,
        one,
        matrix,
        one,
        one,
        one,
        matrix,
        one,
        one,
        one,
        P(None, EVERY),
        one,
    )
    out_specs = (
        tokens3,
        whole,
        tokens3,
        matrix,
        one,
        one,
        matrix,
        one,
        one,
        one,
        matrix,
        one,
        matrix,
        one,
        one,
        one,
        matrix,
        one,
        one,
        one,
        P(None, EVERY),
        one,
    )
    return jax.shard_map(body, mesh=split, in_specs=in_specs, out_specs=out_specs, check_vma=False)
```

```python
import functools

import jax
import jax.numpy as jnp
from jax import lax
from jax.experimental import pallas as pl
from jax.experimental.pallas import tpu as pltpu
from jax.sharding import Mesh
from jax.sharding import PartitionSpec as P

HEAD_DIM = 64
EPS = 1e-05
HALF_ROOT = 0.7071067811865476
NORMAL_PEAK = 0.3989422804014327
MASKED = -1e30

BF = jnp.bfloat16
F32 = jnp.float32
NY, NC, NZ, NX = 4, 2, 4, 4
SIZES = {"y": NY, "c": NC, "z": NZ, "x": NX}
EVERY = ("y", "c", "z", "x")


def fetch(array, axis, k):
    n = SIZES[axis]
    return lax.ppermute(array, axis, [((i + k) % n, i) for i in range(n)])


def give(array, axis, k):
    n = SIZES[axis]
    return lax.ppermute(array, axis, [(i, (i + k) % n) for i in range(n)])


def in_order(pieces, index):
    n = len(pieces)
    twice = jnp.stack(pieces + pieces)
    return lax.dynamic_slice_in_dim(twice, (n - index) % n, n, 0)


def gather_x(shard):
    pieces = [shard] + [fetch(shard, "x", k) for k in (1, 2, 3)]
    return in_order(pieces, lax.axis_index("x"))


def swap(array, axes):
    return lax.all_to_all(array, axes, 0, 0, tiled=True)


def blocks(grad):
    return grad.astype(BF).reshape(NY, NC, NZ, -1, grad.shape[1])


def half(grads, core, axis):
    cut = [lax.dynamic_index_in_dim(grad, core, 1, False) for grad in grads]
    cut = [part.reshape((NY * NZ,) + part.shape[2:]) for part in cut]
    return cut[0] if len(cut) == 1 else jnp.concatenate(cut, axis=axis)


def sum_cores(grads, axis):
    core = lax.axis_index("c")
    return half(grads, core, axis), give(half(grads, 1 - core, axis), "c", 1)


def add_cores(pair):
    return (pair[0].astype(F32) + pair[1].astype(F32)).astype(BF)


def sum_yz(mine):
    return jnp.sum(swap(mine, ("y", "z")).astype(F32), axis=0).astype(BF)


def sum_x(mine):
    return jnp.sum(swap(mine, "x").astype(F32), axis=0)


def split_three(value):
    return jnp.pad(jnp.stack(three(value)), (0, 765)).astype(BF)


def after(*arrays):
    return lax.optimization_barrier(arrays)


def total(parts):
    out = parts[0].astype(F32)
    for part in parts[1:]:
        out = out + part.astype(F32)
    return out


def three(value):
    high = lax.reduce_precision(value, 8, 7)
    rest = value - high
    middle = lax.reduce_precision(rest, 8, 7)
    return [high, middle, lax.reduce_precision(rest - middle, 8, 7)]


def gelu_value(values):
    return 0.5 * values * (1.0 + lax.erf(values * HALF_ROOT))


def gelu_slope(values):
    return 0.5 * (1.0 + lax.erf(values * HALF_ROOT)) + values * NORMAL_PEAK * jnp.exp(
        -0.5 * values * values
    )


def layer_norm(values, gain, shift):
    center = values - jnp.mean(values, axis=-1, keepdims=True)
    inverse = lax.rsqrt(jnp.mean(center * center, axis=-1, keepdims=True) + EPS)
    normed = center * inverse
    return (normed * gain + shift, normed, inverse)


def norm_back(grad, normed, inverse, gain):
    scaled = grad * gain
    inner = (
        scaled
        - jnp.mean(scaled, axis=-1, keepdims=True)
        - normed * jnp.mean(scaled * normed, axis=-1, keepdims=True)
    )
    return inner * inverse


def column_sum(values):
    return jnp.sum(values, axis=0, dtype=F32)


def matmul(left, right):
    return jnp.dot(left, right, preferred_element_type=F32)


def matmul_tn(left, right):
    return lax.dot_general(left, right, (((0,), (0,)), ((), ())), preferred_element_type=F32)


def matmul_nt(left, right):
    return lax.dot_general(left, right, (((1,), (1,)), ((), ())), preferred_element_type=F32)


def dot_nn(left, right):
    return lax.dot_general(left, right, (((1,), (0,)), ((), ())), preferred_element_type=F32)


def dot_nt(left, right):
    return lax.dot_general(left, right, (((1,), (1,)), ((), ())), preferred_element_type=F32)


def dot_tn(left, right):
    return lax.dot_general(left, right, (((0,), (0,)), ((), ())), preferred_element_type=F32)


def attention_forward_kernel(
    x_ref,
    row_ref,
    col_ref,
    wq_ref,
    wk_ref,
    wv_ref,
    wa_ref,
    vec_ref,
    qkv_ref,
    probs_ref,
    attended_ref,
    first_ref,
    low_ref,
    normed_ref,
    inverse_ref,
):
    tokens, width = x_ref.shape
    pair = 2 * HEAD_DIM
    factor = HEAD_DIM ** (-0.5)
    x = x_ref[...]
    qkv_ref[:, :width] = (dot_nn(x, wq_ref[...]) + vec_ref[0:1]).astype(BF)
    qkv_ref[:, width : 2 * width] = dot_nn(x, wk_ref[...]).astype(BF)
    qkv_ref[:, 2 * width :] = (dot_nn(x, wv_ref[...]) + vec_ref[1:2]).astype(BF)
    allowed = row_ref[...] == col_ref[...]
    lower = lax.broadcasted_iota(jnp.int32, (tokens, pair), 1) < HEAD_DIM
    for h in range(width // pair):
        lanes = slice(h * pair, (h + 1) * pair)
        query = qkv_ref[:, lanes]
        keys = qkv_ref[:, width + h * pair : width + (h + 1) * pair]
        values = qkv_ref[:, 2 * width + h * pair : 2 * width + (h + 1) * pair]
        zero = jnp.zeros_like(query)
        outs = []
        for side in range(2):
            mine = jnp.where(lower, query, zero) if side == 0 else jnp.where(lower, zero, query)
            scores = jnp.where(allowed, dot_nt(mine, keys) * factor, MASKED)
            expo = jnp.exp(scores - jnp.max(scores, axis=1, keepdims=True))
            probs = (expo / jnp.sum(expo, axis=1, keepdims=True)).astype(BF)
            probs_ref[2 * h + side] = probs
            outs.append(dot_nn(probs, values))
        attended_ref[:, lanes] = jnp.where(lower, outs[0], outs[1]).astype(BF)
    branch = dot_nn(attended_ref[...], wa_ref[...]) + vec_ref[2:3]
    first, normed, inverse = layer_norm(x.astype(F32) + branch, vec_ref[3:4], vec_ref[4:5])
    first_ref[...] = first
    low_ref[...] = first.astype(BF)
    normed_ref[...] = normed
    inverse_ref[...] = inverse


def weight_spec(width, block):
    return pl.BlockSpec((width, width), lambda m: (0, block))


def attention_forward(x, segments, layer, first_block, vec):
    micro, block = segments.shape
    tokens, width = x.shape
    heads = width // HEAD_DIM
    here = lambda n: pl.BlockSpec((block, n), lambda m: (m, 0))
    return pl.pallas_call(
        attention_forward_kernel,
        grid=(micro,),
        in_specs=[
            here(width),
            pl.BlockSpec((None, 1, block), lambda m: (m, 0, 0)),
            pl.BlockSpec((None, block, 1), lambda m: (m, 0, 0)),
            weight_spec(width, first_block),
            weight_spec(width, first_block + 1),
            weight_spec(width, first_block + 2),
            weight_spec(width, first_block + 3),
            pl.BlockSpec(vec.shape, lambda m: (0, 0)),
        ],
        out_specs=[
            here(3 * width),
            pl.BlockSpec((None, heads, block, block), lambda m: (m, 0, 0, 0)),
            here(width),
            here(width),
            here(width),
            here(width),
            here(1),
        ],
        out_shape=[
            jax.ShapeDtypeStruct((tokens, 3 * width), BF),
            jax.ShapeDtypeStruct((micro, heads, block, block), BF),
            jax.ShapeDtypeStruct((tokens, width), BF),
            jax.ShapeDtypeStruct((tokens, width), F32),
            jax.ShapeDtypeStruct((tokens, width), BF),
            jax.ShapeDtypeStruct((tokens, width), F32),
            jax.ShapeDtypeStruct((tokens, 1), F32),
        ],
        compiler_params=pltpu.CompilerParams(vmem_limit_bytes=48 * 1024 * 1024),
        cost_estimate=pl.CostEstimate(
            flops=4_000_000_000, bytes_accessed=16_000_000, transcendentals=2_000_000
        ),
    )(x, segments[:, None, :], segments[:, :, None], layer, layer, layer, layer, vec)


def attention_backward_kernel(dbranch_ref, qkv_ref, probs_ref, wa_ref, out_ref, sum_ref):
    tokens, width = dbranch_ref.shape
    pair = 2 * HEAD_DIM
    factor = HEAD_DIM ** (-0.5)
    dattended = dot_nt(dbranch_ref[...], wa_ref[...]).astype(BF)
    lower = lax.broadcasted_iota(jnp.int32, (tokens, pair), 1) < HEAD_DIM
    for h in range(width // pair):
        lanes = slice(h * pair, (h + 1) * pair)
        query = qkv_ref[:, lanes]
        keys = qkv_ref[:, width + h * pair : width + (h + 1) * pair]
        values = qkv_ref[:, 2 * width + h * pair : 2 * width + (h + 1) * pair]
        grad = dattended[:, lanes]
        zero = jnp.zeros_like(grad)
        parts = []
        for side in range(2):
            mine = jnp.where(lower, grad, zero) if side == 0 else jnp.where(lower, zero, grad)
            low = probs_ref[2 * h + side]
            probs = low.astype(F32)
            dprobs = dot_nt(mine, values)
            inner = jnp.sum(probs * dprobs, axis=1, keepdims=True)
            dscores = (probs * (dprobs - inner)).astype(BF)
            parts.append(
                (dot_nn(dscores, keys) * factor, dot_tn(dscores, query) * factor, dot_tn(low, grad))
            )
        for i in range(3):
            start = i * width + h * pair
            out_ref[:, start : start + pair] = jnp.where(lower, parts[0][i], parts[1][i]).astype(BF)
    seen = jnp.sum(out_ref[...].astype(F32), axis=0, keepdims=True)

    @pl.when(pl.program_id(0) == 0)
    def _():
        sum_ref[...] = seen

    @pl.when(pl.program_id(0) > 0)
    def _():
        sum_ref[...] += seen


def attention_backward(dbranch, qkv, probs, layer, attn_block):
    micro, heads, block, _ = probs.shape
    tokens, width = dbranch.shape
    here = lambda n: pl.BlockSpec((block, n), lambda m: (m, 0))
    return pl.pallas_call(
        attention_backward_kernel,
        grid=(micro,),
        in_specs=[
            here(width),
            here(3 * width),
            pl.BlockSpec((None, heads, block, block), lambda m: (m, 0, 0, 0)),
            weight_spec(width, attn_block),
        ],
        out_specs=[here(3 * width), pl.BlockSpec((1, 3 * width), lambda m: (0, 0))],
        out_shape=[
            jax.ShapeDtypeStruct((tokens, 3 * width), BF),
            jax.ShapeDtypeStruct((1, 3 * width), F32),
        ],
        compiler_params=pltpu.CompilerParams(vmem_limit_bytes=48 * 1024 * 1024),
        cost_estimate=pl.CostEstimate(
            flops=1000, bytes_accessed=1000, transcendentals=0
        ),
    )(dbranch, qkv, probs, layer)


LIMIT = 56 * 1024 * 1024


def whole_spec(array):
    return pl.BlockSpec(array.shape, lambda *_: (0,) * len(array.shape))


def call(kernel, grid, ins, in_specs, outs, out_specs, scratch, flops, size):
    return pl.pallas_call(
        kernel,
        grid=grid,
        in_specs=in_specs,
        out_specs=out_specs,
        out_shape=[jax.ShapeDtypeStruct(shape, kind) for shape, kind in outs],
        scratch_shapes=scratch,
        compiler_params=pltpu.CompilerParams(vmem_limit_bytes=LIMIT),
        cost_estimate=pl.CostEstimate(flops=flops, bytes_accessed=size, transcendentals=0),
    )(*ins)


def low_three(value):
    high = value.astype(BF).astype(F32)
    middle = (value - high).astype(BF).astype(F32)
    rest = (value - high - middle).astype(BF).astype(F32)
    return [high, middle, rest]


def logits_kernel(
    spread_ref, w_ref, b_ref, column_ref, label_ref, expl_ref, stat_ref, part_ref, flat_ref, logits_ref
):
    step = pl.program_id(0)
    count, width = spread_ref.shape
    peers, high, _ = part_ref.shape
    rows = high - 16
    spread = spread_ref[...]
    entries = w_ref.shape[0]
    chunks = [slice(i, i + entries // 5) for i in range(0, entries, entries // 5)]
    peak = None
    for cut in chunks:
        logits = dot_nt(spread, w_ref[cut, :]) + b_ref[:, cut]
        logits_ref[:, cut] = logits
        most = jnp.max(logits, axis=1, keepdims=True)
        peak = most if peak is None else jnp.maximum(peak, most)
    top = peak
    sums = jnp.zeros((count, 1), F32)
    label = jnp.zeros((count, 1), F32)
    part = jnp.zeros((count, width), F32)
    for cut in chunks:
        expl = jnp.exp(logits_ref[:, cut] - top)
        sums += jnp.sum(expl, axis=1, keepdims=True)
        hit = label_ref[...] == column_ref[:, cut]
        rest = jnp.where(hit, 0.0, expl)
        label += jnp.sum(expl - rest, axis=1, keepdims=True)
        other = rest.astype(BF)
        expl_ref[:, cut] = other
        part += dot_nn(other, w_ref[cut, :])
    part = part.astype(BF)
    for i in range(count // rows):
        part_ref[step * (count // rows) + i, 0:rows, :] = part[i * rows : (i + 1) * rows]
    lane = lax.broadcasted_iota(jnp.int32, (count, 128), 1)
    stat = jnp.where(lane == 0, top, jnp.where(lane == 1, label, 0.0))
    stat_ref[...] = stat
    parts = jnp.zeros((count, 128), F32)
    for i, value in enumerate(low_three(top) + low_three(sums)):
        parts = jnp.where(lane == i, value, parts)
    flat_ref[step] = parts.T[0:8]

    @pl.when(step == pl.num_programs(0) - 1)
    def _():
        told = jnp.concatenate([flat_ref[i] for i in range(flat_ref.shape[0])], axis=1)
        rest = told.shape[1] - width
        last = jnp.concatenate([told[:, width:], jnp.zeros((8, width - rest), F32)], axis=1)
        told = jnp.concatenate([told[:, :width], last], axis=0).astype(BF)
        for i in range(peers):
            part_ref[i, rows:, :] = told


def logits_call(spread, vocab_w, vocab_b, column, labels, rows):
    count, width = spread.shape
    entries = vocab_w.shape[0]
    block = count // 2
    here = lambda n: pl.BlockSpec((block, n), lambda i: (i, 0))
    ins = (spread, vocab_w, vocab_b[None, :], column[None, :], labels)
    specs = [here(width)] + [whole_spec(a) for a in ins[1:4]] + [here(1)]
    part = (count // rows, rows + 16, width)
    return call(
        logits_kernel,
        (2,),
        ins,
        specs,
        [((count, entries), BF), ((count, 128), F32), (part, BF)],
        [here(entries), here(128), pl.BlockSpec(part, lambda i: (0, 0, 0))],
        [pltpu.VMEM((2, 8, block), F32), pltpu.VMEM((block, entries), F32)],
        10_000_000_000,
        20_000_000,
    )


def decoder_kernel(
    expl_ref, spread_ref, column_ref, label_ref, scale_ref, stat_ref, lse_ref, out_ref, sum_ref
):
    count = spread_ref.shape[0]
    lse = jnp.broadcast_to(lse_ref[...], (8, count)).T[:, 0:1]
    share = jnp.exp(stat_ref[:, 0:1] - lse)
    scale = scale_ref[...]
    hit = label_ref[...] == column_ref[...]
    other = (scale * share) * expl_ref[...].astype(F32)
    dlogits = jnp.where(hit, scale * (stat_ref[:, 1:2] * share - 1.0), other).astype(BF)
    out_ref[...] = dot_tn(dlogits, spread_ref[...]).astype(BF)
    sum_ref[...] = jnp.sum(dlogits.astype(F32), axis=0, keepdims=True)


def decoder_call(expl, spread, column, labels, scale, stat, lse):
    count, width = spread.shape
    entries = expl.shape[1]
    block = entries // 5
    ins = (expl, spread, column[None, :], labels, scale, stat, lse)
    return call(
        decoder_kernel,
        (5,),
        ins,
        [
            pl.BlockSpec((count, block), lambda j: (0, j)),
            whole_spec(spread),
            pl.BlockSpec((1, block), lambda j: (0, j)),
        ]
        + [whole_spec(a) for a in ins[3:]],
        [((entries, width), BF), ((1, entries), F32)],
        [
            pl.BlockSpec((block, width), lambda j: (j, 0)),
            pl.BlockSpec((1, block), lambda j: (0, j)),
        ],
        [],
        1000,
        1000,
    )


def merge_kernel(
    own_ref,
    part_ref,
    head_ref,
    label_ref,
    scalar_ref,
    normed3_ref,
    slope3_ref,
    vec_ref,
    picked_ref,
    dense_ref,
    select_ref,
    grad_ref,
    normed2_ref,
    inverse2_ref,
    lse_ref,
    loss_ref,
    g_dense_ref,
    dsecond_ref,
    dffn_ref,
    sums_ref,
):
    peers, high, width = part_ref.shape
    rows = high - 16
    tail = peers * rows - width

    def told(i):
        first = part_ref[:, rows : rows + 8, :].astype(F32)[:, i]
        rest = part_ref[:, rows + 8 :, :].astype(F32)[:, i, :tail]
        return jnp.concatenate([first, rest], axis=1)

    tops = told(0) + told(1) + told(2)
    sums = told(3) + told(4) + told(5)
    top = jnp.max(tops, axis=0, keepdims=True)
    share = jnp.exp(tops - top)
    total_sum = jnp.sum(sums * share, axis=0, keepdims=True)
    lse = top + jnp.log(total_sum)
    share = share / total_sum
    lse_ref[...] = lse
    mine = own_ref[0] + lax.broadcasted_iota(jnp.int32, (rows, peers * rows), 0)
    mine = mine == lax.broadcasted_iota(jnp.int32, (rows, peers * rows), 1)
    own_lse = jnp.sum(jnp.where(mine, lse, 0.0), axis=1, keepdims=True)
    mixed = jnp.zeros((rows, width), F32)
    for i in range(peers):
        weight = jnp.sum(jnp.where(mine, share[i : i + 1], 0.0), axis=1, keepdims=True)
        mixed += weight * part_ref[i, 0:rows, :].astype(F32)
    label = label_ref[...]
    label_logit = jnp.sum(head_ref[...].astype(F32) * label, axis=1, keepdims=True)
    label_logit += scalar_ref[:, 0:1]
    grad = scalar_ref[:, 2:3] * (mixed + (jnp.exp(label_logit - own_lse) - 1.0) * label)
    loss_ref[...] = jnp.zeros(loss_ref.shape, F32) + jnp.sum(
        scalar_ref[:, 1:2] * (own_lse - label_logit)
    )
    normed3 = normed3_ref[...]
    ddense = norm_back(grad, normed3, scalar_ref[:, 3:4], vec_ref[9:10]) * slope3_ref[...]
    low = ddense.astype(BF)
    column = lambda v: jnp.sum(v, axis=0, keepdims=True)
    g_dense_ref[...] = dot_tn(picked_ref[...], low)
    drows = dot_nt(low, dense_ref[...]).astype(BF)
    dout = grad_ref[...].astype(F32) + dot_tn(select_ref[...], drows)
    normed2 = normed2_ref[...]
    dsecond = norm_back(dout, normed2, inverse2_ref[...], vec_ref[6:7])
    dffn = dsecond.astype(BF)
    dsecond_ref[...] = dsecond
    dffn_ref[...] = dffn
    parts = [
        column(low.astype(F32)),
        column(grad * normed3),
        column(grad),
        column(dout * normed2),
        column(dout),
        column(dffn.astype(F32)),
    ]
    for i, value in enumerate(parts):
        sums_ref[i : i + 1] = value


def merge_call(own, *arrays, layer, dense_block):
    part, head = arrays[0], arrays[1]
    width = head.shape[1]
    tokens = arrays[-1].shape[0]
    count = part.shape[0] * (part.shape[1] - 16)
    ins = list(arrays)
    ins.insert(8, layer)
    specs = [whole_spec(a) for a in arrays]
    specs.insert(8, pl.BlockSpec((width, width), lambda *_: (0, dense_block)))
    outs = [
        ((1, count), F32),
        ((8, 128), F32),
        ((width, width), F32),
        ((tokens, width), F32),
        ((tokens, width), BF),
        ((8, width), F32),
    ]
    return call(
        merge_kernel,
        (1,),
        [own] + ins,
        [pl.BlockSpec(memory_space=pltpu.SMEM)] + specs,
        outs,
        [pl.BlockSpec(shape, lambda *_: (0, 0)) for shape, _ in outs],
        [],
        300_000_000,
        10_000_000,
    )


def shrink_kernel(
    core_ref, act_ref, dffn_ref, dense_ref, loss_ref, here_ref, away_ref, grad_ref
):
    width = dffn_ref.shape[1]
    grad_ref[...] = dot_tn(act_ref[...], dffn_ref[...])
    core = core_ref[0]
    spot = lax.broadcasted_iota(jnp.int32, (8, width), 1)
    first = lax.broadcasted_iota(jnp.int32, (8, width), 0) == 0
    told = jnp.zeros((8, width), F32)
    for i, value in enumerate(low_three(loss_ref[0:1, 0:1])):
        told = jnp.where(first & (spot == i + 3 * core), value, told)
    for ref, c in ((here_ref, core), (away_ref, 1 - core)):
        for z in range(NZ):
            tall = pl.ds(pl.multiple_of(c * (width // 2) + z * 96, 8), 96)
            flat = pl.ds(pl.multiple_of(c * 96 + z * 24, 8), 24)
            ref[z, 0:96, :] = grad_ref[tall, :].astype(BF)
            ref[z, 96:128, :] = jnp.concatenate([dense_ref[flat, :], told], axis=0).astype(BF)


def shrink_call(core, act, dffn, g_dense, loss):
    tokens, width = dffn.shape
    out = ((NY * NZ, 128, width), BF)
    half_spec = pl.BlockSpec((NZ, 128, width), lambda y: (y, 0, 0))
    return call(
        shrink_kernel,
        (NY,),
        (core, act, dffn, g_dense, loss),
        [
            pl.BlockSpec(memory_space=pltpu.SMEM),
            pl.BlockSpec((tokens, width), lambda y: (0, y)),
            whole_spec(dffn),
            pl.BlockSpec((width // NY, width), lambda y: (y, 0)),
            whole_spec(loss),
        ],
        [out, out],
        [half_spec, half_spec],
        [pltpu.VMEM((width, width), F32)],
        1000,
        1000,
    )


def put_wide(grad_ref, core, here_ref, away_ref, lanes):
    for ref, c in ((here_ref, core), (away_ref, 1 - core)):
        for y in range(NY):
            rows = pl.ds(pl.multiple_of((NC * y + c) * 96, 8), 96)
            ref[y * NZ : (y + 1) * NZ, :, lanes] = (
                grad_ref[rows, :].reshape(NZ, 24, -1).astype(BF)
            )


def feed_back_kernel(closing, core_ref, *refs):
    dffn_ref, shrink_ref, slope_ref, low_ref, expand_ref, before_ref = refs[:6]
    if closing:
        normed_ref, inverse_ref, vec_ref = refs[6:9]
        here_ref, away_ref, bias_ref, dresidual_ref, dbranch_ref, sums_ref = refs[11:17]
        grad_ref, total_ref = refs[17:]
    else:
        here_ref, away_ref, bias_ref, total_ref, grad_ref = refs[6:]
    step = pl.program_id(0)
    dpre = (dot_nt(dffn_ref[...], shrink_ref[...]) * slope_ref[...].astype(F32)).astype(BF)
    bias_ref[...] = jnp.sum(dpre.astype(F32), axis=0, keepdims=True)
    more = dot_nt(dpre, expand_ref[...])

    @pl.when(step == 0)
    def _():
        total_ref[...] = before_ref[...] + more

    @pl.when(step > 0)
    def _():
        total_ref[...] += more

    grad_ref[...] = dot_tn(low_ref[...], dpre)
    put_wide(grad_ref, core_ref[0], here_ref, away_ref, slice(None))
    if not closing:
        return

    @pl.when(step == pl.num_programs(0) - 1)
    def _():
        dfirst = total_ref[...]
        normed = normed_ref[...]
        dresidual = norm_back(dfirst, normed, inverse_ref[...], vec_ref[3:4])
        dbranch = dresidual.astype(BF)
        dresidual_ref[...] = dresidual
        dbranch_ref[...] = dbranch
        sums_ref[0:1] = jnp.sum(dfirst * normed, axis=0, keepdims=True)
        sums_ref[1:2] = jnp.sum(dfirst, axis=0, keepdims=True)
        sums_ref[2:3] = jnp.sum(dbranch.astype(F32), axis=0, keepdims=True)


def feed_back_call(core, dffn, shrink, slope, low, layer, expand_block, before, rest=None):
    tokens, width = dffn.shape
    wide = slope.shape[1]
    steps = wide // width // 2
    closing = rest is not None
    at = steps if closing else 0
    half = ((NY * NZ, 24, wide), BF)
    half_spec = pl.BlockSpec((NY * NZ, 24, width), lambda j: (0, 0, at + j))
    flat = pl.BlockSpec((tokens, width), lambda j: (0, 0))
    outs = [half, half, ((1, wide // 2), F32), ((tokens, width), F32)]
    out_specs = [half_spec, half_spec, pl.BlockSpec((1, width), lambda j: (0, j)), flat]
    ins = [core, dffn, shrink, slope, low, layer, before]
    in_specs = [
        pl.BlockSpec(memory_space=pltpu.SMEM),
        whole_spec(dffn),
        pl.BlockSpec((width, width), lambda j: (at + j, 0)),
        pl.BlockSpec((tokens, width), lambda j: (0, at + j)),
        whole_spec(low),
        pl.BlockSpec((width, width), lambda j: (0, expand_block + at + j)),
        whole_spec(before),
    ]
    if closing:
        outs += [((tokens, width), BF), ((8, width), F32)]
        out_specs += [flat, pl.BlockSpec((8, width), lambda j: (0, 0))]
        ins += rest
        in_specs += [whole_spec(a) for a in rest[:3]] + [pl.BlockSpec(memory_space=pl.ANY)] * 2
    return pl.pallas_call(
        functools.partial(feed_back_kernel, closing),
        grid=(steps,),
        in_specs=in_specs,
        out_specs=out_specs,
        out_shape=[jax.ShapeDtypeStruct(shape, kind) for shape, kind in outs],
        scratch_shapes=[pltpu.VMEM((width, width), F32)]
        + ([pltpu.VMEM((tokens, width), F32)] if closing else []),
        input_output_aliases={10: 0, 11: 1} if closing else {},
        compiler_params=pltpu.CompilerParams(vmem_limit_bytes=LIMIT),
        cost_estimate=pl.CostEstimate(flops=1000, bytes_accessed=1000, transcendentals=0),
    )(*ins)


def last_kernel(
    core_ref, x_ref, dfused_ref, attended_ref, dbranch_ref, sums_ref, here_ref, away_ref, grad_ref
):
    width = x_ref.shape[1]
    core = core_ref[0]
    for i in range(4):
        lanes = slice(i * width, (i + 1) * width)
        if i < 3:
            grad_ref[i % 2] = dot_tn(x_ref[...], dfused_ref[:, lanes])
        else:
            grad_ref[i % 2] = dot_tn(attended_ref[...], dbranch_ref[...])
        put_wide(grad_ref.at[i % 2], core, here_ref, away_ref, lanes)
    put_wide(sums_ref, core, here_ref, away_ref, slice(4 * width, 4 * width + 128))


def last_call(core, x, dfused, attended, dbranch, sums):
    width = x.shape[1]
    out = ((NY * NZ, 24, 4 * width + 128), BF)
    ins = (x, dfused, attended, dbranch, sums)
    half_spec = pl.BlockSpec(out[0], lambda *_: (0, 0, 0))
    return call(
        last_kernel,
        (1,),
        (core,) + ins,
        [pl.BlockSpec(memory_space=pltpu.SMEM)] + [whole_spec(a) for a in ins],
        [out, out],
        [half_spec, half_spec],
        [pltpu.VMEM((2, width, width), F32)],
        1000,
        1000,
    )


def tall_kernel(in_ref, out_ref):
    blocks_, rows, width = out_ref.shape
    out_ref[...] = in_ref[...].astype(F32).reshape(blocks_, rows, width).astype(BF)


def tall_call(layer, width):
    places = NY * NC * NZ
    rows = layer.shape[0] // places
    return call(
        tall_kernel,
        (2, NX),
        (layer,),
        [pl.BlockSpec((layer.shape[0] // 2, width), lambda j, k: (j, k))],
        [((places, NX, rows, width), BF)],
        [pl.BlockSpec((places // 2, None, rows, width), lambda j, k: (j, k, 0, 0))],
        [],
        1000,
        1000,
    )[0].reshape(-1, width)


def body(
    hidden_in,
    out_grad,
    segments,
    mask_pos,
    mask_labels,
    loss_scale,
    w_qkv,
    b_query,
    b_value,
    w_attn,
    b_attn,
    attn_gain,
    attn_shift,
    w_expand,
    b_expand,
    w_shrink,
    b_shrink,
    ffn_gain,
    ffn_shift,
    w_dense,
    b_dense,
    dense_gain,
    dense_shift,
    w_vocab,
    b_vocab,
):
    micro, block, width = hidden_in.shape
    tokens = micro * block
    heads = width // HEAD_DIM
    factor = HEAD_DIM ** (-0.5)
    at = {axis: lax.axis_index(axis) for axis in EVERY}
    core = at["c"].astype(jnp.int32)[None]

    vectors = (
        b_query,
        b_value,
        b_attn,
        attn_gain,
        attn_shift,
        b_shrink,
        ffn_gain,
        ffn_shift,
        b_dense,
        dense_gain,
        dense_shift,
    )
    small = after(jnp.stack(vectors))[0].T
    small = jnp.concatenate([small, b_expand.reshape(w_qkv.shape[0], -1)], axis=1)
    small = jnp.pad(small, ((0, 0), (0, 128 - small.shape[1])))
    fused = jnp.concatenate([w_expand, w_qkv, w_attn, w_dense, small], axis=1)
    fused = gather_x(fused).reshape(-1, fused.shape[1])
    tall = gather_x(w_shrink)
    tall = tall.transpose(1, 0, 2).reshape(fused.shape[0], -1)
    layer = lax.all_gather(
        jnp.concatenate([tall, fused], axis=1), ("y", "c", "z"), axis=0, tiled=True
    )
    own_w = w_vocab.T
    piece_w = [own_w] + [fetch(own_w, "x", k) for k in (1, 2, 3)]
    piece_b = [b_vocab] + [fetch(b_vocab, "x", k) for k in (1, 2, 3)]
    half_w = jnp.stack(piece_w)
    half_b = jnp.stack(piece_b)
    per = own_w.shape[0]
    vocab_w = jnp.concatenate([half_w, fetch(half_w, "c", 1)]).reshape(-1, width)
    vocab_b = jnp.concatenate([half_b, fetch(half_b, "c", 1)]).reshape(-1).astype(F32)
    start = jnp.stack(
        [
            (((at["y"] * NC + (at["c"] + kc) % NC) * NZ + at["z"]) * NX + (at["x"] + kx) % NX)
            * per
            for kc in range(NC)
            for kx in range(NX)
        ]
    )
    column = (start[:, None] + jnp.arange(per, dtype=jnp.int32)[None, :]).reshape(-1)

    flat_labels = mask_labels.reshape(micro, -1)
    counts = jnp.sum((flat_labels >= 0).astype(F32), axis=1)
    norms = 1.0 / (counts * micro)
    slots = mask_labels.shape[-1]
    peers = NZ * NX
    grid = mask_labels.reshape(micro, NY, NC, peers, NZ, NX, slots)
    grid = lax.dynamic_index_in_dim(grid, at["c"], 2, False)
    grid = lax.dynamic_index_in_dim(grid, at["x"], 4, False)
    labels = grid.transpose(1, 3, 0, 2, 4).reshape(-1)
    rows = micro * peers * slots
    row_norm = jnp.broadcast_to(norms[None, :, None], (NY * NZ, micro, peers * slots)).reshape(-1)
    live = (labels >= 0).astype(F32)
    row_weight = live * row_norm
    hit = labels[:, None] == column[None, :]
    scale = loss_scale * row_weight
    own_first = (at["y"] * NZ + at["z"]) * rows
    own_weight = lax.dynamic_slice_in_dim(row_weight, own_first, rows)
    label_w = matmul(hit.astype(BF), vocab_w)
    label_b = jnp.sum(jnp.where(hit, vocab_b, 0.0), axis=1, keepdims=True)
    label_w = jnp.concatenate([label_w, jnp.pad(label_b, ((0, 0), (0, 127)))], axis=1)
    label_w = label_w.astype(BF).reshape(NY * NZ, rows, -1)
    positions = mask_pos.reshape(micro, -1)
    shifted = jnp.where(
        positions >= 0, positions + block * jnp.arange(micro, dtype=jnp.int32)[:, None], -1
    ).reshape(-1)
    select = (shifted[:, None] == jnp.arange(tokens, dtype=jnp.int32)[None, :]).astype(BF)

    scale, labels = scale[:, None], labels[:, None]
    layer, label_w, vocab_w, select, scale, labels = after(
        layer, label_w, vocab_w, select, scale, labels
    )
    label_w = swap(label_w, ("y", "z"))
    ends = [NX * width, w_expand.shape[1], 3 * width, width, width, 128]
    ends = [sum(ends[: i + 1]) for i in range(len(ends))]
    expand_full = layer[:, ends[0] : ends[1]]
    qkv_full = layer[:, ends[1] : ends[2]]
    attn_block = ends[2] // width
    dense_full = layer[:, ends[3] : ends[4]]
    vec_full = layer[:, ends[4] :]
    shrink_full = tall_call(layer, width)
    rows_of = vec_full[:, :16].T.astype(F32)
    (
        b_query,
        b_value,
        b_attn,
        attn_gain,
        attn_shift,
        b_shrink,
        ffn_gain,
        ffn_shift,
        b_dense,
        dense_gain,
        dense_shift,
    ) = (rows_of[i] for i in range(len(vectors)))
    b_expand = vec_full[:, 11:15].astype(F32).reshape(-1)

    x = hidden_in.reshape(tokens, width)
    qkv, probs, attended, first, first_low, normed1, inverse1 = attention_forward(
        x, segments, layer, attn_block - 3, rows_of
    )
    pre = matmul(first_low, expand_full) + b_expand
    act = gelu_value(pre).astype(BF)
    slope = gelu_slope(pre).astype(BF)
    second = first + matmul(act, shrink_full) + b_shrink
    settled, normed2, inverse2 = layer_norm(second, ffn_gain, ffn_shift)
    settled_low = settled.astype(BF)

    select, label_w = after(select, label_w)
    label_w = jnp.sum(label_w.astype(F32), axis=0)
    label_w, label_b = label_w[:, :width], label_w[:, width]
    picked = matmul(select, settled_low).astype(BF)
    dense_pre = matmul(picked, dense_full) + b_dense
    head_val, normed3, inverse3 = layer_norm(gelu_value(dense_pre), dense_gain, dense_shift)
    head_out = head_val.astype(BF)
    spread = swap(
        jnp.broadcast_to(head_out, (NY * NZ,) + head_out.shape), ("y", "z")
    ).reshape(-1, width)
    expl, stat, part = logits_call(spread, vocab_w, vocab_b, column, labels, rows)
    part = swap(part, ("y", "z"))
    scalars = jnp.stack(
        [label_b, own_weight, loss_scale * own_weight, inverse3[:, 0]], axis=1
    )
    lse, loss_own, g_dense, dsecond, dffn, sums_a = merge_call(
        own_first.astype(jnp.int32)[None],
        part,
        head_out,
        label_w,
        jnp.pad(scalars, ((0, 0), (0, 124))),
        normed3,
        gelu_slope(dense_pre),
        rows_of,
        picked,
        select,
        out_grad.reshape(tokens, width),
        normed2,
        inverse2,
        layer=layer,
        dense_block=attn_block + 1,
    )

    tall_pair = shrink_call(core, act, dffn, g_dense, loss_own)
    tall_here, tall_away, dffn = after(*tall_pair, dffn)
    tall_pair = (tall_here, give(tall_away, "c", 1))
    wide_here, wide_away, bias_low, half_first = feed_back_call(
        core, dffn, shrink_full, slope, first_low, layer, 4, dsecond
    )
    half_first, tall_mine = after(half_first, add_cores(tall_pair))
    wide_here, wide_away, bias_high, dresidual, dbranch, sums_b = feed_back_call(
        core,
        dffn,
        shrink_full,
        slope,
        first_low,
        layer,
        4,
        half_first,
        [normed1, inverse1, rows_of, wide_here, wide_away],
    )
    g_expand_bias = jnp.concatenate([bias_low, bias_high], axis=1)
    wide_pair = (wide_here, give(wide_away, "c", 1))
    tall_all = swap(tall_mine, ("y", "z"))
    dfused, fused_sum = attention_backward(dbranch, qkv, probs, layer, attn_block)

    sums = jnp.stack(
        [
            fused_sum[0, :width],
            fused_sum[0, 2 * width :],
            sums_b[2],
            sums_b[0],
            sums_b[1],
            sums_a[5],
            sums_a[3],
            sums_a[4],
            sums_a[0],
            sums_a[1],
            sums_a[2],
        ]
    )
    sums = jnp.concatenate([after(sums)[0].T, g_expand_bias.reshape(width, -1)], axis=1)
    sums = jnp.pad(sums, ((0, 0), (0, 128 - sums.shape[1])))
    last_here, last_away = last_call(core, x, dfused, attended, dbranch, sums)
    last_away, tall_all = after(last_away, tall_all)
    last_pair = (last_here, give(last_away, "c", 1))
    wide_mine, tall_all = after(add_cores(wide_pair), tall_all)
    wide_all = swap(wide_mine, ("y", "z"))
    last_mine, wide_all = after(add_cores(last_pair), wide_all)
    last_all = swap(last_mine, ("y", "z"))

    lse, wide_mine = after(lse, wide_mine)
    grad_w, grad_b = decoder_call(expl, spread, column, labels, scale, stat, lse)
    grad_b = grad_b.reshape(NC, NX, 1, per)
    grad_b = jnp.pad(grad_b, ((0, 0), (0, 0), (0, 7), (0, width - per))).astype(BF)
    grad_w = grad_w.reshape(NC, NX, per, width)
    grad_w, grad_away = (jnp.concatenate([grad_w[i], grad_b[i]], axis=1) for i in range(NC))
    grad_w, grad_away, wide_all = after(grad_w, grad_away, wide_all)
    grad_away, tall_all = after(give(grad_away, "c", 1), tall_all)
    grad_w = add_cores((grad_w, grad_away))
    grad_w = total([grad_w[0]] + [give(grad_w[k], "x", k) for k in (1, 2, 3)])

    tall = jnp.sum(tall_all[:, :120].astype(F32), axis=0).astype(BF)
    loss_row = split_three(jnp.sum(tall_all[:, 120, :6].astype(F32)))[:128]
    tall_low = tall[:96].reshape(NX, 4, 6, width).transpose(0, 2, 1, 3).reshape(NX, 6, 4 * width)
    early = jnp.concatenate(
        [
            tall_low,
            tall[96:].reshape(NX, 6, width),
            jnp.broadcast_to(loss_row, (NX, 6, 128)),
        ],
        axis=2,
    )
    wide = jnp.sum(wide_all.astype(F32), axis=0).astype(BF)
    last_all, grad_w, dfused = after(last_all, grad_w, dfused)
    dinput = dresidual + matmul_nt(dfused, qkv_full)
    g_vocab, g_vocab_bias = grad_w[:per].T, grad_w[per, :per]
    last = jnp.sum(last_all.astype(F32), axis=0).astype(BF)
    last = sum_x(
        jnp.concatenate([early, wide.reshape(NX, 6, -1), last.reshape(NX, 6, -1)], axis=2)
    )
    ends = [4 * width, width, 128, w_expand.shape[1], 3 * width, width, 128]
    ends = [sum(ends[: i + 1]) for i in range(len(ends))]
    g_shrink = last[:, : ends[0]].reshape(6, 4, width).transpose(1, 0, 2).reshape(24, width)
    g_dense = last[:, ends[0] : ends[1]]
    loss = jnp.sum(last[0, ends[1] : ends[1] + 3])
    g_expand = last[:, ends[2] : ends[3]]
    g_qkv = last[:, ends[3] : ends[4]]
    g_attn = last[:, ends[4] : ends[5]]
    sums = last[:, ends[5] :]
    return (
        settled_low.reshape(hidden_in.shape),
        loss,
        dinput.reshape(hidden_in.shape),
        g_qkv,
        sums[:, 0],
        sums[:, 1],
        g_attn,
        sums[:, 2],
        sums[:, 3],
        sums[:, 4],
        g_expand,
        sums[:, 11:15].reshape(-1),
        g_shrink,
        sums[:, 5],
        sums[:, 6],
        sums[:, 7],
        g_dense,
        sums[:, 8],
        sums[:, 9],
        sums[:, 10],
        g_vocab,
        g_vocab_bias,
    )


def solution(mesh):
    split = Mesh(mesh.devices.reshape(NY, NC, NZ, NX), EVERY)
    whole, one = P(), P(EVERY)
    tokens3 = P(None, EVERY, None)
    matrix = P(EVERY, None)
    in_specs = (
        tokens3,
        tokens3,
        P(None, EVERY),
        P(None, EVERY, None, None),
        whole,
        whole,
        matrix,
        one,
        one,
        matrix,
        one,
        one,
        one,
        matrix,
        one,
        matrix,
        one,
        one,
        one,
        matrix,
        one,
        one,
        one,
        P(None, EVERY),
        one,
    )
    out_specs = (
        tokens3,
        whole,
        tokens3,
        matrix,
        one,
        one,
        matrix,
        one,
        one,
        one,
        matrix,
        one,
        matrix,
        one,
        one,
        one,
        matrix,
        one,
        one,
        one,
        P(None, EVERY),
        one,
    )
    return jax.shard_map(body, mesh=split, in_specs=in_specs, out_specs=out_specs, check_vma=False)
```

```python
import functools

import jax
import jax.numpy as jnp
from jax import lax
from jax.experimental import pallas as pl
from jax.experimental.pallas import tpu as pltpu
from jax.sharding import Mesh
from jax.sharding import PartitionSpec as P

HEAD_DIM = 64
EPS = 1e-05
HALF_ROOT = 0.7071067811865476
NORMAL_PEAK = 0.3989422804014327
MASKED = -1e30

BF = jnp.bfloat16
F32 = jnp.float32
NY, NC, NZ, NX = 4, 2, 4, 4
SIZES = {"y": NY, "c": NC, "z": NZ, "x": NX}
EVERY = ("y", "c", "z", "x")


def fetch(array, axis, k):
    n = SIZES[axis]
    return lax.ppermute(array, axis, [((i + k) % n, i) for i in range(n)])


def give(array, axis, k):
    n = SIZES[axis]
    return lax.ppermute(array, axis, [(i, (i + k) % n) for i in range(n)])


def in_order(pieces, index):
    n = len(pieces)
    twice = jnp.stack(pieces + pieces)
    return lax.dynamic_slice_in_dim(twice, (n - index) % n, n, 0)


def gather_x(shard):
    pieces = [shard] + [fetch(shard, "x", k) for k in (1, 2, 3)]
    return in_order(pieces, lax.axis_index("x"))


def swap(array, axes):
    return lax.all_to_all(array, axes, 0, 0, tiled=True)


def blocks(grad):
    return grad.astype(BF).reshape(NY, NC, NZ, -1, grad.shape[1])


def half(grads, core, axis):
    cut = [lax.dynamic_index_in_dim(grad, core, 1, False) for grad in grads]
    cut = [part.reshape((NY * NZ,) + part.shape[2:]) for part in cut]
    return cut[0] if len(cut) == 1 else jnp.concatenate(cut, axis=axis)


def sum_cores(grads, axis):
    core = lax.axis_index("c")
    return half(grads, core, axis), give(half(grads, 1 - core, axis), "c", 1)


def add_cores(pair):
    return (pair[0].astype(F32) + pair[1].astype(F32)).astype(BF)


def sum_yz(mine):
    return jnp.sum(swap(mine, ("y", "z")).astype(F32), axis=0).astype(BF)


def sum_x(mine):
    return jnp.sum(swap(mine, "x").astype(F32), axis=0)


def split_three(value):
    return jnp.pad(jnp.stack(three(value)), (0, 765)).astype(BF)


def after(*arrays):
    return lax.optimization_barrier(arrays)


def total(parts):
    out = parts[0].astype(F32)
    for part in parts[1:]:
        out = out + part.astype(F32)
    return out


def three(value):
    high = lax.reduce_precision(value, 8, 7)
    rest = value - high
    middle = lax.reduce_precision(rest, 8, 7)
    return [high, middle, lax.reduce_precision(rest - middle, 8, 7)]


def gelu_value(values):
    return 0.5 * values * (1.0 + lax.erf(values * HALF_ROOT))


def gelu_slope(values):
    return 0.5 * (1.0 + lax.erf(values * HALF_ROOT)) + values * NORMAL_PEAK * jnp.exp(
        -0.5 * values * values
    )


def layer_norm(values, gain, shift):
    center = values - jnp.mean(values, axis=-1, keepdims=True)
    inverse = lax.rsqrt(jnp.mean(center * center, axis=-1, keepdims=True) + EPS)
    normed = center * inverse
    return (normed * gain + shift, normed, inverse)


def norm_back(grad, normed, inverse, gain):
    scaled = grad * gain
    inner = (
        scaled
        - jnp.mean(scaled, axis=-1, keepdims=True)
        - normed * jnp.mean(scaled * normed, axis=-1, keepdims=True)
    )
    return inner * inverse


def column_sum(values):
    return jnp.sum(values, axis=0, dtype=F32)


def matmul(left, right):
    return jnp.dot(left, right, preferred_element_type=F32)


def matmul_tn(left, right):
    return lax.dot_general(left, right, (((0,), (0,)), ((), ())), preferred_element_type=F32)


def matmul_nt(left, right):
    return lax.dot_general(left, right, (((1,), (1,)), ((), ())), preferred_element_type=F32)


def dot_nn(left, right):
    return lax.dot_general(left, right, (((1,), (0,)), ((), ())), preferred_element_type=F32)


def dot_nt(left, right):
    return lax.dot_general(left, right, (((1,), (1,)), ((), ())), preferred_element_type=F32)


def dot_tn(left, right):
    return lax.dot_general(left, right, (((0,), (0,)), ((), ())), preferred_element_type=F32)


def attention_forward_kernel(
    x_ref,
    row_ref,
    col_ref,
    wq_ref,
    wk_ref,
    wv_ref,
    wa_ref,
    vec_ref,
    qkv_ref,
    probs_ref,
    attended_ref,
    first_ref,
    low_ref,
    normed_ref,
    inverse_ref,
):
    tokens, width = x_ref.shape
    pair = 2 * HEAD_DIM
    factor = HEAD_DIM ** (-0.5)
    x = x_ref[...]
    qkv_ref[:, :width] = (dot_nn(x, wq_ref[...]) + vec_ref[0:1]).astype(BF)
    qkv_ref[:, width : 2 * width] = dot_nn(x, wk_ref[...]).astype(BF)
    qkv_ref[:, 2 * width :] = (dot_nn(x, wv_ref[...]) + vec_ref[1:2]).astype(BF)
    allowed = row_ref[...] == col_ref[...]
    lower = lax.broadcasted_iota(jnp.int32, (tokens, pair), 1) < HEAD_DIM
    for h in range(width // pair):
        lanes = slice(h * pair, (h + 1) * pair)
        query = qkv_ref[:, lanes]
        keys = qkv_ref[:, width + h * pair : width + (h + 1) * pair]
        values = qkv_ref[:, 2 * width + h * pair : 2 * width + (h + 1) * pair]
        zero = jnp.zeros_like(query)
        outs = []
        for side in range(2):
            mine = jnp.where(lower, query, zero) if side == 0 else jnp.where(lower, zero, query)
            scores = jnp.where(allowed, dot_nt(mine, keys) * factor, MASKED)
            expo = jnp.exp(scores - jnp.max(scores, axis=1, keepdims=True))
            probs = (expo / jnp.sum(expo, axis=1, keepdims=True)).astype(BF)
            probs_ref[2 * h + side] = probs
            outs.append(dot_nn(probs, values))
        attended_ref[:, lanes] = jnp.where(lower, outs[0], outs[1]).astype(BF)
    branch = dot_nn(attended_ref[...], wa_ref[...]) + vec_ref[2:3]
    first, normed, inverse = layer_norm(x.astype(F32) + branch, vec_ref[3:4], vec_ref[4:5])
    first_ref[...] = first
    low_ref[...] = first.astype(BF)
    normed_ref[...] = normed
    inverse_ref[...] = inverse


def weight_spec(width, block):
    return pl.BlockSpec((width, width), lambda m: (0, block))


def attention_forward(x, segments, layer, first_block, vec):
    micro, block = segments.shape
    tokens, width = x.shape
    heads = width // HEAD_DIM
    here = lambda n: pl.BlockSpec((block, n), lambda m: (m, 0))
    return pl.pallas_call(
        attention_forward_kernel,
        grid=(micro,),
        in_specs=[
            here(width),
            pl.BlockSpec((None, 1, block), lambda m: (m, 0, 0)),
            pl.BlockSpec((None, block, 1), lambda m: (m, 0, 0)),
            weight_spec(width, first_block),
            weight_spec(width, first_block + 1),
            weight_spec(width, first_block + 2),
            weight_spec(width, first_block + 3),
            pl.BlockSpec(vec.shape, lambda m: (0, 0)),
        ],
        out_specs=[
            here(3 * width),
            pl.BlockSpec((None, heads, block, block), lambda m: (m, 0, 0, 0)),
            here(width),
            here(width),
            here(width),
            here(width),
            here(1),
        ],
        out_shape=[
            jax.ShapeDtypeStruct((tokens, 3 * width), BF),
            jax.ShapeDtypeStruct((micro, heads, block, block), BF),
            jax.ShapeDtypeStruct((tokens, width), BF),
            jax.ShapeDtypeStruct((tokens, width), F32),
            jax.ShapeDtypeStruct((tokens, width), BF),
            jax.ShapeDtypeStruct((tokens, width), F32),
            jax.ShapeDtypeStruct((tokens, 1), F32),
        ],
        compiler_params=pltpu.CompilerParams(vmem_limit_bytes=48 * 1024 * 1024),
        cost_estimate=pl.CostEstimate(
            flops=1000, bytes_accessed=1000, transcendentals=0
        ),
    )(x, segments[:, None, :], segments[:, :, None], layer, layer, layer, layer, vec)


def attention_backward_kernel(dbranch_ref, qkv_ref, probs_ref, wa_ref, out_ref, sum_ref):
    tokens, width = dbranch_ref.shape
    pair = 2 * HEAD_DIM
    factor = HEAD_DIM ** (-0.5)
    dattended = dot_nt(dbranch_ref[...], wa_ref[...]).astype(BF)
    lower = lax.broadcasted_iota(jnp.int32, (tokens, pair), 1) < HEAD_DIM
    for h in range(width // pair):
        lanes = slice(h * pair, (h + 1) * pair)
        query = qkv_ref[:, lanes]
        keys = qkv_ref[:, width + h * pair : width + (h + 1) * pair]
        values = qkv_ref[:, 2 * width + h * pair : 2 * width + (h + 1) * pair]
        grad = dattended[:, lanes]
        zero = jnp.zeros_like(grad)
        parts = []
        for side in range(2):
            mine = jnp.where(lower, grad, zero) if side == 0 else jnp.where(lower, zero, grad)
            low = probs_ref[2 * h + side]
            probs = low.astype(F32)
            dprobs = dot_nt(mine, values)
            inner = jnp.sum(probs * dprobs, axis=1, keepdims=True)
            dscores = (probs * (dprobs - inner)).astype(BF)
            parts.append(
                (dot_nn(dscores, keys) * factor, dot_tn(dscores, query) * factor, dot_tn(low, grad))
            )
        for i in range(3):
            start = i * width + h * pair
            out_ref[:, start : start + pair] = jnp.where(lower, parts[0][i], parts[1][i]).astype(BF)
    seen = jnp.sum(out_ref[...].astype(F32), axis=0, keepdims=True)

    @pl.when(pl.program_id(0) == 0)
    def _():
        sum_ref[...] = seen

    @pl.when(pl.program_id(0) > 0)
    def _():
        sum_ref[...] += seen


def attention_backward(dbranch, qkv, probs, layer, attn_block):
    micro, heads, block, _ = probs.shape
    tokens, width = dbranch.shape
    here = lambda n: pl.BlockSpec((block, n), lambda m: (m, 0))
    return pl.pallas_call(
        attention_backward_kernel,
        grid=(micro,),
        in_specs=[
            here(width),
            here(3 * width),
            pl.BlockSpec((None, heads, block, block), lambda m: (m, 0, 0, 0)),
            weight_spec(width, attn_block),
        ],
        out_specs=[here(3 * width), pl.BlockSpec((1, 3 * width), lambda m: (0, 0))],
        out_shape=[
            jax.ShapeDtypeStruct((tokens, 3 * width), BF),
            jax.ShapeDtypeStruct((1, 3 * width), F32),
        ],
        compiler_params=pltpu.CompilerParams(vmem_limit_bytes=48 * 1024 * 1024),
        cost_estimate=pl.CostEstimate(
            flops=1000, bytes_accessed=1000, transcendentals=0
        ),
    )(dbranch, qkv, probs, layer)


LIMIT = 56 * 1024 * 1024


def whole_spec(array):
    return pl.BlockSpec(array.shape, lambda *_: (0,) * len(array.shape))


def call(kernel, grid, ins, in_specs, outs, out_specs, scratch, flops, size):
    return pl.pallas_call(
        kernel,
        grid=grid,
        in_specs=in_specs,
        out_specs=out_specs,
        out_shape=[jax.ShapeDtypeStruct(shape, kind) for shape, kind in outs],
        scratch_shapes=scratch,
        compiler_params=pltpu.CompilerParams(vmem_limit_bytes=LIMIT),
        cost_estimate=pl.CostEstimate(flops=flops, bytes_accessed=size, transcendentals=0),
    )(*ins)


def low_three(value):
    high = value.astype(BF).astype(F32)
    middle = (value - high).astype(BF).astype(F32)
    rest = (value - high - middle).astype(BF).astype(F32)
    return [high, middle, rest]


def logits_kernel(
    spread_ref, w_ref, b_ref, column_ref, label_ref, expl_ref, stat_ref, part_ref, flat_ref, logits_ref
):
    step = pl.program_id(0)
    count, width = spread_ref.shape
    peers, high, _ = part_ref.shape
    rows = high - 16
    spread = spread_ref[...]
    entries = w_ref.shape[0]
    chunks = [slice(i, i + entries // 5) for i in range(0, entries, entries // 5)]
    peak = None
    for cut in chunks:
        logits = dot_nt(spread, w_ref[cut, :]) + b_ref[:, cut]
        logits_ref[:, cut] = logits
        most = jnp.max(logits, axis=1, keepdims=True)
        peak = most if peak is None else jnp.maximum(peak, most)
    top = peak
    sums = jnp.zeros((count, 1), F32)
    label = jnp.zeros((count, 1), F32)
    part = jnp.zeros((count, width), F32)
    for cut in chunks:
        expl = jnp.exp(logits_ref[:, cut] - top)
        sums += jnp.sum(expl, axis=1, keepdims=True)
        hit = label_ref[...] == column_ref[:, cut]
        rest = jnp.where(hit, 0.0, expl)
        label += jnp.sum(expl - rest, axis=1, keepdims=True)
        other = rest.astype(BF)
        expl_ref[:, cut] = other
        part += dot_nn(other, w_ref[cut, :])
    part = part.astype(BF)
    for i in range(count // rows):
        part_ref[step * (count // rows) + i, 0:rows, :] = part[i * rows : (i + 1) * rows]
    lane = lax.broadcasted_iota(jnp.int32, (count, 128), 1)
    stat = jnp.where(lane == 0, top, jnp.where(lane == 1, label, 0.0))
    stat_ref[...] = stat
    parts = jnp.zeros((count, 128), F32)
    for i, value in enumerate(low_three(top) + low_three(sums)):
        parts = jnp.where(lane == i, value, parts)
    flat_ref[step] = parts.T[0:8]

    @pl.when(step == pl.num_programs(0) - 1)
    def _():
        told = jnp.concatenate([flat_ref[i] for i in range(flat_ref.shape[0])], axis=1)
        rest = told.shape[1] - width
        last = jnp.concatenate([told[:, width:], jnp.zeros((8, width - rest), F32)], axis=1)
        told = jnp.concatenate([told[:, :width], last], axis=0).astype(BF)
        for i in range(peers):
            part_ref[i, rows:, :] = told


def logits_call(spread, vocab_w, vocab_b, column, labels, rows):
    count, width = spread.shape
    entries = vocab_w.shape[0]
    block = count // 2
    here = lambda n: pl.BlockSpec((block, n), lambda i: (i, 0))
    ins = (spread, vocab_w, vocab_b[None, :], column[None, :], labels)
    specs = [here(width)] + [whole_spec(a) for a in ins[1:4]] + [here(1)]
    part = (count // rows, rows + 16, width)
    return call(
        logits_kernel,
        (2,),
        ins,
        specs,
        [((count, entries), BF), ((count, 128), F32), (part, BF)],
        [here(entries), here(128), pl.BlockSpec(part, lambda i: (0, 0, 0))],
        [pltpu.VMEM((2, 8, block), F32), pltpu.VMEM((block, entries), F32)],
        10_000_000_000,
        20_000_000,
    )


def decoder_kernel(
    expl_ref, spread_ref, column_ref, label_ref, scale_ref, stat_ref, lse_ref, out_ref, sum_ref
):
    count = spread_ref.shape[0]
    lse = jnp.broadcast_to(lse_ref[...], (8, count)).T[:, 0:1]
    share = jnp.exp(stat_ref[:, 0:1] - lse)
    scale = scale_ref[...]
    hit = label_ref[...] == column_ref[...]
    other = (scale * share) * expl_ref[...].astype(F32)
    dlogits = jnp.where(hit, scale * (stat_ref[:, 1:2] * share - 1.0), other).astype(BF)
    out_ref[...] = dot_tn(dlogits, spread_ref[...]).astype(BF)
    sum_ref[...] = jnp.sum(dlogits.astype(F32), axis=0, keepdims=True)


def decoder_call(expl, spread, column, labels, scale, stat, lse):
    count, width = spread.shape
    entries = expl.shape[1]
    block = entries // 5
    ins = (expl, spread, column[None, :], labels, scale, stat, lse)
    return call(
        decoder_kernel,
        (5,),
        ins,
        [
            pl.BlockSpec((count, block), lambda j: (0, j)),
            whole_spec(spread),
            pl.BlockSpec((1, block), lambda j: (0, j)),
        ]
        + [whole_spec(a) for a in ins[3:]],
        [((entries, width), BF), ((1, entries), F32)],
        [
            pl.BlockSpec((block, width), lambda j: (j, 0)),
            pl.BlockSpec((1, block), lambda j: (0, j)),
        ],
        [],
        1000,
        1000,
    )


def merge_kernel(
    own_ref,
    part_ref,
    head_ref,
    label_ref,
    scalar_ref,
    normed3_ref,
    slope3_ref,
    vec_ref,
    picked_ref,
    dense_ref,
    select_ref,
    grad_ref,
    normed2_ref,
    inverse2_ref,
    lse_ref,
    loss_ref,
    g_dense_ref,
    dsecond_ref,
    dffn_ref,
    sums_ref,
):
    peers, high, width = part_ref.shape
    rows = high - 16
    tail = peers * rows - width

    def told(i):
        first = part_ref[:, rows : rows + 8, :].astype(F32)[:, i]
        rest = part_ref[:, rows + 8 :, :].astype(F32)[:, i, :tail]
        return jnp.concatenate([first, rest], axis=1)

    tops = told(0) + told(1) + told(2)
    sums = told(3) + told(4) + told(5)
    top = jnp.max(tops, axis=0, keepdims=True)
    share = jnp.exp(tops - top)
    total_sum = jnp.sum(sums * share, axis=0, keepdims=True)
    lse = top + jnp.log(total_sum)
    share = share / total_sum
    lse_ref[...] = lse
    mine = own_ref[0] + lax.broadcasted_iota(jnp.int32, (rows, peers * rows), 0)
    mine = mine == lax.broadcasted_iota(jnp.int32, (rows, peers * rows), 1)
    own_lse = jnp.sum(jnp.where(mine, lse, 0.0), axis=1, keepdims=True)
    mixed = jnp.zeros((rows, width), F32)
    for i in range(peers):
        weight = jnp.sum(jnp.where(mine, share[i : i + 1], 0.0), axis=1, keepdims=True)
        mixed += weight * part_ref[i, 0:rows, :].astype(F32)
    label = label_ref[...]
    label_logit = jnp.sum(head_ref[...].astype(F32) * label, axis=1, keepdims=True)
    label_logit += scalar_ref[:, 0:1]
    grad = scalar_ref[:, 2:3] * (mixed + (jnp.exp(label_logit - own_lse) - 1.0) * label)
    loss_ref[...] = jnp.zeros(loss_ref.shape, F32) + jnp.sum(
        scalar_ref[:, 1:2] * (own_lse - label_logit)
    )
    normed3 = normed3_ref[...]
    ddense = norm_back(grad, normed3, scalar_ref[:, 3:4], vec_ref[9:10]) * slope3_ref[...]
    low = ddense.astype(BF)
    column = lambda v: jnp.sum(v, axis=0, keepdims=True)
    g_dense_ref[...] = dot_tn(picked_ref[...], low)
    drows = dot_nt(low, dense_ref[...]).astype(BF)
    dout = grad_ref[...].astype(F32) + dot_tn(select_ref[...], drows)
    normed2 = normed2_ref[...]
    dsecond = norm_back(dout, normed2, inverse2_ref[...], vec_ref[6:7])
    dffn = dsecond.astype(BF)
    dsecond_ref[...] = dsecond
    dffn_ref[...] = dffn
    parts = [
        column(low.astype(F32)),
        column(grad * normed3),
        column(grad),
        column(dout * normed2),
        column(dout),
        column(dffn.astype(F32)),
    ]
    for i, value in enumerate(parts):
        sums_ref[i : i + 1] = value


def merge_call(own, *arrays, layer, dense_block):
    part, head = arrays[0], arrays[1]
    width = head.shape[1]
    tokens = arrays[-1].shape[0]
    count = part.shape[0] * (part.shape[1] - 16)
    ins = list(arrays)
    ins.insert(8, layer)
    specs = [whole_spec(a) for a in arrays]
    specs.insert(8, pl.BlockSpec((width, width), lambda *_: (0, dense_block)))
    outs = [
        ((1, count), F32),
        ((8, 128), F32),
        ((width, width), F32),
        ((tokens, width), F32),
        ((tokens, width), BF),
        ((8, width), F32),
    ]
    return call(
        merge_kernel,
        (1,),
        [own] + ins,
        [pl.BlockSpec(memory_space=pltpu.SMEM)] + specs,
        outs,
        [pl.BlockSpec(shape, lambda *_: (0, 0)) for shape, _ in outs],
        [],
        300_000_000,
        10_000_000,
    )


def shrink_kernel(
    core_ref, act_ref, dffn_ref, dense_ref, loss_ref, here_ref, away_ref, grad_ref
):
    width = dffn_ref.shape[1]
    grad_ref[...] = dot_tn(act_ref[...], dffn_ref[...])
    core = core_ref[0]
    spot = lax.broadcasted_iota(jnp.int32, (8, width), 1)
    first = lax.broadcasted_iota(jnp.int32, (8, width), 0) == 0
    told = jnp.zeros((8, width), F32)
    for i, value in enumerate(low_three(loss_ref[0:1, 0:1])):
        told = jnp.where(first & (spot == i + 3 * core), value, told)
    for ref, c in ((here_ref, core), (away_ref, 1 - core)):
        for z in range(NZ):
            tall = pl.ds(pl.multiple_of(c * (width // 2) + z * 96, 8), 96)
            flat = pl.ds(pl.multiple_of(c * 96 + z * 24, 8), 24)
            ref[z, 0:96, :] = grad_ref[tall, :].astype(BF)
            ref[z, 96:128, :] = jnp.concatenate([dense_ref[flat, :], told], axis=0).astype(BF)


def shrink_call(core, act, dffn, g_dense, loss):
    tokens, width = dffn.shape
    out = ((NY * NZ, 128, width), BF)
    half_spec = pl.BlockSpec((NZ, 128, width), lambda y: (y, 0, 0))
    return call(
        shrink_kernel,
        (NY,),
        (core, act, dffn, g_dense, loss),
        [
            pl.BlockSpec(memory_space=pltpu.SMEM),
            pl.BlockSpec((tokens, width), lambda y: (0, y)),
            whole_spec(dffn),
            pl.BlockSpec((width // NY, width), lambda y: (y, 0)),
            whole_spec(loss),
        ],
        [out, out],
        [half_spec, half_spec],
        [pltpu.VMEM((width, width), F32)],
        1000,
        1000,
    )


def put_wide(grad_ref, core, here_ref, away_ref, lanes):
    for ref, c in ((here_ref, core), (away_ref, 1 - core)):
        for y in range(NY):
            rows = pl.ds(pl.multiple_of((NC * y + c) * 96, 8), 96)
            ref[y * NZ : (y + 1) * NZ, :, lanes] = (
                grad_ref[rows, :].reshape(NZ, 24, -1).astype(BF)
            )


def feed_back_kernel(closing, core_ref, *refs):
    dffn_ref, shrink_ref, slope_ref, low_ref, expand_ref, before_ref = refs[:6]
    if closing:
        normed_ref, inverse_ref, vec_ref = refs[6:9]
        here_ref, away_ref, bias_ref, dresidual_ref, dbranch_ref, sums_ref = refs[11:17]
        grad_ref, total_ref = refs[17:]
    else:
        here_ref, away_ref, bias_ref, total_ref, grad_ref = refs[6:]
    step = pl.program_id(0)
    dpre = (dot_nt(dffn_ref[...], shrink_ref[...]) * slope_ref[...].astype(F32)).astype(BF)
    bias_ref[...] = jnp.sum(dpre.astype(F32), axis=0, keepdims=True)
    more = dot_nt(dpre, expand_ref[...])

    @pl.when(step == 0)
    def _():
        total_ref[...] = before_ref[...] + more

    @pl.when(step > 0)
    def _():
        total_ref[...] += more

    grad_ref[...] = dot_tn(low_ref[...], dpre)
    put_wide(grad_ref, core_ref[0], here_ref, away_ref, slice(None))
    if not closing:
        return

    @pl.when(step == pl.num_programs(0) - 1)
    def _():
        dfirst = total_ref[...]
        normed = normed_ref[...]
        dresidual = norm_back(dfirst, normed, inverse_ref[...], vec_ref[3:4])
        dbranch = dresidual.astype(BF)
        dresidual_ref[...] = dresidual
        dbranch_ref[...] = dbranch
        sums_ref[0:1] = jnp.sum(dfirst * normed, axis=0, keepdims=True)
        sums_ref[1:2] = jnp.sum(dfirst, axis=0, keepdims=True)
        sums_ref[2:3] = jnp.sum(dbranch.astype(F32), axis=0, keepdims=True)


def feed_back_call(core, dffn, shrink, slope, low, layer, expand_block, before, rest=None):
    tokens, width = dffn.shape
    wide = slope.shape[1]
    steps = wide // width // 2
    closing = rest is not None
    at = steps if closing else 0
    half = ((NY * NZ, 24, wide), BF)
    half_spec = pl.BlockSpec((NY * NZ, 24, width), lambda j: (0, 0, at + j))
    flat = pl.BlockSpec((tokens, width), lambda j: (0, 0))
    outs = [half, half, ((1, wide // 2), F32), ((tokens, width), F32)]
    out_specs = [half_spec, half_spec, pl.BlockSpec((1, width), lambda j: (0, j)), flat]
    ins = [core, dffn, shrink, slope, low, layer, before]
    in_specs = [
        pl.BlockSpec(memory_space=pltpu.SMEM),
        whole_spec(dffn),
        pl.BlockSpec((width, width), lambda j: (at + j, 0)),
        pl.BlockSpec((tokens, width), lambda j: (0, at + j)),
        whole_spec(low),
        pl.BlockSpec((width, width), lambda j: (0, expand_block + at + j)),
        whole_spec(before),
    ]
    if closing:
        outs += [((tokens, width), BF), ((8, width), F32)]
        out_specs += [flat, pl.BlockSpec((8, width), lambda j: (0, 0))]
        ins += rest
        in_specs += [whole_spec(a) for a in rest[:3]] + [pl.BlockSpec(memory_space=pl.ANY)] * 2
    return pl.pallas_call(
        functools.partial(feed_back_kernel, closing),
        grid=(steps,),
        in_specs=in_specs,
        out_specs=out_specs,
        out_shape=[jax.ShapeDtypeStruct(shape, kind) for shape, kind in outs],
        scratch_shapes=[pltpu.VMEM((width, width), F32)]
        + ([pltpu.VMEM((tokens, width), F32)] if closing else []),
        input_output_aliases={10: 0, 11: 1} if closing else {},
        compiler_params=pltpu.CompilerParams(vmem_limit_bytes=LIMIT),
        cost_estimate=pl.CostEstimate(flops=1000, bytes_accessed=1000, transcendentals=0),
    )(*ins)


def last_kernel(
    core_ref, x_ref, dfused_ref, attended_ref, dbranch_ref, sums_ref, here_ref, away_ref, grad_ref
):
    width = x_ref.shape[1]
    core = core_ref[0]
    for i in range(4):
        lanes = slice(i * width, (i + 1) * width)
        if i < 3:
            grad_ref[i % 2] = dot_tn(x_ref[...], dfused_ref[:, lanes])
        else:
            grad_ref[i % 2] = dot_tn(attended_ref[...], dbranch_ref[...])
        put_wide(grad_ref.at[i % 2], core, here_ref, away_ref, lanes)
    put_wide(sums_ref, core, here_ref, away_ref, slice(4 * width, 4 * width + 128))


def last_call(core, x, dfused, attended, dbranch, sums):
    width = x.shape[1]
    out = ((NY * NZ, 24, 4 * width + 128), BF)
    ins = (x, dfused, attended, dbranch, sums)
    half_spec = pl.BlockSpec(out[0], lambda *_: (0, 0, 0))
    return call(
        last_kernel,
        (1,),
        (core,) + ins,
        [pl.BlockSpec(memory_space=pltpu.SMEM)] + [whole_spec(a) for a in ins],
        [out, out],
        [half_spec, half_spec],
        [pltpu.VMEM((2, width, width), F32)],
        1000,
        1000,
    )


def feed_kernel(
    low_ref,
    expand_ref,
    bias_ref,
    tall_ref,
    first_ref,
    vec_ref,
    select_ref,
    dense_ref,
    act_ref,
    slope_ref,
    shrink_ref,
    settled_ref,
    normed2_ref,
    inverse2_ref,
    picked_ref,
    head_ref,
    spread_ref,
    normed3_ref,
    inverse3_ref,
    slope3_ref,
    total_ref,
    rows_ref,
):
    step = pl.program_id(0)
    width = low_ref.shape[1]
    groups, places, rows, _ = rows_ref.shape
    for k in range(places):
        part = tall_ref[:, k * width : (k + 1) * width].astype(F32)
        rows_ref[:, k] = part.reshape(groups, rows, width)
    shrink = rows_ref[...].reshape(width, width).astype(BF)
    shrink_ref[...] = shrink
    pre = dot_nn(low_ref[...], expand_ref[...]) + bias_ref[...]
    half = 0.5 * (1.0 + lax.erf(pre * HALF_ROOT))
    act = (pre * half).astype(BF)
    act_ref[...] = act
    slope_ref[...] = (half + pre * NORMAL_PEAK * jnp.exp(-0.5 * pre * pre)).astype(BF)
    more = dot_nn(act, shrink)

    @pl.when(step == 0)
    def _():
        total_ref[...] = first_ref[...] + more

    @pl.when(step > 0)
    def _():
        total_ref[...] += more

    @pl.when(step == pl.num_programs(0) - 1)
    def _():
        second = total_ref[...] + vec_ref[5:6]
        settled, normed2, inverse2 = layer_norm(second, vec_ref[6:7], vec_ref[7:8])
        low = settled.astype(BF)
        settled_ref[...] = low
        normed2_ref[...] = normed2
        inverse2_ref[...] = inverse2
        picked = dot_nn(select_ref[...], low).astype(BF)
        picked_ref[...] = picked
        dense = dot_nn(picked, dense_ref[...]) + vec_ref[8:9]
        value, normed3, inverse3 = layer_norm(gelu_value(dense), vec_ref[9:10], vec_ref[10:11])
        head = value.astype(BF)
        head_ref[...] = head
        for i in range(spread_ref.shape[0]):
            spread_ref[i] = head
        normed3_ref[...] = normed3
        inverse3_ref[...] = inverse3
        slope3_ref[...] = gelu_slope(dense)


def feed_call(low, layer, expand_block, dense_block, b_expand, first, vec, select):
    tokens, width = low.shape
    wide = b_expand.shape[0]
    steps = wide // width
    count = select.shape[0]
    places = NY * NC * NZ // steps
    rows = layer.shape[0] // (NY * NC * NZ)
    bias = b_expand[None, :]
    chunk = pl.BlockSpec((tokens, width), lambda j: (0, j))
    outs = [
        ((tokens, wide), BF),
        ((tokens, wide), BF),
        ((wide, width), BF),
        ((tokens, width), BF),
        ((tokens, width), F32),
        ((tokens, 1), F32),
        ((count, width), BF),
        ((count, width), BF),
        ((NY * NZ, count, width), BF),
        ((count, width), F32),
        ((count, 1), F32),
        ((count, width), F32),
    ]
    out_specs = [chunk, chunk, pl.BlockSpec((width, width), lambda j: (j, 0))]
    for shape, _ in outs[3:]:
        out_specs.append(
            pl.BlockSpec(shape, (lambda j: (0, 0)) if len(shape) == 2 else (lambda j: (0, 0, 0)))
        )
    return call(
        feed_kernel,
        (steps,),
        (low, layer, bias, layer, first, vec, select, layer),
        [
            whole_spec(low),
            pl.BlockSpec((width, width), lambda j: (0, expand_block + j)),
            pl.BlockSpec((1, width), lambda j: (0, j)),
            pl.BlockSpec((places * rows, NX * width), lambda j: (j, 0)),
            whole_spec(first),
            whole_spec(vec),
            whole_spec(select),
            pl.BlockSpec((width, width), lambda j: (0, dense_block)),
        ],
        outs,
        out_specs,
        [pltpu.VMEM((tokens, width), F32), pltpu.VMEM((places, NX, rows, width), F32)],
        1000,
        1000,
    )


def body(
    hidden_in,
    out_grad,
    segments,
    mask_pos,
    mask_labels,
    loss_scale,
    w_qkv,
    b_query,
    b_value,
    w_attn,
    b_attn,
    attn_gain,
    attn_shift,
    w_expand,
    b_expand,
    w_shrink,
    b_shrink,
    ffn_gain,
    ffn_shift,
    w_dense,
    b_dense,
    dense_gain,
    dense_shift,
    w_vocab,
    b_vocab,
):
    micro, block, width = hidden_in.shape
    tokens = micro * block
    heads = width // HEAD_DIM
    factor = HEAD_DIM ** (-0.5)
    at = {axis: lax.axis_index(axis) for axis in EVERY}
    core = at["c"].astype(jnp.int32)[None]

    vectors = (
        b_query,
        b_value,
        b_attn,
        attn_gain,
        attn_shift,
        b_shrink,
        ffn_gain,
        ffn_shift,
        b_dense,
        dense_gain,
        dense_shift,
    )
    small = after(jnp.stack(vectors))[0].T
    small = jnp.concatenate([small, b_expand.reshape(w_qkv.shape[0], -1)], axis=1)
    small = jnp.pad(small, ((0, 0), (0, 128 - small.shape[1])))
    fused = jnp.concatenate([w_expand, w_qkv, w_attn, w_dense, small], axis=1)
    fused = gather_x(fused).reshape(-1, fused.shape[1])
    tall = gather_x(w_shrink)
    tall = tall.transpose(1, 0, 2).reshape(fused.shape[0], -1)
    layer = lax.all_gather(
        jnp.concatenate([tall, fused], axis=1), ("y", "c", "z"), axis=0, tiled=True
    )
    own_w = w_vocab.T
    piece_w = [own_w] + [fetch(own_w, "x", k) for k in (1, 2, 3)]
    piece_b = [b_vocab] + [fetch(b_vocab, "x", k) for k in (1, 2, 3)]
    half_w = jnp.stack(piece_w)
    half_b = jnp.stack(piece_b)
    per = own_w.shape[0]
    vocab_w = jnp.concatenate([half_w, fetch(half_w, "c", 1)]).reshape(-1, width)
    vocab_b = jnp.concatenate([half_b, fetch(half_b, "c", 1)]).reshape(-1).astype(F32)
    start = jnp.stack(
        [
            (((at["y"] * NC + (at["c"] + kc) % NC) * NZ + at["z"]) * NX + (at["x"] + kx) % NX)
            * per
            for kc in range(NC)
            for kx in range(NX)
        ]
    )
    column = (start[:, None] + jnp.arange(per, dtype=jnp.int32)[None, :]).reshape(-1)

    flat_labels = mask_labels.reshape(micro, -1)
    counts = jnp.sum((flat_labels >= 0).astype(F32), axis=1)
    norms = 1.0 / (counts * micro)
    slots = mask_labels.shape[-1]
    peers = NZ * NX
    grid = mask_labels.reshape(micro, NY, NC, peers, NZ, NX, slots)
    grid = lax.dynamic_index_in_dim(grid, at["c"], 2, False)
    grid = lax.dynamic_index_in_dim(grid, at["x"], 4, False)
    labels = grid.transpose(1, 3, 0, 2, 4).reshape(-1)
    rows = micro * peers * slots
    row_norm = jnp.broadcast_to(norms[None, :, None], (NY * NZ, micro, peers * slots)).reshape(-1)
    live = (labels >= 0).astype(F32)
    row_weight = live * row_norm
    hit = labels[:, None] == column[None, :]
    scale = loss_scale * row_weight
    own_first = (at["y"] * NZ + at["z"]) * rows
    own_weight = lax.dynamic_slice_in_dim(row_weight, own_first, rows)
    label_w = matmul(hit.astype(BF), vocab_w)
    label_b = jnp.sum(jnp.where(hit, vocab_b, 0.0), axis=1, keepdims=True)
    label_w = jnp.concatenate([label_w, jnp.pad(label_b, ((0, 0), (0, 127)))], axis=1)
    label_w = label_w.astype(BF).reshape(NY * NZ, rows, -1)
    positions = mask_pos.reshape(micro, -1)
    shifted = jnp.where(
        positions >= 0, positions + block * jnp.arange(micro, dtype=jnp.int32)[:, None], -1
    ).reshape(-1)
    select = (shifted[:, None] == jnp.arange(tokens, dtype=jnp.int32)[None, :]).astype(BF)

    scale, labels = scale[:, None], labels[:, None]
    layer, label_w, vocab_w, select, scale, labels = after(
        layer, label_w, vocab_w, select, scale, labels
    )
    label_w = swap(label_w, ("y", "z"))
    ends = [NX * width, w_expand.shape[1], 3 * width, width, width, 128]
    ends = [sum(ends[: i + 1]) for i in range(len(ends))]
    expand_full = layer[:, ends[0] : ends[1]]
    qkv_full = layer[:, ends[1] : ends[2]]
    attn_block = ends[2] // width
    dense_full = layer[:, ends[3] : ends[4]]
    vec_full = layer[:, ends[4] :]
    rows_of = vec_full[:, :16].T.astype(F32)
    (
        b_query,
        b_value,
        b_attn,
        attn_gain,
        attn_shift,
        b_shrink,
        ffn_gain,
        ffn_shift,
        b_dense,
        dense_gain,
        dense_shift,
    ) = (rows_of[i] for i in range(len(vectors)))
    b_expand = vec_full[:, 11:15].astype(F32).reshape(-1)

    x = hidden_in.reshape(tokens, width)
    qkv, probs, attended, first, first_low, normed1, inverse1 = attention_forward(
        x, segments, layer, attn_block - 3, rows_of
    )
    (
        act,
        slope,
        shrink_full,
        settled_low,
        normed2,
        inverse2,
        picked,
        head_out,
        head_sent,
        normed3,
        inverse3,
        slope3,
    ) = feed_call(first_low, layer, 4, attn_block + 1, b_expand, first, rows_of, select)

    head_sent, label_w = after(head_sent, label_w)
    label_w = jnp.sum(label_w.astype(F32), axis=0)
    label_w, label_b = label_w[:, :width], label_w[:, width]
    spread = swap(head_sent, ("y", "z")).reshape(-1, width)
    expl, stat, part = logits_call(spread, vocab_w, vocab_b, column, labels, rows)
    part = swap(part, ("y", "z"))
    scalars = jnp.stack(
        [label_b, own_weight, loss_scale * own_weight, inverse3[:, 0]], axis=1
    )
    lse, loss_own, g_dense, dsecond, dffn, sums_a = merge_call(
        own_first.astype(jnp.int32)[None],
        part,
        head_out,
        label_w,
        jnp.pad(scalars, ((0, 0), (0, 124))),
        normed3,
        slope3,
        rows_of,
        picked,
        select,
        out_grad.reshape(tokens, width),
        normed2,
        inverse2,
        layer=layer,
        dense_block=attn_block + 1,
    )

    tall_pair = shrink_call(core, act, dffn, g_dense, loss_own)
    tall_here, tall_away, dffn = after(*tall_pair, dffn)
    tall_pair = (tall_here, give(tall_away, "c", 1))
    wide_here, wide_away, bias_low, half_first = feed_back_call(
        core, dffn, shrink_full, slope, first_low, layer, 4, dsecond
    )
    half_first, tall_mine = after(half_first, add_cores(tall_pair))
    wide_here, wide_away, bias_high, dresidual, dbranch, sums_b = feed_back_call(
        core,
        dffn,
        shrink_full,
        slope,
        first_low,
        layer,
        4,
        half_first,
        [normed1, inverse1, rows_of, wide_here, wide_away],
    )
    g_expand_bias = jnp.concatenate([bias_low, bias_high], axis=1)
    wide_pair = (wide_here, give(wide_away, "c", 1))
    tall_all = swap(tall_mine, ("y", "z"))
    dfused, fused_sum = attention_backward(dbranch, qkv, probs, layer, attn_block)

    sums = jnp.stack(
        [
            fused_sum[0, :width],
            fused_sum[0, 2 * width :],
            sums_b[2],
            sums_b[0],
            sums_b[1],
            sums_a[5],
            sums_a[3],
            sums_a[4],
            sums_a[0],
            sums_a[1],
            sums_a[2],
        ]
    )
    sums = jnp.concatenate([after(sums)[0].T, g_expand_bias.reshape(width, -1)], axis=1)
    sums = jnp.pad(sums, ((0, 0), (0, 128 - sums.shape[1])))
    last_here, last_away = last_call(core, x, dfused, attended, dbranch, sums)
    last_away, tall_all = after(last_away, tall_all)
    last_pair = (last_here, give(last_away, "c", 1))
    wide_mine, tall_all = after(add_cores(wide_pair), tall_all)
    wide_all = swap(wide_mine, ("y", "z"))
    last_mine, wide_all = after(add_cores(last_pair), wide_all)
    last_all = swap(last_mine, ("y", "z"))

    lse, wide_mine = after(lse, wide_mine)
    grad_w, grad_b = decoder_call(expl, spread, column, labels, scale, stat, lse)
    grad_b = grad_b.reshape(NC, NX, 1, per)
    grad_b = jnp.pad(grad_b, ((0, 0), (0, 0), (0, 7), (0, width - per))).astype(BF)
    grad_w = grad_w.reshape(NC, NX, per, width)
    grad_w, grad_away = (jnp.concatenate([grad_w[i], grad_b[i]], axis=1) for i in range(NC))
    grad_w, grad_away, wide_all = after(grad_w, grad_away, wide_all)
    grad_away, tall_all = after(give(grad_away, "c", 1), tall_all)
    grad_w = add_cores((grad_w, grad_away))
    grad_w = total([grad_w[0]] + [give(grad_w[k], "x", k) for k in (1, 2, 3)])

    tall = jnp.sum(tall_all[:, :120].astype(F32), axis=0).astype(BF)
    loss_row = split_three(jnp.sum(tall_all[:, 120, :6].astype(F32)))[:128]
    tall_low = tall[:96].reshape(NX, 4, 6, width).transpose(0, 2, 1, 3).reshape(NX, 6, 4 * width)
    early = jnp.concatenate(
        [
            tall_low,
            tall[96:].reshape(NX, 6, width),
            jnp.broadcast_to(loss_row, (NX, 6, 128)),
        ],
        axis=2,
    )
    wide = jnp.sum(wide_all.astype(F32), axis=0).astype(BF)
    last_all, grad_w, dfused = after(last_all, grad_w, dfused)
    dinput = dresidual + matmul_nt(dfused, qkv_full)
    g_vocab, g_vocab_bias = grad_w[:per].T, grad_w[per, :per]
    last = jnp.sum(last_all.astype(F32), axis=0).astype(BF)
    last = sum_x(
        jnp.concatenate([early, wide.reshape(NX, 6, -1), last.reshape(NX, 6, -1)], axis=2)
    )
    ends = [4 * width, width, 128, w_expand.shape[1], 3 * width, width, 128]
    ends = [sum(ends[: i + 1]) for i in range(len(ends))]
    g_shrink = last[:, : ends[0]].reshape(6, 4, width).transpose(1, 0, 2).reshape(24, width)
    g_dense = last[:, ends[0] : ends[1]]
    loss = jnp.sum(last[0, ends[1] : ends[1] + 3])
    g_expand = last[:, ends[2] : ends[3]]
    g_qkv = last[:, ends[3] : ends[4]]
    g_attn = last[:, ends[4] : ends[5]]
    sums = last[:, ends[5] :]
    return (
        settled_low.reshape(hidden_in.shape),
        loss,
        dinput.reshape(hidden_in.shape),
        g_qkv,
        sums[:, 0],
        sums[:, 1],
        g_attn,
        sums[:, 2],
        sums[:, 3],
        sums[:, 4],
        g_expand,
        sums[:, 11:15].reshape(-1),
        g_shrink,
        sums[:, 5],
        sums[:, 6],
        sums[:, 7],
        g_dense,
        sums[:, 8],
        sums[:, 9],
        sums[:, 10],
        g_vocab,
        g_vocab_bias,
    )


def solution(mesh):
    split = Mesh(mesh.devices.reshape(NY, NC, NZ, NX), EVERY)
    whole, one = P(), P(EVERY)
    tokens3 = P(None, EVERY, None)
    matrix = P(EVERY, None)
    in_specs = (
        tokens3,
        tokens3,
        P(None, EVERY),
        P(None, EVERY, None, None),
        whole,
        whole,
        matrix,
        one,
        one,
        matrix,
        one,
        one,
        one,
        matrix,
        one,
        matrix,
        one,
        one,
        one,
        matrix,
        one,
        one,
        one,
        P(None, EVERY),
        one,
    )
    out_specs = (
        tokens3,
        whole,
        tokens3,
        matrix,
        one,
        one,
        matrix,
        one,
        one,
        one,
        matrix,
        one,
        matrix,
        one,
        one,
        one,
        matrix,
        one,
        one,
        one,
        P(None, EVERY),
        one,
    )
    return jax.shard_map(body, mesh=split, in_specs=in_specs, out_specs=out_specs, check_vma=False)
```

```python
import functools

import jax
import jax.numpy as jnp
from jax import lax
from jax.experimental import pallas as pl
from jax.experimental.pallas import tpu as pltpu
from jax.sharding import Mesh
from jax.sharding import PartitionSpec as P

HEAD_DIM = 64
EPS = 1e-05
HALF_ROOT = 0.7071067811865476
NORMAL_PEAK = 0.3989422804014327
MASKED = -1e30

BF = jnp.bfloat16
F32 = jnp.float32
NY, NC, NZ, NX = 4, 2, 4, 4
SIZES = {"y": NY, "c": NC, "z": NZ, "x": NX}
EVERY = ("y", "c", "z", "x")


def fetch(array, axis, k):
    n = SIZES[axis]
    return lax.ppermute(array, axis, [((i + k) % n, i) for i in range(n)])


def give(array, axis, k):
    n = SIZES[axis]
    return lax.ppermute(array, axis, [(i, (i + k) % n) for i in range(n)])


def in_order(pieces, index):
    n = len(pieces)
    twice = jnp.stack(pieces + pieces)
    return lax.dynamic_slice_in_dim(twice, (n - index) % n, n, 0)


def gather_x(shard):
    pieces = [shard] + [fetch(shard, "x", k) for k in (1, 2, 3)]
    return in_order(pieces, lax.axis_index("x"))


def swap(array, axes):
    return lax.all_to_all(array, axes, 0, 0, tiled=True)


def blocks(grad):
    return grad.astype(BF).reshape(NY, NC, NZ, -1, grad.shape[1])


def half(grads, core, axis):
    cut = [lax.dynamic_index_in_dim(grad, core, 1, False) for grad in grads]
    cut = [part.reshape((NY * NZ,) + part.shape[2:]) for part in cut]
    return cut[0] if len(cut) == 1 else jnp.concatenate(cut, axis=axis)


def sum_cores(grads, axis):
    core = lax.axis_index("c")
    return half(grads, core, axis), give(half(grads, 1 - core, axis), "c", 1)


def add_cores(pair):
    return (pair[0].astype(F32) + pair[1].astype(F32)).astype(BF)


def sum_yz(mine):
    return jnp.sum(swap(mine, ("y", "z")).astype(F32), axis=0).astype(BF)


def sum_x(mine):
    return jnp.sum(swap(mine, "x").astype(F32), axis=0)


def split_three(value):
    return jnp.pad(jnp.stack(three(value)), (0, 765)).astype(BF)


def after(*arrays):
    return lax.optimization_barrier(arrays)


def total(parts):
    out = parts[0].astype(F32)
    for part in parts[1:]:
        out = out + part.astype(F32)
    return out


def three(value):
    high = lax.reduce_precision(value, 8, 7)
    rest = value - high
    middle = lax.reduce_precision(rest, 8, 7)
    return [high, middle, lax.reduce_precision(rest - middle, 8, 7)]


def gelu_value(values):
    return 0.5 * values * (1.0 + lax.erf(values * HALF_ROOT))


def gelu_slope(values):
    return 0.5 * (1.0 + lax.erf(values * HALF_ROOT)) + values * NORMAL_PEAK * jnp.exp(
        -0.5 * values * values
    )


def layer_norm(values, gain, shift):
    center = values - jnp.mean(values, axis=-1, keepdims=True)
    inverse = lax.rsqrt(jnp.mean(center * center, axis=-1, keepdims=True) + EPS)
    normed = center * inverse
    return (normed * gain + shift, normed, inverse)


def norm_back(grad, normed, inverse, gain):
    scaled = grad * gain
    inner = (
        scaled
        - jnp.mean(scaled, axis=-1, keepdims=True)
        - normed * jnp.mean(scaled * normed, axis=-1, keepdims=True)
    )
    return inner * inverse


def column_sum(values):
    return jnp.sum(values, axis=0, dtype=F32)


def matmul(left, right):
    return jnp.dot(left, right, preferred_element_type=F32)


def matmul_tn(left, right):
    return lax.dot_general(left, right, (((0,), (0,)), ((), ())), preferred_element_type=F32)


def matmul_nt(left, right):
    return lax.dot_general(left, right, (((1,), (1,)), ((), ())), preferred_element_type=F32)


def dot_nn(left, right):
    return lax.dot_general(left, right, (((1,), (0,)), ((), ())), preferred_element_type=F32)


def dot_nt(left, right):
    return lax.dot_general(left, right, (((1,), (1,)), ((), ())), preferred_element_type=F32)


def dot_tn(left, right):
    return lax.dot_general(left, right, (((0,), (0,)), ((), ())), preferred_element_type=F32)


def attention_forward_kernel(
    x_ref,
    row_ref,
    col_ref,
    wq_ref,
    wk_ref,
    wv_ref,
    wa_ref,
    vec_ref,
    qkv_ref,
    probs_ref,
    attended_ref,
    first_ref,
    low_ref,
    normed_ref,
    inverse_ref,
):
    tokens, width = x_ref.shape
    pair = 2 * HEAD_DIM
    factor = HEAD_DIM ** (-0.5)
    x = x_ref[...]
    qkv_ref[:, :width] = (dot_nn(x, wq_ref[...]) + vec_ref[0:1]).astype(BF)
    qkv_ref[:, width : 2 * width] = dot_nn(x, wk_ref[...]).astype(BF)
    qkv_ref[:, 2 * width :] = (dot_nn(x, wv_ref[...]) + vec_ref[1:2]).astype(BF)
    allowed = row_ref[...] == col_ref[...]
    lower = lax.broadcasted_iota(jnp.int32, (tokens, pair), 1) < HEAD_DIM
    for h in range(width // pair):
        lanes = slice(h * pair, (h + 1) * pair)
        query = qkv_ref[:, lanes]
        keys = qkv_ref[:, width + h * pair : width + (h + 1) * pair]
        values = qkv_ref[:, 2 * width + h * pair : 2 * width + (h + 1) * pair]
        zero = jnp.zeros_like(query)
        outs = []
        for side in range(2):
            mine = jnp.where(lower, query, zero) if side == 0 else jnp.where(lower, zero, query)
            scores = jnp.where(allowed, dot_nt(mine, keys) * factor, MASKED)
            expo = jnp.exp(scores - jnp.max(scores, axis=1, keepdims=True))
            probs = (expo / jnp.sum(expo, axis=1, keepdims=True)).astype(BF)
            probs_ref[2 * h + side] = probs
            outs.append(dot_nn(probs, values))
        attended_ref[:, lanes] = jnp.where(lower, outs[0], outs[1]).astype(BF)
    branch = dot_nn(attended_ref[...], wa_ref[...]) + vec_ref[2:3]
    first, normed, inverse = layer_norm(x.astype(F32) + branch, vec_ref[3:4], vec_ref[4:5])
    first_ref[...] = first
    low_ref[...] = first.astype(BF)
    normed_ref[...] = normed
    inverse_ref[...] = inverse


def weight_spec(width, block):
    return pl.BlockSpec((width, width), lambda m: (0, block))


def attention_forward(x, segments, layer, first_block, vec):
    micro, block = segments.shape
    tokens, width = x.shape
    heads = width // HEAD_DIM
    here = lambda n: pl.BlockSpec((block, n), lambda m: (m, 0))
    return pl.pallas_call(
        attention_forward_kernel,
        grid=(micro,),
        in_specs=[
            here(width),
            pl.BlockSpec((None, 1, block), lambda m: (m, 0, 0)),
            pl.BlockSpec((None, block, 1), lambda m: (m, 0, 0)),
            weight_spec(width, first_block),
            weight_spec(width, first_block + 1),
            weight_spec(width, first_block + 2),
            weight_spec(width, first_block + 3),
            pl.BlockSpec(vec.shape, lambda m: (0, 0)),
        ],
        out_specs=[
            here(3 * width),
            pl.BlockSpec((None, heads, block, block), lambda m: (m, 0, 0, 0)),
            here(width),
            here(width),
            here(width),
            here(width),
            here(1),
        ],
        out_shape=[
            jax.ShapeDtypeStruct((tokens, 3 * width), BF),
            jax.ShapeDtypeStruct((micro, heads, block, block), BF),
            jax.ShapeDtypeStruct((tokens, width), BF),
            jax.ShapeDtypeStruct((tokens, width), F32),
            jax.ShapeDtypeStruct((tokens, width), BF),
            jax.ShapeDtypeStruct((tokens, width), F32),
            jax.ShapeDtypeStruct((tokens, 1), F32),
        ],
        compiler_params=pltpu.CompilerParams(vmem_limit_bytes=36 * 1024 * 1024),
        cost_estimate=pl.CostEstimate(
            flops=1000, bytes_accessed=1000, transcendentals=0
        ),
    )(x, segments[:, None, :], segments[:, :, None], layer, layer, layer, layer, vec)


def attention_backward_kernel(dbranch_ref, qkv_ref, probs_ref, wa_ref, out_ref, sum_ref):
    tokens, width = dbranch_ref.shape
    pair = 2 * HEAD_DIM
    factor = HEAD_DIM ** (-0.5)
    dattended = dot_nt(dbranch_ref[...], wa_ref[...]).astype(BF)
    lower = lax.broadcasted_iota(jnp.int32, (tokens, pair), 1) < HEAD_DIM
    for h in range(width // pair):
        lanes = slice(h * pair, (h + 1) * pair)
        query = qkv_ref[:, lanes]
        keys = qkv_ref[:, width + h * pair : width + (h + 1) * pair]
        values = qkv_ref[:, 2 * width + h * pair : 2 * width + (h + 1) * pair]
        grad = dattended[:, lanes]
        zero = jnp.zeros_like(grad)
        parts = []
        for side in range(2):
            mine = jnp.where(lower, grad, zero) if side == 0 else jnp.where(lower, zero, grad)
            low = probs_ref[2 * h + side]
            probs = low.astype(F32)
            dprobs = dot_nt(mine, values)
            inner = jnp.sum(probs * dprobs, axis=1, keepdims=True)
            dscores = (probs * (dprobs - inner)).astype(BF)
            parts.append(
                (dot_nn(dscores, keys) * factor, dot_tn(dscores, query) * factor, dot_tn(low, grad))
            )
        for i in range(3):
            start = i * width + h * pair
            out_ref[:, start : start + pair] = jnp.where(lower, parts[0][i], parts[1][i]).astype(BF)
    seen = jnp.sum(out_ref[...].astype(F32), axis=0, keepdims=True)

    @pl.when(pl.program_id(0) == 0)
    def _():
        sum_ref[...] = seen

    @pl.when(pl.program_id(0) > 0)
    def _():
        sum_ref[...] += seen


def attention_backward(dbranch, qkv, probs, layer, attn_block):
    micro, heads, block, _ = probs.shape
    tokens, width = dbranch.shape
    here = lambda n: pl.BlockSpec((block, n), lambda m: (m, 0))
    return pl.pallas_call(
        attention_backward_kernel,
        grid=(micro,),
        in_specs=[
            here(width),
            here(3 * width),
            pl.BlockSpec((None, heads, block, block), lambda m: (m, 0, 0, 0)),
            weight_spec(width, attn_block),
        ],
        out_specs=[here(3 * width), pl.BlockSpec((1, 3 * width), lambda m: (0, 0))],
        out_shape=[
            jax.ShapeDtypeStruct((tokens, 3 * width), BF),
            jax.ShapeDtypeStruct((1, 3 * width), F32),
        ],
        compiler_params=pltpu.CompilerParams(vmem_limit_bytes=36 * 1024 * 1024),
        cost_estimate=pl.CostEstimate(
            flops=1000, bytes_accessed=1000, transcendentals=0
        ),
    )(dbranch, qkv, probs, layer)


LIMIT = 40 * 1024 * 1024


def whole_spec(array):
    return pl.BlockSpec(array.shape, lambda *_: (0,) * len(array.shape))


def call(kernel, grid, ins, in_specs, outs, out_specs, scratch, flops, size, limit=LIMIT):
    return pl.pallas_call(
        kernel,
        grid=grid,
        in_specs=in_specs,
        out_specs=out_specs,
        out_shape=[jax.ShapeDtypeStruct(shape, kind) for shape, kind in outs],
        scratch_shapes=scratch,
        compiler_params=pltpu.CompilerParams(vmem_limit_bytes=limit),
        cost_estimate=pl.CostEstimate(flops=flops, bytes_accessed=size, transcendentals=0),
    )(*ins)


def low_three(value):
    high = value.astype(BF).astype(F32)
    middle = (value - high).astype(BF).astype(F32)
    rest = (value - high - middle).astype(BF).astype(F32)
    return [high, middle, rest]


def logits_kernel(
    spread_ref, w_ref, b_ref, column_ref, label_ref, expl_ref, stat_ref, part_ref, flat_ref, logits_ref
):
    step = pl.program_id(0)
    count, width = spread_ref.shape
    peers, high, _ = part_ref.shape
    rows = high - 16
    spread = spread_ref[...]
    entries = w_ref.shape[0]
    chunks = [slice(i, i + entries // 5) for i in range(0, entries, entries // 5)]
    peak = None
    for cut in chunks:
        logits = dot_nt(spread, w_ref[cut, :]) + b_ref[:, cut]
        logits_ref[:, cut] = logits
        most = jnp.max(logits, axis=1, keepdims=True)
        peak = most if peak is None else jnp.maximum(peak, most)
    top = peak
    sums = jnp.zeros((count, 1), F32)
    label = jnp.zeros((count, 1), F32)
    part = jnp.zeros((count, width), F32)
    for cut in chunks:
        expl = jnp.exp(logits_ref[:, cut] - top)
        sums += jnp.sum(expl, axis=1, keepdims=True)
        hit = label_ref[...] == column_ref[:, cut]
        rest = jnp.where(hit, 0.0, expl)
        label += jnp.sum(expl - rest, axis=1, keepdims=True)
        other = rest.astype(BF)
        expl_ref[:, cut] = other
        part += dot_nn(other, w_ref[cut, :])
    part = part.astype(BF)
    for i in range(count // rows):
        part_ref[step * (count // rows) + i, 0:rows, :] = part[i * rows : (i + 1) * rows]
    lane = lax.broadcasted_iota(jnp.int32, (count, 128), 1)
    stat = jnp.where(lane == 0, top, jnp.where(lane == 1, label, 0.0))
    stat_ref[...] = stat
    parts = jnp.zeros((count, 128), F32)
    for i, value in enumerate(low_three(top) + low_three(sums)):
        parts = jnp.where(lane == i, value, parts)
    flat_ref[step] = parts.T[0:8]

    @pl.when(step == pl.num_programs(0) - 1)
    def _():
        told = jnp.concatenate([flat_ref[i] for i in range(flat_ref.shape[0])], axis=1)
        rest = told.shape[1] - width
        last = jnp.concatenate([told[:, width:], jnp.zeros((8, width - rest), F32)], axis=1)
        told = jnp.concatenate([told[:, :width], last], axis=0).astype(BF)
        for i in range(peers):
            part_ref[i, rows:, :] = told


def logits_call(spread, vocab_w, vocab_b, column, labels, rows):
    count, width = spread.shape
    entries = vocab_w.shape[0]
    block = count // 2
    here = lambda n: pl.BlockSpec((block, n), lambda i: (i, 0))
    ins = (spread, vocab_w, vocab_b[None, :], column[None, :], labels)
    specs = [here(width)] + [whole_spec(a) for a in ins[1:4]] + [here(1)]
    part = (count // rows, rows + 16, width)
    return call(
        logits_kernel,
        (2,),
        ins,
        specs,
        [((count, entries), BF), ((count, 128), F32), (part, BF)],
        [here(entries), here(128), pl.BlockSpec(part, lambda i: (0, 0, 0))],
        [pltpu.VMEM((2, 8, block), F32), pltpu.VMEM((block, entries), F32)],
        10_000_000_000,
        20_000_000,
        56 * 1024 * 1024,
    )


def decoder_kernel(
    expl_ref, spread_ref, column_ref, label_ref, scale_ref, stat_ref, lse_ref, out_ref, sum_ref
):
    count = spread_ref.shape[0]
    lse = jnp.broadcast_to(lse_ref[...], (8, count)).T[:, 0:1]
    share = jnp.exp(stat_ref[:, 0:1] - lse)
    scale = scale_ref[...]
    hit = label_ref[...] == column_ref[...]
    other = (scale * share) * expl_ref[...].astype(F32)
    dlogits = jnp.where(hit, scale * (stat_ref[:, 1:2] * share - 1.0), other).astype(BF)
    out_ref[...] = dot_tn(dlogits, spread_ref[...]).astype(BF)
    sum_ref[...] = jnp.sum(dlogits.astype(F32), axis=0, keepdims=True)


def decoder_call(expl, spread, column, labels, scale, stat, lse):
    count, width = spread.shape
    entries = expl.shape[1]
    block = entries // 5
    ins = (expl, spread, column[None, :], labels, scale, stat, lse)
    return call(
        decoder_kernel,
        (5,),
        ins,
        [
            pl.BlockSpec((count, block), lambda j: (0, j)),
            whole_spec(spread),
            pl.BlockSpec((1, block), lambda j: (0, j)),
        ]
        + [whole_spec(a) for a in ins[3:]],
        [((entries, width), BF), ((1, entries), F32)],
        [
            pl.BlockSpec((block, width), lambda j: (j, 0)),
            pl.BlockSpec((1, block), lambda j: (0, j)),
        ],
        [],
        1000,
        1000,
    )


def merge_kernel(
    own_ref,
    part_ref,
    head_ref,
    label_ref,
    scalar_ref,
    normed3_ref,
    slope3_ref,
    vec_ref,
    picked_ref,
    dense_ref,
    select_ref,
    grad_ref,
    normed2_ref,
    inverse2_ref,
    lse_ref,
    loss_ref,
    g_dense_ref,
    dsecond_ref,
    dffn_ref,
    sums_ref,
):
    peers, high, width = part_ref.shape
    rows = high - 16
    tail = peers * rows - width

    def told(i):
        first = part_ref[:, rows : rows + 8, :].astype(F32)[:, i]
        rest = part_ref[:, rows + 8 :, :].astype(F32)[:, i, :tail]
        return jnp.concatenate([first, rest], axis=1)

    tops = told(0) + told(1) + told(2)
    sums = told(3) + told(4) + told(5)
    top = jnp.max(tops, axis=0, keepdims=True)
    share = jnp.exp(tops - top)
    total_sum = jnp.sum(sums * share, axis=0, keepdims=True)
    lse = top + jnp.log(total_sum)
    share = share / total_sum
    lse_ref[...] = lse
    mine = own_ref[0] + lax.broadcasted_iota(jnp.int32, (rows, peers * rows), 0)
    mine = mine == lax.broadcasted_iota(jnp.int32, (rows, peers * rows), 1)
    own_lse = jnp.sum(jnp.where(mine, lse, 0.0), axis=1, keepdims=True)
    mixed = jnp.zeros((rows, width), F32)
    for i in range(peers):
        weight = jnp.sum(jnp.where(mine, share[i : i + 1], 0.0), axis=1, keepdims=True)
        mixed += weight * part_ref[i, 0:rows, :].astype(F32)
    label = label_ref[...]
    label_logit = jnp.sum(head_ref[...].astype(F32) * label, axis=1, keepdims=True)
    label_logit += scalar_ref[:, 0:1]
    grad = scalar_ref[:, 2:3] * (mixed + (jnp.exp(label_logit - own_lse) - 1.0) * label)
    loss_ref[...] = jnp.zeros(loss_ref.shape, F32) + jnp.sum(
        scalar_ref[:, 1:2] * (own_lse - label_logit)
    )
    normed3 = normed3_ref[...]
    ddense = norm_back(grad, normed3, scalar_ref[:, 3:4], vec_ref[9:10]) * slope3_ref[...]
    low = ddense.astype(BF)
    column = lambda v: jnp.sum(v, axis=0, keepdims=True)
    g_dense_ref[...] = dot_tn(picked_ref[...], low)
    drows = dot_nt(low, dense_ref[...]).astype(BF)
    dout = grad_ref[...].astype(F32) + dot_tn(select_ref[...], drows)
    normed2 = normed2_ref[...]
    dsecond = norm_back(dout, normed2, inverse2_ref[...], vec_ref[6:7])
    dffn = dsecond.astype(BF)
    dsecond_ref[...] = dsecond
    dffn_ref[...] = dffn
    parts = [
        column(low.astype(F32)),
        column(grad * normed3),
        column(grad),
        column(dout * normed2),
        column(dout),
        column(dffn.astype(F32)),
    ]
    for i, value in enumerate(parts):
        sums_ref[i : i + 1] = value


def merge_call(own, *arrays, layer, dense_block):
    part, head = arrays[0], arrays[1]
    width = head.shape[1]
    tokens = arrays[-1].shape[0]
    count = part.shape[0] * (part.shape[1] - 16)
    ins = list(arrays)
    ins.insert(8, layer)
    specs = [whole_spec(a) for a in arrays]
    specs.insert(8, pl.BlockSpec((width, width), lambda *_: (0, dense_block)))
    outs = [
        ((1, count), F32),
        ((8, 128), F32),
        ((width, width), F32),
        ((tokens, width), F32),
        ((tokens, width), BF),
        ((8, width), F32),
    ]
    return call(
        merge_kernel,
        (1,),
        [own] + ins,
        [pl.BlockSpec(memory_space=pltpu.SMEM)] + specs,
        outs,
        [pl.BlockSpec(shape, lambda *_: (0, 0)) for shape, _ in outs],
        [],
        300_000_000,
        10_000_000,
    )


def shrink_kernel(
    core_ref, act_ref, dffn_ref, dense_ref, loss_ref, here_ref, away_ref, grad_ref
):
    width = dffn_ref.shape[1]
    grad_ref[...] = dot_tn(act_ref[...], dffn_ref[...])
    core = core_ref[0]
    spot = lax.broadcasted_iota(jnp.int32, (8, width), 1)
    first = lax.broadcasted_iota(jnp.int32, (8, width), 0) == 0
    told = jnp.zeros((8, width), F32)
    for i, value in enumerate(low_three(loss_ref[0:1, 0:1])):
        told = jnp.where(first & (spot == i + 3 * core), value, told)
    for ref, c in ((here_ref, core), (away_ref, 1 - core)):
        for z in range(NZ):
            tall = pl.ds(pl.multiple_of(c * (width // 2) + z * 96, 8), 96)
            flat = pl.ds(pl.multiple_of(c * 96 + z * 24, 8), 24)
            ref[z, 0:96, :] = grad_ref[tall, :].astype(BF)
            ref[z, 96:128, :] = jnp.concatenate([dense_ref[flat, :], told], axis=0).astype(BF)


def shrink_call(core, act, dffn, g_dense, loss):
    tokens, width = dffn.shape
    out = ((NY * NZ, 128, width), BF)
    half_spec = pl.BlockSpec((NZ, 128, width), lambda y: (y, 0, 0))
    return call(
        shrink_kernel,
        (NY,),
        (core, act, dffn, g_dense, loss),
        [
            pl.BlockSpec(memory_space=pltpu.SMEM),
            pl.BlockSpec((tokens, width), lambda y: (0, y)),
            whole_spec(dffn),
            pl.BlockSpec((width // NY, width), lambda y: (y, 0)),
            whole_spec(loss),
        ],
        [out, out],
        [half_spec, half_spec],
        [pltpu.VMEM((width, width), F32)],
        1000,
        1000,
    )


def put_wide(grad_ref, core, here_ref, away_ref, lanes):
    for ref, c in ((here_ref, core), (away_ref, 1 - core)):
        for y in range(NY):
            rows = pl.ds(pl.multiple_of((NC * y + c) * 96, 8), 96)
            ref[y * NZ : (y + 1) * NZ, :, lanes] = (
                grad_ref[rows, :].reshape(NZ, 24, -1).astype(BF)
            )


def feed_back_kernel(closing, core_ref, *refs):
    dffn_ref, shrink_ref, slope_ref, low_ref, expand_ref, before_ref = refs[:6]
    if closing:
        normed_ref, inverse_ref, vec_ref = refs[6:9]
        here_ref, away_ref, bias_ref, dresidual_ref, dbranch_ref, sums_ref = refs[11:17]
        grad_ref, total_ref = refs[17:]
    else:
        here_ref, away_ref, bias_ref, total_ref, grad_ref = refs[6:]
    step = pl.program_id(0)
    dpre = (dot_nt(dffn_ref[...], shrink_ref[...]) * slope_ref[...].astype(F32)).astype(BF)
    bias_ref[...] = jnp.sum(dpre.astype(F32), axis=0, keepdims=True)
    more = dot_nt(dpre, expand_ref[...])

    @pl.when(step == 0)
    def _():
        total_ref[...] = before_ref[...] + more

    @pl.when(step > 0)
    def _():
        total_ref[...] += more

    grad_ref[...] = dot_tn(low_ref[...], dpre)
    put_wide(grad_ref, core_ref[0], here_ref, away_ref, slice(None))
    if not closing:
        return

    @pl.when(step == pl.num_programs(0) - 1)
    def _():
        dfirst = total_ref[...]
        normed = normed_ref[...]
        dresidual = norm_back(dfirst, normed, inverse_ref[...], vec_ref[3:4])
        dbranch = dresidual.astype(BF)
        dresidual_ref[...] = dresidual
        dbranch_ref[...] = dbranch
        sums_ref[0:1] = jnp.sum(dfirst * normed, axis=0, keepdims=True)
        sums_ref[1:2] = jnp.sum(dfirst, axis=0, keepdims=True)
        sums_ref[2:3] = jnp.sum(dbranch.astype(F32), axis=0, keepdims=True)


def feed_back_call(core, dffn, shrink, slope, low, layer, expand_block, before, rest=None):
    tokens, width = dffn.shape
    wide = slope.shape[1]
    steps = wide // width // 2
    closing = rest is not None
    at = steps if closing else 0
    half = ((NY * NZ, 24, wide), BF)
    half_spec = pl.BlockSpec((NY * NZ, 24, width), lambda j: (0, 0, at + j))
    flat = pl.BlockSpec((tokens, width), lambda j: (0, 0))
    outs = [half, half, ((1, wide // 2), F32), ((tokens, width), F32)]
    out_specs = [half_spec, half_spec, pl.BlockSpec((1, width), lambda j: (0, j)), flat]
    ins = [core, dffn, shrink, slope, low, layer, before]
    in_specs = [
        pl.BlockSpec(memory_space=pltpu.SMEM),
        whole_spec(dffn),
        pl.BlockSpec((width, width), lambda j: (at + j, 0)),
        pl.BlockSpec((tokens, width), lambda j: (0, at + j)),
        whole_spec(low),
        pl.BlockSpec((width, width), lambda j: (0, expand_block + at + j)),
        whole_spec(before),
    ]
    if closing:
        outs += [((tokens, width), BF), ((8, width), F32)]
        out_specs += [flat, pl.BlockSpec((8, width), lambda j: (0, 0))]
        ins += rest
        in_specs += [whole_spec(a) for a in rest[:3]] + [pl.BlockSpec(memory_space=pl.ANY)] * 2
    return pl.pallas_call(
        functools.partial(feed_back_kernel, closing),
        grid=(steps,),
        in_specs=in_specs,
        out_specs=out_specs,
        out_shape=[jax.ShapeDtypeStruct(shape, kind) for shape, kind in outs],
        scratch_shapes=[pltpu.VMEM((width, width), F32)]
        + ([pltpu.VMEM((tokens, width), F32)] if closing else []),
        input_output_aliases={10: 0, 11: 1} if closing else {},
        compiler_params=pltpu.CompilerParams(vmem_limit_bytes=LIMIT),
        cost_estimate=pl.CostEstimate(flops=1000, bytes_accessed=1000, transcendentals=0),
    )(*ins)


def last_kernel(
    core_ref,
    x_ref,
    dfused_ref,
    attended_ref,
    dbranch_ref,
    fused_ref,
    low_ref,
    high_ref,
    bias_ref,
    here_ref,
    away_ref,
    grad_ref,
    sums_ref,
    flat_ref,
):
    width = x_ref.shape[1]
    core = core_ref[0]
    flat_ref[...] = jnp.zeros(flat_ref.shape, F32)
    rows = [
        fused_ref[:, :width],
        fused_ref[:, 2 * width :],
        high_ref[2:3],
        high_ref[0:1],
        high_ref[1:2],
        low_ref[5:6],
        low_ref[3:4],
        low_ref[4:5],
        low_ref[0:1],
        low_ref[1:2],
        low_ref[2:3],
    ]
    for i, row in enumerate(rows):
        flat_ref[i : i + 1] = row
    sums = flat_ref[...].T
    lane = lax.broadcasted_iota(jnp.int32, sums.shape, 1)
    for i in range(4):
        sums = jnp.where(lane == len(rows) + i, bias_ref[:, i : i + 1], sums)
    sums_ref[...] = sums
    for i in range(4):
        lanes = slice(i * width, (i + 1) * width)
        if i < 3:
            grad_ref[i % 2] = dot_tn(x_ref[...], dfused_ref[:, lanes])
        else:
            grad_ref[i % 2] = dot_tn(attended_ref[...], dbranch_ref[...])
        put_wide(grad_ref.at[i % 2], core, here_ref, away_ref, lanes)
    put_wide(sums_ref, core, here_ref, away_ref, slice(4 * width, 4 * width + 128))


def last_call(core, *ins):
    width = ins[0].shape[1]
    out = ((NY * NZ, 24, 4 * width + 128), BF)
    half_spec = pl.BlockSpec(out[0], lambda *_: (0, 0, 0))
    return call(
        last_kernel,
        (1,),
        (core,) + ins,
        [pl.BlockSpec(memory_space=pltpu.SMEM)] + [whole_spec(a) for a in ins],
        [out, out],
        [half_spec, half_spec],
        [
            pltpu.VMEM((2, width, width), F32),
            pltpu.VMEM((width, 128), F32),
            pltpu.VMEM((128, width), F32),
        ],
        1000,
        1000,
    )


def feed_kernel(
    low_ref,
    expand_ref,
    bias_ref,
    tall_ref,
    first_ref,
    vec_ref,
    select_ref,
    dense_ref,
    act_ref,
    slope_ref,
    shrink_ref,
    settled_ref,
    normed2_ref,
    inverse2_ref,
    picked_ref,
    head_ref,
    spread_ref,
    normed3_ref,
    inverse3_ref,
    slope3_ref,
    total_ref,
    rows_ref,
):
    step = pl.program_id(0)
    width = low_ref.shape[1]
    groups, places, rows, _ = rows_ref.shape
    for k in range(places):
        part = tall_ref[:, k * width : (k + 1) * width].astype(F32)
        rows_ref[:, k] = part.reshape(groups, rows, width)
    shrink = rows_ref[...].reshape(width, width).astype(BF)
    shrink_ref[...] = shrink
    pre = dot_nn(low_ref[...], expand_ref[...]) + bias_ref[...]
    half = 0.5 * (1.0 + lax.erf(pre * HALF_ROOT))
    act = (pre * half).astype(BF)
    act_ref[...] = act
    slope_ref[...] = (half + pre * NORMAL_PEAK * jnp.exp(-0.5 * pre * pre)).astype(BF)
    more = dot_nn(act, shrink)

    @pl.when(step == 0)
    def _():
        total_ref[...] = first_ref[...] + more

    @pl.when(step > 0)
    def _():
        total_ref[...] += more

    @pl.when(step == pl.num_programs(0) - 1)
    def _():
        second = total_ref[...] + vec_ref[5:6]
        settled, normed2, inverse2 = layer_norm(second, vec_ref[6:7], vec_ref[7:8])
        low = settled.astype(BF)
        settled_ref[...] = low
        normed2_ref[...] = normed2
        inverse2_ref[...] = inverse2
        picked = dot_nn(select_ref[...], low).astype(BF)
        picked_ref[...] = picked
        dense = dot_nn(picked, dense_ref[...]) + vec_ref[8:9]
        value, normed3, inverse3 = layer_norm(gelu_value(dense), vec_ref[9:10], vec_ref[10:11])
        head = value.astype(BF)
        head_ref[...] = head
        for i in range(spread_ref.shape[0]):
            spread_ref[i] = head
        normed3_ref[...] = normed3
        inverse3_ref[...] = inverse3
        slope3_ref[...] = gelu_slope(dense)


def feed_call(low, layer, expand_block, dense_block, b_expand, first, vec, select):
    tokens, width = low.shape
    wide = b_expand.shape[0]
    steps = wide // width
    count = select.shape[0]
    places = NY * NC * NZ // steps
    rows = layer.shape[0] // (NY * NC * NZ)
    bias = b_expand[None, :]
    chunk = pl.BlockSpec((tokens, width), lambda j: (0, j))
    outs = [
        ((tokens, wide), BF),
        ((tokens, wide), BF),
        ((wide, width), BF),
        ((tokens, width), BF),
        ((tokens, width), F32),
        ((tokens, 1), F32),
        ((count, width), BF),
        ((count, width), BF),
        ((NY * NZ, count, width), BF),
        ((count, width), F32),
        ((count, 1), F32),
        ((count, width), F32),
    ]
    out_specs = [chunk, chunk, pl.BlockSpec((width, width), lambda j: (j, 0))]
    for shape, _ in outs[3:]:
        out_specs.append(
            pl.BlockSpec(shape, (lambda j: (0, 0)) if len(shape) == 2 else (lambda j: (0, 0, 0)))
        )
    return call(
        feed_kernel,
        (steps,),
        (low, layer, bias, layer, first, vec, select, layer),
        [
            whole_spec(low),
            pl.BlockSpec((width, width), lambda j: (0, expand_block + j)),
            pl.BlockSpec((1, width), lambda j: (0, j)),
            pl.BlockSpec((places * rows, NX * width), lambda j: (j, 0)),
            whole_spec(first),
            whole_spec(vec),
            whole_spec(select),
            pl.BlockSpec((width, width), lambda j: (0, dense_block)),
        ],
        outs,
        out_specs,
        [pltpu.VMEM((tokens, width), F32), pltpu.VMEM((places, NX, rows, width), F32)],
        1000,
        1000,
    )


def body(
    hidden_in,
    out_grad,
    segments,
    mask_pos,
    mask_labels,
    loss_scale,
    w_qkv,
    b_query,
    b_value,
    w_attn,
    b_attn,
    attn_gain,
    attn_shift,
    w_expand,
    b_expand,
    w_shrink,
    b_shrink,
    ffn_gain,
    ffn_shift,
    w_dense,
    b_dense,
    dense_gain,
    dense_shift,
    w_vocab,
    b_vocab,
):
    micro, block, width = hidden_in.shape
    tokens = micro * block
    heads = width // HEAD_DIM
    factor = HEAD_DIM ** (-0.5)
    at = {axis: lax.axis_index(axis) for axis in EVERY}
    core = at["c"].astype(jnp.int32)[None]

    vectors = (
        b_query,
        b_value,
        b_attn,
        attn_gain,
        attn_shift,
        b_shrink,
        ffn_gain,
        ffn_shift,
        b_dense,
        dense_gain,
        dense_shift,
    )
    small = after(jnp.stack(vectors))[0].T
    small = jnp.concatenate([small, b_expand.reshape(w_qkv.shape[0], -1)], axis=1)
    small = jnp.pad(small, ((0, 0), (0, 128 - small.shape[1])))
    fused = jnp.concatenate([w_expand, w_qkv, w_attn, w_dense, small], axis=1)
    fused = gather_x(fused).reshape(-1, fused.shape[1])
    tall = gather_x(w_shrink)
    tall = tall.transpose(1, 0, 2).reshape(fused.shape[0], -1)
    layer = lax.all_gather(
        jnp.concatenate([tall, fused], axis=1), ("y", "c", "z"), axis=0, tiled=True
    )
    own_w = w_vocab.T
    piece_w = [own_w] + [fetch(own_w, "x", k) for k in (1, 2, 3)]
    piece_b = [b_vocab] + [fetch(b_vocab, "x", k) for k in (1, 2, 3)]
    half_w = jnp.stack(piece_w)
    half_b = jnp.stack(piece_b)
    per = own_w.shape[0]
    vocab_w = jnp.concatenate([half_w, fetch(half_w, "c", 1)]).reshape(-1, width)
    vocab_b = jnp.concatenate([half_b, fetch(half_b, "c", 1)]).reshape(-1).astype(F32)
    start = jnp.stack(
        [
            (((at["y"] * NC + (at["c"] + kc) % NC) * NZ + at["z"]) * NX + (at["x"] + kx) % NX)
            * per
            for kc in range(NC)
            for kx in range(NX)
        ]
    )
    column = (start[:, None] + jnp.arange(per, dtype=jnp.int32)[None, :]).reshape(-1)

    flat_labels = mask_labels.reshape(micro, -1)
    counts = jnp.sum((flat_labels >= 0).astype(F32), axis=1)
    norms = 1.0 / (counts * micro)
    slots = mask_labels.shape[-1]
    peers = NZ * NX
    grid = mask_labels.reshape(micro, NY, NC, peers, NZ, NX, slots)
    grid = lax.dynamic_index_in_dim(grid, at["c"], 2, False)
    grid = lax.dynamic_index_in_dim(grid, at["x"], 4, False)
    labels = grid.transpose(1, 3, 0, 2, 4).reshape(-1)
    rows = micro * peers * slots
    row_norm = jnp.broadcast_to(norms[None, :, None], (NY * NZ, micro, peers * slots)).reshape(-1)
    live = (labels >= 0).astype(F32)
    row_weight = live * row_norm
    hit = labels[:, None] == column[None, :]
    scale = loss_scale * row_weight
    own_first = (at["y"] * NZ + at["z"]) * rows
    own_weight = lax.dynamic_slice_in_dim(row_weight, own_first, rows)
    label_w = matmul(hit.astype(BF), vocab_w)
    label_b = jnp.sum(jnp.where(hit, vocab_b, 0.0), axis=1, keepdims=True)
    label_w = jnp.concatenate([label_w, jnp.pad(label_b, ((0, 0), (0, 127)))], axis=1)
    label_w = label_w.astype(BF).reshape(NY * NZ, rows, -1)
    positions = mask_pos.reshape(micro, -1)
    shifted = jnp.where(
        positions >= 0, positions + block * jnp.arange(micro, dtype=jnp.int32)[:, None], -1
    ).reshape(-1)
    select = (shifted[:, None] == jnp.arange(tokens, dtype=jnp.int32)[None, :]).astype(BF)

    scale, labels = scale[:, None], labels[:, None]
    layer, label_w, vocab_w, select, scale, labels = after(
        layer, label_w, vocab_w, select, scale, labels
    )
    label_w = swap(label_w, ("y", "z"))
    ends = [NX * width, w_expand.shape[1], 3 * width, width, width, 128]
    ends = [sum(ends[: i + 1]) for i in range(len(ends))]
    expand_full = layer[:, ends[0] : ends[1]]
    qkv_full = layer[:, ends[1] : ends[2]]
    attn_block = ends[2] // width
    dense_full = layer[:, ends[3] : ends[4]]
    vec_full = layer[:, ends[4] :]
    rows_of = vec_full[:, :16].T.astype(F32)
    (
        b_query,
        b_value,
        b_attn,
        attn_gain,
        attn_shift,
        b_shrink,
        ffn_gain,
        ffn_shift,
        b_dense,
        dense_gain,
        dense_shift,
    ) = (rows_of[i] for i in range(len(vectors)))
    b_expand = vec_full[:, 11:15].astype(F32).reshape(-1)

    x = hidden_in.reshape(tokens, width)
    qkv, probs, attended, first, first_low, normed1, inverse1 = attention_forward(
        x, segments, layer, attn_block - 3, rows_of
    )
    (
        act,
        slope,
        shrink_full,
        settled_low,
        normed2,
        inverse2,
        picked,
        head_out,
        head_sent,
        normed3,
        inverse3,
        slope3,
    ) = feed_call(first_low, layer, 4, attn_block + 1, b_expand, first, rows_of, select)

    head_sent, label_w = after(head_sent, label_w)
    label_w = jnp.sum(label_w.astype(F32), axis=0)
    label_w, label_b = label_w[:, :width], label_w[:, width]
    spread = swap(head_sent, ("y", "z")).reshape(-1, width)
    expl, stat, part = logits_call(spread, vocab_w, vocab_b, column, labels, rows)
    part = swap(part, ("y", "z"))
    scalars = jnp.stack(
        [label_b, own_weight, loss_scale * own_weight, inverse3[:, 0]], axis=1
    )
    lse, loss_own, g_dense, dsecond, dffn, sums_a = merge_call(
        own_first.astype(jnp.int32)[None],
        part,
        head_out,
        label_w,
        jnp.pad(scalars, ((0, 0), (0, 124))),
        normed3,
        slope3,
        rows_of,
        picked,
        select,
        out_grad.reshape(tokens, width),
        normed2,
        inverse2,
        layer=layer,
        dense_block=attn_block + 1,
    )

    tall_pair = shrink_call(core, act, dffn, g_dense, loss_own)
    tall_here, tall_away, dffn = after(*tall_pair, dffn)
    tall_pair = (tall_here, give(tall_away, "c", 1))
    wide_here, wide_away, bias_low, half_first = feed_back_call(
        core, dffn, shrink_full, slope, first_low, layer, 4, dsecond
    )
    half_first, tall_mine = after(half_first, add_cores(tall_pair))
    wide_here, wide_away, bias_high, dresidual, dbranch, sums_b = feed_back_call(
        core,
        dffn,
        shrink_full,
        slope,
        first_low,
        layer,
        4,
        half_first,
        [normed1, inverse1, rows_of, wide_here, wide_away],
    )
    g_expand_bias = jnp.concatenate([bias_low, bias_high], axis=1)
    wide_pair = (wide_here, give(wide_away, "c", 1))
    tall_all = swap(tall_mine, ("y", "z"))
    dfused, fused_sum = attention_backward(dbranch, qkv, probs, layer, attn_block)

    last_here, last_away = last_call(
        core,
        x,
        dfused,
        attended,
        dbranch,
        fused_sum,
        sums_a,
        sums_b,
        g_expand_bias.reshape(width, -1),
    )
    last_away, tall_all = after(last_away, tall_all)
    last_pair = (last_here, give(last_away, "c", 1))
    wide_mine, tall_all = after(add_cores(wide_pair), tall_all)
    wide_all = swap(wide_mine, ("y", "z"))
    last_mine, wide_all = after(add_cores(last_pair), wide_all)
    last_all = swap(last_mine, ("y", "z"))

    lse, wide_mine = after(lse, wide_mine)
    grad_w, grad_b = decoder_call(expl, spread, column, labels, scale, stat, lse)
    grad_b = grad_b.reshape(NC, NX, 1, per)
    grad_b = jnp.pad(grad_b, ((0, 0), (0, 0), (0, 7), (0, width - per))).astype(BF)
    grad_w = grad_w.reshape(NC, NX, per, width)
    grad_w, grad_away = (jnp.concatenate([grad_w[i], grad_b[i]], axis=1) for i in range(NC))
    grad_w, grad_away, wide_all = after(grad_w, grad_away, wide_all)
    grad_away, tall_all = after(give(grad_away, "c", 1), tall_all)
    grad_w = add_cores((grad_w, grad_away))
    grad_w = total([grad_w[0]] + [give(grad_w[k], "x", k) for k in (1, 2, 3)])

    tall = jnp.sum(tall_all[:, :120].astype(F32), axis=0).astype(BF)
    loss_row = split_three(jnp.sum(tall_all[:, 120, :6].astype(F32)))[:128]
    tall_low = tall[:96].reshape(NX, 4, 6, width).transpose(0, 2, 1, 3).reshape(NX, 6, 4 * width)
    early = jnp.concatenate(
        [
            tall_low,
            tall[96:].reshape(NX, 6, width),
            jnp.broadcast_to(loss_row, (NX, 6, 128)),
        ],
        axis=2,
    )
    wide = jnp.sum(wide_all.astype(F32), axis=0).astype(BF)
    last_all, grad_w, dfused = after(last_all, grad_w, dfused)
    dinput = dresidual + matmul_nt(dfused, qkv_full)
    g_vocab, g_vocab_bias = grad_w[:per].T, grad_w[per, :per]
    last = jnp.sum(last_all.astype(F32), axis=0).astype(BF)
    last = sum_x(
        jnp.concatenate([early, wide.reshape(NX, 6, -1), last.reshape(NX, 6, -1)], axis=2)
    )
    ends = [4 * width, width, 128, w_expand.shape[1], 3 * width, width, 128]
    ends = [sum(ends[: i + 1]) for i in range(len(ends))]
    g_shrink = last[:, : ends[0]].reshape(6, 4, width).transpose(1, 0, 2).reshape(24, width)
    g_dense = last[:, ends[0] : ends[1]]
    loss = jnp.sum(last[0, ends[1] : ends[1] + 3])
    g_expand = last[:, ends[2] : ends[3]]
    g_qkv = last[:, ends[3] : ends[4]]
    g_attn = last[:, ends[4] : ends[5]]
    sums = last[:, ends[5] :]
    return (
        settled_low.reshape(hidden_in.shape),
        loss,
        dinput.reshape(hidden_in.shape),
        g_qkv,
        sums[:, 0],
        sums[:, 1],
        g_attn,
        sums[:, 2],
        sums[:, 3],
        sums[:, 4],
        g_expand,
        sums[:, 11:15].reshape(-1),
        g_shrink,
        sums[:, 5],
        sums[:, 6],
        sums[:, 7],
        g_dense,
        sums[:, 8],
        sums[:, 9],
        sums[:, 10],
        g_vocab,
        g_vocab_bias,
    )


def solution(mesh):
    split = Mesh(mesh.devices.reshape(NY, NC, NZ, NX), EVERY)
    whole, one = P(), P(EVERY)
    tokens3 = P(None, EVERY, None)
    matrix = P(EVERY, None)
    in_specs = (
        tokens3,
        tokens3,
        P(None, EVERY),
        P(None, EVERY, None, None),
        whole,
        whole,
        matrix,
        one,
        one,
        matrix,
        one,
        one,
        one,
        matrix,
        one,
        matrix,
        one,
        one,
        one,
        matrix,
        one,
        one,
        one,
        P(None, EVERY),
        one,
    )
    out_specs = (
        tokens3,
        whole,
        tokens3,
        matrix,
        one,
        one,
        matrix,
        one,
        one,
        one,
        matrix,
        one,
        matrix,
        one,
        one,
        one,
        matrix,
        one,
        one,
        one,
        P(None, EVERY),
        one,
    )
    return jax.shard_map(body, mesh=split, in_specs=in_specs, out_specs=out_specs, check_vma=False)
```

```python
import functools

import jax
import jax.numpy as jnp
from jax import lax
from jax.experimental import pallas as pl
from jax.experimental.pallas import tpu as pltpu
from jax.sharding import Mesh
from jax.sharding import PartitionSpec as P

HEAD_DIM = 64
EPS = 1e-05
HALF_ROOT = 0.7071067811865476
NORMAL_PEAK = 0.3989422804014327
MASKED = -1e30

BF = jnp.bfloat16
F32 = jnp.float32
NY, NC, NZ, NX = 4, 2, 4, 4
SIZES = {"y": NY, "c": NC, "z": NZ, "x": NX}
EVERY = ("y", "c", "z", "x")


def fetch(array, axis, k):
    n = SIZES[axis]
    return lax.ppermute(array, axis, [((i + k) % n, i) for i in range(n)])


def give(array, axis, k):
    n = SIZES[axis]
    return lax.ppermute(array, axis, [(i, (i + k) % n) for i in range(n)])


def in_order(pieces, index):
    n = len(pieces)
    twice = jnp.stack(pieces + pieces)
    return lax.dynamic_slice_in_dim(twice, (n - index) % n, n, 0)


def gather_x(shard):
    pieces = [shard] + [fetch(shard, "x", k) for k in (1, 2, 3)]
    return in_order(pieces, lax.axis_index("x"))


def swap(array, axes):
    return lax.all_to_all(array, axes, 0, 0, tiled=True)


def blocks(grad):
    return grad.astype(BF).reshape(NY, NC, NZ, -1, grad.shape[1])


def half(grads, core, axis):
    cut = [lax.dynamic_index_in_dim(grad, core, 1, False) for grad in grads]
    cut = [part.reshape((NY * NZ,) + part.shape[2:]) for part in cut]
    return cut[0] if len(cut) == 1 else jnp.concatenate(cut, axis=axis)


def sum_cores(grads, axis):
    core = lax.axis_index("c")
    return half(grads, core, axis), give(half(grads, 1 - core, axis), "c", 1)


def add_cores(pair):
    return (pair[0].astype(F32) + pair[1].astype(F32)).astype(BF)


def sum_yz(mine):
    return jnp.sum(swap(mine, ("y", "z")).astype(F32), axis=0).astype(BF)


def sum_x(mine):
    return jnp.sum(swap(mine, "x").astype(F32), axis=0)


def split_three(value):
    return jnp.pad(jnp.stack(three(value)), (0, 765)).astype(BF)


def after(*arrays):
    return lax.optimization_barrier(arrays)


def total(parts):
    out = parts[0].astype(F32)
    for part in parts[1:]:
        out = out + part.astype(F32)
    return out


def three(value):
    high = lax.reduce_precision(value, 8, 7)
    rest = value - high
    middle = lax.reduce_precision(rest, 8, 7)
    return [high, middle, lax.reduce_precision(rest - middle, 8, 7)]


def gelu_value(values):
    return 0.5 * values * (1.0 + lax.erf(values * HALF_ROOT))


def gelu_slope(values):
    return 0.5 * (1.0 + lax.erf(values * HALF_ROOT)) + values * NORMAL_PEAK * jnp.exp(
        -0.5 * values * values
    )


def layer_norm(values, gain, shift):
    center = values - jnp.mean(values, axis=-1, keepdims=True)
    inverse = lax.rsqrt(jnp.mean(center * center, axis=-1, keepdims=True) + EPS)
    normed = center * inverse
    return (normed * gain + shift, normed, inverse)


def norm_back(grad, normed, inverse, gain):
    scaled = grad * gain
    inner = (
        scaled
        - jnp.mean(scaled, axis=-1, keepdims=True)
        - normed * jnp.mean(scaled * normed, axis=-1, keepdims=True)
    )
    return inner * inverse


def column_sum(values):
    return jnp.sum(values, axis=0, dtype=F32)


def matmul(left, right):
    return jnp.dot(left, right, preferred_element_type=F32)


def matmul_tn(left, right):
    return lax.dot_general(left, right, (((0,), (0,)), ((), ())), preferred_element_type=F32)


def matmul_nt(left, right):
    return lax.dot_general(left, right, (((1,), (1,)), ((), ())), preferred_element_type=F32)


def dot_nn(left, right):
    return lax.dot_general(left, right, (((1,), (0,)), ((), ())), preferred_element_type=F32)


def dot_nt(left, right):
    return lax.dot_general(left, right, (((1,), (1,)), ((), ())), preferred_element_type=F32)


def dot_tn(left, right):
    return lax.dot_general(left, right, (((0,), (0,)), ((), ())), preferred_element_type=F32)


def attention_forward_kernel(
    x_ref,
    row_ref,
    col_ref,
    wq_ref,
    wk_ref,
    wv_ref,
    wa_ref,
    vec_ref,
    qkv_ref,
    probs_ref,
    attended_ref,
    first_ref,
    low_ref,
    normed_ref,
    inverse_ref,
):
    tokens, width = x_ref.shape
    pair = 2 * HEAD_DIM
    factor = HEAD_DIM ** (-0.5)
    x = x_ref[...]
    qkv_ref[:, :width] = (dot_nn(x, wq_ref[...]) + vec_ref[0:1]).astype(BF)
    qkv_ref[:, width : 2 * width] = dot_nn(x, wk_ref[...]).astype(BF)
    qkv_ref[:, 2 * width :] = (dot_nn(x, wv_ref[...]) + vec_ref[1:2]).astype(BF)
    allowed = row_ref[...] == col_ref[...]
    lower = lax.broadcasted_iota(jnp.int32, (tokens, pair), 1) < HEAD_DIM
    for h in range(width // pair):
        lanes = slice(h * pair, (h + 1) * pair)
        query = qkv_ref[:, lanes]
        keys = qkv_ref[:, width + h * pair : width + (h + 1) * pair]
        values = qkv_ref[:, 2 * width + h * pair : 2 * width + (h + 1) * pair]
        zero = jnp.zeros_like(query)
        outs = []
        for side in range(2):
            mine = jnp.where(lower, query, zero) if side == 0 else jnp.where(lower, zero, query)
            scores = jnp.where(allowed, dot_nt(mine, keys) * factor, MASKED)
            expo = jnp.exp(scores - jnp.max(scores, axis=1, keepdims=True))
            probs = (expo / jnp.sum(expo, axis=1, keepdims=True)).astype(BF)
            probs_ref[2 * h + side] = probs
            outs.append(dot_nn(probs, values))
        attended_ref[:, lanes] = jnp.where(lower, outs[0], outs[1]).astype(BF)
    branch = dot_nn(attended_ref[...], wa_ref[...]) + vec_ref[2:3]
    first, normed, inverse = layer_norm(x.astype(F32) + branch, vec_ref[3:4], vec_ref[4:5])
    first_ref[...] = first
    low_ref[...] = first.astype(BF)
    normed_ref[...] = normed
    inverse_ref[...] = inverse


def weight_spec(width, block):
    return pl.BlockSpec((width, width), lambda m: (0, block))


def attention_forward(x, segments, layer, first_block, vec):
    micro, block = segments.shape
    tokens, width = x.shape
    heads = width // HEAD_DIM
    here = lambda n: pl.BlockSpec((block, n), lambda m: (m, 0))
    return pl.pallas_call(
        attention_forward_kernel,
        grid=(micro,),
        in_specs=[
            here(width),
            pl.BlockSpec((None, 1, block), lambda m: (m, 0, 0)),
            pl.BlockSpec((None, block, 1), lambda m: (m, 0, 0)),
            weight_spec(width, first_block),
            weight_spec(width, first_block + 1),
            weight_spec(width, first_block + 2),
            weight_spec(width, first_block + 3),
            pl.BlockSpec(vec.shape, lambda m: (0, 0)),
        ],
        out_specs=[
            here(3 * width),
            pl.BlockSpec((None, heads, block, block), lambda m: (m, 0, 0, 0)),
            here(width),
            here(width),
            here(width),
            here(width),
            here(1),
        ],
        out_shape=[
            jax.ShapeDtypeStruct((tokens, 3 * width), BF),
            jax.ShapeDtypeStruct((micro, heads, block, block), BF),
            jax.ShapeDtypeStruct((tokens, width), BF),
            jax.ShapeDtypeStruct((tokens, width), F32),
            jax.ShapeDtypeStruct((tokens, width), BF),
            jax.ShapeDtypeStruct((tokens, width), F32),
            jax.ShapeDtypeStruct((tokens, 1), F32),
        ],
        compiler_params=pltpu.CompilerParams(vmem_limit_bytes=60 * 1024 * 1024),
        cost_estimate=pl.CostEstimate(
            flops=1000, bytes_accessed=1000, transcendentals=0
        ),
    )(x, segments[:, None, :], segments[:, :, None], layer, layer, layer, layer, vec)


def attention_backward_kernel(dbranch_ref, qkv_ref, probs_ref, wa_ref, out_ref, sum_ref):
    tokens, width = dbranch_ref.shape
    pair = 2 * HEAD_DIM
    factor = HEAD_DIM ** (-0.5)
    dattended = dot_nt(dbranch_ref[...], wa_ref[...]).astype(BF)
    lower = lax.broadcasted_iota(jnp.int32, (tokens, pair), 1) < HEAD_DIM
    for h in range(width // pair):
        lanes = slice(h * pair, (h + 1) * pair)
        query = qkv_ref[:, lanes]
        keys = qkv_ref[:, width + h * pair : width + (h + 1) * pair]
        values = qkv_ref[:, 2 * width + h * pair : 2 * width + (h + 1) * pair]
        grad = dattended[:, lanes]
        zero = jnp.zeros_like(grad)
        parts = []
        for side in range(2):
            mine = jnp.where(lower, grad, zero) if side == 0 else jnp.where(lower, zero, grad)
            low = probs_ref[2 * h + side]
            probs = low.astype(F32)
            dprobs = dot_nt(mine, values)
            inner = jnp.sum(probs * dprobs, axis=1, keepdims=True)
            dscores = (probs * (dprobs - inner)).astype(BF)
            parts.append(
                (dot_nn(dscores, keys) * factor, dot_tn(dscores, query) * factor, dot_tn(low, grad))
            )
        for i in range(3):
            start = i * width + h * pair
            out_ref[:, start : start + pair] = jnp.where(lower, parts[0][i], parts[1][i]).astype(BF)
    seen = jnp.sum(out_ref[...].astype(F32), axis=0, keepdims=True)

    @pl.when(pl.program_id(0) == 0)
    def _():
        sum_ref[...] = seen

    @pl.when(pl.program_id(0) > 0)
    def _():
        sum_ref[...] += seen


def attention_backward(dbranch, qkv, probs, layer, attn_block):
    micro, heads, block, _ = probs.shape
    tokens, width = dbranch.shape
    here = lambda n: pl.BlockSpec((block, n), lambda m: (m, 0))
    return pl.pallas_call(
        attention_backward_kernel,
        grid=(micro,),
        in_specs=[
            here(width),
            here(3 * width),
            pl.BlockSpec((None, heads, block, block), lambda m: (m, 0, 0, 0)),
            weight_spec(width, attn_block),
        ],
        out_specs=[here(3 * width), pl.BlockSpec((1, 3 * width), lambda m: (0, 0))],
        out_shape=[
            jax.ShapeDtypeStruct((tokens, 3 * width), BF),
            jax.ShapeDtypeStruct((1, 3 * width), F32),
        ],
        compiler_params=pltpu.CompilerParams(vmem_limit_bytes=60 * 1024 * 1024),
        cost_estimate=pl.CostEstimate(
            flops=1000, bytes_accessed=1000, transcendentals=0
        ),
    )(dbranch, qkv, probs, layer)


LIMIT = 56 * 1024 * 1024
SMALL = 56 * 1024 * 1024


def whole_spec(array):
    return pl.BlockSpec(array.shape, lambda *_: (0,) * len(array.shape))


def call(kernel, grid, ins, in_specs, outs, out_specs, scratch, flops, size, limit=LIMIT):
    return pl.pallas_call(
        kernel,
        grid=grid,
        in_specs=in_specs,
        out_specs=out_specs,
        out_shape=[jax.ShapeDtypeStruct(shape, kind) for shape, kind in outs],
        scratch_shapes=scratch,
        compiler_params=pltpu.CompilerParams(vmem_limit_bytes=limit),
        cost_estimate=pl.CostEstimate(flops=flops, bytes_accessed=size, transcendentals=0),
    )(*ins)


def low_three(value):
    high = value.astype(BF).astype(F32)
    middle = (value - high).astype(BF).astype(F32)
    rest = (value - high - middle).astype(BF).astype(F32)
    return [high, middle, rest]


def logits_kernel(
    spread_ref, w_ref, b_ref, column_ref, label_ref, expl_ref, stat_ref, part_ref, flat_ref, logits_ref
):
    step = pl.program_id(0)
    count, width = spread_ref.shape
    peers, high, _ = part_ref.shape
    rows = high - 16
    spread = spread_ref[...]
    entries = w_ref.shape[0]
    chunks = [slice(i, i + entries // 5) for i in range(0, entries, entries // 5)]
    peak = None
    for cut in chunks:
        logits = dot_nt(spread, w_ref[cut, :]) + b_ref[:, cut]
        logits_ref[:, cut] = logits
        most = jnp.max(logits, axis=1, keepdims=True)
        peak = most if peak is None else jnp.maximum(peak, most)
    top = peak
    sums = jnp.zeros((count, 1), F32)
    label = jnp.zeros((count, 1), F32)
    part = jnp.zeros((count, width), F32)
    for cut in chunks:
        expl = jnp.exp(logits_ref[:, cut] - top)
        sums += jnp.sum(expl, axis=1, keepdims=True)
        hit = label_ref[...] == column_ref[:, cut]
        rest = jnp.where(hit, 0.0, expl)
        label += jnp.sum(expl - rest, axis=1, keepdims=True)
        other = rest.astype(BF)
        expl_ref[:, cut] = other
        part += dot_nn(other, w_ref[cut, :])
    part = part.astype(BF)
    for i in range(count // rows):
        part_ref[step * (count // rows) + i, 0:rows, :] = part[i * rows : (i + 1) * rows]
    lane = lax.broadcasted_iota(jnp.int32, (count, 128), 1)
    stat = jnp.where(lane == 0, top, jnp.where(lane == 1, label, 0.0))
    stat_ref[...] = stat
    parts = jnp.zeros((count, 128), F32)
    for i, value in enumerate(low_three(top) + low_three(sums)):
        parts = jnp.where(lane == i, value, parts)
    flat_ref[step] = parts.T[0:8]

    @pl.when(step == pl.num_programs(0) - 1)
    def _():
        told = jnp.concatenate([flat_ref[i] for i in range(flat_ref.shape[0])], axis=1)
        rest = told.shape[1] - width
        last = jnp.concatenate([told[:, width:], jnp.zeros((8, width - rest), F32)], axis=1)
        told = jnp.concatenate([told[:, :width], last], axis=0).astype(BF)
        for i in range(peers):
            part_ref[i, rows:, :] = told


def logits_call(spread, vocab_w, vocab_b, column, labels, rows):
    count, width = spread.shape
    entries = vocab_w.shape[0]
    block = count // 2
    here = lambda n: pl.BlockSpec((block, n), lambda i: (i, 0))
    ins = (spread, vocab_w, vocab_b[None, :], column[None, :], labels)
    specs = [here(width)] + [whole_spec(a) for a in ins[1:4]] + [here(1)]
    part = (count // rows, rows + 16, width)
    return call(
        logits_kernel,
        (2,),
        ins,
        specs,
        [((count, entries), BF), ((count, 128), F32), (part, BF)],
        [here(entries), here(128), pl.BlockSpec(part, lambda i: (0, 0, 0))],
        [pltpu.VMEM((2, 8, block), F32), pltpu.VMEM((block, entries), F32)],
        10_000_000_000,
        20_000_000,
        56 * 1024 * 1024,
    )


def decoder_kernel(
    expl_ref, spread_ref, column_ref, label_ref, scale_ref, stat_ref, lse_ref, out_ref, sum_ref
):
    count = spread_ref.shape[0]
    lse = jnp.broadcast_to(lse_ref[...], (8, count)).T[:, 0:1]
    share = jnp.exp(stat_ref[:, 0:1] - lse)
    scale = scale_ref[...]
    hit = label_ref[...] == column_ref[...]
    other = (scale * share) * expl_ref[...].astype(F32)
    dlogits = jnp.where(hit, scale * (stat_ref[:, 1:2] * share - 1.0), other).astype(BF)
    out_ref[...] = dot_tn(dlogits, spread_ref[...]).astype(BF)
    sum_ref[...] = jnp.sum(dlogits.astype(F32), axis=0, keepdims=True)


def decoder_call(expl, spread, column, labels, scale, stat, lse):
    count, width = spread.shape
    entries = expl.shape[1]
    block = entries // 5
    ins = (expl, spread, column[None, :], labels, scale, stat, lse)
    return call(
        decoder_kernel,
        (5,),
        ins,
        [
            pl.BlockSpec((count, block), lambda j: (0, j)),
            whole_spec(spread),
            pl.BlockSpec((1, block), lambda j: (0, j)),
        ]
        + [whole_spec(a) for a in ins[3:]],
        [((entries, width), BF), ((1, entries), F32)],
        [
            pl.BlockSpec((block, width), lambda j: (j, 0)),
            pl.BlockSpec((1, block), lambda j: (0, j)),
        ],
        [],
        1000,
        1000,
    )


def merge_kernel(
    own_ref,
    part_ref,
    head_ref,
    label_ref,
    scalar_ref,
    normed3_ref,
    slope3_ref,
    vec_ref,
    picked_ref,
    dense_ref,
    select_ref,
    grad_ref,
    normed2_ref,
    inverse2_ref,
    lse_ref,
    loss_ref,
    g_dense_ref,
    dsecond_ref,
    dffn_ref,
    sums_ref,
):
    peers, high, width = part_ref.shape
    rows = high - 16
    tail = peers * rows - width

    def told(i):
        first = part_ref[:, rows : rows + 8, :].astype(F32)[:, i]
        rest = part_ref[:, rows + 8 :, :].astype(F32)[:, i, :tail]
        return jnp.concatenate([first, rest], axis=1)

    tops = told(0) + told(1) + told(2)
    sums = told(3) + told(4) + told(5)
    top = jnp.max(tops, axis=0, keepdims=True)
    share = jnp.exp(tops - top)
    total_sum = jnp.sum(sums * share, axis=0, keepdims=True)
    lse = top + jnp.log(total_sum)
    share = share / total_sum
    lse_ref[...] = lse
    mine = own_ref[0] + lax.broadcasted_iota(jnp.int32, (rows, peers * rows), 0)
    mine = mine == lax.broadcasted_iota(jnp.int32, (rows, peers * rows), 1)
    own_lse = jnp.sum(jnp.where(mine, lse, 0.0), axis=1, keepdims=True)
    mixed = jnp.zeros((rows, width), F32)
    for i in range(peers):
        weight = jnp.sum(jnp.where(mine, share[i : i + 1], 0.0), axis=1, keepdims=True)
        mixed += weight * part_ref[i, 0:rows, :].astype(F32)
    label = label_ref[...]
    label_logit = jnp.sum(head_ref[...].astype(F32) * label, axis=1, keepdims=True)
    label_logit += scalar_ref[:, 0:1]
    grad = scalar_ref[:, 2:3] * (mixed + (jnp.exp(label_logit - own_lse) - 1.0) * label)
    loss_ref[...] = jnp.zeros(loss_ref.shape, F32) + jnp.sum(
        scalar_ref[:, 1:2] * (own_lse - label_logit)
    )
    normed3 = normed3_ref[...]
    ddense = norm_back(grad, normed3, scalar_ref[:, 3:4], vec_ref[9:10]) * slope3_ref[...]
    low = ddense.astype(BF)
    column = lambda v: jnp.sum(v, axis=0, keepdims=True)
    g_dense_ref[...] = dot_tn(picked_ref[...], low)
    drows = dot_nt(low, dense_ref[...]).astype(BF)
    dout = grad_ref[...].astype(F32) + dot_tn(select_ref[...], drows)
    normed2 = normed2_ref[...]
    dsecond = norm_back(dout, normed2, inverse2_ref[...], vec_ref[6:7])
    dffn = dsecond.astype(BF)
    dsecond_ref[...] = dsecond
    dffn_ref[...] = dffn
    parts = [
        column(low.astype(F32)),
        column(grad * normed3),
        column(grad),
        column(dout * normed2),
        column(dout),
        column(dffn.astype(F32)),
    ]
    for i, value in enumerate(parts):
        sums_ref[i : i + 1] = value


def merge_call(own, *arrays, layer, dense_block):
    part, head = arrays[0], arrays[1]
    width = head.shape[1]
    tokens = arrays[-1].shape[0]
    count = part.shape[0] * (part.shape[1] - 16)
    ins = list(arrays)
    ins.insert(8, layer)
    specs = [whole_spec(a) for a in arrays]
    specs.insert(8, pl.BlockSpec((width, width), lambda *_: (0, dense_block)))
    outs = [
        ((1, count), F32),
        ((8, 128), F32),
        ((width, width), F32),
        ((tokens, width), F32),
        ((tokens, width), BF),
        ((8, width), F32),
    ]
    return call(
        merge_kernel,
        (1,),
        [own] + ins,
        [pl.BlockSpec(memory_space=pltpu.SMEM)] + specs,
        outs,
        [pl.BlockSpec(shape, lambda *_: (0, 0)) for shape, _ in outs],
        [],
        300_000_000,
        10_000_000,
    )


def shrink_kernel(
    core_ref, act_ref, dffn_ref, dense_ref, loss_ref, here_ref, away_ref, grad_ref
):
    width = dffn_ref.shape[1]
    grad_ref[...] = dot_tn(act_ref[...], dffn_ref[...])
    core = core_ref[0]
    spot = lax.broadcasted_iota(jnp.int32, (8, width), 1)
    first = lax.broadcasted_iota(jnp.int32, (8, width), 0) == 0
    told = jnp.zeros((8, width), F32)
    for i, value in enumerate(low_three(loss_ref[0:1, 0:1])):
        told = jnp.where(first & (spot == i + 3 * core), value, told)
    for ref, c in ((here_ref, core), (away_ref, 1 - core)):
        for z in range(NZ):
            tall = pl.ds(pl.multiple_of(c * (width // 2) + z * 96, 8), 96)
            flat = pl.ds(pl.multiple_of(c * 96 + z * 24, 8), 24)
            ref[z, 0:96, :] = grad_ref[tall, :].astype(BF)
            ref[z, 96:128, :] = jnp.concatenate([dense_ref[flat, :], told], axis=0).astype(BF)


def shrink_call(core, act, dffn, g_dense, loss):
    tokens, width = dffn.shape
    out = ((NY * NZ, 128, width), BF)
    half_spec = pl.BlockSpec((NZ, 128, width), lambda y: (y, 0, 0))
    return call(
        shrink_kernel,
        (NY,),
        (core, act, dffn, g_dense, loss),
        [
            pl.BlockSpec(memory_space=pltpu.SMEM),
            pl.BlockSpec((tokens, width), lambda y: (0, y)),
            whole_spec(dffn),
            pl.BlockSpec((width // NY, width), lambda y: (y, 0)),
            whole_spec(loss),
        ],
        [out, out],
        [half_spec, half_spec],
        [pltpu.VMEM((width, width), F32)],
        1000,
        1000,
        SMALL,
    )


def put_wide(grad_ref, core, here_ref, away_ref, lanes):
    for ref, c in ((here_ref, core), (away_ref, 1 - core)):
        for y in range(NY):
            rows = pl.ds(pl.multiple_of((NC * y + c) * 96, 8), 96)
            ref[y * NZ : (y + 1) * NZ, :, lanes] = (
                grad_ref[rows, :].reshape(NZ, 24, -1).astype(BF)
            )


def feed_back_kernel(closing, core_ref, *refs):
    dffn_ref, shrink_ref, slope_ref, low_ref, expand_ref, before_ref = refs[:6]
    if closing:
        normed_ref, inverse_ref, vec_ref = refs[6:9]
        here_ref, away_ref, bias_ref, dresidual_ref, dbranch_ref, sums_ref = refs[11:17]
        grad_ref, total_ref = refs[17:]
    else:
        here_ref, away_ref, bias_ref, total_ref, grad_ref = refs[6:]
    step = pl.program_id(0)
    dpre = (dot_nt(dffn_ref[...], shrink_ref[...]) * slope_ref[...].astype(F32)).astype(BF)
    bias_ref[...] = jnp.sum(dpre.astype(F32), axis=0, keepdims=True)
    more = dot_nt(dpre, expand_ref[...])

    @pl.when(step == 0)
    def _():
        total_ref[...] = before_ref[...] + more

    @pl.when(step > 0)
    def _():
        total_ref[...] += more

    grad_ref[...] = dot_tn(low_ref[...], dpre)
    put_wide(grad_ref, core_ref[0], here_ref, away_ref, slice(None))
    if not closing:
        return

    @pl.when(step == pl.num_programs(0) - 1)
    def _():
        dfirst = total_ref[...]
        normed = normed_ref[...]
        dresidual = norm_back(dfirst, normed, inverse_ref[...], vec_ref[3:4])
        dbranch = dresidual.astype(BF)
        dresidual_ref[...] = dresidual
        dbranch_ref[...] = dbranch
        sums_ref[0:1] = jnp.sum(dfirst * normed, axis=0, keepdims=True)
        sums_ref[1:2] = jnp.sum(dfirst, axis=0, keepdims=True)
        sums_ref[2:3] = jnp.sum(dbranch.astype(F32), axis=0, keepdims=True)


def feed_back_call(core, dffn, shrink, slope, low, layer, expand_block, before, rest=None):
    tokens, width = dffn.shape
    wide = slope.shape[1]
    steps = wide // width // 2
    closing = rest is not None
    at = steps if closing else 0
    half = ((NY * NZ, 24, wide), BF)
    half_spec = pl.BlockSpec((NY * NZ, 24, width), lambda j: (0, 0, at + j))
    flat = pl.BlockSpec((tokens, width), lambda j: (0, 0))
    outs = [half, half, ((1, wide // 2), F32), ((tokens, width), F32)]
    out_specs = [half_spec, half_spec, pl.BlockSpec((1, width), lambda j: (0, j)), flat]
    ins = [core, dffn, shrink, slope, low, layer, before]
    in_specs = [
        pl.BlockSpec(memory_space=pltpu.SMEM),
        whole_spec(dffn),
        pl.BlockSpec((width, width), lambda j: (at + j, 0)),
        pl.BlockSpec((tokens, width), lambda j: (0, at + j)),
        whole_spec(low),
        pl.BlockSpec((width, width), lambda j: (0, expand_block + at + j)),
        whole_spec(before),
    ]
    if closing:
        outs += [((tokens, width), BF), ((8, width), F32)]
        out_specs += [flat, pl.BlockSpec((8, width), lambda j: (0, 0))]
        ins += rest
        in_specs += [whole_spec(a) for a in rest[:3]] + [pl.BlockSpec(memory_space=pl.ANY)] * 2
    return pl.pallas_call(
        functools.partial(feed_back_kernel, closing),
        grid=(steps,),
        in_specs=in_specs,
        out_specs=out_specs,
        out_shape=[jax.ShapeDtypeStruct(shape, kind) for shape, kind in outs],
        scratch_shapes=[pltpu.VMEM((width, width), F32)]
        + ([pltpu.VMEM((tokens, width), F32)] if closing else []),
        input_output_aliases={10: 0, 11: 1} if closing else {},
        compiler_params=pltpu.CompilerParams(vmem_limit_bytes=LIMIT),
        cost_estimate=pl.CostEstimate(flops=1000, bytes_accessed=1000, transcendentals=0),
    )(*ins)


def last_kernel(
    core_ref,
    x_ref,
    dfused_ref,
    attended_ref,
    dbranch_ref,
    fused_ref,
    low_ref,
    high_ref,
    bias_ref,
    here_ref,
    away_ref,
    grad_ref,
    sums_ref,
    flat_ref,
):
    width = x_ref.shape[1]
    core = core_ref[0]
    flat_ref[...] = jnp.zeros(flat_ref.shape, F32)
    rows = [
        fused_ref[:, :width],
        fused_ref[:, 2 * width :],
        high_ref[2:3],
        high_ref[0:1],
        high_ref[1:2],
        low_ref[5:6],
        low_ref[3:4],
        low_ref[4:5],
        low_ref[0:1],
        low_ref[1:2],
        low_ref[2:3],
    ]
    for i, row in enumerate(rows):
        flat_ref[i : i + 1] = row
    sums = flat_ref[...].T
    lane = lax.broadcasted_iota(jnp.int32, sums.shape, 1)
    for i in range(4):
        sums = jnp.where(lane == len(rows) + i, bias_ref[:, i : i + 1], sums)
    sums_ref[...] = sums
    for i in range(4):
        lanes = slice(i * width, (i + 1) * width)
        if i < 3:
            grad_ref[i % 2] = dot_tn(x_ref[...], dfused_ref[:, lanes])
        else:
            grad_ref[i % 2] = dot_tn(attended_ref[...], dbranch_ref[...])
        put_wide(grad_ref.at[i % 2], core, here_ref, away_ref, lanes)
    put_wide(sums_ref, core, here_ref, away_ref, slice(4 * width, 4 * width + 128))


def last_call(core, *ins):
    width = ins[0].shape[1]
    out = ((NY * NZ, 24, 4 * width + 128), BF)
    half_spec = pl.BlockSpec(out[0], lambda *_: (0, 0, 0))
    return call(
        last_kernel,
        (1,),
        (core,) + ins,
        [pl.BlockSpec(memory_space=pltpu.SMEM)] + [whole_spec(a) for a in ins],
        [out, out],
        [half_spec, half_spec],
        [
            pltpu.VMEM((2, width, width), F32),
            pltpu.VMEM((width, 128), F32),
            pltpu.VMEM((128, width), F32),
        ],
        1000,
        1000,
    )


def feed_kernel(
    low_ref,
    expand_ref,
    bias_ref,
    tall_ref,
    first_ref,
    vec_ref,
    select_ref,
    dense_ref,
    act_ref,
    slope_ref,
    shrink_ref,
    settled_ref,
    normed2_ref,
    inverse2_ref,
    picked_ref,
    head_ref,
    spread_ref,
    normed3_ref,
    inverse3_ref,
    slope3_ref,
    total_ref,
    rows_ref,
):
    step = pl.program_id(0)
    width = low_ref.shape[1]
    groups, places, rows, _ = rows_ref.shape
    for k in range(places):
        part = tall_ref[:, k * width : (k + 1) * width].astype(F32)
        rows_ref[:, k] = part.reshape(groups, rows, width)
    shrink = rows_ref[...].reshape(width, width).astype(BF)
    shrink_ref[...] = shrink
    pre = dot_nn(low_ref[...], expand_ref[...]) + bias_ref[...]
    half = 0.5 * (1.0 + lax.erf(pre * HALF_ROOT))
    act = (pre * half).astype(BF)
    act_ref[...] = act
    slope_ref[...] = (half + pre * NORMAL_PEAK * jnp.exp(-0.5 * pre * pre)).astype(BF)
    more = dot_nn(act, shrink)

    @pl.when(step == 0)
    def _():
        total_ref[...] = first_ref[...] + more

    @pl.when(step > 0)
    def _():
        total_ref[...] += more

    @pl.when(step == pl.num_programs(0) - 1)
    def _():
        second = total_ref[...] + vec_ref[5:6]
        settled, normed2, inverse2 = layer_norm(second, vec_ref[6:7], vec_ref[7:8])
        low = settled.astype(BF)
        settled_ref[...] = low
        normed2_ref[...] = normed2
        inverse2_ref[...] = inverse2
        picked = dot_nn(select_ref[...], low).astype(BF)
        picked_ref[...] = picked
        dense = dot_nn(picked, dense_ref[...]) + vec_ref[8:9]
        value, normed3, inverse3 = layer_norm(gelu_value(dense), vec_ref[9:10], vec_ref[10:11])
        head = value.astype(BF)
        head_ref[...] = head
        for i in range(spread_ref.shape[0]):
            spread_ref[i] = head
        normed3_ref[...] = normed3
        inverse3_ref[...] = inverse3
        slope3_ref[...] = gelu_slope(dense)


def feed_call(low, layer, expand_block, dense_block, b_expand, first, vec, select):
    tokens, width = low.shape
    wide = b_expand.shape[0]
    steps = wide // width
    count = select.shape[0]
    places = NY * NC * NZ // steps
    rows = layer.shape[0] // (NY * NC * NZ)
    bias = b_expand[None, :]
    chunk = pl.BlockSpec((tokens, width), lambda j: (0, j))
    outs = [
        ((tokens, wide), BF),
        ((tokens, wide), BF),
        ((wide, width), BF),
        ((tokens, width), BF),
        ((tokens, width), F32),
        ((tokens, 1), F32),
        ((count, width), BF),
        ((count, width), BF),
        ((NY * NZ, count, width), BF),
        ((count, width), F32),
        ((count, 1), F32),
        ((count, width), F32),
    ]
    out_specs = [chunk, chunk, pl.BlockSpec((width, width), lambda j: (j, 0))]
    for shape, _ in outs[3:]:
        out_specs.append(
            pl.BlockSpec(shape, (lambda j: (0, 0)) if len(shape) == 2 else (lambda j: (0, 0, 0)))
        )
    return call(
        feed_kernel,
        (steps,),
        (low, layer, bias, layer, first, vec, select, layer),
        [
            whole_spec(low),
            pl.BlockSpec((width, width), lambda j: (0, expand_block + j)),
            pl.BlockSpec((1, width), lambda j: (0, j)),
            pl.BlockSpec((places * rows, NX * width), lambda j: (j, 0)),
            whole_spec(first),
            whole_spec(vec),
            whole_spec(select),
            pl.BlockSpec((width, width), lambda j: (0, dense_block)),
        ],
        outs,
        out_specs,
        [pltpu.VMEM((tokens, width), F32), pltpu.VMEM((places, NX, rows, width), F32)],
        1000,
        1000,
    )


def body(
    hidden_in,
    out_grad,
    segments,
    mask_pos,
    mask_labels,
    loss_scale,
    w_qkv,
    b_query,
    b_value,
    w_attn,
    b_attn,
    attn_gain,
    attn_shift,
    w_expand,
    b_expand,
    w_shrink,
    b_shrink,
    ffn_gain,
    ffn_shift,
    w_dense,
    b_dense,
    dense_gain,
    dense_shift,
    w_vocab,
    b_vocab,
):
    micro, block, width = hidden_in.shape
    tokens = micro * block
    heads = width // HEAD_DIM
    factor = HEAD_DIM ** (-0.5)
    at = {axis: lax.axis_index(axis) for axis in EVERY}
    core = at["c"].astype(jnp.int32)[None]

    vectors = (
        b_query,
        b_value,
        b_attn,
        attn_gain,
        attn_shift,
        b_shrink,
        ffn_gain,
        ffn_shift,
        b_dense,
        dense_gain,
        dense_shift,
    )
    small = after(jnp.stack(vectors))[0].T
    small = jnp.concatenate([small, b_expand.reshape(w_qkv.shape[0], -1)], axis=1)
    small = jnp.pad(small, ((0, 0), (0, 128 - small.shape[1])))
    fused = jnp.concatenate([w_expand, w_qkv, w_attn, w_dense, small], axis=1)
    fused = gather_x(fused).reshape(-1, fused.shape[1])
    tall = gather_x(w_shrink)
    tall = tall.transpose(1, 0, 2).reshape(fused.shape[0], -1)
    layer = lax.all_gather(
        jnp.concatenate([tall, fused], axis=1), ("y", "c", "z"), axis=0, tiled=True
    )
    own_w = w_vocab.T
    piece_w = [own_w] + [fetch(own_w, "x", k) for k in (1, 2, 3)]
    piece_b = [b_vocab] + [fetch(b_vocab, "x", k) for k in (1, 2, 3)]
    half_w = jnp.stack(piece_w)
    half_b = jnp.stack(piece_b)
    per = own_w.shape[0]
    vocab_w = jnp.concatenate([half_w, fetch(half_w, "c", 1)]).reshape(-1, width)
    vocab_b = jnp.concatenate([half_b, fetch(half_b, "c", 1)]).reshape(-1).astype(F32)
    start = jnp.stack(
        [
            (((at["y"] * NC + (at["c"] + kc) % NC) * NZ + at["z"]) * NX + (at["x"] + kx) % NX)
            * per
            for kc in range(NC)
            for kx in range(NX)
        ]
    )
    column = (start[:, None] + jnp.arange(per, dtype=jnp.int32)[None, :]).reshape(-1)

    flat_labels = mask_labels.reshape(micro, -1)
    counts = jnp.sum((flat_labels >= 0).astype(F32), axis=1)
    norms = 1.0 / (counts * micro)
    slots = mask_labels.shape[-1]
    peers = NZ * NX
    grid = mask_labels.reshape(micro, NY, NC, peers, NZ, NX, slots)
    grid = lax.dynamic_index_in_dim(grid, at["c"], 2, False)
    grid = lax.dynamic_index_in_dim(grid, at["x"], 4, False)
    labels = grid.transpose(1, 3, 0, 2, 4).reshape(-1)
    rows = micro * peers * slots
    row_norm = jnp.broadcast_to(norms[None, :, None], (NY * NZ, micro, peers * slots)).reshape(-1)
    live = (labels >= 0).astype(F32)
    row_weight = live * row_norm
    hit = labels[:, None] == column[None, :]
    scale = loss_scale * row_weight
    own_first = (at["y"] * NZ + at["z"]) * rows
    own_weight = lax.dynamic_slice_in_dim(row_weight, own_first, rows)
    label_w = matmul(hit.astype(BF), vocab_w)
    label_b = jnp.sum(jnp.where(hit, vocab_b, 0.0), axis=1, keepdims=True)
    label_w = jnp.concatenate([label_w, jnp.pad(label_b, ((0, 0), (0, 127)))], axis=1)
    label_w = label_w.astype(BF).reshape(NY * NZ, rows, -1)
    positions = mask_pos.reshape(micro, -1)
    shifted = jnp.where(
        positions >= 0, positions + block * jnp.arange(micro, dtype=jnp.int32)[:, None], -1
    ).reshape(-1)
    select = (shifted[:, None] == jnp.arange(tokens, dtype=jnp.int32)[None, :]).astype(BF)

    scale, labels = scale[:, None], labels[:, None]
    layer, label_w, vocab_w, select, scale, labels = after(
        layer, label_w, vocab_w, select, scale, labels
    )
    label_w = swap(label_w, ("y", "z"))
    ends = [NX * width, w_expand.shape[1], 3 * width, width, width, 128]
    ends = [sum(ends[: i + 1]) for i in range(len(ends))]
    expand_full = layer[:, ends[0] : ends[1]]
    qkv_full = layer[:, ends[1] : ends[2]]
    attn_block = ends[2] // width
    dense_full = layer[:, ends[3] : ends[4]]
    vec_full = layer[:, ends[4] :]
    rows_of = vec_full[:, :16].T.astype(F32)
    (
        b_query,
        b_value,
        b_attn,
        attn_gain,
        attn_shift,
        b_shrink,
        ffn_gain,
        ffn_shift,
        b_dense,
        dense_gain,
        dense_shift,
    ) = (rows_of[i] for i in range(len(vectors)))
    b_expand = vec_full[:, 11:15].astype(F32).reshape(-1)

    x = hidden_in.reshape(tokens, width)
    qkv, probs, attended, first, first_low, normed1, inverse1 = attention_forward(
        x, segments, layer, attn_block - 3, rows_of
    )
    (
        act,
        slope,
        shrink_full,
        settled_low,
        normed2,
        inverse2,
        picked,
        head_out,
        head_sent,
        normed3,
        inverse3,
        slope3,
    ) = feed_call(first_low, layer, 4, attn_block + 1, b_expand, first, rows_of, select)

    head_sent, label_w = after(head_sent, label_w)
    label_w = jnp.sum(label_w.astype(F32), axis=0)
    label_w, label_b = label_w[:, :width], label_w[:, width]
    spread = swap(head_sent, ("y", "z")).reshape(-1, width)
    expl, stat, part = logits_call(spread, vocab_w, vocab_b, column, labels, rows)
    part = swap(part, ("y", "z"))
    scalars = jnp.stack(
        [label_b, own_weight, loss_scale * own_weight, inverse3[:, 0]], axis=1
    )
    lse, loss_own, g_dense, dsecond, dffn, sums_a = merge_call(
        own_first.astype(jnp.int32)[None],
        part,
        head_out,
        label_w,
        jnp.pad(scalars, ((0, 0), (0, 124))),
        normed3,
        slope3,
        rows_of,
        picked,
        select,
        out_grad.reshape(tokens, width),
        normed2,
        inverse2,
        layer=layer,
        dense_block=attn_block + 1,
    )

    tall_pair = shrink_call(core, act, dffn, g_dense, loss_own)
    tall_here, tall_away, dffn = after(*tall_pair, dffn)
    tall_pair = (tall_here, give(tall_away, "c", 1))
    wide_here, wide_away, bias_low, half_first = feed_back_call(
        core, dffn, shrink_full, slope, first_low, layer, 4, dsecond
    )
    half_first, tall_mine = after(half_first, add_cores(tall_pair))
    wide_here, wide_away, bias_high, dresidual, dbranch, sums_b = feed_back_call(
        core,
        dffn,
        shrink_full,
        slope,
        first_low,
        layer,
        4,
        half_first,
        [normed1, inverse1, rows_of, wide_here, wide_away],
    )
    g_expand_bias = jnp.concatenate([bias_low, bias_high], axis=1)
    wide_pair = (wide_here, give(wide_away, "c", 1))
    tall_all = swap(tall_mine, ("y", "z"))
    dfused, fused_sum = attention_backward(dbranch, qkv, probs, layer, attn_block)

    last_here, last_away = last_call(
        core,
        x,
        dfused,
        attended,
        dbranch,
        fused_sum,
        sums_a,
        sums_b,
        g_expand_bias.reshape(width, -1),
    )
    last_away, tall_all = after(last_away, tall_all)
    last_pair = (last_here, give(last_away, "c", 1))
    wide_mine, tall_all = after(add_cores(wide_pair), tall_all)
    wide_all = swap(wide_mine, ("y", "z"))
    last_mine, wide_all = after(add_cores(last_pair), wide_all)
    last_all = swap(last_mine, ("y", "z"))

    lse, wide_mine = after(lse, wide_mine)
    grad_w, grad_b = decoder_call(expl, spread, column, labels, scale, stat, lse)
    grad_b = grad_b.reshape(NC, NX, 1, per)
    grad_b = jnp.pad(grad_b, ((0, 0), (0, 0), (0, 7), (0, width - per))).astype(BF)
    grad_w = grad_w.reshape(NC, NX, per, width)
    grad_w, grad_away = (jnp.concatenate([grad_w[i], grad_b[i]], axis=1) for i in range(NC))
    grad_w, grad_away, wide_all = after(grad_w, grad_away, wide_all)
    grad_away, tall_all = after(give(grad_away, "c", 1), tall_all)
    grad_w = add_cores((grad_w, grad_away))
    grad_w = total([grad_w[0]] + [give(grad_w[k], "x", k) for k in (1, 2, 3)])

    tall = jnp.sum(tall_all[:, :120].astype(F32), axis=0).astype(BF)
    loss_row = split_three(jnp.sum(tall_all[:, 120, :6].astype(F32)))[:128]
    tall_low = tall[:96].reshape(NX, 4, 6, width).transpose(0, 2, 1, 3).reshape(NX, 6, 4 * width)
    early = jnp.concatenate(
        [
            tall_low,
            tall[96:].reshape(NX, 6, width),
            jnp.broadcast_to(loss_row, (NX, 6, 128)),
        ],
        axis=2,
    )
    wide = jnp.sum(wide_all.astype(F32), axis=0).astype(BF)
    last_all, grad_w, dfused = after(last_all, grad_w, dfused)
    dinput = dresidual + matmul_nt(dfused, qkv_full)
    g_vocab, g_vocab_bias = grad_w[:per].T, grad_w[per, :per]
    last = jnp.sum(last_all.astype(F32), axis=0).astype(BF)
    last = sum_x(
        jnp.concatenate([early, wide.reshape(NX, 6, -1), last.reshape(NX, 6, -1)], axis=2)
    )
    ends = [4 * width, width, 128, w_expand.shape[1], 3 * width, width, 128]
    ends = [sum(ends[: i + 1]) for i in range(len(ends))]
    g_shrink = last[:, : ends[0]].reshape(6, 4, width).transpose(1, 0, 2).reshape(24, width)
    g_dense = last[:, ends[0] : ends[1]]
    loss = jnp.sum(last[0, ends[1] : ends[1] + 3])
    g_expand = last[:, ends[2] : ends[3]]
    g_qkv = last[:, ends[3] : ends[4]]
    g_attn = last[:, ends[4] : ends[5]]
    sums = last[:, ends[5] :]
    return (
        settled_low.reshape(hidden_in.shape),
        loss,
        dinput.reshape(hidden_in.shape),
        g_qkv,
        sums[:, 0],
        sums[:, 1],
        g_attn,
        sums[:, 2],
        sums[:, 3],
        sums[:, 4],
        g_expand,
        sums[:, 11:15].reshape(-1),
        g_shrink,
        sums[:, 5],
        sums[:, 6],
        sums[:, 7],
        g_dense,
        sums[:, 8],
        sums[:, 9],
        sums[:, 10],
        g_vocab,
        g_vocab_bias,
    )


def solution(mesh):
    split = Mesh(mesh.devices.reshape(NY, NC, NZ, NX), EVERY)
    whole, one = P(), P(EVERY)
    tokens3 = P(None, EVERY, None)
    matrix = P(EVERY, None)
    in_specs = (
        tokens3,
        tokens3,
        P(None, EVERY),
        P(None, EVERY, None, None),
        whole,
        whole,
        matrix,
        one,
        one,
        matrix,
        one,
        one,
        one,
        matrix,
        one,
        matrix,
        one,
        one,
        one,
        matrix,
        one,
        one,
        one,
        P(None, EVERY),
        one,
    )
    out_specs = (
        tokens3,
        whole,
        tokens3,
        matrix,
        one,
        one,
        matrix,
        one,
        one,
        one,
        matrix,
        one,
        matrix,
        one,
        one,
        one,
        matrix,
        one,
        one,
        one,
        P(None, EVERY),
        one,
    )
    return jax.shard_map(body, mesh=split, in_specs=in_specs, out_specs=out_specs, check_vma=False)
```

```python
import functools

import jax
import jax.numpy as jnp
from jax import lax
from jax.experimental import pallas as pl
from jax.experimental.pallas import tpu as pltpu
from jax.sharding import Mesh
from jax.sharding import PartitionSpec as P

HEAD_DIM = 64
EPS = 1e-05
HALF_ROOT = 0.7071067811865476
NORMAL_PEAK = 0.3989422804014327
MASKED = -1e30

BF = jnp.bfloat16
F32 = jnp.float32
NY, NC, NZ, NX = 4, 2, 4, 4
SIZES = {"y": NY, "c": NC, "z": NZ, "x": NX}
EVERY = ("y", "c", "z", "x")


def fetch(array, axis, k):
    n = SIZES[axis]
    return lax.ppermute(array, axis, [((i + k) % n, i) for i in range(n)])


def give(array, axis, k):
    n = SIZES[axis]
    return lax.ppermute(array, axis, [(i, (i + k) % n) for i in range(n)])


def in_order(pieces, index):
    n = len(pieces)
    twice = jnp.stack(pieces + pieces)
    return lax.dynamic_slice_in_dim(twice, (n - index) % n, n, 0)


def gather_x(shard):
    pieces = [shard] + [fetch(shard, "x", k) for k in (1, 2, 3)]
    return in_order(pieces, lax.axis_index("x"))


def swap(array, axes):
    return lax.all_to_all(array, axes, 0, 0, tiled=True)


def blocks(grad):
    return grad.astype(BF).reshape(NY, NC, NZ, -1, grad.shape[1])


def half(grads, core, axis):
    cut = [lax.dynamic_index_in_dim(grad, core, 1, False) for grad in grads]
    cut = [part.reshape((NY * NZ,) + part.shape[2:]) for part in cut]
    return cut[0] if len(cut) == 1 else jnp.concatenate(cut, axis=axis)


def sum_cores(grads, axis):
    core = lax.axis_index("c")
    return half(grads, core, axis), give(half(grads, 1 - core, axis), "c", 1)


def add_cores(pair):
    return (pair[0].astype(F32) + pair[1].astype(F32)).astype(BF)


def sum_yz(mine):
    return jnp.sum(swap(mine, ("y", "z")).astype(F32), axis=0).astype(BF)


def sum_x(mine):
    return jnp.sum(swap(mine, "x").astype(F32), axis=0)


def split_three(value):
    return jnp.pad(jnp.stack(three(value)), (0, 765)).astype(BF)


def after(*arrays):
    return lax.optimization_barrier(arrays)


def total(parts):
    out = parts[0].astype(F32)
    for part in parts[1:]:
        out = out + part.astype(F32)
    return out


def three(value):
    high = lax.reduce_precision(value, 8, 7)
    rest = value - high
    middle = lax.reduce_precision(rest, 8, 7)
    return [high, middle, lax.reduce_precision(rest - middle, 8, 7)]


def gelu_value(values):
    return 0.5 * values * (1.0 + lax.erf(values * HALF_ROOT))


def gelu_slope(values):
    return 0.5 * (1.0 + lax.erf(values * HALF_ROOT)) + values * NORMAL_PEAK * jnp.exp(
        -0.5 * values * values
    )


def layer_norm(values, gain, shift):
    center = values - jnp.mean(values, axis=-1, keepdims=True)
    inverse = lax.rsqrt(jnp.mean(center * center, axis=-1, keepdims=True) + EPS)
    normed = center * inverse
    return (normed * gain + shift, normed, inverse)


def norm_back(grad, normed, inverse, gain):
    scaled = grad * gain
    inner = (
        scaled
        - jnp.mean(scaled, axis=-1, keepdims=True)
        - normed * jnp.mean(scaled * normed, axis=-1, keepdims=True)
    )
    return inner * inverse


def column_sum(values):
    return jnp.sum(values, axis=0, dtype=F32)


def matmul(left, right):
    return jnp.dot(left, right, preferred_element_type=F32)


def matmul_tn(left, right):
    return lax.dot_general(left, right, (((0,), (0,)), ((), ())), preferred_element_type=F32)


def matmul_nt(left, right):
    return lax.dot_general(left, right, (((1,), (1,)), ((), ())), preferred_element_type=F32)


def dot_nn(left, right):
    return lax.dot_general(left, right, (((1,), (0,)), ((), ())), preferred_element_type=F32)


def dot_nt(left, right):
    return lax.dot_general(left, right, (((1,), (1,)), ((), ())), preferred_element_type=F32)


def dot_tn(left, right):
    return lax.dot_general(left, right, (((0,), (0,)), ((), ())), preferred_element_type=F32)


def attention_forward_kernel(
    x_ref,
    row_ref,
    col_ref,
    wq_ref,
    wk_ref,
    wv_ref,
    wa_ref,
    vec_ref,
    qkv_ref,
    probs_ref,
    attended_ref,
    first_ref,
    low_ref,
    normed_ref,
    inverse_ref,
):
    tokens, width = x_ref.shape
    pair = 2 * HEAD_DIM
    factor = HEAD_DIM ** (-0.5)
    x = x_ref[...]
    qkv_ref[:, :width] = (dot_nn(x, wq_ref[...]) + vec_ref[0:1]).astype(BF)
    qkv_ref[:, width : 2 * width] = dot_nn(x, wk_ref[...]).astype(BF)
    qkv_ref[:, 2 * width :] = (dot_nn(x, wv_ref[...]) + vec_ref[1:2]).astype(BF)
    allowed = row_ref[...] == col_ref[...]
    lower = lax.broadcasted_iota(jnp.int32, (tokens, pair), 1) < HEAD_DIM
    for h in range(width // pair):
        lanes = slice(h * pair, (h + 1) * pair)
        query = qkv_ref[:, lanes]
        keys = qkv_ref[:, width + h * pair : width + (h + 1) * pair]
        values = qkv_ref[:, 2 * width + h * pair : 2 * width + (h + 1) * pair]
        zero = jnp.zeros_like(query)
        outs = []
        for side in range(2):
            mine = jnp.where(lower, query, zero) if side == 0 else jnp.where(lower, zero, query)
            scores = jnp.where(allowed, dot_nt(mine, keys) * factor, MASKED)
            expo = jnp.exp(scores - jnp.max(scores, axis=1, keepdims=True))
            probs = (expo / jnp.sum(expo, axis=1, keepdims=True)).astype(BF)
            probs_ref[2 * h + side] = probs
            outs.append(dot_nn(probs, values))
        attended_ref[:, lanes] = jnp.where(lower, outs[0], outs[1]).astype(BF)
    branch = dot_nn(attended_ref[...], wa_ref[...]) + vec_ref[2:3]
    first, normed, inverse = layer_norm(x.astype(F32) + branch, vec_ref[3:4], vec_ref[4:5])
    first_ref[...] = first
    low_ref[...] = first.astype(BF)
    normed_ref[...] = normed
    inverse_ref[...] = inverse


def weight_spec(width, block):
    return pl.BlockSpec((width, width), lambda m: (0, block))


def attention_forward(x, segments, layer, first_block, vec):
    micro, block = segments.shape
    tokens, width = x.shape
    heads = width // HEAD_DIM
    here = lambda n: pl.BlockSpec((block, n), lambda m: (m, 0))
    return pl.pallas_call(
        attention_forward_kernel,
        grid=(micro,),
        in_specs=[
            here(width),
            pl.BlockSpec((None, 1, block), lambda m: (m, 0, 0)),
            pl.BlockSpec((None, block, 1), lambda m: (m, 0, 0)),
            weight_spec(width, first_block),
            weight_spec(width, first_block + 1),
            weight_spec(width, first_block + 2),
            weight_spec(width, first_block + 3),
            pl.BlockSpec(vec.shape, lambda m: (0, 0)),
        ],
        out_specs=[
            here(3 * width),
            pl.BlockSpec((None, heads, block, block), lambda m: (m, 0, 0, 0)),
            here(width),
            here(width),
            here(width),
            here(width),
            here(1),
        ],
        out_shape=[
            jax.ShapeDtypeStruct((tokens, 3 * width), BF),
            jax.ShapeDtypeStruct((micro, heads, block, block), BF),
            jax.ShapeDtypeStruct((tokens, width), BF),
            jax.ShapeDtypeStruct((tokens, width), F32),
            jax.ShapeDtypeStruct((tokens, width), BF),
            jax.ShapeDtypeStruct((tokens, width), F32),
            jax.ShapeDtypeStruct((tokens, 1), F32),
        ],
        compiler_params=pltpu.CompilerParams(vmem_limit_bytes=60 * 1024 * 1024),
        cost_estimate=pl.CostEstimate(
            flops=1000, bytes_accessed=1000, transcendentals=0
        ),
    )(x, segments[:, None, :], segments[:, :, None], layer, layer, layer, layer, vec)


def attention_backward_kernel(dbranch_ref, qkv_ref, probs_ref, wa_ref, out_ref, sum_ref):
    tokens, width = dbranch_ref.shape
    pair = 2 * HEAD_DIM
    factor = HEAD_DIM ** (-0.5)
    dattended = dot_nt(dbranch_ref[...], wa_ref[...]).astype(BF)
    lower = lax.broadcasted_iota(jnp.int32, (tokens, pair), 1) < HEAD_DIM
    for h in range(width // pair):
        lanes = slice(h * pair, (h + 1) * pair)
        query = qkv_ref[:, lanes]
        keys = qkv_ref[:, width + h * pair : width + (h + 1) * pair]
        values = qkv_ref[:, 2 * width + h * pair : 2 * width + (h + 1) * pair]
        grad = dattended[:, lanes]
        zero = jnp.zeros_like(grad)
        parts = []
        for side in range(2):
            mine = jnp.where(lower, grad, zero) if side == 0 else jnp.where(lower, zero, grad)
            low = probs_ref[2 * h + side]
            probs = low.astype(F32)
            dprobs = dot_nt(mine, values)
            inner = jnp.sum(probs * dprobs, axis=1, keepdims=True)
            dscores = (probs * (dprobs - inner)).astype(BF)
            parts.append(
                (dot_nn(dscores, keys) * factor, dot_tn(dscores, query) * factor, dot_tn(low, grad))
            )
        for i in range(3):
            start = i * width + h * pair
            out_ref[:, start : start + pair] = jnp.where(lower, parts[0][i], parts[1][i]).astype(BF)
    seen = jnp.sum(out_ref[...].astype(F32), axis=0, keepdims=True)

    @pl.when(pl.program_id(0) == 0)
    def _():
        sum_ref[...] = seen

    @pl.when(pl.program_id(0) > 0)
    def _():
        sum_ref[...] += seen


def attention_backward(dbranch, qkv, probs, layer, attn_block):
    micro, heads, block, _ = probs.shape
    tokens, width = dbranch.shape
    here = lambda n: pl.BlockSpec((block, n), lambda m: (m, 0))
    return pl.pallas_call(
        attention_backward_kernel,
        grid=(micro,),
        in_specs=[
            here(width),
            here(3 * width),
            pl.BlockSpec((None, heads, block, block), lambda m: (m, 0, 0, 0)),
            weight_spec(width, attn_block),
        ],
        out_specs=[here(3 * width), pl.BlockSpec((1, 3 * width), lambda m: (0, 0))],
        out_shape=[
            jax.ShapeDtypeStruct((tokens, 3 * width), BF),
            jax.ShapeDtypeStruct((1, 3 * width), F32),
        ],
        compiler_params=pltpu.CompilerParams(vmem_limit_bytes=60 * 1024 * 1024),
        cost_estimate=pl.CostEstimate(
            flops=1000, bytes_accessed=1000, transcendentals=0
        ),
    )(dbranch, qkv, probs, layer)


LIMIT = 56 * 1024 * 1024
SMALL = 56 * 1024 * 1024


def whole_spec(array):
    return pl.BlockSpec(array.shape, lambda *_: (0,) * len(array.shape))


def call(kernel, grid, ins, in_specs, outs, out_specs, scratch, flops, size, limit=LIMIT):
    return pl.pallas_call(
        kernel,
        grid=grid,
        in_specs=in_specs,
        out_specs=out_specs,
        out_shape=[jax.ShapeDtypeStruct(shape, kind) for shape, kind in outs],
        scratch_shapes=scratch,
        compiler_params=pltpu.CompilerParams(vmem_limit_bytes=limit),
        cost_estimate=pl.CostEstimate(flops=flops, bytes_accessed=size, transcendentals=0),
    )(*ins)


def low_three(value):
    high = value.astype(BF).astype(F32)
    middle = (value - high).astype(BF).astype(F32)
    rest = (value - high - middle).astype(BF).astype(F32)
    return [high, middle, rest]


def logits_kernel(
    spread_ref, w_ref, b_ref, column_ref, label_ref, expl_ref, stat_ref, part_ref, flat_ref, logits_ref
):
    step = pl.program_id(0)
    count, width = spread_ref.shape
    peers, high, _ = part_ref.shape
    rows = high - 16
    spread = spread_ref[...]
    entries = w_ref.shape[0]
    chunks = [slice(i, i + entries // 5) for i in range(0, entries, entries // 5)]
    peak = None
    for cut in chunks:
        logits = dot_nt(spread, w_ref[cut, :]) + b_ref[:, cut]
        logits_ref[:, cut] = logits
        most = jnp.max(logits, axis=1, keepdims=True)
        peak = most if peak is None else jnp.maximum(peak, most)
    top = peak
    sums = jnp.zeros((count, 1), F32)
    label = jnp.zeros((count, 1), F32)
    part = jnp.zeros((count, width), F32)
    for cut in chunks:
        expl = jnp.exp(logits_ref[:, cut] - top)
        sums += jnp.sum(expl, axis=1, keepdims=True)
        hit = label_ref[...] == column_ref[:, cut]
        rest = jnp.where(hit, 0.0, expl)
        label += jnp.sum(expl - rest, axis=1, keepdims=True)
        other = rest.astype(BF)
        expl_ref[:, cut] = other
        part += dot_nn(other, w_ref[cut, :])
    part = part.astype(BF)
    for i in range(count // rows):
        part_ref[step * (count // rows) + i, 0:rows, :] = part[i * rows : (i + 1) * rows]
    lane = lax.broadcasted_iota(jnp.int32, (count, 128), 1)
    stat = jnp.where(lane == 0, top, jnp.where(lane == 1, label, 0.0))
    stat_ref[...] = stat
    parts = jnp.zeros((count, 128), F32)
    for i, value in enumerate(low_three(top) + low_three(sums)):
        parts = jnp.where(lane == i, value, parts)
    flat_ref[step] = parts.T[0:8]

    @pl.when(step == pl.num_programs(0) - 1)
    def _():
        told = jnp.concatenate([flat_ref[i] for i in range(flat_ref.shape[0])], axis=1)
        rest = told.shape[1] - width
        last = jnp.concatenate([told[:, width:], jnp.zeros((8, width - rest), F32)], axis=1)
        told = jnp.concatenate([told[:, :width], last], axis=0).astype(BF)
        for i in range(peers):
            part_ref[i, rows:, :] = told


def logits_call(spread, vocab_w, vocab_b, column, labels, rows):
    count, width = spread.shape
    entries = vocab_w.shape[0]
    block = count // 2
    here = lambda n: pl.BlockSpec((block, n), lambda i: (i, 0))
    ins = (spread, vocab_w, vocab_b[None, :], column[None, :], labels)
    specs = [here(width)] + [whole_spec(a) for a in ins[1:4]] + [here(1)]
    part = (count // rows, rows + 16, width)
    return call(
        logits_kernel,
        (2,),
        ins,
        specs,
        [((count, entries), BF), ((count, 128), F32), (part, BF)],
        [here(entries), here(128), pl.BlockSpec(part, lambda i: (0, 0, 0))],
        [pltpu.VMEM((2, 8, block), F32), pltpu.VMEM((block, entries), F32)],
        10_000_000_000,
        20_000_000,
        56 * 1024 * 1024,
    )


def decoder_kernel(
    expl_ref, spread_ref, column_ref, label_ref, scale_ref, stat_ref, lse_ref, out_ref, sum_ref
):
    count = spread_ref.shape[0]
    lse = jnp.broadcast_to(lse_ref[...], (8, count)).T[:, 0:1]
    share = jnp.exp(stat_ref[:, 0:1] - lse)
    scale = scale_ref[...]
    hit = label_ref[...] == column_ref[...]
    other = (scale * share) * expl_ref[...].astype(F32)
    dlogits = jnp.where(hit, scale * (stat_ref[:, 1:2] * share - 1.0), other).astype(BF)
    out_ref[...] = dot_tn(dlogits, spread_ref[...]).astype(BF)
    sum_ref[...] = jnp.sum(dlogits.astype(F32), axis=0, keepdims=True)


def decoder_call(expl, spread, column, labels, scale, stat, lse):
    count, width = spread.shape
    entries = expl.shape[1]
    block = entries // 5
    ins = (expl, spread, column[None, :], labels, scale, stat, lse)
    return call(
        decoder_kernel,
        (5,),
        ins,
        [
            pl.BlockSpec((count, block), lambda j: (0, j)),
            whole_spec(spread),
            pl.BlockSpec((1, block), lambda j: (0, j)),
        ]
        + [whole_spec(a) for a in ins[3:]],
        [((entries, width), BF), ((1, entries), F32)],
        [
            pl.BlockSpec((block, width), lambda j: (j, 0)),
            pl.BlockSpec((1, block), lambda j: (0, j)),
        ],
        [],
        1000,
        1000,
    )


def merge_kernel(
    own_ref,
    part_ref,
    head_ref,
    label_ref,
    scalar_ref,
    normed3_ref,
    slope3_ref,
    vec_ref,
    picked_ref,
    dense_ref,
    select_ref,
    grad_ref,
    normed2_ref,
    inverse2_ref,
    lse_ref,
    loss_ref,
    g_dense_ref,
    dsecond_ref,
    dffn_ref,
    sums_ref,
):
    peers, high, width = part_ref.shape
    rows = high - 16
    tail = peers * rows - width

    def told(i):
        first = part_ref[:, rows : rows + 8, :].astype(F32)[:, i]
        rest = part_ref[:, rows + 8 :, :].astype(F32)[:, i, :tail]
        return jnp.concatenate([first, rest], axis=1)

    tops = told(0) + told(1) + told(2)
    sums = told(3) + told(4) + told(5)
    top = jnp.max(tops, axis=0, keepdims=True)
    share = jnp.exp(tops - top)
    total_sum = jnp.sum(sums * share, axis=0, keepdims=True)
    lse = top + jnp.log(total_sum)
    share = share / total_sum
    lse_ref[...] = lse
    mine = own_ref[0] + lax.broadcasted_iota(jnp.int32, (rows, peers * rows), 0)
    mine = mine == lax.broadcasted_iota(jnp.int32, (rows, peers * rows), 1)
    own_lse = jnp.sum(jnp.where(mine, lse, 0.0), axis=1, keepdims=True)
    mixed = jnp.zeros((rows, width), F32)
    for i in range(peers):
        weight = jnp.sum(jnp.where(mine, share[i : i + 1], 0.0), axis=1, keepdims=True)
        mixed += weight * part_ref[i, 0:rows, :].astype(F32)
    label = label_ref[...]
    label_logit = jnp.sum(head_ref[...].astype(F32) * label, axis=1, keepdims=True)
    label_logit += scalar_ref[:, 0:1]
    grad = scalar_ref[:, 2:3] * (mixed + (jnp.exp(label_logit - own_lse) - 1.0) * label)
    loss_ref[...] = jnp.zeros(loss_ref.shape, F32) + jnp.sum(
        scalar_ref[:, 1:2] * (own_lse - label_logit)
    )
    normed3 = normed3_ref[...]
    ddense = norm_back(grad, normed3, scalar_ref[:, 3:4], vec_ref[9:10]) * slope3_ref[...]
    low = ddense.astype(BF)
    column = lambda v: jnp.sum(v, axis=0, keepdims=True)
    g_dense_ref[...] = dot_tn(picked_ref[...], low)
    drows = dot_nt(low, dense_ref[...]).astype(BF)
    dout = grad_ref[...].astype(F32) + dot_tn(select_ref[...], drows)
    normed2 = normed2_ref[...]
    dsecond = norm_back(dout, normed2, inverse2_ref[...], vec_ref[6:7])
    dffn = dsecond.astype(BF)
    dsecond_ref[...] = dsecond
    dffn_ref[...] = dffn
    parts = [
        column(low.astype(F32)),
        column(grad * normed3),
        column(grad),
        column(dout * normed2),
        column(dout),
        column(dffn.astype(F32)),
    ]
    for i, value in enumerate(parts):
        sums_ref[i : i + 1] = value


def merge_call(own, *arrays, layer, dense_block):
    part, head = arrays[0], arrays[1]
    width = head.shape[1]
    tokens = arrays[-1].shape[0]
    count = part.shape[0] * (part.shape[1] - 16)
    ins = list(arrays)
    ins.insert(8, layer)
    specs = [whole_spec(a) for a in arrays]
    specs.insert(8, pl.BlockSpec((width, width), lambda *_: (0, dense_block)))
    outs = [
        ((1, count), F32),
        ((8, 128), F32),
        ((width, width), F32),
        ((tokens, width), F32),
        ((tokens, width), BF),
        ((8, width), F32),
    ]
    return call(
        merge_kernel,
        (1,),
        [own] + ins,
        [pl.BlockSpec(memory_space=pltpu.SMEM)] + specs,
        outs,
        [pl.BlockSpec(shape, lambda *_: (0, 0)) for shape, _ in outs],
        [],
        300_000_000,
        10_000_000,
    )


def shrink_kernel(
    core_ref, act_ref, dffn_ref, dense_ref, loss_ref, here_ref, away_ref, grad_ref
):
    width = dffn_ref.shape[1]
    grad_ref[...] = dot_tn(act_ref[...], dffn_ref[...])
    core = core_ref[0]
    spot = lax.broadcasted_iota(jnp.int32, (8, width), 1)
    first = lax.broadcasted_iota(jnp.int32, (8, width), 0) == 0
    told = jnp.zeros((8, width), F32)
    for i, value in enumerate(low_three(loss_ref[0:1, 0:1])):
        told = jnp.where(first & (spot == i + 3 * core), value, told)
    for ref, c in ((here_ref, core), (away_ref, 1 - core)):
        for z in range(NZ):
            tall = pl.ds(pl.multiple_of(c * (width // 2) + z * 96, 8), 96)
            flat = pl.ds(pl.multiple_of(c * 96 + z * 24, 8), 24)
            ref[z, 0:96, :] = grad_ref[tall, :].astype(BF)
            ref[z, 96:128, :] = jnp.concatenate([dense_ref[flat, :], told], axis=0).astype(BF)


def shrink_call(core, act, dffn, g_dense, loss):
    tokens, width = dffn.shape
    out = ((NY * NZ, 128, width), BF)
    half_spec = pl.BlockSpec((NZ, 128, width), lambda y: (y, 0, 0))
    return call(
        shrink_kernel,
        (NY,),
        (core, act, dffn, g_dense, loss),
        [
            pl.BlockSpec(memory_space=pltpu.SMEM),
            pl.BlockSpec((tokens, width), lambda y: (0, y)),
            whole_spec(dffn),
            pl.BlockSpec((width // NY, width), lambda y: (y, 0)),
            whole_spec(loss),
        ],
        [out, out],
        [half_spec, half_spec],
        [pltpu.VMEM((width, width), F32)],
        1000,
        1000,
        SMALL,
    )


def put_wide(grad_ref, core, here_ref, away_ref, lanes):
    for ref, c in ((here_ref, core), (away_ref, 1 - core)):
        for y in range(NY):
            rows = pl.ds(pl.multiple_of((NC * y + c) * 96, 8), 96)
            ref[y * NZ : (y + 1) * NZ, :, lanes] = (
                grad_ref[rows, :].reshape(NZ, 24, -1).astype(BF)
            )


def feed_back_kernel(closing, core_ref, *refs):
    dffn_ref, shrink_ref, slope_ref, low_ref, expand_ref, before_ref = refs[:6]
    if closing:
        normed_ref, inverse_ref, vec_ref = refs[6:9]
        here_ref, away_ref, bias_ref, dresidual_ref, dbranch_ref, sums_ref = refs[11:17]
        grad_ref, total_ref = refs[17:]
    else:
        here_ref, away_ref, bias_ref, total_ref, grad_ref = refs[6:]
    step = pl.program_id(0)
    dpre = (dot_nt(dffn_ref[...], shrink_ref[...]) * slope_ref[...].astype(F32)).astype(BF)
    bias_ref[...] = jnp.sum(dpre.astype(F32), axis=0, keepdims=True)
    more = dot_nt(dpre, expand_ref[...])

    @pl.when(step == 0)
    def _():
        total_ref[...] = before_ref[...] + more

    @pl.when(step > 0)
    def _():
        total_ref[...] += more

    grad_ref[...] = dot_tn(low_ref[...], dpre)
    put_wide(grad_ref, core_ref[0], here_ref, away_ref, slice(None))
    if not closing:
        return

    @pl.when(step == pl.num_programs(0) - 1)
    def _():
        dfirst = total_ref[...]
        normed = normed_ref[...]
        dresidual = norm_back(dfirst, normed, inverse_ref[...], vec_ref[3:4])
        dbranch = dresidual.astype(BF)
        dresidual_ref[...] = dresidual
        dbranch_ref[...] = dbranch
        sums_ref[0:1] = jnp.sum(dfirst * normed, axis=0, keepdims=True)
        sums_ref[1:2] = jnp.sum(dfirst, axis=0, keepdims=True)
        sums_ref[2:3] = jnp.sum(dbranch.astype(F32), axis=0, keepdims=True)


def feed_back_call(core, dffn, shrink, slope, low, layer, expand_block, before, rest=None):
    tokens, width = dffn.shape
    wide = slope.shape[1]
    steps = wide // width // 2
    closing = rest is not None
    at = steps if closing else 0
    half = ((NY * NZ, 24, wide), BF)
    half_spec = pl.BlockSpec((NY * NZ, 24, width), lambda j: (0, 0, at + j))
    flat = pl.BlockSpec((tokens, width), lambda j: (0, 0))
    outs = [half, half, ((1, wide // 2), F32), ((tokens, width), F32)]
    out_specs = [half_spec, half_spec, pl.BlockSpec((1, width), lambda j: (0, j)), flat]
    ins = [core, dffn, shrink, slope, low, layer, before]
    in_specs = [
        pl.BlockSpec(memory_space=pltpu.SMEM),
        whole_spec(dffn),
        pl.BlockSpec((width, width), lambda j: (at + j, 0)),
        pl.BlockSpec((tokens, width), lambda j: (0, at + j)),
        whole_spec(low),
        pl.BlockSpec((width, width), lambda j: (0, expand_block + at + j)),
        whole_spec(before),
    ]
    if closing:
        outs += [((tokens, width), BF), ((8, width), F32)]
        out_specs += [flat, pl.BlockSpec((8, width), lambda j: (0, 0))]
        ins += rest
        in_specs += [whole_spec(a) for a in rest[:3]] + [pl.BlockSpec(memory_space=pl.ANY)] * 2
    return pl.pallas_call(
        functools.partial(feed_back_kernel, closing),
        grid=(steps,),
        in_specs=in_specs,
        out_specs=out_specs,
        out_shape=[jax.ShapeDtypeStruct(shape, kind) for shape, kind in outs],
        scratch_shapes=[pltpu.VMEM((width, width), F32)]
        + ([pltpu.VMEM((tokens, width), F32)] if closing else []),
        input_output_aliases={10: 0, 11: 1} if closing else {},
        compiler_params=pltpu.CompilerParams(vmem_limit_bytes=LIMIT),
        cost_estimate=pl.CostEstimate(flops=1000, bytes_accessed=1000, transcendentals=0),
    )(*ins)


def last_kernel(
    core_ref,
    x_ref,
    dfused_ref,
    attended_ref,
    dbranch_ref,
    fused_ref,
    low_ref,
    high_ref,
    bias_ref,
    here_ref,
    away_ref,
    grad_ref,
    sums_ref,
    flat_ref,
):
    width = x_ref.shape[1]
    core = core_ref[0]
    flat_ref[...] = jnp.zeros(flat_ref.shape, F32)
    rows = [
        fused_ref[:, :width],
        fused_ref[:, 2 * width :],
        high_ref[2:3],
        high_ref[0:1],
        high_ref[1:2],
        low_ref[5:6],
        low_ref[3:4],
        low_ref[4:5],
        low_ref[0:1],
        low_ref[1:2],
        low_ref[2:3],
    ]
    for i, row in enumerate(rows):
        flat_ref[i : i + 1] = row
    sums = flat_ref[...].T
    lane = lax.broadcasted_iota(jnp.int32, sums.shape, 1)
    for i in range(4):
        sums = jnp.where(lane == len(rows) + i, bias_ref[:, i : i + 1], sums)
    sums_ref[...] = sums
    for i in range(4):
        lanes = slice(i * width, (i + 1) * width)
        if i < 3:
            grad_ref[i % 2] = dot_tn(x_ref[...], dfused_ref[:, lanes])
        else:
            grad_ref[i % 2] = dot_tn(attended_ref[...], dbranch_ref[...])
        put_wide(grad_ref.at[i % 2], core, here_ref, away_ref, lanes)
    put_wide(sums_ref, core, here_ref, away_ref, slice(4 * width, 4 * width + 128))


def last_call(core, *ins):
    width = ins[0].shape[1]
    out = ((NY * NZ, 24, 4 * width + 128), BF)
    half_spec = pl.BlockSpec(out[0], lambda *_: (0, 0, 0))
    return call(
        last_kernel,
        (1,),
        (core,) + ins,
        [pl.BlockSpec(memory_space=pltpu.SMEM)] + [whole_spec(a) for a in ins],
        [out, out],
        [half_spec, half_spec],
        [
            pltpu.VMEM((2, width, width), F32),
            pltpu.VMEM((width, 128), F32),
            pltpu.VMEM((128, width), F32),
        ],
        1000,
        1000,
    )


def pair_kernel(own_ref, got_ref, out_ref):
    out_ref[...] = (own_ref[...].astype(F32) + got_ref[...].astype(F32)).astype(BF)


def pair_call(own, got):
    places, rows, width = own.shape
    spec = pl.BlockSpec((places // 4, rows, width), lambda i: (i, 0, 0))
    return call(
        pair_kernel, (4,), (own, got), [spec] * 2, [(own.shape, BF)], [spec], [], 1000, 1000
    )[0]


def feed_kernel(
    low_ref,
    expand_ref,
    bias_ref,
    tall_ref,
    first_ref,
    vec_ref,
    select_ref,
    dense_ref,
    act_ref,
    slope_ref,
    shrink_ref,
    settled_ref,
    normed2_ref,
    inverse2_ref,
    picked_ref,
    head_ref,
    spread_ref,
    normed3_ref,
    inverse3_ref,
    slope3_ref,
    total_ref,
    rows_ref,
):
    step = pl.program_id(0)
    width = low_ref.shape[1]
    groups, places, rows, _ = rows_ref.shape
    for k in range(places):
        part = tall_ref[:, k * width : (k + 1) * width].astype(F32)
        rows_ref[:, k] = part.reshape(groups, rows, width)
    shrink = rows_ref[...].reshape(width, width).astype(BF)
    shrink_ref[...] = shrink
    pre = dot_nn(low_ref[...], expand_ref[...]) + bias_ref[...]
    half = 0.5 * (1.0 + lax.erf(pre * HALF_ROOT))
    act = (pre * half).astype(BF)
    act_ref[...] = act
    slope_ref[...] = (half + pre * NORMAL_PEAK * jnp.exp(-0.5 * pre * pre)).astype(BF)
    more = dot_nn(act, shrink)

    @pl.when(step == 0)
    def _():
        total_ref[...] = first_ref[...] + more

    @pl.when(step > 0)
    def _():
        total_ref[...] += more

    @pl.when(step == pl.num_programs(0) - 1)
    def _():
        second = total_ref[...] + vec_ref[5:6]
        settled, normed2, inverse2 = layer_norm(second, vec_ref[6:7], vec_ref[7:8])
        low = settled.astype(BF)
        settled_ref[...] = low
        normed2_ref[...] = normed2
        inverse2_ref[...] = inverse2
        picked = dot_nn(select_ref[...], low).astype(BF)
        picked_ref[...] = picked
        dense = dot_nn(picked, dense_ref[...]) + vec_ref[8:9]
        value, normed3, inverse3 = layer_norm(gelu_value(dense), vec_ref[9:10], vec_ref[10:11])
        head = value.astype(BF)
        head_ref[...] = head
        for i in range(spread_ref.shape[0]):
            spread_ref[i] = head
        normed3_ref[...] = normed3
        inverse3_ref[...] = inverse3
        slope3_ref[...] = gelu_slope(dense)


def feed_call(low, layer, expand_block, dense_block, b_expand, first, vec, select):
    tokens, width = low.shape
    wide = b_expand.shape[0]
    steps = wide // width
    count = select.shape[0]
    places = NY * NC * NZ // steps
    rows = layer.shape[0] // (NY * NC * NZ)
    bias = b_expand[None, :]
    chunk = pl.BlockSpec((tokens, width), lambda j: (0, j))
    outs = [
        ((tokens, wide), BF),
        ((tokens, wide), BF),
        ((wide, width), BF),
        ((tokens, width), BF),
        ((tokens, width), F32),
        ((tokens, 1), F32),
        ((count, width), BF),
        ((count, width), BF),
        ((NY * NZ, count, width), BF),
        ((count, width), F32),
        ((count, 1), F32),
        ((count, width), F32),
    ]
    out_specs = [chunk, chunk, pl.BlockSpec((width, width), lambda j: (j, 0))]
    for shape, _ in outs[3:]:
        out_specs.append(
            pl.BlockSpec(shape, (lambda j: (0, 0)) if len(shape) == 2 else (lambda j: (0, 0, 0)))
        )
    return call(
        feed_kernel,
        (steps,),
        (low, layer, bias, layer, first, vec, select, layer),
        [
            whole_spec(low),
            pl.BlockSpec((width, width), lambda j: (0, expand_block + j)),
            pl.BlockSpec((1, width), lambda j: (0, j)),
            pl.BlockSpec((places * rows, NX * width), lambda j: (j, 0)),
            whole_spec(first),
            whole_spec(vec),
            whole_spec(select),
            pl.BlockSpec((width, width), lambda j: (0, dense_block)),
        ],
        outs,
        out_specs,
        [pltpu.VMEM((tokens, width), F32), pltpu.VMEM((places, NX, rows, width), F32)],
        1000,
        1000,
    )


def body(
    hidden_in,
    out_grad,
    segments,
    mask_pos,
    mask_labels,
    loss_scale,
    w_qkv,
    b_query,
    b_value,
    w_attn,
    b_attn,
    attn_gain,
    attn_shift,
    w_expand,
    b_expand,
    w_shrink,
    b_shrink,
    ffn_gain,
    ffn_shift,
    w_dense,
    b_dense,
    dense_gain,
    dense_shift,
    w_vocab,
    b_vocab,
):
    micro, block, width = hidden_in.shape
    tokens = micro * block
    heads = width // HEAD_DIM
    factor = HEAD_DIM ** (-0.5)
    at = {axis: lax.axis_index(axis) for axis in EVERY}
    core = at["c"].astype(jnp.int32)[None]

    vectors = (
        b_query,
        b_value,
        b_attn,
        attn_gain,
        attn_shift,
        b_shrink,
        ffn_gain,
        ffn_shift,
        b_dense,
        dense_gain,
        dense_shift,
    )
    small = after(jnp.stack(vectors))[0].T
    small = jnp.concatenate([small, b_expand.reshape(w_qkv.shape[0], -1)], axis=1)
    small = jnp.pad(small, ((0, 0), (0, 128 - small.shape[1])))
    fused = jnp.concatenate([w_expand, w_qkv, w_attn, w_dense, small], axis=1)
    fused = gather_x(fused).reshape(-1, fused.shape[1])
    tall = gather_x(w_shrink)
    tall = tall.transpose(1, 0, 2).reshape(fused.shape[0], -1)
    layer = lax.all_gather(
        jnp.concatenate([tall, fused], axis=1), ("y", "c", "z"), axis=0, tiled=True
    )
    own_w = w_vocab.T
    piece_w = [own_w] + [fetch(own_w, "x", k) for k in (1, 2, 3)]
    piece_b = [b_vocab] + [fetch(b_vocab, "x", k) for k in (1, 2, 3)]
    half_w = jnp.stack(piece_w)
    half_b = jnp.stack(piece_b)
    per = own_w.shape[0]
    vocab_w = jnp.concatenate([half_w, fetch(half_w, "c", 1)]).reshape(-1, width)
    vocab_b = jnp.concatenate([half_b, fetch(half_b, "c", 1)]).reshape(-1).astype(F32)
    start = jnp.stack(
        [
            (((at["y"] * NC + (at["c"] + kc) % NC) * NZ + at["z"]) * NX + (at["x"] + kx) % NX)
            * per
            for kc in range(NC)
            for kx in range(NX)
        ]
    )
    column = (start[:, None] + jnp.arange(per, dtype=jnp.int32)[None, :]).reshape(-1)

    flat_labels = mask_labels.reshape(micro, -1)
    counts = jnp.sum((flat_labels >= 0).astype(F32), axis=1)
    norms = 1.0 / (counts * micro)
    slots = mask_labels.shape[-1]
    peers = NZ * NX
    grid = mask_labels.reshape(micro, NY, NC, peers, NZ, NX, slots)
    grid = lax.dynamic_index_in_dim(grid, at["c"], 2, False)
    grid = lax.dynamic_index_in_dim(grid, at["x"], 4, False)
    labels = grid.transpose(1, 3, 0, 2, 4).reshape(-1)
    rows = micro * peers * slots
    row_norm = jnp.broadcast_to(norms[None, :, None], (NY * NZ, micro, peers * slots)).reshape(-1)
    live = (labels >= 0).astype(F32)
    row_weight = live * row_norm
    hit = labels[:, None] == column[None, :]
    scale = loss_scale * row_weight
    own_first = (at["y"] * NZ + at["z"]) * rows
    own_weight = lax.dynamic_slice_in_dim(row_weight, own_first, rows)
    label_w = matmul(hit.astype(BF), vocab_w)
    label_b = jnp.sum(jnp.where(hit, vocab_b, 0.0), axis=1, keepdims=True)
    label_w = jnp.concatenate([label_w, jnp.pad(label_b, ((0, 0), (0, 127)))], axis=1)
    label_w = label_w.astype(BF).reshape(NY * NZ, rows, -1)
    positions = mask_pos.reshape(micro, -1)
    shifted = jnp.where(
        positions >= 0, positions + block * jnp.arange(micro, dtype=jnp.int32)[:, None], -1
    ).reshape(-1)
    select = (shifted[:, None] == jnp.arange(tokens, dtype=jnp.int32)[None, :]).astype(BF)

    scale, labels = scale[:, None], labels[:, None]
    layer, label_w, vocab_w, select, scale, labels = after(
        layer, label_w, vocab_w, select, scale, labels
    )
    label_w = swap(label_w, ("y", "z"))
    ends = [NX * width, w_expand.shape[1], 3 * width, width, width, 128]
    ends = [sum(ends[: i + 1]) for i in range(len(ends))]
    expand_full = layer[:, ends[0] : ends[1]]
    qkv_full = layer[:, ends[1] : ends[2]]
    attn_block = ends[2] // width
    dense_full = layer[:, ends[3] : ends[4]]
    vec_full = layer[:, ends[4] :]
    rows_of = vec_full[:, :16].T.astype(F32)
    (
        b_query,
        b_value,
        b_attn,
        attn_gain,
        attn_shift,
        b_shrink,
        ffn_gain,
        ffn_shift,
        b_dense,
        dense_gain,
        dense_shift,
    ) = (rows_of[i] for i in range(len(vectors)))
    b_expand = vec_full[:, 11:15].astype(F32).reshape(-1)

    x = hidden_in.reshape(tokens, width)
    qkv, probs, attended, first, first_low, normed1, inverse1 = attention_forward(
        x, segments, layer, attn_block - 3, rows_of
    )
    (
        act,
        slope,
        shrink_full,
        settled_low,
        normed2,
        inverse2,
        picked,
        head_out,
        head_sent,
        normed3,
        inverse3,
        slope3,
    ) = feed_call(first_low, layer, 4, attn_block + 1, b_expand, first, rows_of, select)

    head_sent, label_w = after(head_sent, label_w)
    label_w = jnp.sum(label_w.astype(F32), axis=0)
    label_w, label_b = label_w[:, :width], label_w[:, width]
    spread = swap(head_sent, ("y", "z")).reshape(-1, width)
    expl, stat, part = logits_call(spread, vocab_w, vocab_b, column, labels, rows)
    part = swap(part, ("y", "z"))
    scalars = jnp.stack(
        [label_b, own_weight, loss_scale * own_weight, inverse3[:, 0]], axis=1
    )
    lse, loss_own, g_dense, dsecond, dffn, sums_a = merge_call(
        own_first.astype(jnp.int32)[None],
        part,
        head_out,
        label_w,
        jnp.pad(scalars, ((0, 0), (0, 124))),
        normed3,
        slope3,
        rows_of,
        picked,
        select,
        out_grad.reshape(tokens, width),
        normed2,
        inverse2,
        layer=layer,
        dense_block=attn_block + 1,
    )

    tall_pair = shrink_call(core, act, dffn, g_dense, loss_own)
    tall_here, tall_away, dffn = after(*tall_pair, dffn)
    tall_pair = (tall_here, give(tall_away, "c", 1))
    wide_here, wide_away, bias_low, half_first = feed_back_call(
        core, dffn, shrink_full, slope, first_low, layer, 4, dsecond
    )
    half_first, tall_mine = after(half_first, add_cores(tall_pair))
    wide_here, wide_away, bias_high, dresidual, dbranch, sums_b = feed_back_call(
        core,
        dffn,
        shrink_full,
        slope,
        first_low,
        layer,
        4,
        half_first,
        [normed1, inverse1, rows_of, wide_here, wide_away],
    )
    g_expand_bias = jnp.concatenate([bias_low, bias_high], axis=1)
    wide_pair = (wide_here, give(wide_away, "c", 1))
    tall_all = swap(tall_mine, ("y", "z"))
    dfused, fused_sum = attention_backward(dbranch, qkv, probs, layer, attn_block)

    last_here, last_away = last_call(
        core,
        x,
        dfused,
        attended,
        dbranch,
        fused_sum,
        sums_a,
        sums_b,
        g_expand_bias.reshape(width, -1),
    )
    last_away, wide_mine, tall_all = after(last_away, pair_call(*wide_pair), tall_all)
    last_pair = (last_here, give(last_away, "c", 1))
    wide_all = swap(wide_mine, ("y", "z"))
    last_mine, wide_all = after(add_cores(last_pair), wide_all)
    last_all = swap(last_mine, ("y", "z"))

    lse, wide_mine = after(lse, wide_mine)
    grad_w, grad_b = decoder_call(expl, spread, column, labels, scale, stat, lse)
    grad_b = grad_b.reshape(NC, NX, 1, per)
    grad_b = jnp.pad(grad_b, ((0, 0), (0, 0), (0, 7), (0, width - per))).astype(BF)
    grad_w = grad_w.reshape(NC, NX, per, width)
    grad_w, grad_away = (jnp.concatenate([grad_w[i], grad_b[i]], axis=1) for i in range(NC))
    grad_w, grad_away, wide_all = after(grad_w, grad_away, wide_all)
    grad_away, tall_all = after(give(grad_away, "c", 1), tall_all)
    grad_w = add_cores((grad_w, grad_away))
    grad_w = total([grad_w[0]] + [give(grad_w[k], "x", k) for k in (1, 2, 3)])

    tall = jnp.sum(tall_all[:, :120].astype(F32), axis=0).astype(BF)
    loss_row = split_three(jnp.sum(tall_all[:, 120, :6].astype(F32)))[:128]
    tall_low = tall[:96].reshape(NX, 4, 6, width).transpose(0, 2, 1, 3).reshape(NX, 6, 4 * width)
    early = jnp.concatenate(
        [
            tall_low,
            tall[96:].reshape(NX, 6, width),
            jnp.broadcast_to(loss_row, (NX, 6, 128)),
        ],
        axis=2,
    )
    wide = jnp.sum(wide_all.astype(F32), axis=0).astype(BF)
    last_all, grad_w, dfused = after(last_all, grad_w, dfused)
    dinput = dresidual + matmul_nt(dfused, qkv_full)
    g_vocab, g_vocab_bias = grad_w[:per].T, grad_w[per, :per]
    last = jnp.sum(last_all.astype(F32), axis=0).astype(BF)
    last = sum_x(
        jnp.concatenate([early, wide.reshape(NX, 6, -1), last.reshape(NX, 6, -1)], axis=2)
    )
    ends = [4 * width, width, 128, w_expand.shape[1], 3 * width, width, 128]
    ends = [sum(ends[: i + 1]) for i in range(len(ends))]
    g_shrink = last[:, : ends[0]].reshape(6, 4, width).transpose(1, 0, 2).reshape(24, width)
    g_dense = last[:, ends[0] : ends[1]]
    loss = jnp.sum(last[0, ends[1] : ends[1] + 3])
    g_expand = last[:, ends[2] : ends[3]]
    g_qkv = last[:, ends[3] : ends[4]]
    g_attn = last[:, ends[4] : ends[5]]
    sums = last[:, ends[5] :]
    return (
        settled_low.reshape(hidden_in.shape),
        loss,
        dinput.reshape(hidden_in.shape),
        g_qkv,
        sums[:, 0],
        sums[:, 1],
        g_attn,
        sums[:, 2],
        sums[:, 3],
        sums[:, 4],
        g_expand,
        sums[:, 11:15].reshape(-1),
        g_shrink,
        sums[:, 5],
        sums[:, 6],
        sums[:, 7],
        g_dense,
        sums[:, 8],
        sums[:, 9],
        sums[:, 10],
        g_vocab,
        g_vocab_bias,
    )


def solution(mesh):
    split = Mesh(mesh.devices.reshape(NY, NC, NZ, NX), EVERY)
    whole, one = P(), P(EVERY)
    tokens3 = P(None, EVERY, None)
    matrix = P(EVERY, None)
    in_specs = (
        tokens3,
        tokens3,
        P(None, EVERY),
        P(None, EVERY, None, None),
        whole,
        whole,
        matrix,
        one,
        one,
        matrix,
        one,
        one,
        one,
        matrix,
        one,
        matrix,
        one,
        one,
        one,
        matrix,
        one,
        one,
        one,
        P(None, EVERY),
        one,
    )
    out_specs = (
        tokens3,
        whole,
        tokens3,
        matrix,
        one,
        one,
        matrix,
        one,
        one,
        one,
        matrix,
        one,
        matrix,
        one,
        one,
        one,
        matrix,
        one,
        one,
        one,
        P(None, EVERY),
        one,
    )
    return jax.shard_map(body, mesh=split, in_specs=in_specs, out_specs=out_specs, check_vma=False)
```
